32 devices in a mesh: seq: 16 (over z, y, x), batch: 2 (over core).
Axes of the slice: x: 2, y: 2, z: 4, core: 2. Of those that a mesh axis runs over, the one named last changes fastest.
Arguments:
- block_input: float32 [2, 4096, 768], P('batch', 'seq'), may hold values from -6 to 6
- ln1_gain: float32 [768], replicated, may hold values from 0.5 to 1.5
- ln1_bias: float32 [768], replicated, may hold values from -0.5 to 0.5
- w_qkv: bfloat16 [768, 2304], replicated, may hold values from -0.3125 to 0.3125
- w_out: bfloat16 [768, 768], replicated, may hold values from -0.875 to 0.875
- ln2_gain: float32 [768], replicated, may hold values from 0.5 to 1.5
- ln2_bias: float32 [768], replicated, may hold values from -0.5 to 0.5
- w_up: bfloat16 [768, 3072], replicated, may hold values from -0.21875 to 0.21875
- w_down: bfloat16 [3072, 768], replicated, may hold values from -0.109375 to 0.109375
- length_draw: int32 [2], P('batch'), may hold values from 0 to 16383
- threshold_index: int32 [1], replicated, may hold values from 0 to 255
- grad_out: float32 [2, 4096, 768], P('batch', 'seq'), may hold values from -6 to 6
Outputs:
- layer_out: float32 [2, 4096, 768], P('batch', 'seq')
- grad_x: float32 [2, 4096, 768], P('batch', 'seq')
- grad_ln1_gain: float32 [768], replicated
- grad_ln1_bias: float32 [768], replicated
- grad_w_qkv: float32 [768, 2304], replicated
- grad_w_out: float32 [768, 768], replicated
- grad_ln2_gain: float32 [768], replicated
- grad_ln2_bias: float32 [768], replicated
- grad_w_up: float32 [768, 3072], replicated
- grad_w_down: float32 [3072, 768], replicated
- pruned_share: float32 [1], replicated
The draws below stay inside these ranges and needn't reach their ends.
Inputs may be any that keep to these rules, and one draw needn't show every extreme that they name: Group g holds one sequence of 3841 + (length_draw[g] mod 256) tokens from its first slot; the other slots are padding. The threshold is threshold_index / 128.
All inputs are finite; a program needn't handle non-finite values.
Results may differ from the reference program's by a relative error of at most 0.012.
The reference program's roundings to bfloat16 on the way count: a program that leaves them out, or rounds other values in their place, can miss the bound.
Values may be sent and summed in bfloat16 or wider, within the bound.
A program may use at most 512 MiB of HBM per device.

```python
import jax
import jax.numpy as jnp
from jax import lax

D = 768
HEADS = 12
HEAD_DIM = 64
FF = 3072
TOK_DEV = 256
GROUPS = 2
TOKENS_G = 4096


def steps_of(key, shape, shards, smallest, high):
    level, own = 1.0, jax.random.fold_in(key, 6)
    for axis_at, blocks in shards:
        draws = jnp.exp(jax.random.uniform(jax.random.fold_in(own, axis_at), (blocks,), jnp.float32, smallest / len(shards), high / len(shards)))
        level = level * jnp.repeat(draws, shape[axis_at] // blocks).reshape([-1 if axis == axis_at else 1 for axis in range(len(shape))])
    return level


def gaussian(key, extent, width, limit, shards=(), held_as=jnp.bfloat16):
    result = jax.random.normal(key, extent, jnp.float32) * width
    if len(shards) > 0:
        result = steps_of(key, extent, shards, -0.22, 0.18) * result
    return jnp.clip(result, min=-limit, max=limit).astype(held_as)


def setup_inputs(seed: int = 0) -> dict:
    seeds = jax.random.split(jax.random.key(seed), 13)
    return {
        "block_input": gaussian(seeds[0], (GROUPS, TOKENS_G, D), 1.0, 6.0, ((0, 2), (1, 16)), jnp.float32),
        "ln1_gain": jnp.clip(1.0 + 0.1 * jax.random.normal(seeds[1], (D,), jnp.float32), 0.5, 1.5),
        "ln1_bias": jnp.clip(jax.random.uniform(seeds[2], (D,), jnp.float32, -0.5, 0.5), -0.5, 0.5),
        "w_qkv": gaussian(seeds[3], (D, 3 * D), (D // 2) ** -0.5, 0.3125),
        "w_out": gaussian(seeds[4], (D, D), (D // 16) ** -0.5, 0.875),
        "ln2_gain": jnp.clip(1.0 + 0.1 * jax.random.normal(seeds[5], (D,), jnp.float32), 0.5, 1.5),
        "ln2_bias": jnp.clip(jax.random.uniform(seeds[6], (D,), jnp.float32, -0.5, 0.5), -0.5, 0.5),
        "w_up": gaussian(seeds[7], (D, FF), D ** -0.5, 0.21875),
        "w_down": gaussian(seeds[8], (FF, D), FF ** -0.5, 0.109375),
        "length_draw": jax.random.randint(seeds[9], (GROUPS,), 0, 64 * TOK_DEV).astype(jnp.int32),
        "threshold_index": jax.random.randint(seeds[10], (1,), 0, 256).astype(jnp.int32),
        "grad_out": gaussian(seeds[11], (GROUPS, TOKENS_G, D), 1.0, 6.0, ((0, 2), (1, 16)), jnp.float32),
    }


@jax.custom_vjp
def low(v):
    return lax.optimization_barrier(v.astype(jnp.bfloat16)).astype(jnp.float32)

@jax.custom_vjp
def low_back(v):
    return v

def low_keep(v):
    return (low(v), None)

def low_pass(kept, grad):
    return (grad,)

def back_keep(v):
    return (v, None)

def back_low(kept, grad):
    return (low(grad),)
low.defvjp(low_keep, low_pass)
low_back.defvjp(back_keep, back_low)
epsilon = 1e-05
negative = -1e+30
select_scale = 3.0
highest = lax.Precision.HIGHEST

def layer_norm(values, norm_gain, norm_bias):
    row_mean = lax.optimization_barrier(jnp.mean(values, axis=-1, keepdims=True))
    centred = values - row_mean
    variance = lax.optimization_barrier(jnp.mean(centred * centred, axis=-1, keepdims=True))
    return centred * lax.rsqrt(variance + epsilon) * norm_gain + norm_bias

def gelu_tanh(values):
    return jax.nn.gelu(values, approximate=True)

def group_attention(inputs):
    queries, keys, values, valids, threshold = inputs
    group_len = queries.shape[0]
    block_rows = min(512, group_len)
    block_count = group_len // block_rows
    key_index = jnp.arange(group_len, dtype=jnp.int32)

    def step(before, item):
        query_block, valid_block, start = item
        rows_here = start + jnp.arange(block_rows, dtype=jnp.int32)
        raw_scores = jnp.einsum('ihd,jhd->hij', query_block, keys, precision=highest) * HEAD_DIM ** (-0.5)
        scores = low_back(raw_scores)
        allowed = (key_index[None, :] <= rows_here[:, None]) & (valids[None, :] | (key_index[None, :] == rows_here[:, None]))
        chosen = (key_index[None, :] < rows_here[:, None]) & (key_index[None, :] >= 1) & valid_block[:, None]
        selection = select_scale / group_len * jnp.maximum(scores[0], 0.0) * chosen.astype(jnp.float32)
        running = jnp.cumsum(selection, axis=0)
        carried = before[None, :] + jnp.concatenate([jnp.zeros((1, group_len), jnp.float32), running[:-1]], axis=0)
        logits = jnp.where(allowed[None], scores - carried[None], negative)
        prob_low = low(jax.nn.softmax(logits, axis=-1))
        mixed = jnp.einsum('hij,jhd->ihd', prob_low, values, precision=highest) * valid_block.astype(jnp.float32)[:, None, None]
        numerator = jnp.sum(jnp.where(chosen, jnp.clip(carried - threshold, 0.0, 1.0), 0.0))
        pair_count = jnp.sum(chosen.astype(jnp.float32))
        return (before + running[-1], (mixed, numerator, pair_count))
    starts = jnp.arange(block_count, dtype=jnp.int32) * block_rows
    blocks_in = (queries.reshape(block_count, block_rows, HEADS, HEAD_DIM), valids.reshape(block_count, block_rows), starts)
    final_totals, outputs = lax.scan(jax.checkpoint(step), jnp.zeros((group_len,), jnp.float32), blocks_in)
    mixed, numerators, counts = outputs
    return (mixed.reshape(group_len, HEADS, HEAD_DIM), jnp.sum(numerators), jnp.sum(counts))

def reference(block_input, ln1_gain, ln1_bias, w_qkv, w_out, ln2_gain, ln2_bias, w_up, w_down, length_draw, threshold_index, grad_out):
    groups = block_input.shape[0]
    tokens_group = block_input.shape[1]
    model_width = block_input.shape[2]
    lengths = tokens_group - TOK_DEV + 1 + length_draw % TOK_DEV
    valids = jnp.arange(tokens_group, dtype=jnp.int32)[None, :] < lengths[:, None]
    threshold = threshold_index[0].astype(jnp.float32) / 128.0
    thresholds = jnp.broadcast_to(threshold, (groups,))

    def heads_of(part):
        return part.reshape(groups, tokens_group, HEADS, HEAD_DIM)

    def forward(tokens, gain_one, bias_one, weight_qkv, weight_out, gain_two, bias_two, weight_up, weight_down):
        normed = low(layer_norm(tokens, gain_one, bias_one))
        projected = low_back(low(jnp.einsum('gtd,de->gte', normed, weight_qkv, precision=highest)))
        queries = heads_of(projected[..., :model_width])
        key_all = heads_of(projected[..., model_width:2 * model_width])
        value_all = heads_of(projected[..., 2 * model_width:])
        mixed, numerators, counts = lax.map(group_attention, (queries, key_all, value_all, valids, thresholds))
        attn_mixed = low_back(low(mixed.reshape(groups, tokens_group, model_width)))
        residual = tokens + low_back(jnp.einsum('gtd,de->gte', attn_mixed, weight_out, precision=highest))
        normed_two = low(layer_norm(residual, gain_two, bias_two))
        hidden = low_back(jnp.einsum('gtd,df->gtf', normed_two, weight_up, precision=highest))
        activated = low(gelu_tanh(hidden))
        branch = low_back(jnp.einsum('gtf,fd->gtd', activated, weight_down, precision=highest))
        return (residual + branch, (jnp.sum(numerators), jnp.sum(counts)))
    primals = tuple((array_in.astype(jnp.float32) for array_in in (block_input, ln1_gain, ln1_bias, w_qkv, w_out, ln2_gain, ln2_bias, w_up, w_down)))
    layer_out, pull_back, totals = jax.vjp(forward, *primals, has_aux=True)
    gradients = pull_back(grad_out.astype(jnp.float32))
    pruned_share = (totals[0] / totals[1]).reshape(1)
    return (layer_out, gradients[0], gradients[1], gradients[2], gradients[3], gradients[4], gradients[5], gradients[6], gradients[7], gradients[8], pruned_share)
```

```python
import functools

import jax
import jax.numpy as jnp
from jax import lax
from jax.experimental import pallas as pl
from jax.experimental.pallas import tpu as pltpu
from jax.sharding import PartitionSpec as P

HEADS = 12
HEAD_DIM = 64
TEAMS = 4
TEAM_HEADS = HEADS // TEAMS
TEAM_WIDTH = TEAM_HEADS * HEAD_DIM
QUERY_WIDTH = TEAM_WIDTH + HEAD_DIM

epsilon = 1e-05
negative = -1e30
select_scale = 3.0
VMEM_BYTES = 60 * 2**20
MESH = pl.DeviceIdType.MESH


def peers_of(scope):
    count = lax.axis_size("seq")
    lanes = count // TEAMS
    me = lax.axis_index("seq")
    team, lane = me // lanes, lax.rem(me, lanes)
    if scope == "team":
        return lane, lanes, lambda k: team * lanes + k
    if scope == "lane":
        return team, TEAMS, lambda k: k * lanes + lane
    return me, count, lambda k: k


def exchange(scope, kinds, arrays, collective):
    number = len(arrays)

    def body(*refs):
        sources, targets = refs[:number], refs[number : 2 * number]
        send, receive, local = refs[2 * number :]
        mine, peers, index_of = peers_of(scope)
        barrier = pltpu.get_barrier_semaphore()
        for k in range(1, peers):
            pl.semaphore_signal(
                barrier,
                inc=1,
                device_id={"seq": index_of(lax.rem(mine + k, peers))},
                device_id_type=MESH,
            )
        pl.semaphore_wait(barrier, peers - 1)
        copies = []
        for k in range(1, peers):
            peer = lax.rem(mine + k, peers)
            for n in range(number):
                copy = pltpu.make_async_remote_copy(
                    src_ref=sources[n] if kinds[n] == "gather" else sources[n].at[peer],
                    dst_ref=targets[n].at[mine],
                    send_sem=send.at[n, k],
                    recv_sem=receive.at[n, k],
                    device_id={"seq": index_of(peer)},
                    device_id_type=MESH,
                )
                copy.start()
                copies.append(copy)
        for n in range(number):
            copy = pltpu.make_async_copy(
                sources[n] if kinds[n] == "gather" else sources[n].at[mine],
                targets[n].at[mine],
                local.at[n],
            )
            copy.start()
            copies.append(copy)
        for copy in copies:
            copy.wait()

    count = {"team": lax.axis_size("seq") // TEAMS, "lane": TEAMS, "all": lax.axis_size("seq")}[scope]
    shapes = [
        jax.ShapeDtypeStruct(((count,) if kind == "gather" else ()) + x.shape, x.dtype)
        for kind, x in zip(kinds, arrays)
    ]
    return pl.pallas_call(
        body,
        out_shape=shapes,
        in_specs=[pl.BlockSpec(memory_space=pl.ANY)] * number,
        out_specs=[pl.BlockSpec(memory_space=pl.ANY)] * number,
        scratch_shapes=[
            pltpu.SemaphoreType.DMA((number, count)),
            pltpu.SemaphoreType.DMA((number, count)),
            pltpu.SemaphoreType.DMA((number,)),
        ],
        compiler_params=pltpu.CompilerParams(
            collective_id=collective, has_side_effects=True, vmem_limit_bytes=VMEM_BYTES
        ),
    )(*arrays)


def dot(left, right):
    return jnp.dot(left, right, preferred_element_type=jnp.float32)


def attend_body(
    length_ref,
    threshold_ref,
    q_ref,
    kk_ref,
    vv_ref,
    out_ref,
    mass_ref,
    carried_ref,
    excess_ref,
    key_heads,
    value_rows,
    running,
    logits,
    *,
    blocks,
    rows,
):
    lanes = blocks // TEAMS
    me = lax.axis_index("seq")
    team, lane = me // lanes, lax.rem(me, lanes)
    i = pl.program_id(0)
    scale = select_scale / (blocks * rows)

    @pl.when(i == 0)
    def _():
        running[...] = jnp.zeros_like(running)
        excess_ref[...] = jnp.zeros_like(excess_ref)
        for z in range(TEAMS):
            for h in range(TEAM_HEADS + 1):
                key_heads[h, z] = kk_ref[z, :, h * HEAD_DIM : (h + 1) * HEAD_DIM]
            value_rows[z] = vv_ref[z].T

    active = jnp.where(i >= lane, (i - lane) // lanes + 1, 0)
    q_rows = q_ref[0, 0].T
    heads = [q_rows[h * HEAD_DIM : (h + 1) * HEAD_DIM] for h in range(TEAM_HEADS + 1)]
    key_iota = lax.broadcasted_iota(jnp.int32, (rows, rows), 0)
    query_iota = lax.broadcasted_iota(jnp.int32, (rows, rows), 1)
    earlier = (key_iota < query_iota).astype(jnp.bfloat16)
    ones = jnp.ones((rows, rows), jnp.bfloat16)
    query_pos = i * rows + query_iota
    query_valid = query_pos < length_ref[0]
    threshold = threshold_ref[0]

    def score(z, peaks):
        key_pos = (z * lanes + lane) * rows + key_iota
        first = dot(key_heads[TEAM_HEADS, z], heads[TEAM_HEADS])
        chosen = (key_pos < query_pos) & (key_pos >= 1)
        selected = jnp.where(chosen, jnp.maximum(first, 0.0) * scale, 0.0).astype(jnp.bfloat16)
        carried = running[z] + dot(selected, earlier)
        running[z] = running[z] + dot(selected, ones)

        @pl.when(lax.rem(i, TEAMS) == team)
        def _():
            clipped = jnp.where(
                chosen & query_valid, jnp.clip(carried - threshold, 0.0, 1.0), 0.0
            )
            excess_ref[...] += jnp.sum(clipped.reshape(rows // 8, 8, rows), axis=0)

        carried = jnp.where(key_pos <= query_pos, carried, -negative)
        carried_ref[0, z] = carried
        result = []
        for h in range(TEAM_HEADS):
            logit = dot(key_heads[h, z], heads[h]) - carried
            logits[h, z] = logit
            result.append(
                jnp.maximum(peaks[h], jnp.max(logit.reshape(rows // 8, 8, rows), axis=0))
            )
        return tuple(result)

    start = tuple(jnp.full((8, rows), negative, jnp.float32) for _ in range(TEAM_HEADS))
    peaks = lax.fori_loop(0, active, score, start)
    peaks = [jnp.max(peak, axis=0, keepdims=True) for peak in peaks]

    def gather_values(z, state):
        masses, mixed = state
        new_masses, new_mixed = [], []
        for h in range(TEAM_HEADS):
            terms = jnp.exp(logits[h, z] - peaks[h])
            new_masses.append(masses[h] + jnp.sum(terms.reshape(rows // 8, 8, rows), axis=0))
            values = value_rows[z, h * HEAD_DIM : (h + 1) * HEAD_DIM, :]
            new_mixed.append(mixed[h] + dot(values, terms.astype(jnp.bfloat16)))
        return tuple(new_masses), tuple(new_mixed)

    masses, mixed = lax.fori_loop(
        0,
        active,
        gather_values,
        (
            tuple(jnp.zeros((8, rows), jnp.float32) for _ in range(TEAM_HEADS)),
            tuple(jnp.zeros((HEAD_DIM, rows), jnp.float32) for _ in range(TEAM_HEADS)),
        ),
    )
    mass_ref[0] = jnp.zeros((8, rows), jnp.float32)
    for h in range(TEAM_HEADS):
        mass = jnp.sum(masses[h], axis=0, keepdims=True)
        mass = jnp.where(active > 0, mass, 1.0)
        out_ref[0, h * HEAD_DIM : (h + 1) * HEAD_DIM, :] = (mixed[h] * (1.0 / mass)).astype(
            jnp.bfloat16
        )
        mass_ref[0, h : h + 1, :] = jnp.where(
            active > 0, peaks[h] + jnp.log(mass), negative
        )


def attend(length, threshold, queries, keys, values, blocks, rows):
    lanes = blocks // TEAMS
    smem = pl.BlockSpec(memory_space=pltpu.SMEM)
    whole = pl.BlockSpec((TEAMS, rows, QUERY_WIDTH), lambda i: (0, 0, 0))
    return pl.pallas_call(
        functools.partial(attend_body, blocks=blocks, rows=rows),
        grid=(blocks,),
        in_specs=[
            smem,
            smem,
            pl.BlockSpec(
                (1, 1, rows, QUERY_WIDTH), lambda i: (lax.rem(i, lanes), i // lanes, 0, 0)
            ),
            whole,
            pl.BlockSpec((TEAMS, rows, TEAM_WIDTH), lambda i: (0, 0, 0)),
        ],
        out_specs=[
            pl.BlockSpec((1, TEAM_WIDTH, rows), lambda i: (i, 0, 0)),
            pl.BlockSpec((1, 8, rows), lambda i: (i, 0, 0)),
            pl.BlockSpec((1, TEAMS, rows, rows), lambda i: (i, 0, 0, 0)),
            pl.BlockSpec((8, rows), lambda i: (0, 0)),
        ],
        out_shape=[
            jax.ShapeDtypeStruct((blocks, TEAM_WIDTH, rows), jnp.bfloat16),
            jax.ShapeDtypeStruct((blocks, 8, rows), jnp.float32),
            jax.ShapeDtypeStruct((blocks, TEAMS, rows, rows), jnp.float32),
            jax.ShapeDtypeStruct((8, rows), jnp.float32),
        ],
        scratch_shapes=[
            pltpu.VMEM((TEAM_HEADS + 1, TEAMS, rows, HEAD_DIM), jnp.bfloat16),
            pltpu.VMEM((TEAMS, TEAM_WIDTH, rows), jnp.bfloat16),
            pltpu.VMEM((TEAMS, rows, rows), jnp.float32),
            pltpu.VMEM((TEAM_HEADS, TEAMS, rows, rows), jnp.float32),
        ],
        compiler_params=pltpu.CompilerParams(vmem_limit_bytes=VMEM_BYTES),
    )(length, threshold, queries, keys, values)


def attend_back_body(
    q_ref,
    grad_ref,
    stat_ref,
    carried_ref,
    kk_ref,
    vv_ref,
    query_grad_ref,
    key_grad_ref,
    value_grad_ref,
    key_heads,
    key_rows,
    value_heads,
    running,
    key_sum,
    value_sum,
    *,
    blocks,
    rows,
):
    lanes = blocks // TEAMS
    lane = lax.rem(lax.axis_index("seq"), lanes)
    step = pl.program_id(0)
    i = blocks - 1 - step
    scale = select_scale / (blocks * rows)

    @pl.when(step == 0)
    def _():
        running[...] = jnp.zeros_like(running)
        key_sum[...] = jnp.zeros_like(key_sum)
        value_sum[...] = jnp.zeros_like(value_sum)
        for z in range(TEAMS):
            for h in range(TEAM_HEADS + 1):
                key_heads[h, z] = kk_ref[z, :, h * HEAD_DIM : (h + 1) * HEAD_DIM]
            for h in range(TEAM_HEADS):
                value_heads[h, z] = vv_ref[z, :, h * HEAD_DIM : (h + 1) * HEAD_DIM]
            key_rows[z] = kk_ref[z].T

    active = jnp.where(i >= lane, (i - lane) // lanes + 1, 0)
    q_rows = q_ref[0, 0].T
    grad_rows = grad_ref[0, 0].T
    span = [slice(h * HEAD_DIM, (h + 1) * HEAD_DIM) for h in range(TEAM_HEADS + 1)]
    q_row = [q_rows[span[h]] for h in range(TEAM_HEADS + 1)]
    q_col = [q_ref[0, 0, :, span[h]] for h in range(TEAM_HEADS + 1)]
    grad_row = [grad_rows[span[h]] for h in range(TEAM_HEADS)]
    grad_col = [grad_ref[0, 0, :, span[h]] for h in range(TEAM_HEADS)]
    mass = [stat_ref[0, 0, h : h + 1, :] for h in range(TEAM_HEADS)]
    inner = [stat_ref[0, 0, TEAM_HEADS + h : TEAM_HEADS + h + 1, :] for h in range(TEAM_HEADS)]
    key_iota = lax.broadcasted_iota(jnp.int32, (rows, rows), 0)
    query_iota = lax.broadcasted_iota(jnp.int32, (rows, rows), 1)
    later = (key_iota > query_iota).astype(jnp.bfloat16)
    ones = jnp.ones((rows, rows), jnp.bfloat16)
    query_pos = i * rows + query_iota

    def back(z, query_sum):
        key_pos = (z * lanes + lane) * rows + key_iota
        carried = carried_ref[0, z]
        total = None
        new_sum = []
        for h in range(TEAM_HEADS):
            probs = jnp.exp(dot(key_heads[h, z], q_row[h]) - carried - mass[h])
            value_sum[h, z] += dot(probs.astype(jnp.bfloat16), grad_col[h])
            grad_logit = probs * (dot(value_heads[h, z], grad_row[h]) - inner[h])
            total = grad_logit if total is None else total + grad_logit
            low = grad_logit.astype(jnp.bfloat16)
            key_sum[h, z] += dot(low, q_col[h])
            new_sum.append(query_sum[h] + dot(key_rows[z, span[h], :], low))
        total = total.astype(jnp.bfloat16)
        select_grad = running[z] - dot(total, later)
        running[z] = running[z] - dot(total, ones)
        first = dot(key_heads[TEAM_HEADS, z], q_row[TEAM_HEADS])
        live = (key_pos < query_pos) & (key_pos >= 1) & (first > 0.0)
        low = jnp.where(live, select_grad * scale, 0.0).astype(jnp.bfloat16)
        key_sum[TEAM_HEADS, z] += dot(low, q_col[TEAM_HEADS])
        new_sum.append(query_sum[TEAM_HEADS] + dot(key_rows[z, span[TEAM_HEADS], :], low))
        return tuple(new_sum)

    query_sum = lax.fori_loop(
        0,
        active,
        back,
        tuple(jnp.zeros((HEAD_DIM, rows), jnp.float32) for _ in range(TEAM_HEADS + 1)),
    )
    for h in range(TEAM_HEADS + 1):
        query_grad_ref[0, span[h], :] = query_sum[h].astype(jnp.bfloat16)

    @pl.when(step == blocks - 1)
    def _():
        for h in range(TEAM_HEADS + 1):
            key_grad_ref[:, :, span[h]] = key_sum[h].astype(jnp.bfloat16)
        for h in range(TEAM_HEADS):
            value_grad_ref[:, :, span[h]] = value_sum[h].astype(jnp.bfloat16)


def attend_back(queries, grads, stats, carried, keys, values, blocks, rows):
    lanes = blocks // TEAMS

    def place(step):
        i = blocks - 1 - step
        return (lax.rem(i, lanes), i // lanes, 0, 0)

    return pl.pallas_call(
        functools.partial(attend_back_body, blocks=blocks, rows=rows),
        grid=(blocks,),
        in_specs=[
            pl.BlockSpec((1, 1, rows, QUERY_WIDTH), place),
            pl.BlockSpec((1, 1, rows, TEAM_WIDTH), place),
            pl.BlockSpec((1, 1, 8, rows), place),
            pl.BlockSpec((1, TEAMS, rows, rows), lambda step: (blocks - 1 - step, 0, 0, 0)),
            pl.BlockSpec((TEAMS, rows, QUERY_WIDTH), lambda step: (0, 0, 0)),
            pl.BlockSpec((TEAMS, rows, TEAM_WIDTH), lambda step: (0, 0, 0)),
        ],
        out_specs=[
            pl.BlockSpec((1, QUERY_WIDTH, rows), lambda step: (blocks - 1 - step, 0, 0)),
            pl.BlockSpec((TEAMS, rows, QUERY_WIDTH), lambda step: (0, 0, 0)),
            pl.BlockSpec((TEAMS, rows, TEAM_WIDTH), lambda step: (0, 0, 0)),
        ],
        out_shape=[
            jax.ShapeDtypeStruct((blocks, QUERY_WIDTH, rows), jnp.bfloat16),
            jax.ShapeDtypeStruct((TEAMS, rows, QUERY_WIDTH), jnp.bfloat16),
            jax.ShapeDtypeStruct((TEAMS, rows, TEAM_WIDTH), jnp.bfloat16),
        ],
        scratch_shapes=[
            pltpu.VMEM((TEAM_HEADS + 1, TEAMS, rows, HEAD_DIM), jnp.bfloat16),
            pltpu.VMEM((TEAMS, QUERY_WIDTH, rows), jnp.bfloat16),
            pltpu.VMEM((TEAM_HEADS, TEAMS, rows, HEAD_DIM), jnp.bfloat16),
            pltpu.VMEM((TEAMS, rows, rows), jnp.float32),
            pltpu.VMEM((TEAM_HEADS + 1, TEAMS, rows, HEAD_DIM), jnp.float32),
            pltpu.VMEM((TEAM_HEADS, TEAMS, rows, HEAD_DIM), jnp.float32),
        ],
        compiler_params=pltpu.CompilerParams(vmem_limit_bytes=VMEM_BYTES),
    )(queries, grads, stats, carried, keys, values)


def layer_norm(values, norm_gain, norm_bias):
    row_mean = jnp.mean(values, axis=-1, keepdims=True)
    centred = values - row_mean
    variance = jnp.mean(centred * centred, axis=-1, keepdims=True)
    return centred * lax.rsqrt(variance + epsilon) * norm_gain + norm_bias


def gelu_tanh(values):
    return jax.nn.gelu(values, approximate=True)


def contract_rows(left_op, right_op):
    return lax.dot_general(
        left_op, right_op, (((0,), (0,)), ((), ())), preferred_element_type=jnp.float32
    )


def contract_cols(left_op, right_op):
    return lax.dot_general(
        left_op, right_op, (((1,), (1,)), ((), ())), preferred_element_type=jnp.float32
    )


def per_device(
    block_input,
    ln1_gain,
    ln1_bias,
    w_qkv,
    w_out,
    ln2_gain,
    ln2_bias,
    w_up,
    w_down,
    length_draw,
    threshold_index,
    grad_out,
):
    rows = block_input.shape[1]
    width = block_input.shape[2]
    blocks = lax.axis_size("seq")
    lanes = blocks // TEAMS
    group_len = blocks * rows
    me = lax.axis_index("seq")
    team = me // lanes
    score_scale = HEAD_DIM ** (-0.5)
    length = group_len - rows + 1 + length_draw % rows
    row_valid = (me * rows + jnp.arange(rows, dtype=jnp.int32) < length[0])[:, None]
    threshold = threshold_index.astype(jnp.float32) / 128.0
    tokens = block_input[0]
    grad_top = grad_out[0]
    grad_top_low = grad_top.astype(jnp.bfloat16)

    normed, ln1_pull = jax.vjp(layer_norm, tokens, ln1_gain, ln1_bias)
    normed_low = normed.astype(jnp.bfloat16)
    (lane_rows,) = exchange("lane", ["gather"], [normed_low], 0)
    lane_rows = lane_rows.reshape(TEAMS * rows, width)

    def columns(part):
        return lax.dynamic_slice_in_dim(w_qkv, part * width + team * TEAM_WIDTH, TEAM_WIDTH, 1)

    query_weight = jnp.concatenate([columns(0), w_qkv[:, :HEAD_DIM]], axis=1)
    key_weight = jnp.concatenate([columns(1), w_qkv[:, width : width + HEAD_DIM]], axis=1)
    queries = (dot(lane_rows, query_weight).astype(jnp.bfloat16) * score_scale).astype(
        jnp.bfloat16
    )
    keys = dot(lane_rows, key_weight).astype(jnp.bfloat16).reshape(TEAMS, rows, QUERY_WIDTH)
    values = dot(lane_rows, columns(2)).astype(jnp.bfloat16).reshape(TEAMS, rows, TEAM_WIDTH)
    (queries,) = exchange("team", ["gather"], [queries.reshape(TEAMS, rows, QUERY_WIDTH)], 1)

    parts, masses, carried, excess = attend(
        length, threshold, queries, keys, values, blocks, rows
    )
    parts, masses = exchange("all", ["spread", "spread"], [parts, masses], 2)
    parts = parts.astype(jnp.float32).reshape(TEAMS, lanes, TEAM_HEADS, HEAD_DIM, rows)
    masses = masses.reshape(TEAMS, lanes, 8, rows)[:, :, :TEAM_HEADS]
    peak = jnp.max(masses, axis=1, keepdims=True)
    shares = jnp.exp(masses - peak)
    mass = jnp.sum(shares, axis=1, keepdims=True)
    shares = shares / mass
    log_mass = (peak + jnp.log(mass))[:, 0]
    head_out = jnp.sum(parts * shares[:, :, :, None, :], axis=1)
    attn_mixed = jnp.where(
        row_valid, head_out.reshape(width, rows).T, 0.0
    ).astype(jnp.bfloat16)

    residual = tokens + dot(attn_mixed, w_out)
    normed_two, ln2_pull = jax.vjp(layer_norm, residual, ln2_gain, ln2_bias)
    normed_two_low = normed_two.astype(jnp.bfloat16)
    hidden = dot(normed_two_low, w_up)
    activated, gelu_pull = jax.vjp(gelu_tanh, hidden)
    activated_low = activated.astype(jnp.bfloat16)
    layer_out = residual + dot(activated_low, w_down)
    grad_w_down = contract_rows(activated_low, grad_top_low)
    grad_hidden_low = gelu_pull(contract_cols(grad_top_low, w_down))[0].astype(jnp.bfloat16)
    grad_w_up = contract_rows(normed_two_low, grad_hidden_low)
    grad_resid_norm, grad_ln2_gain, grad_ln2_bias = ln2_pull(contract_cols(grad_hidden_low, w_up))
    grad_resid = grad_top + grad_resid_norm
    grad_attn_low = grad_resid.astype(jnp.bfloat16)
    grad_w_out = contract_rows(attn_mixed, grad_attn_low)
    grad_mixed = jnp.where(
        row_valid,
        contract_cols(grad_attn_low, w_out).astype(jnp.bfloat16),
        jnp.zeros((), jnp.bfloat16),
    )
    grad_w_down, grad_w_up, grad_w_out = lax.psum(
        (
            grad_w_down.astype(jnp.bfloat16),
            grad_w_up.astype(jnp.bfloat16),
            grad_w_out.astype(jnp.bfloat16),
        ),
        ("seq", "batch"),
    )

    grad_rows = grad_mixed.T.reshape(TEAMS, TEAM_HEADS, HEAD_DIM, rows).astype(jnp.float32)
    inner = jnp.sum(grad_rows * head_out, axis=2)
    stats = jnp.concatenate(
        [log_mass, inner, jnp.zeros((TEAMS, 8 - 2 * TEAM_HEADS, rows), jnp.float32)], axis=1
    )
    grad_cols = jnp.moveaxis(grad_mixed.reshape(rows, TEAMS, TEAM_WIDTH), 1, 0)
    grad_cols, stats = exchange("lane", ["spread", "spread"], [grad_cols, stats], 3)
    grad_cols, stats = exchange("team", ["gather", "gather"], [grad_cols, stats], 4)
    query_grads, key_grads, value_grads = attend_back(
        queries, grad_cols, stats, carried, keys, values, blocks, rows
    )
    (query_grads,) = exchange("all", ["spread"], [query_grads], 5)
    key_grads, value_grads = exchange("lane", ["spread", "spread"], [key_grads, value_grads], 6)

    query_grads = query_grads.astype(jnp.float32).reshape(TEAMS, lanes, QUERY_WIDTH, rows)
    query_grads = jnp.sum(query_grads, axis=1)
    grad_query = query_grads[:, :TEAM_WIDTH].reshape(width, rows)
    grad_query = grad_query.at[:HEAD_DIM].add(jnp.sum(query_grads[:, TEAM_WIDTH:], axis=0))
    grad_query = grad_query.T * score_scale
    key_grads = key_grads.astype(jnp.float32)
    grad_key = jnp.moveaxis(key_grads[:, :, :TEAM_WIDTH], 0, 1).reshape(rows, width)
    grad_key = grad_key.at[:, :HEAD_DIM].add(jnp.sum(key_grads[:, :, TEAM_WIDTH:], axis=0))
    grad_value = jnp.moveaxis(value_grads, 0, 1).reshape(rows, width)
    grad_qkv_low = jnp.concatenate(
        [grad_query.astype(jnp.bfloat16), grad_key.astype(jnp.bfloat16), grad_value], axis=1
    )
    grad_w_qkv = contract_rows(normed_low, grad_qkv_low)
    grad_tokens_norm, grad_ln1_gain, grad_ln1_bias = ln1_pull(contract_cols(grad_qkv_low, w_qkv))
    grad_x = grad_resid + grad_tokens_norm

    pairs = (length[0] - 1).astype(jnp.float32) * (length[0] - 2).astype(jnp.float32) / 2.0
    counts = jnp.stack([jnp.sum(excess), pairs / blocks])
    vectors = jnp.concatenate(
        [grad_ln1_gain, grad_ln1_bias, grad_ln2_gain, grad_ln2_bias, counts]
    )
    grad_w_qkv, vectors = lax.psum(
        (grad_w_qkv.astype(jnp.bfloat16), vectors), ("seq", "batch")
    )
    pruned_share = (vectors[4 * width] / vectors[4 * width + 1]).reshape(1)
    return (
        layer_out[None],
        grad_x[None],
        vectors[:width],
        vectors[width : 2 * width],
        grad_w_qkv.astype(jnp.float32),
        grad_w_out.astype(jnp.float32),
        vectors[2 * width : 3 * width],
        vectors[3 * width : 4 * width],
        grad_w_up.astype(jnp.float32),
        grad_w_down.astype(jnp.float32),
        pruned_share,
    )


def solution(mesh):
    placed = (
        P("batch", "seq", None),
        P(),
        P(),
        P(),
        P(),
        P(),
        P(),
        P(),
        P(),
        P("batch"),
        P(),
        P("batch", "seq", None),
    )
    return jax.shard_map(
        per_device,
        mesh=mesh,
        in_specs=placed,
        out_specs=(
            P("batch", "seq", None),
            P("batch", "seq", None),
            P(),
            P(),
            P(),
            P(),
            P(),
            P(),
            P(),
            P(),
            P(),
        ),
        check_vma=False,
    )
```

```python
import functools

import jax
import jax.numpy as jnp
from jax import lax
from jax.experimental import pallas as pl
from jax.experimental.pallas import tpu as pltpu
from jax.sharding import PartitionSpec as P

HEADS = 12
HEAD_DIM = 64
TEAMS = 4
TEAM_HEADS = HEADS // TEAMS
TEAM_WIDTH = TEAM_HEADS * HEAD_DIM
QUERY_WIDTH = TEAM_WIDTH + HEAD_DIM

epsilon = 1e-05
negative = -1e30
select_scale = 3.0
VMEM_BYTES = 60 * 2**20
MESH = pl.DeviceIdType.MESH


def peers_of(scope):
    count = lax.axis_size("seq")
    lanes = count // TEAMS
    me = lax.axis_index("seq")
    team, lane = me // lanes, lax.rem(me, lanes)
    if scope == "team":
        return lane, lanes, lambda k: team * lanes + k
    if scope == "lane":
        return team, TEAMS, lambda k: k * lanes + lane
    return me, count, lambda k: k


def exchange(scope, kinds, arrays, collective):
    number = len(arrays)

    def body(*refs):
        sources, targets = refs[:number], refs[number : 2 * number]
        send, receive, local = refs[2 * number :]
        mine, peers, index_of = peers_of(scope)
        barrier = pltpu.get_barrier_semaphore()
        for k in range(1, peers):
            pl.semaphore_signal(
                barrier,
                inc=1,
                device_id={"seq": index_of(lax.rem(mine + k, peers))},
                device_id_type=MESH,
            )
        pl.semaphore_wait(barrier, peers - 1)
        copies = []
        for k in range(1, peers):
            peer = lax.rem(mine + k, peers)
            for n in range(number):
                copy = pltpu.make_async_remote_copy(
                    src_ref=sources[n] if kinds[n] == "gather" else sources[n].at[peer],
                    dst_ref=targets[n].at[mine],
                    send_sem=send.at[n, k],
                    recv_sem=receive.at[n, k],
                    device_id={"seq": index_of(peer)},
                    device_id_type=MESH,
                )
                copy.start()
                copies.append(copy)
        for n in range(number):
            copy = pltpu.make_async_copy(
                sources[n] if kinds[n] == "gather" else sources[n].at[mine],
                targets[n].at[mine],
                local.at[n],
            )
            copy.start()
            copies.append(copy)
        for copy in copies:
            copy.wait()

    count = {"team": lax.axis_size("seq") // TEAMS, "lane": TEAMS, "all": lax.axis_size("seq")}[scope]
    shapes = [
        jax.ShapeDtypeStruct(((count,) if kind == "gather" else ()) + x.shape, x.dtype)
        for kind, x in zip(kinds, arrays)
    ]
    return pl.pallas_call(
        body,
        out_shape=shapes,
        in_specs=[pl.BlockSpec(memory_space=pl.ANY)] * number,
        out_specs=[pl.BlockSpec(memory_space=pl.ANY)] * number,
        scratch_shapes=[
            pltpu.SemaphoreType.DMA((number, count)),
            pltpu.SemaphoreType.DMA((number, count)),
            pltpu.SemaphoreType.DMA((number,)),
        ],
        compiler_params=pltpu.CompilerParams(
            collective_id=collective, has_side_effects=True, vmem_limit_bytes=VMEM_BYTES
        ),
    )(*arrays)


def dot(left, right):
    return jnp.dot(left, right, preferred_element_type=jnp.float32)


def attend_body(
    length_ref,
    threshold_ref,
    q_ref,
    kk_ref,
    vv_ref,
    out_ref,
    mass_ref,
    carried_ref,
    excess_ref,
    key_heads,
    value_rows,
    running,
    logits,
    *,
    blocks,
    rows,
):
    lanes = blocks // TEAMS
    me = lax.axis_index("seq")
    team, lane = me // lanes, lax.rem(me, lanes)
    i = pl.program_id(0)
    scale = select_scale / (blocks * rows)

    @pl.when(i == 0)
    def _():
        running[...] = jnp.zeros_like(running)
        excess_ref[...] = jnp.zeros_like(excess_ref)
        for z in range(TEAMS):
            for h in range(TEAM_HEADS + 1):
                key_heads[h, z] = kk_ref[z, :, h * HEAD_DIM : (h + 1) * HEAD_DIM]
            value_rows[z] = vv_ref[z].T

    active = jnp.where(i >= lane, (i - lane) // lanes + 1, 0)
    q_rows = q_ref[0, 0].T
    heads = [q_rows[h * HEAD_DIM : (h + 1) * HEAD_DIM] for h in range(TEAM_HEADS + 1)]
    key_iota = lax.broadcasted_iota(jnp.int32, (rows, rows), 0)
    query_iota = lax.broadcasted_iota(jnp.int32, (rows, rows), 1)
    earlier = (key_iota < query_iota).astype(jnp.bfloat16)
    ones = jnp.ones((rows, rows), jnp.bfloat16)
    query_pos = i * rows + query_iota
    query_valid = query_pos < length_ref[0]
    threshold = threshold_ref[0]

    def score(z, peaks):
        key_pos = (z * lanes + lane) * rows + key_iota
        first = dot(key_heads[TEAM_HEADS, z], heads[TEAM_HEADS])
        chosen = (key_pos < query_pos) & (key_pos >= 1)
        selected = jnp.where(chosen, jnp.maximum(first, 0.0) * scale, 0.0).astype(jnp.bfloat16)
        carried = running[z] + dot(selected, earlier)
        running[z] = running[z] + dot(selected, ones)

        @pl.when(lax.rem(i, TEAMS) == team)
        def _():
            clipped = jnp.where(
                chosen & query_valid, jnp.clip(carried - threshold, 0.0, 1.0), 0.0
            )
            excess_ref[...] += jnp.sum(clipped.reshape(rows // 8, 8, rows), axis=0)

        carried = jnp.where(key_pos <= query_pos, carried, -negative)
        carried_ref[0, z] = carried
        result = []
        for h in range(TEAM_HEADS):
            logit = dot(key_heads[h, z], heads[h]) - carried
            logits[h, z] = logit
            result.append(
                jnp.maximum(peaks[h], jnp.max(logit.reshape(rows // 8, 8, rows), axis=0))
            )
        return tuple(result)

    start = tuple(jnp.full((8, rows), negative, jnp.float32) for _ in range(TEAM_HEADS))
    peaks = lax.fori_loop(0, active, score, start)
    peaks = [jnp.max(peak, axis=0, keepdims=True) for peak in peaks]

    def gather_values(z, state):
        masses, mixed = state
        new_masses, new_mixed = [], []
        for h in range(TEAM_HEADS):
            terms = jnp.exp(logits[h, z] - peaks[h])
            new_masses.append(masses[h] + jnp.sum(terms.reshape(rows // 8, 8, rows), axis=0))
            values = value_rows[z, h * HEAD_DIM : (h + 1) * HEAD_DIM, :]
            new_mixed.append(mixed[h] + dot(values, terms.astype(jnp.bfloat16)))
        return tuple(new_masses), tuple(new_mixed)

    masses, mixed = lax.fori_loop(
        0,
        active,
        gather_values,
        (
            tuple(jnp.zeros((8, rows), jnp.float32) for _ in range(TEAM_HEADS)),
            tuple(jnp.zeros((HEAD_DIM, rows), jnp.float32) for _ in range(TEAM_HEADS)),
        ),
    )
    mass_ref[0] = jnp.zeros((8, rows), jnp.float32)
    for h in range(TEAM_HEADS):
        mass = jnp.sum(masses[h], axis=0, keepdims=True)
        mass = jnp.where(active > 0, mass, 1.0)
        out_ref[0, h * HEAD_DIM : (h + 1) * HEAD_DIM, :] = (mixed[h] * (1.0 / mass)).astype(
            jnp.bfloat16
        )
        mass_ref[0, h : h + 1, :] = jnp.where(
            active > 0, peaks[h] + jnp.log(mass), negative
        )


def attend(length, threshold, queries, keys, values, blocks, rows):
    lanes = blocks // TEAMS
    smem = pl.BlockSpec(memory_space=pltpu.SMEM)
    whole = pl.BlockSpec((TEAMS, rows, QUERY_WIDTH), lambda i: (0, 0, 0))
    return pl.pallas_call(
        functools.partial(attend_body, blocks=blocks, rows=rows),
        grid=(blocks,),
        in_specs=[
            smem,
            smem,
            pl.BlockSpec(
                (1, 1, rows, QUERY_WIDTH), lambda i: (lax.rem(i, lanes), i // lanes, 0, 0)
            ),
            whole,
            pl.BlockSpec((TEAMS, rows, TEAM_WIDTH), lambda i: (0, 0, 0)),
        ],
        out_specs=[
            pl.BlockSpec((1, TEAM_WIDTH, rows), lambda i: (i, 0, 0)),
            pl.BlockSpec((1, 8, rows), lambda i: (i, 0, 0)),
            pl.BlockSpec((1, TEAMS, rows, rows), lambda i: (i, 0, 0, 0)),
            pl.BlockSpec((8, rows), lambda i: (0, 0)),
        ],
        out_shape=[
            jax.ShapeDtypeStruct((blocks, TEAM_WIDTH, rows), jnp.bfloat16),
            jax.ShapeDtypeStruct((blocks, 8, rows), jnp.float32),
            jax.ShapeDtypeStruct((blocks, TEAMS, rows, rows), jnp.float32),
            jax.ShapeDtypeStruct((8, rows), jnp.float32),
        ],
        scratch_shapes=[
            pltpu.VMEM((TEAM_HEADS + 1, TEAMS, rows, HEAD_DIM), jnp.bfloat16),
            pltpu.VMEM((TEAMS, TEAM_WIDTH, rows), jnp.bfloat16),
            pltpu.VMEM((TEAMS, rows, rows), jnp.float32),
            pltpu.VMEM((TEAM_HEADS, TEAMS, rows, rows), jnp.float32),
        ],
        compiler_params=pltpu.CompilerParams(vmem_limit_bytes=VMEM_BYTES),
    )(length, threshold, queries, keys, values)


def attend_back_body(
    q_ref,
    grad_ref,
    stat_ref,
    carried_ref,
    kk_ref,
    vv_ref,
    query_grad_ref,
    key_grad_ref,
    value_grad_ref,
    key_heads,
    key_rows,
    value_heads,
    running,
    key_sum,
    value_sum,
    *,
    blocks,
    rows,
):
    lanes = blocks // TEAMS
    lane = lax.rem(lax.axis_index("seq"), lanes)
    step = pl.program_id(0)
    i = blocks - 1 - step
    scale = select_scale / (blocks * rows)

    @pl.when(step == 0)
    def _():
        running[...] = jnp.zeros_like(running)
        key_sum[...] = jnp.zeros_like(key_sum)
        value_sum[...] = jnp.zeros_like(value_sum)
        for z in range(TEAMS):
            for h in range(TEAM_HEADS + 1):
                key_heads[h, z] = kk_ref[z, :, h * HEAD_DIM : (h + 1) * HEAD_DIM]
            for h in range(TEAM_HEADS):
                value_heads[h, z] = vv_ref[z, :, h * HEAD_DIM : (h + 1) * HEAD_DIM]
            key_rows[z] = kk_ref[z].T

    active = jnp.where(i >= lane, (i - lane) // lanes + 1, 0)
    q_rows = q_ref[0, 0].T
    grad_rows = grad_ref[0, 0].T
    span = [slice(h * HEAD_DIM, (h + 1) * HEAD_DIM) for h in range(TEAM_HEADS + 1)]
    q_row = [q_rows[span[h]] for h in range(TEAM_HEADS + 1)]
    q_col = [q_ref[0, 0, :, span[h]] for h in range(TEAM_HEADS + 1)]
    grad_row = [grad_rows[span[h]] for h in range(TEAM_HEADS)]
    grad_col = [grad_ref[0, 0, :, span[h]] for h in range(TEAM_HEADS)]
    mass = [stat_ref[0, 0, h : h + 1, :] for h in range(TEAM_HEADS)]
    inner = [stat_ref[0, 0, TEAM_HEADS + h : TEAM_HEADS + h + 1, :] for h in range(TEAM_HEADS)]
    key_iota = lax.broadcasted_iota(jnp.int32, (rows, rows), 0)
    query_iota = lax.broadcasted_iota(jnp.int32, (rows, rows), 1)
    later = (key_iota > query_iota).astype(jnp.bfloat16)
    ones = jnp.ones((rows, rows), jnp.bfloat16)
    query_pos = i * rows + query_iota

    def back(z, query_sum):
        key_pos = (z * lanes + lane) * rows + key_iota
        carried = carried_ref[0, z]
        total = None
        new_sum = []
        for h in range(TEAM_HEADS):
            probs = jnp.exp(dot(key_heads[h, z], q_row[h]) - carried - mass[h])
            value_sum[h, z] += dot(probs.astype(jnp.bfloat16), grad_col[h])
            grad_logit = probs * (dot(value_heads[h, z], grad_row[h]) - inner[h])
            total = grad_logit if total is None else total + grad_logit
            low = grad_logit.astype(jnp.bfloat16)
            key_sum[h, z] += dot(low, q_col[h])
            new_sum.append(query_sum[h] + dot(key_rows[z, span[h], :], low))
        total = total.astype(jnp.bfloat16)
        select_grad = running[z] - dot(total, later)
        running[z] = running[z] - dot(total, ones)
        first = dot(key_heads[TEAM_HEADS, z], q_row[TEAM_HEADS])
        live = (key_pos < query_pos) & (key_pos >= 1) & (first > 0.0)
        low = jnp.where(live, select_grad * scale, 0.0).astype(jnp.bfloat16)
        key_sum[TEAM_HEADS, z] += dot(low, q_col[TEAM_HEADS])
        new_sum.append(query_sum[TEAM_HEADS] + dot(key_rows[z, span[TEAM_HEADS], :], low))
        return tuple(new_sum)

    query_sum = lax.fori_loop(
        0,
        active,
        back,
        tuple(jnp.zeros((HEAD_DIM, rows), jnp.float32) for _ in range(TEAM_HEADS + 1)),
    )
    for h in range(TEAM_HEADS + 1):
        query_grad_ref[0, 0, span[h], :] = query_sum[h].astype(jnp.bfloat16)

    @pl.when(step == blocks - 1)
    def _():
        for h in range(TEAM_HEADS + 1):
            key_grad_ref[:, :, span[h]] = key_sum[h].astype(jnp.bfloat16)
        for h in range(TEAM_HEADS):
            value_grad_ref[:, :, span[h]] = value_sum[h].astype(jnp.bfloat16)


def attend_back(queries, grads, stats, carried, keys, values, blocks, rows):
    lanes = blocks // TEAMS

    def place(step):
        i = blocks - 1 - step
        return (lax.rem(i, lanes), i // lanes, 0, 0)

    return pl.pallas_call(
        functools.partial(attend_back_body, blocks=blocks, rows=rows),
        grid=(blocks,),
        in_specs=[
            pl.BlockSpec((1, 1, rows, QUERY_WIDTH), place),
            pl.BlockSpec((1, 1, rows, TEAM_WIDTH), place),
            pl.BlockSpec((1, 1, 8, rows), place),
            pl.BlockSpec((1, TEAMS, rows, rows), lambda step: (blocks - 1 - step, 0, 0, 0)),
            pl.BlockSpec((TEAMS, rows, QUERY_WIDTH), lambda step: (0, 0, 0)),
            pl.BlockSpec((TEAMS, rows, TEAM_WIDTH), lambda step: (0, 0, 0)),
        ],
        out_specs=[
            pl.BlockSpec((1, 1, QUERY_WIDTH, rows), place),
            pl.BlockSpec((TEAMS, rows, QUERY_WIDTH), lambda step: (0, 0, 0)),
            pl.BlockSpec((TEAMS, rows, TEAM_WIDTH), lambda step: (0, 0, 0)),
        ],
        out_shape=[
            jax.ShapeDtypeStruct((lanes, TEAMS, QUERY_WIDTH, rows), jnp.bfloat16),
            jax.ShapeDtypeStruct((TEAMS, rows, QUERY_WIDTH), jnp.bfloat16),
            jax.ShapeDtypeStruct((TEAMS, rows, TEAM_WIDTH), jnp.bfloat16),
        ],
        scratch_shapes=[
            pltpu.VMEM((TEAM_HEADS + 1, TEAMS, rows, HEAD_DIM), jnp.bfloat16),
            pltpu.VMEM((TEAMS, QUERY_WIDTH, rows), jnp.bfloat16),
            pltpu.VMEM((TEAM_HEADS, TEAMS, rows, HEAD_DIM), jnp.bfloat16),
            pltpu.VMEM((TEAMS, rows, rows), jnp.float32),
            pltpu.VMEM((TEAM_HEADS + 1, TEAMS, rows, HEAD_DIM), jnp.float32),
            pltpu.VMEM((TEAM_HEADS, TEAMS, rows, HEAD_DIM), jnp.float32),
        ],
        compiler_params=pltpu.CompilerParams(vmem_limit_bytes=VMEM_BYTES),
    )(queries, grads, stats, carried, keys, values)


def finish_body(
    main_ref,
    extra_ref,
    rows_ref,
    vector_ref,
    whole_ref,
    home_ref,
    total_ref,
    core_main,
    core_extra,
    send_main,
    send_extra,
    lane_main,
    lane_extra,
    team_send_main,
    team_send_extra,
    team_main,
    team_extra,
    assembled,
    vectors,
    ready,
    core_sems,
    lane_sems,
    team_sems,
    home_sems,
    vector_sems,
    out_lane_sems,
    out_core_send,
    out_core_recv,
    local_sems,
):
    blocks = lax.axis_size("seq")
    lanes = blocks // TEAMS
    me = lax.axis_index("seq")
    core = lax.axis_index("batch")
    team, lane = me // lanes, lax.rem(me, lanes)

    def lane_peer(k):
        other = lax.rem(lane + k, lanes)
        return other, {"seq": team * lanes + other}

    def team_peer(k):
        other = lax.rem(team + k, TEAMS)
        return other, {"seq": other * lanes + lane}

    sibling = {"batch": 1 - core}
    barrier = pltpu.get_barrier_semaphore()
    targets = [sibling]
    targets += [lane_peer(k)[1] for k in range(1, lanes)]
    targets += [team_peer(k)[1] for k in range(1, TEAMS)]
    for target in targets:
        pl.semaphore_signal(barrier, inc=1, device_id=target, device_id_type=MESH)
    pl.semaphore_wait(barrier, len(targets))

    def push(source, destination, send, receive, target):
        copy = pltpu.make_async_remote_copy(
            src_ref=source,
            dst_ref=destination,
            send_sem=send,
            recv_sem=receive,
            device_id=target,
            device_id_type=MESH,
        )
        copy.start()
        return copy

    theirs = pl.ds((1 - core) * lanes, lanes)
    core_copies = [
        push(main_ref.at[theirs], core_main, core_sems.at[0, 0], core_sems.at[1, 0], sibling),
        push(extra_ref.at[theirs], core_extra, core_sems.at[0, 1], core_sems.at[1, 1], sibling),
        push(vector_ref, vectors.at[0], vector_sems.at[0, 0], vector_sems.at[1, 0], sibling),
    ]
    home_copies = []
    for k in range(1, TEAMS):
        other, target = team_peer(k)
        home_copies.append(
            push(rows_ref.at[other], home_ref.at[team], home_sems.at[0, k], home_sems.at[1, k], target)
        )
    own = pltpu.make_async_copy(rows_ref.at[team], home_ref.at[team], local_sems.at[0])
    own.start()
    for copy in core_copies:
        copy.wait()

    both = vector_ref[...] + vectors[0]
    vectors[1 + lane] = both
    ready[0] = both
    for j in range(lanes):
        send_main[j] = (
            main_ref[core * lanes + j].astype(jnp.float32) + core_main[j].astype(jnp.float32)
        ).astype(jnp.bfloat16)
        send_extra[j] = (
            extra_ref[core * lanes + j].astype(jnp.float32) + core_extra[j].astype(jnp.float32)
        ).astype(jnp.bfloat16)
    lane_copies = []
    for k in range(1, lanes):
        other, target = lane_peer(k)
        lane_copies += [
            push(send_main.at[other], lane_main.at[lane], lane_sems.at[0, 0, k], lane_sems.at[1, 0, k], target),
            push(send_extra.at[other], lane_extra.at[lane], lane_sems.at[0, 1, k], lane_sems.at[1, 1, k], target),
            push(ready.at[0], vectors.at[1 + lane], vector_sems.at[0, k], vector_sems.at[1, k], target),
        ]
    lane_main[lane] = send_main[lane]
    lane_extra[lane] = send_extra[lane]
    for copy in lane_copies:
        copy.wait()

    def total(ref, start, number):
        result = ref[start].astype(jnp.float32)
        for j in range(1, number):
            result = result + ref[start + j].astype(jnp.float32)
        return result

    whole_vector = total(vectors, 1, lanes)
    ready[1] = whole_vector
    vectors[1 + lanes + team] = whole_vector
    low_main = total(lane_main, 0, lanes).astype(jnp.bfloat16)
    low_extra = total(lane_extra, 0, lanes).astype(jnp.bfloat16)
    team_send_main[...] = low_main
    team_send_extra[...] = low_extra
    team_main[team] = low_main
    team_extra[team] = low_extra
    team_copies = []
    for k in range(1, TEAMS):
        other, target = team_peer(k)
        at = lanes + k
        team_copies += [
            push(team_send_main, team_main.at[team], team_sems.at[0, 0, k], team_sems.at[1, 0, k], target),
            push(team_send_extra, team_extra.at[team], team_sems.at[0, 1, k], team_sems.at[1, 1, k], target),
            push(ready.at[1], vectors.at[1 + lanes + team], vector_sems.at[0, at], vector_sems.at[1, at], target),
        ]
    for copy in team_copies:
        copy.wait()
    total_ref[...] = total(vectors, 1 + lanes, TEAMS)
    extra = total(team_extra, 0, TEAMS)
    pieces = []
    for part in range(3):
        for g in range(TEAMS):
            piece = team_main[g, :, part * TEAM_WIDTH : (part + 1) * TEAM_WIDTH]
            if g == 0 and part < 2:
                more = extra[:, part * HEAD_DIM : (part + 1) * HEAD_DIM]
                first = (piece[:, :HEAD_DIM].astype(jnp.float32) + more).astype(jnp.bfloat16)
                pieces += [first, piece[:, HEAD_DIM:]]
            else:
                pieces.append(piece)
    assembled[...] = jnp.concatenate(pieces, axis=1)

    mine = core * lanes + lane
    out_copies = []
    for k in range(1, lanes):
        _, target = lane_peer(k)
        out_copies.append(
            push(assembled, whole_ref.at[mine], out_lane_sems.at[0, k], out_lane_sems.at[1, k], target)
        )
    core_out = [
        push(assembled, whole_ref.at[mine], out_core_send.at[0], out_core_recv.at[0], sibling)
    ]
    kept = pltpu.make_async_copy(assembled, whole_ref.at[mine], local_sems.at[1])
    kept.start()
    for k in range(1, lanes):
        source = core * lanes + lax.rem(lane - k + lanes, lanes)
        out_copies[k - 1].wait_recv()
        core_out.append(
            push(whole_ref.at[source], whole_ref.at[source], out_core_send.at[k], out_core_recv.at[k], sibling)
        )
    for copy in out_copies:
        copy.wait_send()
    for copy in core_out + home_copies:
        copy.wait()
    own.wait()
    kept.wait()


def finish(main, extra, rows_out, vector, collective):
    lanes = lax.axis_size("seq") // TEAMS
    chunks, depth, main_width = main.shape
    extra_width = extra.shape[2]
    low = jnp.bfloat16
    dma = pltpu.SemaphoreType.DMA
    return pl.pallas_call(
        finish_body,
        out_shape=[
            jax.ShapeDtypeStruct((chunks, depth, TEAMS * main_width), low),
            jax.ShapeDtypeStruct(rows_out.shape, low),
            jax.ShapeDtypeStruct(vector.shape, jnp.float32),
        ],
        in_specs=[
            pl.BlockSpec(memory_space=pltpu.VMEM),
            pl.BlockSpec(memory_space=pltpu.VMEM),
            pl.BlockSpec(memory_space=pl.ANY),
            pl.BlockSpec(memory_space=pltpu.VMEM),
        ],
        out_specs=[
            pl.BlockSpec(memory_space=pl.ANY),
            pl.BlockSpec(memory_space=pl.ANY),
            pl.BlockSpec(memory_space=pltpu.VMEM),
        ],
        scratch_shapes=[
            pltpu.VMEM((lanes, depth, main_width), low),
            pltpu.VMEM((lanes, depth, extra_width), low),
            pltpu.VMEM((lanes, depth, main_width), low),
            pltpu.VMEM((lanes, depth, extra_width), low),
            pltpu.VMEM((lanes, depth, main_width), low),
            pltpu.VMEM((lanes, depth, extra_width), low),
            pltpu.VMEM((depth, main_width), low),
            pltpu.VMEM((depth, extra_width), low),
            pltpu.VMEM((TEAMS, depth, main_width), low),
            pltpu.VMEM((TEAMS, depth, extra_width), low),
            pltpu.VMEM((depth, TEAMS * main_width), low),
            pltpu.VMEM((1 + lanes + TEAMS,) + vector.shape, jnp.float32),
            pltpu.VMEM((2,) + vector.shape, jnp.float32),
            dma((2, 2)),
            dma((2, 2, lanes)),
            dma((2, 2, TEAMS)),
            dma((2, TEAMS)),
            dma((2, lanes + TEAMS)),
            dma((2, lanes)),
            dma((lanes,)),
            dma((lanes,)),
            dma((2,)),
        ],
        compiler_params=pltpu.CompilerParams(
            collective_id=collective, has_side_effects=True, vmem_limit_bytes=VMEM_BYTES
        ),
    )(main, extra, rows_out, vector)


def layer_norm(values, norm_gain, norm_bias):
    row_mean = jnp.mean(values, axis=-1, keepdims=True)
    centred = values - row_mean
    variance = jnp.mean(centred * centred, axis=-1, keepdims=True)
    return centred * lax.rsqrt(variance + epsilon) * norm_gain + norm_bias


def gelu_tanh(values):
    return jax.nn.gelu(values, approximate=True)


def contract_rows(left_op, right_op):
    return lax.dot_general(
        left_op, right_op, (((0,), (0,)), ((), ())), preferred_element_type=jnp.float32
    )


def contract_cols(left_op, right_op):
    return lax.dot_general(
        left_op, right_op, (((1,), (1,)), ((), ())), preferred_element_type=jnp.float32
    )


def per_device(
    block_input,
    ln1_gain,
    ln1_bias,
    w_qkv,
    w_out,
    ln2_gain,
    ln2_bias,
    w_up,
    w_down,
    length_draw,
    threshold_index,
    grad_out,
):
    rows = block_input.shape[1]
    width = block_input.shape[2]
    blocks = lax.axis_size("seq")
    lanes = blocks // TEAMS
    group_len = blocks * rows
    me = lax.axis_index("seq")
    team = me // lanes
    score_scale = HEAD_DIM ** (-0.5)
    length = group_len - rows + 1 + length_draw % rows
    row_valid = (me * rows + jnp.arange(rows, dtype=jnp.int32) < length[0])[:, None]
    threshold = threshold_index.astype(jnp.float32) / 128.0
    tokens = block_input[0]
    grad_top = grad_out[0]
    grad_top_low = grad_top.astype(jnp.bfloat16)

    normed, ln1_pull = jax.vjp(layer_norm, tokens, ln1_gain, ln1_bias)
    normed_low = normed.astype(jnp.bfloat16)
    (lane_rows,) = exchange("lane", ["gather"], [normed_low], 0)
    lane_rows = lane_rows.reshape(TEAMS * rows, width)

    def columns(part):
        return lax.dynamic_slice_in_dim(w_qkv, part * width + team * TEAM_WIDTH, TEAM_WIDTH, 1)

    team_weight = jnp.concatenate(
        [columns(0), columns(1), columns(2), w_qkv[:, :HEAD_DIM], w_qkv[:, width : width + HEAD_DIM]],
        axis=1,
    )
    projected = dot(lane_rows, team_weight).astype(jnp.bfloat16)
    query_part, key_part, value_part, query_first, key_first = jnp.split(
        projected, [TEAM_WIDTH, 2 * TEAM_WIDTH, 3 * TEAM_WIDTH, 3 * TEAM_WIDTH + HEAD_DIM], axis=1
    )
    queries = jnp.concatenate([query_part, query_first], axis=1) * jnp.bfloat16(score_scale)
    keys = jnp.concatenate([key_part, key_first], axis=1).reshape(TEAMS, rows, QUERY_WIDTH)
    values = value_part.reshape(TEAMS, rows, TEAM_WIDTH)
    (queries,) = exchange("team", ["gather"], [queries.reshape(TEAMS, rows, QUERY_WIDTH)], 1)

    parts, masses, carried, excess = attend(
        length, threshold, queries, keys, values, blocks, rows
    )
    parts, masses = exchange("all", ["spread", "spread"], [parts, masses], 2)
    parts = parts.astype(jnp.float32).reshape(TEAMS, lanes, TEAM_HEADS, HEAD_DIM, rows)
    masses = masses.reshape(TEAMS, lanes, 8, rows)[:, :, :TEAM_HEADS]
    peak = jnp.max(masses, axis=1, keepdims=True)
    shares = jnp.exp(masses - peak)
    mass = jnp.sum(shares, axis=1, keepdims=True)
    shares = shares / mass
    log_mass = (peak + jnp.log(mass))[:, 0]
    head_out = jnp.sum(parts * shares[:, :, :, None, :], axis=1)
    attn_mixed = jnp.where(
        row_valid, head_out.reshape(width, rows).T, 0.0
    ).astype(jnp.bfloat16)

    residual = tokens + dot(attn_mixed, w_out)
    normed_two, ln2_pull = jax.vjp(layer_norm, residual, ln2_gain, ln2_bias)
    normed_two_low = normed_two.astype(jnp.bfloat16)
    hidden = dot(normed_two_low, w_up)
    activated, gelu_pull = jax.vjp(gelu_tanh, hidden)
    activated_low = activated.astype(jnp.bfloat16)
    layer_out = residual + dot(activated_low, w_down)
    grad_w_down = contract_rows(activated_low, grad_top_low)
    grad_hidden_low = gelu_pull(contract_cols(grad_top_low, w_down))[0].astype(jnp.bfloat16)
    grad_w_up = contract_rows(normed_two_low, grad_hidden_low)
    grad_resid_norm, grad_ln2_gain, grad_ln2_bias = ln2_pull(contract_cols(grad_hidden_low, w_up))
    grad_resid = grad_top + grad_resid_norm
    grad_attn_low = grad_resid.astype(jnp.bfloat16)
    grad_w_out = contract_rows(attn_mixed, grad_attn_low)
    grad_mixed = jnp.where(
        row_valid,
        contract_cols(grad_attn_low, w_out).astype(jnp.bfloat16),
        jnp.zeros((), jnp.bfloat16),
    )
    grad_w_down, grad_w_up, grad_w_out = lax.psum(
        (
            grad_w_down.astype(jnp.bfloat16),
            grad_w_up.astype(jnp.bfloat16),
            grad_w_out.astype(jnp.bfloat16),
        ),
        ("seq", "batch"),
    )

    grad_rows = grad_mixed.T.reshape(TEAMS, TEAM_HEADS, HEAD_DIM, rows).astype(jnp.float32)
    inner = jnp.sum(grad_rows * head_out, axis=2)
    stats = jnp.concatenate(
        [log_mass, inner, jnp.zeros((TEAMS, 8 - 2 * TEAM_HEADS, rows), jnp.float32)], axis=1
    )
    grad_cols = jnp.moveaxis(grad_mixed.reshape(rows, TEAMS, TEAM_WIDTH), 1, 0)
    grad_cols, stats = exchange("lane", ["spread", "spread"], [grad_cols, stats], 3)
    grad_cols, stats = exchange("team", ["gather", "gather"], [grad_cols, stats], 4)
    query_grads, key_grads, value_grads = attend_back(
        queries, grad_cols, stats, carried, keys, values, blocks, rows
    )
    (query_grads,) = exchange("team", ["spread"], [query_grads], 5)
    query_grads = jnp.sum(query_grads.astype(jnp.float32), axis=0) * score_scale
    query_grads = jnp.swapaxes(query_grads.astype(jnp.bfloat16), 1, 2)
    grad_projected = jnp.concatenate(
        [
            query_grads[:, :, :TEAM_WIDTH],
            key_grads[:, :, :TEAM_WIDTH],
            value_grads,
            query_grads[:, :, TEAM_WIDTH:],
            key_grads[:, :, TEAM_WIDTH:],
        ],
        axis=2,
    ).reshape(TEAMS * rows, -1)
    chunks = 2 * lanes
    grad_main = contract_rows(lane_rows, grad_projected[:, : 3 * TEAM_WIDTH])
    grad_extra = contract_rows(lane_rows, grad_projected[:, 3 * TEAM_WIDTH :])
    grad_lane_rows = contract_cols(grad_projected, team_weight)
    grad_ln1_bias = jnp.sum(grad_lane_rows, axis=0)
    grad_ln1_gain = (
        jnp.sum(grad_lane_rows * (lane_rows.astype(jnp.float32) - ln1_bias), axis=0) / ln1_gain
    )
    pairs = (length[0] - 1).astype(jnp.float32) * (length[0] - 2).astype(jnp.float32) / 2.0
    vectors = jnp.stack(
        [
            grad_ln1_gain,
            grad_ln1_bias,
            grad_ln2_gain,
            grad_ln2_bias,
            jnp.full((width,), jnp.sum(excess)),
            jnp.full((width,), pairs / blocks),
            jnp.zeros((width,), jnp.float32),
            jnp.zeros((width,), jnp.float32),
        ]
    )
    grad_w_qkv, home_rows, vectors = finish(
        grad_main.astype(jnp.bfloat16).reshape(chunks, width // chunks, -1),
        grad_extra.astype(jnp.bfloat16).reshape(chunks, width // chunks, -1),
        grad_lane_rows.astype(jnp.bfloat16).reshape(TEAMS, rows, width),
        vectors,
        6,
    )
    grad_w_qkv = grad_w_qkv.reshape(width, 3 * width)
    grad_normed = jnp.sum(home_rows.astype(jnp.float32), axis=0)
    grad_x = grad_resid + ln1_pull(grad_normed)[0]
    pruned_share = (vectors[4, 0] / vectors[5, 0]).reshape(1)
    return (
        layer_out[None],
        grad_x[None],
        vectors[0],
        vectors[1],
        grad_w_qkv.astype(jnp.float32),
        grad_w_out.astype(jnp.float32),
        vectors[2],
        vectors[3],
        grad_w_up.astype(jnp.float32),
        grad_w_down.astype(jnp.float32),
        pruned_share,
    )


def solution(mesh):
    placed = (
        P("batch", "seq", None),
        P(),
        P(),
        P(),
        P(),
        P(),
        P(),
        P(),
        P(),
        P("batch"),
        P(),
        P("batch", "seq", None),
    )
    return jax.shard_map(
        per_device,
        mesh=mesh,
        in_specs=placed,
        out_specs=(
            P("batch", "seq", None),
            P("batch", "seq", None),
            P(),
            P(),
            P(),
            P(),
            P(),
            P(),
            P(),
            P(),
            P(),
        ),
        check_vma=False,
    )
```

```python
import functools

import jax
import jax.numpy as jnp
from jax import lax
from jax.experimental import pallas as pl
from jax.experimental.pallas import tpu as pltpu
from jax.sharding import PartitionSpec as P

HEADS = 12
HEAD_DIM = 64
TEAMS = 4
TEAM_HEADS = HEADS // TEAMS
TEAM_WIDTH = TEAM_HEADS * HEAD_DIM
QUERY_WIDTH = TEAM_WIDTH + HEAD_DIM

epsilon = 1e-05
negative = -1e30
select_scale = 3.0
VMEM_BYTES = 60 * 2**20
MESH = pl.DeviceIdType.MESH


def peers_of(scope):
    lanes = lax.axis_size("seq") // TEAMS
    me = lax.axis_index("seq")
    team, lane = me // lanes, lax.rem(me, lanes)
    if scope == "team":
        return lane, lanes, lambda k: {"seq": team * lanes + k}
    if scope == "lane":
        return team, TEAMS, lambda k: {"seq": k * lanes + lane}
    if scope == "core":
        return lax.axis_index("batch"), 2, lambda k: {"batch": k}
    return me, lanes * TEAMS, lambda k: {"seq": k}


def scope_size(scope):
    count = lax.axis_size("seq")
    return {"team": count // TEAMS, "lane": TEAMS, "core": 2, "all": count}[scope]


def greet(scopes):
    barrier = pltpu.get_barrier_semaphore()
    number = 0
    for scope in scopes:
        mine, peers, device_of = peers_of(scope)
        for k in range(1, peers):
            pl.semaphore_signal(
                barrier, inc=1, device_id=device_of(lax.rem(mine + k, peers)), device_id_type=MESH
            )
        number += peers - 1
    pl.semaphore_wait(barrier, number)


def push(source, destination, send, receive, target, start=True):
    copy = pltpu.make_async_remote_copy(
        src_ref=source,
        dst_ref=destination,
        send_sem=send,
        recv_sem=receive,
        device_id=target,
        device_id_type=MESH,
    )
    if start:
        copy.start()
    return copy


def part_of(kind, ref, k):
    if kind == "gather":
        return ref
    if kind == "spread":
        return ref.at[k]
    half = ref.shape[1] // 2
    return ref.at[:, pl.ds(pl.multiple_of(k * half, 128), half)]


def remote_copies(plan, sources, targets, send, receive, start=True):
    copies = []
    for n, (scope, kind) in enumerate(plan):
        mine, peers, device_of = peers_of(scope)
        for k in range(1, peers):
            peer = lax.rem(mine + k, peers)
            copies.append(
                push(
                    part_of(kind, sources[n], peer),
                    targets[n].at[mine],
                    send.at[n, k],
                    receive.at[n, k],
                    device_of(peer),
                    start,
                )
            )
    return copies


def exchange_copies(plan, sources, targets, send, receive, local, start=True):
    copies = remote_copies(plan, sources, targets, send, receive, start)
    for n, (scope, kind) in enumerate(plan):
        mine = peers_of(scope)[0]
        copy = pltpu.make_async_copy(
            part_of(kind, sources[n], mine), targets[n].at[mine], local.at[n]
        )
        if start:
            copy.start()
        copies.append(copy)
    return copies


def exchange_shapes(plan, arrays):
    shapes = []
    for (scope, kind), x in zip(plan, arrays):
        shape = x.shape
        if kind == "gather":
            shape = (scope_size(scope),) + shape
        if kind == "half":
            shape = (2, shape[0], shape[1] // 2)
        shapes.append(jax.ShapeDtypeStruct(shape, x.dtype))
    return shapes


def exchange_sems(plan):
    number, most = len(plan), max(scope_size(scope) for scope, _ in plan)
    return [
        pltpu.SemaphoreType.DMA((number, most)),
        pltpu.SemaphoreType.DMA((number, most)),
        pltpu.SemaphoreType.DMA((number,)),
    ]


def scopes_of(plan):
    return [x for x in ("core", "team", "lane", "all") if x in [scope for scope, _ in plan]]


def exchange(plan, arrays, collective):
    number = len(arrays)
    shapes = exchange_shapes(plan, arrays)

    def body(*refs):
        sources, targets = refs[:number], refs[number : 2 * number]
        send, receive, local = refs[2 * number : 2 * number + 3]
        through = refs[2 * number + 3 :]
        greet(scopes_of(plan))
        copies = remote_copies(plan, sources, targets, send, receive)
        inward = []
        for n, (scope, kind) in enumerate(plan):
            mine = peers_of(scope)[0]
            copy = pltpu.make_async_copy(part_of(kind, sources[n], mine), through[n], local.at[n])
            copy.start()
            inward.append(copy)
        for n, (scope, kind) in enumerate(plan):
            mine = peers_of(scope)[0]
            inward[n].wait()
            copy = pltpu.make_async_copy(through[n], targets[n].at[mine], local.at[n])
            copy.start()
            copies.append(copy)
        for copy in copies:
            copy.wait()

    return pl.pallas_call(
        body,
        out_shape=shapes,
        in_specs=[pl.BlockSpec(memory_space=pl.ANY)] * number,
        out_specs=[pl.BlockSpec(memory_space=pl.ANY)] * number,
        scratch_shapes=exchange_sems(plan) + [pltpu.VMEM(x.shape[1:], x.dtype) for x in shapes],
        compiler_params=pltpu.CompilerParams(
            collective_id=collective, has_side_effects=True, vmem_limit_bytes=VMEM_BYTES
        ),
    )(*arrays)


def dot(left, right):
    return jnp.dot(left, right, preferred_element_type=jnp.float32)


def fold(tile):
    return jnp.sum(tile.reshape(tile.shape[0] // 8, 8, tile.shape[1]), axis=0)


def attend_body(
    length_ref,
    threshold_ref,
    q_ref,
    kk_ref,
    vv_ref,
    out_ref,
    mass_ref,
    carried_ref,
    excess_ref,
    key_heads,
    value_rows,
    running,
    logits,
    *,
    blocks,
    rows,
):
    lanes = blocks // TEAMS
    me = lax.axis_index("seq")
    team, lane = me // lanes, lax.rem(me, lanes)
    i = pl.program_id(0)
    scale = select_scale / (blocks * rows)
    key_iota = lax.broadcasted_iota(jnp.int32, (rows, rows), 0)
    query_iota = lax.broadcasted_iota(jnp.int32, (rows, rows), 1)

    @pl.when(i == 0)
    def _():
        running[...] = jnp.zeros_like(running)
        excess_ref[...] = jnp.zeros_like(excess_ref)
        for z in range(TEAMS):
            for h in range(TEAM_HEADS):
                key_heads[h, z] = kk_ref[z, :, h * HEAD_DIM : (h + 1) * HEAD_DIM]
            first = kk_ref[z, :, TEAM_WIDTH:]
            if z == 0:
                slot = lax.broadcasted_iota(jnp.int32, first.shape, 0) + lane * rows
                first = jnp.where(slot >= 1, first, jnp.zeros_like(first))
            key_heads[TEAM_HEADS, z] = first
            value_rows[z] = vv_ref[z].T

    active = jnp.where(i >= lane, (i - lane) // lanes + 1, 0)
    threshold = threshold_ref[0]

    @pl.when(active == 0)
    def _():
        out_ref[...] = jnp.zeros_like(out_ref)
        mass_ref[...] = jnp.full(mass_ref.shape, negative, jnp.float32)

    def work(count):
        q_rows = q_ref[0, 0].T
        heads = [q_rows[h * HEAD_DIM : (h + 1) * HEAD_DIM] for h in range(TEAM_HEADS + 1)]
        earlier = jnp.where(key_iota < query_iota, scale, 0.0).astype(jnp.bfloat16)
        every = jnp.full((rows, rows), scale, jnp.bfloat16)
        last = ((count - 1) * lanes + lane) * rows + key_iota
        query_pos = i * rows + query_iota
        peaks = [None] * TEAM_HEADS
        for z in range(count):
            first = jnp.maximum(dot(key_heads[TEAM_HEADS, z], heads[TEAM_HEADS]), 0.0)
            if z == count - 1:
                first = jnp.where(last < query_pos, first, 0.0)
            first = first.astype(jnp.bfloat16)
            carried = running[z] + dot(first, earlier)
            running[z] = running[z] + dot(first, every)

            if z == count - 1:
                carried = jnp.where(last <= query_pos, carried, -negative)
            carried_ref[0, z] = carried
            for h in range(TEAM_HEADS):
                logit = dot(key_heads[h, z], heads[h]) - carried
                logits[h, z] = logit
                peak = jnp.max(logit.reshape(rows // 8, 8, rows), axis=0)
                peaks[h] = peak if z == 0 else jnp.maximum(peaks[h], peak)
        mass_ref[0] = jnp.zeros((8, rows), jnp.float32)
        for h in range(TEAM_HEADS):
            peak = jnp.max(peaks[h], axis=0, keepdims=True)
            mass, mixed = None, None
            for z in range(count):
                terms = jnp.exp(logits[h, z] - peak)
                part = fold(terms)
                values = value_rows[z, h * HEAD_DIM : (h + 1) * HEAD_DIM, :]
                product = dot(values, terms.astype(jnp.bfloat16))
                mass = part if z == 0 else mass + part
                mixed = product if z == 0 else mixed + product
            mass = jnp.sum(mass, axis=0, keepdims=True)
            out_ref[0, h * HEAD_DIM : (h + 1) * HEAD_DIM, :] = (mixed * (1.0 / mass)).astype(
                jnp.bfloat16
            )
            mass_ref[0, h : h + 1, :] = peak + jnp.log(mass)

        @pl.when(lax.rem(i, TEAMS) == team)
        def _():
            total = None
            for z in range(count):
                carried = carried_ref[0, z]
                if z == count - 1:
                    carried = jnp.where(last < query_pos, carried, 0.0)
                part = fold(jnp.clip(carried - threshold, 0.0, 1.0))
                total = part if z == 0 else total + part
            valid = i * rows + lax.broadcasted_iota(jnp.int32, (8, rows), 1) < length_ref[0]
            excess_ref[...] += jnp.where(valid, total, 0.0)

    for count in range(1, TEAMS + 1):
        pl.when(active == count)(functools.partial(work, count))


def attend(length, threshold, queries, keys, values, blocks, rows):
    lanes = blocks // TEAMS
    smem = pl.BlockSpec(memory_space=pltpu.SMEM)
    whole = pl.BlockSpec((TEAMS, rows, QUERY_WIDTH), lambda i: (0, 0, 0))
    return pl.pallas_call(
        functools.partial(attend_body, blocks=blocks, rows=rows),
        grid=(blocks,),
        in_specs=[
            smem,
            smem,
            pl.BlockSpec(
                (1, 1, rows, QUERY_WIDTH), lambda i: (lax.rem(i, lanes), i // lanes, 0, 0)
            ),
            whole,
            pl.BlockSpec((TEAMS, rows, TEAM_WIDTH), lambda i: (0, 0, 0)),
        ],
        out_specs=[
            pl.BlockSpec((1, TEAM_WIDTH, rows), lambda i: (i, 0, 0)),
            pl.BlockSpec((1, 8, rows), lambda i: (i, 0, 0)),
            pl.BlockSpec((1, TEAMS, rows, rows), lambda i: (i, 0, 0, 0)),
            pl.BlockSpec((8, rows), lambda i: (0, 0)),
        ],
        out_shape=[
            jax.ShapeDtypeStruct((blocks, TEAM_WIDTH, rows), jnp.bfloat16),
            jax.ShapeDtypeStruct((blocks, 8, rows), jnp.float32),
            jax.ShapeDtypeStruct((blocks, TEAMS, rows, rows), jnp.float32),
            jax.ShapeDtypeStruct((8, rows), jnp.float32),
        ],
        scratch_shapes=[
            pltpu.VMEM((TEAM_HEADS + 1, TEAMS, rows, HEAD_DIM), jnp.bfloat16),
            pltpu.VMEM((TEAMS, TEAM_WIDTH, rows), jnp.bfloat16),
            pltpu.VMEM((TEAMS, rows, rows), jnp.float32),
            pltpu.VMEM((TEAM_HEADS, TEAMS, rows, rows), jnp.float32),
        ],
        compiler_params=pltpu.CompilerParams(vmem_limit_bytes=VMEM_BYTES),
    )(length, threshold, queries, keys, values)


def attend_back_body(
    q_ref,
    grad_ref,
    stat_ref,
    carried_ref,
    kk_ref,
    vv_ref,
    *refs,
    blocks,
    rows,
):
    plan = [("team", "spread")] * 3
    sources, refs = refs[:3], refs[3:]
    (query_grad_ref, key_grad_ref, value_grad_ref), targets, refs = refs[:3], refs[3:6], refs[6:]
    (key_heads, key_rows, value_heads, running, key_sum, value_sum), sems = refs[:6], refs[6:]
    lanes = blocks // TEAMS
    lane = lax.rem(lax.axis_index("seq"), lanes)
    step = pl.program_id(0)
    i = blocks - 1 - step
    scale = select_scale / (blocks * rows)
    span = [slice(h * HEAD_DIM, (h + 1) * HEAD_DIM) for h in range(TEAM_HEADS + 1)]
    key_iota = lax.broadcasted_iota(jnp.int32, (rows, rows), 0)
    query_iota = lax.broadcasted_iota(jnp.int32, (rows, rows), 1)

    @pl.when(step == 0)
    def _():
        greet(["team"])
        exchange_copies(plan, sources, targets, *sems)
        running[...] = jnp.zeros_like(running)
        key_sum[...] = jnp.zeros_like(key_sum)
        value_sum[...] = jnp.zeros_like(value_sum)
        for z in range(TEAMS):
            for h in range(TEAM_HEADS + 1):
                key_heads[h, z] = kk_ref[z, :, span[h]]
            for h in range(TEAM_HEADS):
                value_heads[h, z] = vv_ref[z, :, span[h]]
            key_rows[z] = kk_ref[z].T
        first = kk_ref[0, :, span[TEAM_HEADS]]
        slot = lax.broadcasted_iota(jnp.int32, first.shape, 0) + lane * rows
        key_heads[TEAM_HEADS, 0] = jnp.where(slot >= 1, first, jnp.zeros_like(first))

    active = jnp.where(i >= lane, (i - lane) // lanes + 1, 0)

    @pl.when(active == 0)
    def _():
        query_grad_ref[...] = jnp.zeros_like(query_grad_ref)

    def work(count):
        q_rows = q_ref[0, 0].T
        grad_rows = grad_ref[0, 0].T
        q_row = [q_rows[span[h]] for h in range(TEAM_HEADS + 1)]
        q_col = [q_ref[0, 0, :, span[h]] for h in range(TEAM_HEADS + 1)]
        grad_row = [grad_rows[span[h]] for h in range(TEAM_HEADS)]
        grad_col = [grad_ref[0, 0, :, span[h]] for h in range(TEAM_HEADS)]
        mass = [stat_ref[0, 0, h : h + 1, :] for h in range(TEAM_HEADS)]
        inner = [stat_ref[0, 0, TEAM_HEADS + h : TEAM_HEADS + h + 1, :] for h in range(TEAM_HEADS)]
        later = jnp.where(key_iota > query_iota, -scale, 0.0).astype(jnp.bfloat16)
        every = jnp.full((rows, rows), -scale, jnp.bfloat16)
        last = ((count - 1) * lanes + lane) * rows + key_iota
        query_pos = i * rows + query_iota
        sums = [None] * (TEAM_HEADS + 1)
        for z in range(count):
            carried = carried_ref[0, z]
            total = None
            for h in range(TEAM_HEADS):
                probs = jnp.exp(dot(key_heads[h, z], q_row[h]) - carried - mass[h])
                value_sum[h, z] += dot(probs.astype(jnp.bfloat16), grad_col[h])
                grad_logit = probs * (dot(value_heads[h, z], grad_row[h]) - inner[h])
                total = grad_logit if h == 0 else total + grad_logit
                low = grad_logit.astype(jnp.bfloat16)
                key_sum[h, z] += dot(low, q_col[h])
                part = dot(key_rows[z, span[h], :], low)
                sums[h] = part if z == 0 else sums[h] + part
            total = total.astype(jnp.bfloat16)
            select_grad = running[z] + dot(total, later)
            running[z] = running[z] + dot(total, every)
            first = dot(key_heads[TEAM_HEADS, z], q_row[TEAM_HEADS])
            live = first > 0.0
            if z == count - 1:
                live = live & (last < query_pos)
            low = jnp.where(live, select_grad, 0.0).astype(jnp.bfloat16)
            key_sum[TEAM_HEADS, z] += dot(low, q_col[TEAM_HEADS])
            part = dot(key_rows[z, span[TEAM_HEADS], :], low)
            sums[TEAM_HEADS] = part if z == 0 else sums[TEAM_HEADS] + part
        for h in range(TEAM_HEADS + 1):
            query_grad_ref[0, 0, span[h], :] = sums[h].astype(jnp.bfloat16)

    for count in range(1, TEAMS + 1):
        pl.when(active == count)(functools.partial(work, count))

    @pl.when(step == blocks - 1)
    def _():
        for h in range(TEAM_HEADS + 1):
            key_grad_ref[:, :, span[h]] = key_sum[h].astype(jnp.bfloat16)
        for h in range(TEAM_HEADS):
            value_grad_ref[:, :, span[h]] = value_sum[h].astype(jnp.bfloat16)
        for copy in exchange_copies(plan, sources, targets, *sems, start=False):
            copy.wait()


def attend_back(queries, grads, stats, carried, keys, values, halves, blocks, rows, collective):
    lanes = blocks // TEAMS
    plan = [("team", "spread")] * 3

    def place(step):
        i = blocks - 1 - step
        return (lax.rem(i, lanes), i // lanes, 0, 0)

    return pl.pallas_call(
        functools.partial(attend_back_body, blocks=blocks, rows=rows),
        grid=(blocks,),
        in_specs=[
            pl.BlockSpec((1, 1, rows, QUERY_WIDTH), place),
            pl.BlockSpec((1, 1, rows, TEAM_WIDTH), place),
            pl.BlockSpec((1, 1, 8, rows), place),
            pl.BlockSpec((1, TEAMS, rows, rows), lambda step: (blocks - 1 - step, 0, 0, 0)),
            pl.BlockSpec((TEAMS, rows, QUERY_WIDTH), lambda step: (0, 0, 0)),
            pl.BlockSpec((TEAMS, rows, TEAM_WIDTH), lambda step: (0, 0, 0)),
        ]
        + [pl.BlockSpec(memory_space=pl.ANY)] * 3,
        out_specs=[
            pl.BlockSpec((1, 1, QUERY_WIDTH, rows), place),
            pl.BlockSpec((TEAMS, rows, QUERY_WIDTH), lambda step: (0, 0, 0)),
            pl.BlockSpec((TEAMS, rows, TEAM_WIDTH), lambda step: (0, 0, 0)),
        ]
        + [pl.BlockSpec(memory_space=pl.ANY)] * 3,
        out_shape=[
            jax.ShapeDtypeStruct((lanes, TEAMS, QUERY_WIDTH, rows), jnp.bfloat16),
            jax.ShapeDtypeStruct((TEAMS, rows, QUERY_WIDTH), jnp.bfloat16),
            jax.ShapeDtypeStruct((TEAMS, rows, TEAM_WIDTH), jnp.bfloat16),
        ]
        + exchange_shapes(plan, halves),
        scratch_shapes=[
            pltpu.VMEM((TEAM_HEADS + 1, TEAMS, rows, HEAD_DIM), jnp.bfloat16),
            pltpu.VMEM((TEAMS, QUERY_WIDTH, rows), jnp.bfloat16),
            pltpu.VMEM((TEAM_HEADS, TEAMS, rows, HEAD_DIM), jnp.bfloat16),
            pltpu.VMEM((TEAMS, rows, rows), jnp.float32),
            pltpu.VMEM((TEAM_HEADS + 1, TEAMS, rows, HEAD_DIM), jnp.float32),
            pltpu.VMEM((TEAM_HEADS, TEAMS, rows, HEAD_DIM), jnp.float32),
        ]
        + exchange_sems(plan),
        compiler_params=pltpu.CompilerParams(
            collective_id=collective, has_side_effects=True, vmem_limit_bytes=VMEM_BYTES
        ),
    )(queries, grads, stats, carried, keys, values, *halves)


def finish_body(
    main_ref,
    extra_ref,
    rows_ref,
    vector_ref,
    down_ref,
    up_ref,
    out_ref,
    whole_ref,
    home_ref,
    total_ref,
    whole_down,
    whole_up,
    whole_out,
    core_main,
    core_extra,
    send_main,
    send_extra,
    lane_main,
    lane_extra,
    team_send_main,
    team_send_extra,
    team_main,
    team_extra,
    assembled,
    vectors,
    ready,
    core_sems,
    lane_sems,
    team_sems,
    home_sems,
    vector_sems,
    out_lane_sems,
    out_core_sems,
    local_sems,
    early_team,
    early_lane,
    early_core,
    early_local,
):
    lanes = lax.axis_size("seq") // TEAMS
    me = lax.axis_index("seq")
    core = lax.axis_index("batch")
    team, lane = me // lanes, lax.rem(me, lanes)

    def lane_peer(k):
        other = lax.rem(lane + k, lanes)
        return other, {"seq": team * lanes + other}

    def team_peer(k):
        other = lax.rem(team + k, TEAMS)
        return other, {"seq": other * lanes + lane}

    sibling = {"batch": 1 - core}
    greet(["core", "team", "lane"])

    def place(n, p, t):
        if n == 0:
            return whole_down.at[core, p, t]
        ref = (None, whole_up, whole_out)[n]
        half = ref.shape[3] // 2
        return ref.at[p, t, :, pl.ds(pl.multiple_of(core * half, 128), half)]

    early = (down_ref, up_ref, out_ref)
    number = len(early)
    early_z = [[None] * TEAMS for _ in range(number)]
    for k in range(1, TEAMS):
        _, target = team_peer(k)
        for n in range(number):
            early_z[n][k] = push(
                early[n],
                place(n, lane, team),
                early_team.at[0, n, k],
                early_team.at[1, n, k],
                target,
            )
    early_kept = []
    for n in range(number):
        copy = pltpu.make_async_copy(early[n], place(n, lane, team), early_local.at[n])
        copy.start()
        early_kept.append(copy)
    theirs = pl.ds((1 - core) * lanes, lanes)
    core_copies = [
        push(main_ref.at[theirs], core_main, core_sems.at[0, 0], core_sems.at[1, 0], sibling),
        push(extra_ref.at[theirs], core_extra, core_sems.at[0, 1], core_sems.at[1, 1], sibling),
        push(vector_ref, vectors.at[0], vector_sems.at[0, 0], vector_sems.at[1, 0], sibling),
    ]
    early_out = []
    early_sib = []

    def forward(j):
        t = lax.rem(team - j + TEAMS, TEAMS)
        for n in range(number):
            if j == 0:
                source = early[n]
            else:
                early_z[n][j].wait_recv()
                source = place(n, lane, t)
            for k in range(1, lanes):
                _, target = lane_peer(k)
                early_out.append(
                    push(
                        source,
                        place(n, lane, t),
                        early_lane.at[0, n, j, k],
                        early_lane.at[1, n, j, k],
                        target,
                    )
                )
            early_sib.append(
                push(
                    source,
                    place(n, lane, t),
                    early_core.at[0, n, j, 0],
                    early_core.at[1, n, j, 0],
                    sibling,
                )
            )

    forward(0)
    for copy in core_copies:
        copy.wait()

    both = vector_ref[...] + vectors[0]
    vectors[1 + lane] = both
    ready[0] = both
    for j in range(lanes):
        send_main[j] = (
            main_ref[core * lanes + j].astype(jnp.float32) + core_main[j].astype(jnp.float32)
        ).astype(jnp.bfloat16)
        send_extra[j] = (
            extra_ref[core * lanes + j].astype(jnp.float32) + core_extra[j].astype(jnp.float32)
        ).astype(jnp.bfloat16)
    lane_copies = []
    for k in range(1, lanes):
        other, target = lane_peer(k)
        lane_copies += [
            push(send_main.at[other], lane_main.at[lane], lane_sems.at[0, 0, k], lane_sems.at[1, 0, k], target),
            push(send_extra.at[other], lane_extra.at[lane], lane_sems.at[0, 1, k], lane_sems.at[1, 1, k], target),
            push(ready.at[0], vectors.at[1 + lane], vector_sems.at[0, k], vector_sems.at[1, k], target),
        ]
    lane_main[lane] = send_main[lane]
    lane_extra[lane] = send_extra[lane]
    for copy in lane_copies:
        copy.wait()

    def total(ref, start, number):
        result = ref[start].astype(jnp.float32)
        for j in range(1, number):
            result = result + ref[start + j].astype(jnp.float32)
        return result

    whole_vector = total(vectors, 1, lanes)
    ready[1] = whole_vector
    vectors[1 + lanes + team] = whole_vector
    low_main = total(lane_main, 0, lanes).astype(jnp.bfloat16)
    low_extra = total(lane_extra, 0, lanes).astype(jnp.bfloat16)
    team_send_main[...] = low_main
    team_send_extra[...] = low_extra
    team_main[team] = low_main
    team_extra[team] = low_extra
    team_copies = []
    for k in range(1, TEAMS):
        other, target = team_peer(k)
        at = lanes + k
        team_copies += [
            push(team_send_main, team_main.at[team], team_sems.at[0, 0, k], team_sems.at[1, 0, k], target),
            push(team_send_extra, team_extra.at[team], team_sems.at[0, 1, k], team_sems.at[1, 1, k], target),
            push(ready.at[1], vectors.at[1 + lanes + team], vector_sems.at[0, at], vector_sems.at[1, at], target),
        ]
    home_copies = []
    for k in range(1, TEAMS):
        other, target = team_peer(k)
        home_copies.append(
            push(rows_ref.at[other], home_ref.at[team], home_sems.at[0, k], home_sems.at[1, k], target)
        )
    own = pltpu.make_async_copy(rows_ref.at[team], home_ref.at[team], local_sems.at[0])
    own.start()
    for j in range(1, TEAMS):
        forward(j)
    for copy in team_copies:
        copy.wait()
    total_ref[...] = total(vectors, 1 + lanes, TEAMS)
    extra = total(team_extra, 0, TEAMS)
    pieces = []
    for part in range(3):
        for g in range(TEAMS):
            piece = team_main[g, :, part * TEAM_WIDTH : (part + 1) * TEAM_WIDTH]
            if g == 0 and part < 2:
                more = extra[:, part * HEAD_DIM : (part + 1) * HEAD_DIM]
                first = (piece[:, :HEAD_DIM].astype(jnp.float32) + more).astype(jnp.bfloat16)
                pieces += [first, piece[:, HEAD_DIM:]]
            else:
                pieces.append(piece)
    assembled[...] = jnp.concatenate(pieces, axis=1)

    mine = core * lanes + lane
    out_copies = []
    for k in range(1, lanes):
        _, target = lane_peer(k)
        out_copies.append(
            push(assembled, whole_ref.at[mine], out_lane_sems.at[0, k], out_lane_sems.at[1, k], target)
        )
    core_out = [
        push(assembled, whole_ref.at[mine], out_core_sems.at[0, 0], out_core_sems.at[1, 0], sibling)
    ]
    kept = pltpu.make_async_copy(assembled, whole_ref.at[mine], local_sems.at[1])
    kept.start()
    for j in range(TEAMS):
        for n in range(number):
            for k in range(1, lanes):
                early_out[(j * number + n) * (lanes - 1) + k - 1].wait_recv()
                p = lax.rem(lane - k + lanes, lanes)
                at = place(n, p, lax.rem(team - j + TEAMS, TEAMS))
                early_sib.append(
                    push(at, at, early_core.at[0, n, j, k], early_core.at[1, n, j, k], sibling)
                )
    for k in range(1, lanes):
        source = core * lanes + lax.rem(lane - k + lanes, lanes)
        out_copies[k - 1].wait_recv()
        core_out.append(
            push(
                whole_ref.at[source],
                whole_ref.at[source],
                out_core_sems.at[0, k],
                out_core_sems.at[1, k],
                sibling,
            )
        )
    for copy in out_copies + early_out:
        copy.wait_send()
    for n in range(number):
        for k in range(1, TEAMS):
            early_z[n][k].wait_send()
    for copy in core_out + home_copies + early_sib + early_kept:
        copy.wait()
    own.wait()
    kept.wait()


def finish(main, extra, rows_out, vector, quarters, collective):
    lanes = lax.axis_size("seq") // TEAMS
    chunks, depth, main_width = main.shape
    extra_width = extra.shape[2]
    low = jnp.bfloat16
    dma = pltpu.SemaphoreType.DMA
    down, up, out = quarters
    wholes = [
        (2, lanes, TEAMS) + down.shape,
        (lanes, TEAMS, up.shape[0], 2 * up.shape[1]),
        (lanes, TEAMS, out.shape[0], 2 * out.shape[1]),
    ]
    anywhere = pl.BlockSpec(memory_space=pl.ANY)
    inside = pl.BlockSpec(memory_space=pltpu.VMEM)
    return pl.pallas_call(
        finish_body,
        out_shape=[
            jax.ShapeDtypeStruct((chunks, depth, TEAMS * main_width), low),
            jax.ShapeDtypeStruct(rows_out.shape, low),
            jax.ShapeDtypeStruct(vector.shape, jnp.float32),
        ]
        + [jax.ShapeDtypeStruct(shape, low) for shape in wholes],
        in_specs=[inside, inside, anywhere, inside] + [anywhere] * 3,
        out_specs=[anywhere, anywhere, inside] + [anywhere] * 3,
        scratch_shapes=[
            pltpu.VMEM((lanes, depth, main_width), low),
            pltpu.VMEM((lanes, depth, extra_width), low),
            pltpu.VMEM((lanes, depth, main_width), low),
            pltpu.VMEM((lanes, depth, extra_width), low),
            pltpu.VMEM((lanes, depth, main_width), low),
            pltpu.VMEM((lanes, depth, extra_width), low),
            pltpu.VMEM((depth, main_width), low),
            pltpu.VMEM((depth, extra_width), low),
            pltpu.VMEM((TEAMS, depth, main_width), low),
            pltpu.VMEM((TEAMS, depth, extra_width), low),
            pltpu.VMEM((depth, TEAMS * main_width), low),
            pltpu.VMEM((1 + lanes + TEAMS,) + vector.shape, jnp.float32),
            pltpu.VMEM((2,) + vector.shape, jnp.float32),
            dma((2, 2)),
            dma((2, 2, lanes)),
            dma((2, 2, TEAMS)),
            dma((2, TEAMS)),
            dma((2, lanes + TEAMS)),
            dma((2, lanes)),
            dma((2, lanes)),
            dma((2,)),
            dma((2, 3, TEAMS)),
            dma((2, 3, TEAMS, lanes)),
            dma((2, 3, TEAMS, lanes)),
            dma((3,)),
        ],
        compiler_params=pltpu.CompilerParams(
            collective_id=collective, has_side_effects=True, vmem_limit_bytes=VMEM_BYTES
        ),
    )(main, extra, rows_out, vector, *quarters)


def layer_norm(values, norm_gain, norm_bias):
    row_mean = jnp.mean(values, axis=-1, keepdims=True)
    centred = values - row_mean
    variance = jnp.mean(centred * centred, axis=-1, keepdims=True)
    return centred * lax.rsqrt(variance + epsilon) * norm_gain + norm_bias


def gelu_tanh(values):
    return jax.nn.gelu(values, approximate=True)


def contract_rows(left_op, right_op):
    return lax.dot_general(
        left_op, right_op, (((0,), (0,)), ((), ())), preferred_element_type=jnp.float32
    )


def contract_cols(left_op, right_op):
    return lax.dot_general(
        left_op, right_op, (((1,), (1,)), ((), ())), preferred_element_type=jnp.float32
    )


def per_device(
    block_input,
    ln1_gain,
    ln1_bias,
    w_qkv,
    w_out,
    ln2_gain,
    ln2_bias,
    w_up,
    w_down,
    length_draw,
    threshold_index,
    grad_out,
):
    rows = block_input.shape[1]
    width = block_input.shape[2]
    blocks = lax.axis_size("seq")
    lanes = blocks // TEAMS
    group_len = blocks * rows
    me = lax.axis_index("seq")
    team = me // lanes
    score_scale = HEAD_DIM ** (-0.5)
    length = group_len - rows + 1 + length_draw % rows
    row_valid = (me * rows + jnp.arange(rows, dtype=jnp.int32) < length[0])[:, None]
    threshold = threshold_index.astype(jnp.float32) / 128.0
    tokens = block_input[0]
    grad_top = grad_out[0]
    grad_top_low = grad_top.astype(jnp.bfloat16)

    normed, ln1_pull = jax.vjp(layer_norm, tokens, ln1_gain, ln1_bias)
    normed_low = normed.astype(jnp.bfloat16)
    (lane_rows,) = exchange([("lane", "gather")], [normed_low], 0)
    lane_rows = lane_rows.reshape(TEAMS * rows, width)

    def columns(part):
        return lax.dynamic_slice_in_dim(w_qkv, part * width + team * TEAM_WIDTH, TEAM_WIDTH, 1)

    team_weight = jnp.concatenate(
        [columns(0), columns(1), columns(2), w_qkv[:, :HEAD_DIM], w_qkv[:, width : width + HEAD_DIM]],
        axis=1,
    )
    projected = dot(lane_rows, team_weight).astype(jnp.bfloat16)
    query_part, key_part, value_part, query_first, key_first = jnp.split(
        projected, [TEAM_WIDTH, 2 * TEAM_WIDTH, 3 * TEAM_WIDTH, 3 * TEAM_WIDTH + HEAD_DIM], axis=1
    )
    queries = jnp.concatenate([query_part, query_first], axis=1) * jnp.bfloat16(score_scale)
    keys = jnp.concatenate([key_part, key_first], axis=1).reshape(TEAMS, rows, QUERY_WIDTH)
    values = value_part.reshape(TEAMS, rows, TEAM_WIDTH)
    (queries,) = exchange(
        [("team", "gather")], [queries.reshape(TEAMS, rows, QUERY_WIDTH)], 1
    )

    parts, masses, carried, excess = attend(
        length, threshold, queries, keys, values, blocks, rows
    )
    parts, masses = exchange([("all", "spread"), ("all", "spread")], [parts, masses], 2)
    parts = parts.astype(jnp.float32).reshape(TEAMS, lanes, TEAM_HEADS, HEAD_DIM, rows)
    masses = masses.reshape(TEAMS, lanes, 8, rows)[:, :, :TEAM_HEADS]
    peak = jnp.max(masses, axis=1, keepdims=True)
    shares = jnp.exp(masses - peak)
    mass = jnp.sum(shares, axis=1, keepdims=True)
    shares = shares / mass
    log_mass = (peak + jnp.log(mass))[:, 0]
    head_out = jnp.sum(parts * shares[:, :, :, None, :], axis=1)
    attn_mixed = jnp.where(
        row_valid, head_out.reshape(width, rows).T, 0.0
    ).astype(jnp.bfloat16)

    residual = tokens + dot(attn_mixed, w_out)
    normed_two, ln2_pull = jax.vjp(layer_norm, residual, ln2_gain, ln2_bias)
    normed_two_low = normed_two.astype(jnp.bfloat16)
    hidden = dot(normed_two_low, w_up)
    activated, gelu_pull = jax.vjp(gelu_tanh, hidden)
    activated_low = activated.astype(jnp.bfloat16)
    layer_out = residual + dot(activated_low, w_down)
    grad_hidden_low = gelu_pull(contract_cols(grad_top_low, w_down))[0].astype(jnp.bfloat16)
    grad_resid_norm, grad_ln2_gain, grad_ln2_bias = ln2_pull(contract_cols(grad_hidden_low, w_up))
    grad_resid = grad_top + grad_resid_norm
    grad_attn_low = grad_resid.astype(jnp.bfloat16)
    grad_mixed = jnp.where(
        row_valid,
        contract_cols(grad_attn_low, w_out).astype(jnp.bfloat16),
        jnp.zeros((), jnp.bfloat16),
    )
    grad_rows = grad_mixed.T.reshape(TEAMS, TEAM_HEADS, HEAD_DIM, rows).astype(jnp.float32)
    inner = jnp.sum(grad_rows * head_out, axis=2)
    stats = jnp.concatenate(
        [log_mass, inner, jnp.zeros((TEAMS, 8 - 2 * TEAM_HEADS, rows), jnp.float32)], axis=1
    )
    grad_cols = jnp.moveaxis(grad_mixed.reshape(rows, TEAMS, TEAM_WIDTH), 1, 0)
    grad_cols, stats, *pairs_of = exchange(
        [("lane", "spread"), ("lane", "spread")]
        + [("core", kind) for kind in ("half", "gather", "gather", "half", "gather", "half")],
        [
            grad_cols,
            stats,
            activated_low,
            grad_top_low,
            normed_two_low,
            grad_hidden_low,
            attn_mixed,
            grad_attn_low,
        ],
        3,
    )
    pairs_of = [x.reshape(2 * rows, -1) for x in pairs_of]
    down_half = contract_rows(pairs_of[0], pairs_of[1]).astype(jnp.bfloat16)
    up_half = contract_rows(pairs_of[2], pairs_of[3]).astype(jnp.bfloat16)
    out_half = contract_rows(pairs_of[4], pairs_of[5]).astype(jnp.bfloat16)
    halves = [x.reshape(lanes, TEAMS, -1, x.shape[1]) for x in (down_half, up_half, out_half)]
    grad_cols, stats = exchange([("team", "gather"), ("team", "gather")], [grad_cols, stats], 4)
    query_grads, key_grads, value_grads, *halves = attend_back(
        queries, grad_cols, stats, carried, keys, values, halves, blocks, rows, 7
    )

    def summed(x):
        return jnp.sum(x.astype(jnp.float32), axis=0).astype(jnp.bfloat16)

    query_grads, *quarters = exchange(
        [("team", "spread")] + [("lane", "spread")] * 3,
        [query_grads] + [summed(x) for x in halves],
        5,
    )
    quarters = [summed(x) for x in quarters]
    query_grads = jnp.sum(query_grads.astype(jnp.float32), axis=0) * score_scale
    query_grads = jnp.swapaxes(query_grads.astype(jnp.bfloat16), 1, 2)
    grad_projected = jnp.concatenate(
        [
            query_grads[:, :, :TEAM_WIDTH],
            key_grads[:, :, :TEAM_WIDTH],
            value_grads,
            query_grads[:, :, TEAM_WIDTH:],
            key_grads[:, :, TEAM_WIDTH:],
        ],
        axis=2,
    ).reshape(TEAMS * rows, -1)
    chunks = 2 * lanes
    grad_main = contract_rows(lane_rows, grad_projected[:, : 3 * TEAM_WIDTH])
    grad_extra = contract_rows(lane_rows, grad_projected[:, 3 * TEAM_WIDTH :])
    grad_lane_rows = contract_cols(grad_projected, team_weight)
    grad_ln1_bias = jnp.sum(grad_lane_rows, axis=0)
    grad_ln1_gain = (
        jnp.sum(grad_lane_rows * (lane_rows.astype(jnp.float32) - ln1_bias), axis=0) / ln1_gain
    )
    pairs = (length[0] - 1).astype(jnp.float32) * (length[0] - 2).astype(jnp.float32) / 2.0
    vectors = jnp.stack(
        [
            grad_ln1_gain,
            grad_ln1_bias,
            grad_ln2_gain,
            grad_ln2_bias,
            jnp.full((width,), jnp.sum(excess)),
            jnp.full((width,), pairs / blocks),
            jnp.zeros((width,), jnp.float32),
            jnp.zeros((width,), jnp.float32),
        ]
    )
    grad_w_qkv, home_rows, vectors, grad_w_down, grad_w_up, grad_w_out = finish(
        grad_main.astype(jnp.bfloat16).reshape(chunks, width // chunks, -1),
        grad_extra.astype(jnp.bfloat16).reshape(chunks, width // chunks, -1),
        grad_lane_rows.astype(jnp.bfloat16).reshape(TEAMS, rows, width),
        vectors,
        quarters,
        6,
    )
    grad_w_down = grad_w_down.reshape(w_down.shape)
    grad_w_up = grad_w_up.reshape(w_up.shape)
    grad_w_out = grad_w_out.reshape(w_out.shape)
    grad_w_qkv = grad_w_qkv.reshape(width, 3 * width)
    grad_normed = jnp.sum(home_rows.astype(jnp.float32), axis=0)
    grad_x = grad_resid + ln1_pull(grad_normed)[0]
    pruned_share = (vectors[4, 0] / vectors[5, 0]).reshape(1)
    return (
        layer_out[None],
        grad_x[None],
        vectors[0],
        vectors[1],
        grad_w_qkv.astype(jnp.float32),
        grad_w_out.astype(jnp.float32),
        vectors[2],
        vectors[3],
        grad_w_up.astype(jnp.float32),
        grad_w_down.astype(jnp.float32),
        pruned_share,
    )


def solution(mesh):
    placed = (
        P("batch", "seq", None),
        P(),
        P(),
        P(),
        P(),
        P(),
        P(),
        P(),
        P(),
        P("batch"),
        P(),
        P("batch", "seq", None),
    )
    return jax.shard_map(
        per_device,
        mesh=mesh,
        in_specs=placed,
        out_specs=(
            P("batch", "seq", None),
            P("batch", "seq", None),
            P(),
            P(),
            P(),
            P(),
            P(),
            P(),
            P(),
            P(),
            P(),
        ),
        check_vma=False,
    )
```

```python
import functools

import jax
import jax.numpy as jnp
from jax import lax
from jax.experimental import pallas as pl
from jax.experimental.pallas import tpu as pltpu
from jax.sharding import PartitionSpec as P

HEADS = 12
HEAD_DIM = 64
TEAMS = 4
TEAM_HEADS = HEADS // TEAMS
TEAM_WIDTH = TEAM_HEADS * HEAD_DIM
QUERY_WIDTH = TEAM_WIDTH + HEAD_DIM

epsilon = 1e-05
negative = -1e30
select_scale = 3.0
VMEM_BYTES = 60 * 2**20
MESH = pl.DeviceIdType.MESH


def peers_of(scope):
    lanes = lax.axis_size("seq") // TEAMS
    me = lax.axis_index("seq")
    team, lane = me // lanes, lax.rem(me, lanes)
    if scope == "team":
        return lane, lanes, lambda k: {"seq": team * lanes + k}
    if scope == "lane":
        return team, TEAMS, lambda k: {"seq": k * lanes + lane}
    if scope == "core":
        return lax.axis_index("batch"), 2, lambda k: {"batch": k}
    return me, lanes * TEAMS, lambda k: {"seq": k}


def scope_size(scope):
    count = lax.axis_size("seq")
    return {"team": count // TEAMS, "lane": TEAMS, "core": 2, "all": count}[scope]


def greet(scopes):
    barrier = pltpu.get_barrier_semaphore()
    number = 0
    for scope in scopes:
        mine, peers, device_of = peers_of(scope)
        for k in range(1, peers):
            pl.semaphore_signal(
                barrier, inc=1, device_id=device_of(lax.rem(mine + k, peers)), device_id_type=MESH
            )
        number += peers - 1
    pl.semaphore_wait(barrier, number)


def push(source, destination, send, receive, target, start=True):
    copy = pltpu.make_async_remote_copy(
        src_ref=source,
        dst_ref=destination,
        send_sem=send,
        recv_sem=receive,
        device_id=target,
        device_id_type=MESH,
    )
    if start:
        copy.start()
    return copy


def part_of(kind, ref, k):
    if kind == "gather":
        return ref
    if kind == "spread":
        return ref.at[k]
    half = ref.shape[1] // 2
    return ref.at[:, pl.ds(pl.multiple_of(k * half, 128), half)]


def remote_copies(plan, sources, targets, send, receive, start=True):
    copies = []
    for n, (scope, kind) in enumerate(plan):
        mine, peers, device_of = peers_of(scope)
        for k in range(1, peers):
            peer = lax.rem(mine + k, peers)
            copies.append(
                push(
                    part_of(kind, sources[n], peer),
                    targets[n].at[mine],
                    send.at[n, k],
                    receive.at[n, k],
                    device_of(peer),
                    start,
                )
            )
    return copies


def exchange_copies(plan, sources, targets, send, receive, local, start=True):
    copies = remote_copies(plan, sources, targets, send, receive, start)
    for n, (scope, kind) in enumerate(plan):
        mine = peers_of(scope)[0]
        copy = pltpu.make_async_copy(
            part_of(kind, sources[n], mine), targets[n].at[mine], local.at[n]
        )
        if start:
            copy.start()
        copies.append(copy)
    return copies


def exchange_shapes(plan, arrays):
    shapes = []
    for (scope, kind), x in zip(plan, arrays):
        shape = x.shape
        if kind == "gather":
            shape = (scope_size(scope),) + shape
        if kind == "half":
            shape = (2, shape[0], shape[1] // 2)
        shapes.append(jax.ShapeDtypeStruct(shape, x.dtype))
    return shapes


def exchange_sems(plan):
    number, most = len(plan), max(scope_size(scope) for scope, _ in plan)
    return [
        pltpu.SemaphoreType.DMA((number, most)),
        pltpu.SemaphoreType.DMA((number, most)),
        pltpu.SemaphoreType.DMA((number,)),
    ]


def scopes_of(plan):
    return [x for x in ("core", "team", "lane", "all") if x in [scope for scope, _ in plan]]


def exchange(plan, arrays, collective):
    number = len(arrays)
    shapes = exchange_shapes(plan, arrays)

    def body(*refs):
        sources, targets = refs[:number], refs[number : 2 * number]
        send, receive, local = refs[2 * number : 2 * number + 3]
        through = refs[2 * number + 3 :]
        greet(scopes_of(plan))
        copies = remote_copies(plan, sources, targets, send, receive)
        inward = []
        for n, (scope, kind) in enumerate(plan):
            mine = peers_of(scope)[0]
            copy = pltpu.make_async_copy(part_of(kind, sources[n], mine), through[n], local.at[n])
            copy.start()
            inward.append(copy)
        for n, (scope, kind) in enumerate(plan):
            mine = peers_of(scope)[0]
            inward[n].wait()
            copy = pltpu.make_async_copy(through[n], targets[n].at[mine], local.at[n])
            copy.start()
            copies.append(copy)
        for copy in copies:
            copy.wait()

    return pl.pallas_call(
        body,
        out_shape=shapes,
        in_specs=[pl.BlockSpec(memory_space=pl.ANY)] * number,
        out_specs=[pl.BlockSpec(memory_space=pl.ANY)] * number,
        scratch_shapes=exchange_sems(plan) + [pltpu.VMEM(x.shape[1:], x.dtype) for x in shapes],
        compiler_params=pltpu.CompilerParams(
            collective_id=collective, has_side_effects=True, vmem_limit_bytes=VMEM_BYTES
        ),
    )(*arrays)


def dot(left, right):
    return jnp.dot(left, right, preferred_element_type=jnp.float32)


def project_body(
    tokens_ref,
    gain_ref,
    bias_ref,
    w_ref,
    lane_ref,
    weight_ref,
    query_ref,
    key_ref,
    value_ref,
    held,
    ready,
    windows,
    firsts,
    hop_send,
    hop_recv,
    team_send,
    team_recv,
    weight_sems,
    local_sems,
):
    lanes = lax.axis_size("seq") // TEAMS
    me = lax.axis_index("seq")
    team, lane = me // lanes, lax.rem(me, lanes)
    width = tokens_ref.shape[1]
    wide = windows.shape[2]
    start = (3 * team // 2) * 128
    loads = []
    for part in range(3):
        at = pl.ds(pl.multiple_of(part * width + start, 128), wide)
        loads.append(pltpu.make_async_copy(w_ref.at[:, at], windows.at[part], weight_sems.at[part]))
    for part in range(2):
        at = pl.ds(part * width, 128)
        loads.append(
            pltpu.make_async_copy(w_ref.at[:, at], firsts.at[part], weight_sems.at[3 + part])
        )
    for load in loads:
        load.start()
    tokens = tokens_ref[...]
    row_mean = jnp.mean(tokens, axis=1, keepdims=True)
    centred = tokens - row_mean
    variance = jnp.mean(centred * centred, axis=1, keepdims=True)
    normed = centred * lax.rsqrt(variance + epsilon) * gain_ref[...] + bias_ref[...]
    held[team] = normed.astype(jnp.bfloat16)
    greet(["team", "lane"])

    def hop(side, distance, start=True):
        block = team - distance if side == 0 else team + distance
        target = me + lanes if side == 0 else me - lanes
        return push(
            held.at[block],
            held.at[block],
            hop_send.at[side, distance],
            hop_recv.at[side, distance],
            {"seq": target},
            start,
        )

    @pl.when(team < TEAMS - 1)
    def _():
        hop(0, 0)

    @pl.when(team > 0)
    def _():
        hop(1, 0)

    for load in loads:
        load.wait()
    odd = lax.rem(team, 2) == 1
    pieces = []
    for part in range(3):
        window = windows[part]
        pieces.append(
            jnp.where(odd, window[:, wide - TEAM_WIDTH :], window[:, :TEAM_WIDTH])
        )
        if part < 2:
            pieces.append(firsts[part][:, :HEAD_DIM])
    weight_ref[...] = jnp.concatenate(pieces, axis=1)

    def block_copies(block, start):
        copies = []
        for k in range(1, lanes):
            target = {"seq": team * lanes + lax.rem(lane + k, lanes)}
            copies.append(
                push(
                    ready.at[block],
                    query_ref.at[lane, block],
                    team_send.at[block, k],
                    team_recv.at[block, k],
                    target,
                    start,
                )
            )
        for n, (source, destination) in enumerate(
            ((ready.at[block], query_ref.at[lane, block]), (held.at[block], lane_ref.at[block]))
        ):
            copy = pltpu.make_async_copy(source, destination, local_sems.at[n, block])
            if start:
                copy.start()
            copies.append(copy)
        return copies

    def project(block):
        result = dot(held[block], weight_ref[...]).astype(jnp.bfloat16)
        ready[block] = result[:, :QUERY_WIDTH] * jnp.bfloat16(HEAD_DIM ** (-0.5))
        block_copies(block, True)
        key_ref[block] = result[:, QUERY_WIDTH : 2 * QUERY_WIDTH]
        value_ref[block] = result[:, 2 * QUERY_WIDTH :]

    project(team)

    def arrive(step, _):
        distance, side = step // 2 + 1, lax.rem(step, 2)
        for which in range(2):
            block = team - distance if which == 0 else team + distance
            there = (block >= 0) if which == 0 else (block < TEAMS)
            further = (team < TEAMS - 1) if which == 0 else (team > 0)

            @pl.when((side == which) & there)
            def _():
                hop(which, distance - 1, False).wait_recv()

                @pl.when(further)
                def _():
                    hop(which, distance)

                project(block)

        return 0

    lax.fori_loop(0, 2 * (TEAMS - 1), arrive, 0)
    for distance in range(TEAMS - 1):

        @pl.when((team < TEAMS - 1) & (team >= distance))
        def _():
            hop(0, distance, False).wait_send()

        @pl.when((team > 0) & (team + distance < TEAMS))
        def _():
            hop(1, distance, False).wait_send()

    for block in range(TEAMS):
        for copy in block_copies(block, False):
            copy.wait()


def project(tokens, gain, bias, weight, collective):
    lanes = lax.axis_size("seq") // TEAMS
    rows, width = tokens.shape
    inside = pl.BlockSpec(memory_space=pltpu.VMEM)
    anywhere = pl.BlockSpec(memory_space=pl.ANY)
    columns = 2 * QUERY_WIDTH + TEAM_WIDTH
    low = jnp.bfloat16
    dma = pltpu.SemaphoreType.DMA
    return pl.pallas_call(
        project_body,
        out_shape=[
            jax.ShapeDtypeStruct((TEAMS, rows, width), low),
            jax.ShapeDtypeStruct((width, columns), low),
            jax.ShapeDtypeStruct((lanes, TEAMS, rows, QUERY_WIDTH), low),
            jax.ShapeDtypeStruct((TEAMS, rows, QUERY_WIDTH), low),
            jax.ShapeDtypeStruct((TEAMS, rows, TEAM_WIDTH), low),
        ],
        in_specs=[inside, inside, inside, anywhere],
        out_specs=[anywhere, inside, anywhere, inside, inside],
        scratch_shapes=[
            pltpu.VMEM((TEAMS, rows, width), low),
            pltpu.VMEM((TEAMS, rows, QUERY_WIDTH), low),
            pltpu.VMEM((3, width, 256), low),
            pltpu.VMEM((2, width, 128), low),
            dma((2, TEAMS)),
            dma((2, TEAMS)),
            dma((TEAMS, lanes)),
            dma((TEAMS, lanes)),
            dma((5,)),
            dma((2, TEAMS)),
        ],
        compiler_params=pltpu.CompilerParams(
            collective_id=collective, has_side_effects=True, vmem_limit_bytes=VMEM_BYTES
        ),
    )(tokens, gain[None], bias[None], weight)


def fold(tile):
    return jnp.sum(tile.reshape(tile.shape[0] // 8, 8, tile.shape[1]), axis=0)


def attend_body(
    length_ref,
    threshold_ref,
    q_ref,
    kk_ref,
    vv_ref,
    out_ref,
    mass_ref,
    carried_ref,
    excess_ref,
    key_heads,
    value_rows,
    running,
    logits,
    out_all,
    mass_all,
    lane_out,
    lane_mass,
    joined_out,
    joined_mass,
    home_out,
    home_mass,
    lane_send,
    lane_recv,
    home_send,
    home_recv,
    *,
    blocks,
    rows,
):
    lanes = blocks // TEAMS
    me = lax.axis_index("seq")
    team, lane = me // lanes, lax.rem(me, lanes)
    i = pl.program_id(0)
    scale = select_scale / (blocks * rows)
    key_iota = lax.broadcasted_iota(jnp.int32, (rows, rows), 0)
    query_iota = lax.broadcasted_iota(jnp.int32, (rows, rows), 1)

    def part_copies(j, start):
        z, owner = j // lanes, lax.rem(j, lanes)
        return [
            push(
                source.at[j],
                destination.at[z, lane],
                lane_send.at[n, j],
                lane_recv.at[n, z, lane],
                {"seq": team * lanes + owner},
                start,
            )
            for n, (source, destination) in enumerate(
                ((out_all, lane_out), (mass_all, lane_mass))
            )
        ]

    def home_copies(z, start):
        return [
            push(
                source.at[z],
                destination.at[team],
                home_send.at[n, z],
                home_recv.at[n, team],
                {"seq": z * lanes + lane},
                start,
            )
            for n, (source, destination) in enumerate(
                ((joined_out, home_out), (joined_mass, home_mass))
            )
        ]

    def join(z):
        for k in range(1, lanes):
            other = lax.rem(lane + k, lanes)
            for n, buffer in enumerate((lane_out, lane_mass)):
                pltpu.make_async_copy(
                    buffer.at[z, other], buffer.at[z, other], lane_recv.at[n, z, other]
                ).wait()
        masses = [lane_mass[z, p] for p in range(lanes)]
        peak = masses[0]
        for p in range(1, lanes):
            peak = jnp.maximum(peak, masses[p])
        shares = [jnp.exp(mass - peak) for mass in masses]
        whole = shares[0]
        for p in range(1, lanes):
            whole = whole + shares[p]
        joined_mass[z] = peak + jnp.log(whole)
        inverse = 1.0 / whole
        for h in range(TEAM_HEADS):
            span = slice(h * HEAD_DIM, (h + 1) * HEAD_DIM)
            mixed = None
            for p in range(lanes):
                share = (shares[p] * inverse)[h : h + 1, :]
                part = lane_out[z, p, span, :].astype(jnp.float32) * share
                mixed = part if p == 0 else mixed + part
            joined_out[z, span, :] = mixed.astype(jnp.bfloat16)

        @pl.when(team != z)
        def _():
            home_copies(z, True)

        @pl.when(team == z)
        def _():
            home_out[team] = joined_out[z]
            home_mass[team] = joined_mass[z]

    @pl.when(i == 0)
    def _():
        greet(["team", "lane"])
        running[...] = jnp.zeros_like(running)
        excess_ref[...] = jnp.zeros_like(excess_ref)
        for z in range(TEAMS):
            for h in range(TEAM_HEADS):
                key_heads[h, z] = kk_ref[z, :, h * HEAD_DIM : (h + 1) * HEAD_DIM]
            first = kk_ref[z, :, TEAM_WIDTH:]
            if z == 0:
                slot = lax.broadcasted_iota(jnp.int32, first.shape, 0) + lane * rows
                first = jnp.where(slot >= 1, first, jnp.zeros_like(first))
            key_heads[TEAM_HEADS, z] = first
            value_rows[z] = vv_ref[z].T

    active = jnp.where(i >= lane, (i - lane) // lanes + 1, 0)
    threshold = threshold_ref[0]

    @pl.when(active == 0)
    def _():
        out_all[i] = jnp.zeros((TEAM_WIDTH, rows), jnp.bfloat16)
        mass_all[i] = jnp.full((8, rows), negative, jnp.float32)

    def work(count):
        q_rows = q_ref[0, 0].T
        heads = [q_rows[h * HEAD_DIM : (h + 1) * HEAD_DIM] for h in range(TEAM_HEADS + 1)]
        earlier = jnp.where(key_iota < query_iota, scale, 0.0).astype(jnp.bfloat16)
        every = jnp.full((rows, rows), scale, jnp.bfloat16)
        last = ((count - 1) * lanes + lane) * rows + key_iota
        query_pos = i * rows + query_iota
        peaks = [None] * TEAM_HEADS
        for z in range(count):
            first = jnp.maximum(dot(key_heads[TEAM_HEADS, z], heads[TEAM_HEADS]), 0.0)
            if z == count - 1:
                first = jnp.where(last < query_pos, first, 0.0)
            first = first.astype(jnp.bfloat16)
            carried = running[z] + dot(first, earlier)
            running[z] = running[z] + dot(first, every)

            if z == count - 1:
                carried = jnp.where(last <= query_pos, carried, -negative)
            carried_ref[0, z] = carried
            for h in range(TEAM_HEADS):
                logit = dot(key_heads[h, z], heads[h]) - carried
                logits[h, z] = logit
                peak = jnp.max(logit.reshape(rows // 8, 8, rows), axis=0)
                peaks[h] = peak if z == 0 else jnp.maximum(peaks[h], peak)
        mass_all[i] = jnp.zeros((8, rows), jnp.float32)
        for h in range(TEAM_HEADS):
            peak = jnp.max(peaks[h], axis=0, keepdims=True)
            mass, mixed = None, None
            for z in range(count):
                terms = jnp.exp(logits[h, z] - peak)
                part = fold(terms)
                values = value_rows[z, h * HEAD_DIM : (h + 1) * HEAD_DIM, :]
                product = dot(values, terms.astype(jnp.bfloat16))
                mass = part if z == 0 else mass + part
                mixed = product if z == 0 else mixed + product
            mass = jnp.sum(mass, axis=0, keepdims=True)
            out_all[i, h * HEAD_DIM : (h + 1) * HEAD_DIM, :] = (mixed * (1.0 / mass)).astype(
                jnp.bfloat16
            )
            mass_all[i, h : h + 1, :] = peak + jnp.log(mass)

        @pl.when(lax.rem(i, TEAMS) == team)
        def _():
            total = None
            for z in range(count):
                carried = carried_ref[0, z]
                if z == count - 1:
                    carried = jnp.where(last < query_pos, carried, 0.0)
                part = fold(jnp.clip(carried - threshold, 0.0, 1.0))
                total = part if z == 0 else total + part
            valid = i * rows + lax.broadcasted_iota(jnp.int32, (8, rows), 1) < length_ref[0]
            excess_ref[...] += jnp.where(valid, total, 0.0)

    for count in range(1, TEAMS + 1):
        pl.when(active == count)(functools.partial(work, count))

    @pl.when(lax.rem(i, lanes) != lane)
    def _():
        part_copies(i, True)

    @pl.when(lax.rem(i, lanes) == lane)
    def _():
        lane_out[i // lanes, lane] = out_all[i]
        lane_mass[i // lanes, lane] = mass_all[i]

    for z in range(TEAMS - 1):
        pl.when(i == (z + 1) * lanes + 1)(functools.partial(join, z))

    @pl.when(i == blocks - 1)
    def _():
        join(TEAMS - 1)

        def drain(j, _):
            @pl.when(lax.rem(j, lanes) != lane)
            def _():
                for copy in part_copies(j, False):
                    copy.wait_send()

            return 0

        lax.fori_loop(0, blocks, drain, 0)
        for z in range(TEAMS):

            @pl.when(team != z)
            def _():
                for copy in home_copies(z, False):
                    copy.wait_send()
                for n, buffer in enumerate((home_out, home_mass)):
                    pltpu.make_async_copy(
                        buffer.at[z], buffer.at[z], home_recv.at[n, z]
                    ).wait()

        out_ref[...] = home_out[...]
        mass_ref[...] = home_mass[...]

def attend(length, threshold, queries, keys, values, blocks, rows, collective):
    lanes = blocks // TEAMS
    smem = pl.BlockSpec(memory_space=pltpu.SMEM)
    whole = pl.BlockSpec((TEAMS, rows, QUERY_WIDTH), lambda i: (0, 0, 0))
    return pl.pallas_call(
        functools.partial(attend_body, blocks=blocks, rows=rows),
        grid=(blocks,),
        in_specs=[
            smem,
            smem,
            pl.BlockSpec(
                (1, 1, rows, QUERY_WIDTH), lambda i: (lax.rem(i, lanes), i // lanes, 0, 0)
            ),
            whole,
            pl.BlockSpec((TEAMS, rows, TEAM_WIDTH), lambda i: (0, 0, 0)),
        ],
        out_specs=[
            pl.BlockSpec((TEAMS, TEAM_WIDTH, rows), lambda i: (0, 0, 0)),
            pl.BlockSpec((TEAMS, 8, rows), lambda i: (0, 0, 0)),
            pl.BlockSpec((1, TEAMS, rows, rows), lambda i: (i, 0, 0, 0)),
            pl.BlockSpec((8, rows), lambda i: (0, 0)),
        ],
        out_shape=[
            jax.ShapeDtypeStruct((TEAMS, TEAM_WIDTH, rows), jnp.bfloat16),
            jax.ShapeDtypeStruct((TEAMS, 8, rows), jnp.float32),
            jax.ShapeDtypeStruct((blocks, TEAMS, rows, rows), jnp.float32),
            jax.ShapeDtypeStruct((8, rows), jnp.float32),
        ],
        scratch_shapes=[
            pltpu.VMEM((TEAM_HEADS + 1, TEAMS, rows, HEAD_DIM), jnp.bfloat16),
            pltpu.VMEM((TEAMS, TEAM_WIDTH, rows), jnp.bfloat16),
            pltpu.VMEM((TEAMS, rows, rows), jnp.float32),
            pltpu.VMEM((TEAM_HEADS, TEAMS, rows, rows), jnp.float32),
            pltpu.VMEM((blocks, TEAM_WIDTH, rows), jnp.bfloat16),
            pltpu.VMEM((blocks, 8, rows), jnp.float32),
            pltpu.VMEM((TEAMS, lanes, TEAM_WIDTH, rows), jnp.bfloat16),
            pltpu.VMEM((TEAMS, lanes, 8, rows), jnp.float32),
            pltpu.VMEM((TEAMS, TEAM_WIDTH, rows), jnp.bfloat16),
            pltpu.VMEM((TEAMS, 8, rows), jnp.float32),
            pltpu.VMEM((TEAMS, TEAM_WIDTH, rows), jnp.bfloat16),
            pltpu.VMEM((TEAMS, 8, rows), jnp.float32),
            pltpu.SemaphoreType.DMA((2, blocks)),
            pltpu.SemaphoreType.DMA((2, TEAMS, lanes)),
            pltpu.SemaphoreType.DMA((2, TEAMS)),
            pltpu.SemaphoreType.DMA((2, TEAMS)),
        ],
        compiler_params=pltpu.CompilerParams(
            collective_id=collective, has_side_effects=True, vmem_limit_bytes=VMEM_BYTES
        ),
    )(length, threshold, queries, keys, values)


def attend_back_body(
    q_ref,
    grad_ref,
    stat_ref,
    carried_ref,
    kk_ref,
    vv_ref,
    *refs,
    blocks,
    rows,
):
    plan = [("team", "spread")] * 3
    sources, refs = refs[:3], refs[3:]
    (query_grad_ref, key_grad_ref, value_grad_ref), targets, refs = refs[:3], refs[3:6], refs[6:]
    (key_heads, key_rows, value_heads, running, key_sum, value_sum), sems = refs[:6], refs[6:]
    lanes = blocks // TEAMS
    lane = lax.rem(lax.axis_index("seq"), lanes)
    step = pl.program_id(0)
    i = blocks - 1 - step
    scale = select_scale / (blocks * rows)
    span = [slice(h * HEAD_DIM, (h + 1) * HEAD_DIM) for h in range(TEAM_HEADS + 1)]
    key_iota = lax.broadcasted_iota(jnp.int32, (rows, rows), 0)
    query_iota = lax.broadcasted_iota(jnp.int32, (rows, rows), 1)

    @pl.when(step == 0)
    def _():
        greet(["team"])
        exchange_copies(plan, sources, targets, *sems)
        running[...] = jnp.zeros_like(running)
        key_sum[...] = jnp.zeros_like(key_sum)
        value_sum[...] = jnp.zeros_like(value_sum)
        for z in range(TEAMS):
            for h in range(TEAM_HEADS + 1):
                key_heads[h, z] = kk_ref[z, :, span[h]]
            for h in range(TEAM_HEADS):
                value_heads[h, z] = vv_ref[z, :, span[h]]
            key_rows[z] = kk_ref[z].T
        first = kk_ref[0, :, span[TEAM_HEADS]]
        slot = lax.broadcasted_iota(jnp.int32, first.shape, 0) + lane * rows
        key_heads[TEAM_HEADS, 0] = jnp.where(slot >= 1, first, jnp.zeros_like(first))

    active = jnp.where(i >= lane, (i - lane) // lanes + 1, 0)

    @pl.when(active == 0)
    def _():
        query_grad_ref[...] = jnp.zeros_like(query_grad_ref)

    def work(count):
        q_rows = q_ref[0, 0].T
        grad_rows = grad_ref[0, 0].T
        q_row = [q_rows[span[h]] for h in range(TEAM_HEADS + 1)]
        q_col = [q_ref[0, 0, :, span[h]] for h in range(TEAM_HEADS + 1)]
        grad_row = [grad_rows[span[h]] for h in range(TEAM_HEADS)]
        grad_col = [grad_ref[0, 0, :, span[h]] for h in range(TEAM_HEADS)]
        mass = [stat_ref[0, 0, h : h + 1, :] for h in range(TEAM_HEADS)]
        inner = [stat_ref[0, 0, TEAM_HEADS + h : TEAM_HEADS + h + 1, :] for h in range(TEAM_HEADS)]
        later = jnp.where(key_iota > query_iota, -scale, 0.0).astype(jnp.bfloat16)
        every = jnp.full((rows, rows), -scale, jnp.bfloat16)
        last = ((count - 1) * lanes + lane) * rows + key_iota
        query_pos = i * rows + query_iota
        sums = [None] * (TEAM_HEADS + 1)
        for z in range(count):
            carried = carried_ref[0, z]
            total = None
            for h in range(TEAM_HEADS):
                probs = jnp.exp(dot(key_heads[h, z], q_row[h]) - carried - mass[h])
                value_sum[h, z] += dot(probs.astype(jnp.bfloat16), grad_col[h])
                grad_logit = probs * (dot(value_heads[h, z], grad_row[h]) - inner[h])
                total = grad_logit if h == 0 else total + grad_logit
                low = grad_logit.astype(jnp.bfloat16)
                key_sum[h, z] += dot(low, q_col[h])
                part = dot(key_rows[z, span[h], :], low)
                sums[h] = part if z == 0 else sums[h] + part
            total = total.astype(jnp.bfloat16)
            select_grad = running[z] + dot(total, later)
            running[z] = running[z] + dot(total, every)
            first = dot(key_heads[TEAM_HEADS, z], q_row[TEAM_HEADS])
            live = first > 0.0
            if z == count - 1:
                live = live & (last < query_pos)
            low = jnp.where(live, select_grad, 0.0).astype(jnp.bfloat16)
            key_sum[TEAM_HEADS, z] += dot(low, q_col[TEAM_HEADS])
            part = dot(key_rows[z, span[TEAM_HEADS], :], low)
            sums[TEAM_HEADS] = part if z == 0 else sums[TEAM_HEADS] + part
        for h in range(TEAM_HEADS + 1):
            query_grad_ref[0, 0, span[h], :] = sums[h].astype(jnp.bfloat16)

    for count in range(1, TEAMS + 1):
        pl.when(active == count)(functools.partial(work, count))

    @pl.when(step == blocks - 1)
    def _():
        for h in range(TEAM_HEADS + 1):
            key_grad_ref[:, :, span[h]] = key_sum[h].astype(jnp.bfloat16)
        for h in range(TEAM_HEADS):
            value_grad_ref[:, :, span[h]] = value_sum[h].astype(jnp.bfloat16)
        for copy in exchange_copies(plan, sources, targets, *sems, start=False):
            copy.wait()


def attend_back(queries, grads, stats, carried, keys, values, halves, blocks, rows, collective):
    lanes = blocks // TEAMS
    plan = [("team", "spread")] * 3

    def place(step):
        i = blocks - 1 - step
        return (lax.rem(i, lanes), i // lanes, 0, 0)

    return pl.pallas_call(
        functools.partial(attend_back_body, blocks=blocks, rows=rows),
        grid=(blocks,),
        in_specs=[
            pl.BlockSpec((1, 1, rows, QUERY_WIDTH), place),
            pl.BlockSpec((1, 1, rows, TEAM_WIDTH), place),
            pl.BlockSpec((1, 1, 8, rows), place),
            pl.BlockSpec((1, TEAMS, rows, rows), lambda step: (blocks - 1 - step, 0, 0, 0)),
            pl.BlockSpec((TEAMS, rows, QUERY_WIDTH), lambda step: (0, 0, 0)),
            pl.BlockSpec((TEAMS, rows, TEAM_WIDTH), lambda step: (0, 0, 0)),
        ]
        + [pl.BlockSpec(memory_space=pl.ANY)] * 3,
        out_specs=[
            pl.BlockSpec((1, 1, QUERY_WIDTH, rows), place),
            pl.BlockSpec((TEAMS, rows, QUERY_WIDTH), lambda step: (0, 0, 0)),
            pl.BlockSpec((TEAMS, rows, TEAM_WIDTH), lambda step: (0, 0, 0)),
        ]
        + [pl.BlockSpec(memory_space=pl.ANY)] * 3,
        out_shape=[
            jax.ShapeDtypeStruct((lanes, TEAMS, QUERY_WIDTH, rows), jnp.bfloat16),
            jax.ShapeDtypeStruct((TEAMS, rows, QUERY_WIDTH), jnp.bfloat16),
            jax.ShapeDtypeStruct((TEAMS, rows, TEAM_WIDTH), jnp.bfloat16),
        ]
        + exchange_shapes(plan, halves),
        scratch_shapes=[
            pltpu.VMEM((TEAM_HEADS + 1, TEAMS, rows, HEAD_DIM), jnp.bfloat16),
            pltpu.VMEM((TEAMS, QUERY_WIDTH, rows), jnp.bfloat16),
            pltpu.VMEM((TEAM_HEADS, TEAMS, rows, HEAD_DIM), jnp.bfloat16),
            pltpu.VMEM((TEAMS, rows, rows), jnp.float32),
            pltpu.VMEM((TEAM_HEADS + 1, TEAMS, rows, HEAD_DIM), jnp.float32),
            pltpu.VMEM((TEAM_HEADS, TEAMS, rows, HEAD_DIM), jnp.float32),
        ]
        + exchange_sems(plan),
        compiler_params=pltpu.CompilerParams(
            collective_id=collective, has_side_effects=True, vmem_limit_bytes=VMEM_BYTES
        ),
    )(queries, grads, stats, carried, keys, values, *halves)


def finish_body(
    main_ref,
    rows_ref,
    vector_ref,
    down_ref,
    up_ref,
    out_ref,
    whole_ref,
    home_ref,
    total_ref,
    whole_down,
    whole_up,
    whole_out,
    core_main,
    send_main,
    lane_main,
    team_send_main,
    team_main,
    assembled,
    vectors,
    ready,
    core_sems,
    lane_sems,
    team_sems,
    home_sems,
    vector_sems,
    out_lane_sems,
    out_core_sems,
    local_sems,
    early_team,
    early_lane,
    early_core,
    early_local,
):
    lanes = lax.axis_size("seq") // TEAMS
    me = lax.axis_index("seq")
    core = lax.axis_index("batch")
    team, lane = me // lanes, lax.rem(me, lanes)

    def lane_peer(k):
        other = lax.rem(lane + k, lanes)
        return other, {"seq": team * lanes + other}

    def team_peer(k):
        other = lax.rem(team + k, TEAMS)
        return other, {"seq": other * lanes + lane}

    sibling = {"batch": 1 - core}
    greet(["core", "team", "lane"])

    def place(n, p, t):
        if n == 0:
            return whole_down.at[core, p, t]
        ref = (None, whole_up, whole_out)[n]
        half = ref.shape[3] // 2
        return ref.at[p, t, :, pl.ds(pl.multiple_of(core * half, 128), half)]

    early = (down_ref, up_ref, out_ref)
    number = len(early)
    early_z = [[None] * TEAMS for _ in range(number)]
    for k in range(1, TEAMS):
        _, target = team_peer(k)
        for n in range(number):
            early_z[n][k] = push(
                early[n],
                place(n, lane, team),
                early_team.at[0, n, k],
                early_team.at[1, n, k],
                target,
            )
    early_kept = []
    for n in range(number):
        copy = pltpu.make_async_copy(early[n], place(n, lane, team), early_local.at[n])
        copy.start()
        early_kept.append(copy)
    theirs = pl.ds((1 - core) * lanes, lanes)
    core_copies = [
        push(main_ref.at[theirs], core_main, core_sems.at[0, 0], core_sems.at[1, 0], sibling),
        push(vector_ref, vectors.at[0], vector_sems.at[0, 0], vector_sems.at[1, 0], sibling),
    ]
    early_out = []
    early_sib = []

    def forward(j):
        t = lax.rem(team - j + TEAMS, TEAMS)
        for n in range(number):
            if j == 0:
                source = early[n]
            else:
                early_z[n][j].wait_recv()
                source = place(n, lane, t)
            for k in range(1, lanes):
                _, target = lane_peer(k)
                early_out.append(
                    push(
                        source,
                        place(n, lane, t),
                        early_lane.at[0, n, j, k],
                        early_lane.at[1, n, j, k],
                        target,
                    )
                )
            early_sib.append(
                push(
                    source,
                    place(n, lane, t),
                    early_core.at[0, n, j, 0],
                    early_core.at[1, n, j, 0],
                    sibling,
                )
            )

    forward(0)
    for copy in core_copies:
        copy.wait()

    both = vector_ref[...] + vectors[0]
    vectors[1 + lane] = both
    ready[0] = both
    for j in range(lanes):
        send_main[j] = (
            main_ref[core * lanes + j].astype(jnp.float32) + core_main[j].astype(jnp.float32)
        ).astype(jnp.bfloat16)
    lane_copies = []
    for k in range(1, lanes):
        other, target = lane_peer(k)
        lane_copies += [
            push(send_main.at[other], lane_main.at[lane], lane_sems.at[0, 0, k], lane_sems.at[1, 0, k], target),
            push(ready.at[0], vectors.at[1 + lane], vector_sems.at[0, k], vector_sems.at[1, k], target),
        ]
    lane_main[lane] = send_main[lane]
    for copy in lane_copies:
        copy.wait()

    def total(ref, start, number):
        result = ref[start].astype(jnp.float32)
        for j in range(1, number):
            result = result + ref[start + j].astype(jnp.float32)
        return result

    whole_vector = total(vectors, 1, lanes)
    ready[1] = whole_vector
    vectors[1 + lanes + team] = whole_vector
    low_main = total(lane_main, 0, lanes).astype(jnp.bfloat16)
    team_send_main[...] = low_main
    team_main[team] = low_main
    team_copies = []
    for k in range(1, TEAMS):
        other, target = team_peer(k)
        at = lanes + k
        team_copies += [
            push(team_send_main, team_main.at[team], team_sems.at[0, 0, k], team_sems.at[1, 0, k], target),
            push(ready.at[1], vectors.at[1 + lanes + team], vector_sems.at[0, at], vector_sems.at[1, at], target),
        ]
    home_copies = []
    for k in range(1, TEAMS):
        other, target = team_peer(k)
        home_copies.append(
            push(rows_ref.at[other], home_ref.at[team], home_sems.at[0, k], home_sems.at[1, k], target)
        )
    own = pltpu.make_async_copy(rows_ref.at[team], home_ref.at[team], local_sems.at[0])
    own.start()
    for j in range(1, TEAMS):
        forward(j)
    for copy in team_copies:
        copy.wait()
    total_ref[...] = total(vectors, 1 + lanes, TEAMS)
    pieces = []
    for part in range(3):
        first = part * QUERY_WIDTH
        for g in range(TEAMS):
            piece = team_main[g, :, first : first + TEAM_WIDTH]
            if g == 0 and part < 2:
                more = piece[:, :HEAD_DIM].astype(jnp.float32)
                for other in range(TEAMS):
                    more = more + team_main[
                        other, :, first + TEAM_WIDTH : first + QUERY_WIDTH
                    ].astype(jnp.float32)
                pieces += [more.astype(jnp.bfloat16), piece[:, HEAD_DIM:]]
            else:
                pieces.append(piece)
    assembled[...] = jnp.concatenate(pieces, axis=1)

    mine = core * lanes + lane
    out_copies = []
    for k in range(1, lanes):
        _, target = lane_peer(k)
        out_copies.append(
            push(assembled, whole_ref.at[mine], out_lane_sems.at[0, k], out_lane_sems.at[1, k], target)
        )
    core_out = [
        push(assembled, whole_ref.at[mine], out_core_sems.at[0, 0], out_core_sems.at[1, 0], sibling)
    ]
    kept = pltpu.make_async_copy(assembled, whole_ref.at[mine], local_sems.at[1])
    kept.start()
    for j in range(TEAMS):
        for n in range(number):
            for k in range(1, lanes):
                early_out[(j * number + n) * (lanes - 1) + k - 1].wait_recv()
                p = lax.rem(lane - k + lanes, lanes)
                at = place(n, p, lax.rem(team - j + TEAMS, TEAMS))
                early_sib.append(
                    push(at, at, early_core.at[0, n, j, k], early_core.at[1, n, j, k], sibling)
                )
    for k in range(1, lanes):
        source = core * lanes + lax.rem(lane - k + lanes, lanes)
        out_copies[k - 1].wait_recv()
        core_out.append(
            push(
                whole_ref.at[source],
                whole_ref.at[source],
                out_core_sems.at[0, k],
                out_core_sems.at[1, k],
                sibling,
            )
        )
    for copy in out_copies + early_out:
        copy.wait_send()
    for n in range(number):
        for k in range(1, TEAMS):
            early_z[n][k].wait_send()
    for copy in core_out + home_copies + early_sib + early_kept:
        copy.wait()
    own.wait()
    kept.wait()


def finish(main, rows_out, vector, quarters, collective):
    lanes = lax.axis_size("seq") // TEAMS
    chunks, depth, main_width = main.shape
    low = jnp.bfloat16
    dma = pltpu.SemaphoreType.DMA
    down, up, out = quarters
    wholes = [
        (2, lanes, TEAMS) + down.shape,
        (lanes, TEAMS, up.shape[0], 2 * up.shape[1]),
        (lanes, TEAMS, out.shape[0], 2 * out.shape[1]),
    ]
    anywhere = pl.BlockSpec(memory_space=pl.ANY)
    inside = pl.BlockSpec(memory_space=pltpu.VMEM)
    return pl.pallas_call(
        finish_body,
        out_shape=[
            jax.ShapeDtypeStruct((chunks, depth, TEAMS * 3 * TEAM_WIDTH), low),
            jax.ShapeDtypeStruct(rows_out.shape, low),
            jax.ShapeDtypeStruct(vector.shape, jnp.float32),
        ]
        + [jax.ShapeDtypeStruct(shape, low) for shape in wholes],
        in_specs=[inside, anywhere, inside] + [anywhere] * 3,
        out_specs=[anywhere, anywhere, inside] + [anywhere] * 3,
        scratch_shapes=[
            pltpu.VMEM((lanes, depth, main_width), low),
            pltpu.VMEM((lanes, depth, main_width), low),
            pltpu.VMEM((lanes, depth, main_width), low),
            pltpu.VMEM((depth, main_width), low),
            pltpu.VMEM((TEAMS, depth, main_width), low),
            pltpu.VMEM((depth, TEAMS * 3 * TEAM_WIDTH), low),
            pltpu.VMEM((1 + lanes + TEAMS,) + vector.shape, jnp.float32),
            pltpu.VMEM((2,) + vector.shape, jnp.float32),
            dma((2, 2)),
            dma((2, 2, lanes)),
            dma((2, 2, TEAMS)),
            dma((2, TEAMS)),
            dma((2, lanes + TEAMS)),
            dma((2, lanes)),
            dma((2, lanes)),
            dma((2,)),
            dma((2, 3, TEAMS)),
            dma((2, 3, TEAMS, lanes)),
            dma((2, 3, TEAMS, lanes)),
            dma((3,)),
        ],
        compiler_params=pltpu.CompilerParams(
            collective_id=collective, has_side_effects=True, vmem_limit_bytes=VMEM_BYTES
        ),
    )(main, rows_out, vector, *quarters)


def layer_norm(values, norm_gain, norm_bias):
    row_mean = jnp.mean(values, axis=-1, keepdims=True)
    centred = values - row_mean
    variance = jnp.mean(centred * centred, axis=-1, keepdims=True)
    return centred * lax.rsqrt(variance + epsilon) * norm_gain + norm_bias


def gelu_tanh(values):
    return jax.nn.gelu(values, approximate=True)


def contract_rows(left_op, right_op):
    return lax.dot_general(
        left_op, right_op, (((0,), (0,)), ((), ())), preferred_element_type=jnp.float32
    )


def contract_cols(left_op, right_op):
    return lax.dot_general(
        left_op, right_op, (((1,), (1,)), ((), ())), preferred_element_type=jnp.float32
    )


def per_device(
    block_input,
    ln1_gain,
    ln1_bias,
    w_qkv,
    w_out,
    ln2_gain,
    ln2_bias,
    w_up,
    w_down,
    length_draw,
    threshold_index,
    grad_out,
):
    rows = block_input.shape[1]
    width = block_input.shape[2]
    blocks = lax.axis_size("seq")
    lanes = blocks // TEAMS
    group_len = blocks * rows
    me = lax.axis_index("seq")
    team = me // lanes
    score_scale = HEAD_DIM ** (-0.5)
    length = group_len - rows + 1 + length_draw % rows
    row_valid = (me * rows + jnp.arange(rows, dtype=jnp.int32) < length[0])[:, None]
    threshold = threshold_index.astype(jnp.float32) / 128.0
    tokens = block_input[0]
    grad_top = grad_out[0]
    grad_top_low = grad_top.astype(jnp.bfloat16)

    ln1_pull = jax.vjp(layer_norm, tokens, ln1_gain, ln1_bias)[1]
    lane_rows, team_weight, queries, keys, values = project(tokens, ln1_gain, ln1_bias, w_qkv, 0)
    lane_rows = lane_rows.reshape(TEAMS * rows, width)

    head_out, masses, carried, excess = attend(
        length, threshold, queries, keys, values, blocks, rows, 1
    )
    head_out = head_out.reshape(TEAMS, TEAM_HEADS, HEAD_DIM, rows)
    log_mass = masses[:, :TEAM_HEADS]
    attn_mixed = jnp.where(row_valid, head_out.reshape(width, rows).T, jnp.zeros((), jnp.bfloat16))

    residual = tokens + dot(attn_mixed, w_out)
    normed_two, ln2_pull = jax.vjp(layer_norm, residual, ln2_gain, ln2_bias)
    normed_two_low = normed_two.astype(jnp.bfloat16)
    hidden = dot(normed_two_low, w_up)
    activated, gelu_pull = jax.vjp(gelu_tanh, hidden)
    activated_low = activated.astype(jnp.bfloat16)
    layer_out = residual + dot(activated_low, w_down)
    grad_hidden_low = gelu_pull(contract_cols(grad_top_low, w_down))[0].astype(jnp.bfloat16)
    grad_resid_norm, grad_ln2_gain, grad_ln2_bias = ln2_pull(contract_cols(grad_hidden_low, w_up))
    grad_resid = grad_top + grad_resid_norm
    grad_attn_low = grad_resid.astype(jnp.bfloat16)
    grad_mixed = jnp.where(
        row_valid,
        contract_cols(grad_attn_low, w_out).astype(jnp.bfloat16),
        jnp.zeros((), jnp.bfloat16),
    )
    grad_rows = grad_mixed.T.reshape(TEAMS, TEAM_HEADS, HEAD_DIM, rows).astype(jnp.float32)
    inner = jnp.sum(grad_rows * head_out.astype(jnp.float32), axis=2)
    stats = jnp.concatenate(
        [log_mass, inner, jnp.zeros((TEAMS, 8 - 2 * TEAM_HEADS, rows), jnp.float32)], axis=1
    )
    grad_cols = jnp.moveaxis(grad_mixed.reshape(rows, TEAMS, TEAM_WIDTH), 1, 0)
    grad_cols, stats, *pairs_of = exchange(
        [("lane", "spread"), ("lane", "spread")]
        + [("core", kind) for kind in ("half", "gather", "gather", "half", "gather", "half")],
        [
            grad_cols,
            stats,
            activated_low,
            grad_top_low,
            normed_two_low,
            grad_hidden_low,
            attn_mixed,
            grad_attn_low,
        ],
        3,
    )
    pairs_of = [x.reshape(2 * rows, -1) for x in pairs_of]
    down_half = contract_rows(pairs_of[0], pairs_of[1]).astype(jnp.bfloat16)
    up_half = contract_rows(pairs_of[2], pairs_of[3]).astype(jnp.bfloat16)
    out_half = contract_rows(pairs_of[4], pairs_of[5]).astype(jnp.bfloat16)
    halves = [x.reshape(lanes, TEAMS, -1, x.shape[1]) for x in (down_half, up_half, out_half)]
    grad_cols, stats = exchange([("team", "gather"), ("team", "gather")], [grad_cols, stats], 4)
    query_grads, key_grads, value_grads, *halves = attend_back(
        queries, grad_cols, stats, carried, keys, values, halves, blocks, rows, 7
    )

    def summed(x):
        return jnp.sum(x.astype(jnp.float32), axis=0).astype(jnp.bfloat16)

    query_grads, *quarters = exchange(
        [("team", "spread")] + [("lane", "spread")] * 3,
        [query_grads] + [summed(x) for x in halves],
        5,
    )
    quarters = [summed(x) for x in quarters]
    query_grads = jnp.sum(query_grads.astype(jnp.float32), axis=0) * score_scale
    query_grads = jnp.swapaxes(query_grads.astype(jnp.bfloat16), 1, 2)
    grad_projected = jnp.concatenate([query_grads, key_grads, value_grads], axis=2)
    grad_projected = grad_projected.reshape(TEAMS * rows, -1)
    chunks = 2 * lanes
    grad_main = contract_rows(lane_rows, grad_projected)
    grad_lane_rows = contract_cols(grad_projected, team_weight)
    grad_ln1_bias = jnp.sum(grad_lane_rows, axis=0)
    grad_ln1_gain = (
        jnp.sum(grad_lane_rows * (lane_rows.astype(jnp.float32) - ln1_bias), axis=0) / ln1_gain
    )
    pairs = (length[0] - 1).astype(jnp.float32) * (length[0] - 2).astype(jnp.float32) / 2.0
    vectors = jnp.stack(
        [
            grad_ln1_gain,
            grad_ln1_bias,
            grad_ln2_gain,
            grad_ln2_bias,
            jnp.full((width,), jnp.sum(excess)),
            jnp.full((width,), pairs / blocks),
            jnp.zeros((width,), jnp.float32),
            jnp.zeros((width,), jnp.float32),
        ]
    )
    grad_w_qkv, home_rows, vectors, grad_w_down, grad_w_up, grad_w_out = finish(
        grad_main.astype(jnp.bfloat16).reshape(chunks, width // chunks, -1),
        grad_lane_rows.astype(jnp.bfloat16).reshape(TEAMS, rows, width),
        vectors,
        quarters,
        6,
    )
    grad_w_down = grad_w_down.reshape(w_down.shape)
    grad_w_up = grad_w_up.reshape(w_up.shape)
    grad_w_out = grad_w_out.reshape(w_out.shape)
    grad_w_qkv = grad_w_qkv.reshape(width, 3 * width)
    grad_normed = jnp.sum(home_rows.astype(jnp.float32), axis=0)
    grad_x = grad_resid + ln1_pull(grad_normed)[0]
    pruned_share = (vectors[4, 0] / vectors[5, 0]).reshape(1)
    return (
        layer_out[None],
        grad_x[None],
        vectors[0],
        vectors[1],
        grad_w_qkv.astype(jnp.float32),
        grad_w_out.astype(jnp.float32),
        vectors[2],
        vectors[3],
        grad_w_up.astype(jnp.float32),
        grad_w_down.astype(jnp.float32),
        pruned_share,
    )


def solution(mesh):
    placed = (
        P("batch", "seq", None),
        P(),
        P(),
        P(),
        P(),
        P(),
        P(),
        P(),
        P(),
        P("batch"),
        P(),
        P("batch", "seq", None),
    )
    return jax.shard_map(
        per_device,
        mesh=mesh,
        in_specs=placed,
        out_specs=(
            P("batch", "seq", None),
            P("batch", "seq", None),
            P(),
            P(),
            P(),
            P(),
            P(),
            P(),
            P(),
            P(),
            P(),
        ),
        check_vma=False,
    )
```

```python
import functools

import jax
import jax.numpy as jnp
from jax import lax
from jax.experimental import pallas as pl
from jax.experimental.pallas import tpu as pltpu
from jax.sharding import PartitionSpec as P

HEADS = 12
HEAD_DIM = 64
TEAMS = 4
TEAM_HEADS = HEADS // TEAMS
TEAM_WIDTH = TEAM_HEADS * HEAD_DIM
QUERY_WIDTH = TEAM_WIDTH + HEAD_DIM

epsilon = 1e-05
negative = -1e30
select_scale = 3.0
VMEM_BYTES = 60 * 2**20
MESH = pl.DeviceIdType.MESH


def peers_of(scope):
    lanes = lax.axis_size("seq") // TEAMS
    me = lax.axis_index("seq")
    team, lane = me // lanes, lax.rem(me, lanes)
    if scope == "team":
        return lane, lanes, lambda k: {"seq": team * lanes + k}
    if scope == "lane":
        return team, TEAMS, lambda k: {"seq": k * lanes + lane}
    if scope == "core":
        return lax.axis_index("batch"), 2, lambda k: {"batch": k}
    return me, lanes * TEAMS, lambda k: {"seq": k}


def scope_size(scope):
    count = lax.axis_size("seq")
    return {"team": count // TEAMS, "lane": TEAMS, "core": 2, "all": count}[scope]


def greet(scopes):
    barrier = pltpu.get_barrier_semaphore()
    number = 0
    for scope in scopes:
        mine, peers, device_of = peers_of(scope)
        for k in range(1, peers):
            pl.semaphore_signal(
                barrier, inc=1, device_id=device_of(lax.rem(mine + k, peers)), device_id_type=MESH
            )
        number += peers - 1
    pl.semaphore_wait(barrier, number)


def push(source, destination, send, receive, target, start=True):
    copy = pltpu.make_async_remote_copy(
        src_ref=source,
        dst_ref=destination,
        send_sem=send,
        recv_sem=receive,
        device_id=target,
        device_id_type=MESH,
    )
    if start:
        copy.start()
    return copy


def part_of(kind, ref, k):
    if kind == "gather":
        return ref
    if kind == "spread":
        return ref.at[k]
    if kind == "second":
        return ref.at[:, k]
    half = ref.shape[1] // 2
    return ref.at[:, pl.ds(pl.multiple_of(k * half, 128), half)]


def remote_copies(plan, sources, targets, send, receive, start=True):
    copies = []
    for n, (scope, kind) in enumerate(plan):
        mine, peers, device_of = peers_of(scope)
        for k in range(1, peers):
            peer = lax.rem(mine + k, peers)
            copies.append(
                push(
                    part_of(kind, sources[n], peer),
                    targets[n].at[mine],
                    send.at[n, k],
                    receive.at[n, k],
                    device_of(peer),
                    start,
                )
            )
    return copies


def exchange_shapes(plan, arrays):
    shapes = []
    for (scope, kind), x in zip(plan, arrays):
        shape = x.shape
        if kind == "gather":
            shape = (scope_size(scope),) + shape
        if kind == "half":
            shape = (2, shape[0], shape[1] // 2)
        if kind == "second":
            shape = (shape[1], shape[0]) + shape[2:]
        shapes.append(jax.ShapeDtypeStruct(shape, x.dtype))
    return shapes


def exchange_sems(plan):
    number, most = len(plan), max(scope_size(scope) for scope, _ in plan)
    return [
        pltpu.SemaphoreType.DMA((number, most)),
        pltpu.SemaphoreType.DMA((number, most)),
        pltpu.SemaphoreType.DMA((number,)),
    ]


def scopes_of(plan):
    return [x for x in ("core", "team", "lane", "all") if x in [scope for scope, _ in plan]]


def exchange(plan, arrays, collective):
    number = len(arrays)
    shapes = exchange_shapes(plan, arrays)

    def body(*refs):
        sources, targets = refs[:number], refs[number : 2 * number]
        send, receive, local = refs[2 * number : 2 * number + 3]
        through = refs[2 * number + 3 :]
        greet(scopes_of(plan))
        copies = remote_copies(plan, sources, targets, send, receive)
        inward = []
        for n, (scope, kind) in enumerate(plan):
            mine = peers_of(scope)[0]
            copy = pltpu.make_async_copy(part_of(kind, sources[n], mine), through[n], local.at[n])
            copy.start()
            inward.append(copy)
        for n, (scope, kind) in enumerate(plan):
            mine = peers_of(scope)[0]
            inward[n].wait()
            copy = pltpu.make_async_copy(through[n], targets[n].at[mine], local.at[n])
            copy.start()
            copies.append(copy)
        for copy in copies:
            copy.wait()

    return pl.pallas_call(
        body,
        out_shape=shapes,
        in_specs=[pl.BlockSpec(memory_space=pl.ANY)] * number,
        out_specs=[pl.BlockSpec(memory_space=pl.ANY)] * number,
        scratch_shapes=exchange_sems(plan) + [pltpu.VMEM(x.shape[1:], x.dtype) for x in shapes],
        compiler_params=pltpu.CompilerParams(
            collective_id=collective, has_side_effects=True, vmem_limit_bytes=VMEM_BYTES
        ),
    )(*arrays)


def dot(left, right):
    return jnp.dot(left, right, preferred_element_type=jnp.float32)


def project_body(
    tokens_ref,
    gain_ref,
    bias_ref,
    w_ref,
    lane_ref,
    weight_ref,
    query_ref,
    key_ref,
    value_ref,
    held,
    ready,
    windows,
    firsts,
    hop_send,
    hop_recv,
    team_send,
    team_recv,
    weight_sems,
    local_sems,
):
    lanes = lax.axis_size("seq") // TEAMS
    me = lax.axis_index("seq")
    team, lane = me // lanes, lax.rem(me, lanes)
    width = tokens_ref.shape[1]
    wide = windows.shape[2]
    start = (3 * team // 2) * 128
    loads = []
    for part in range(3):
        at = pl.ds(pl.multiple_of(part * width + start, 128), wide)
        loads.append(pltpu.make_async_copy(w_ref.at[:, at], windows.at[part], weight_sems.at[part]))
    for part in range(2):
        at = pl.ds(part * width, 128)
        loads.append(
            pltpu.make_async_copy(w_ref.at[:, at], firsts.at[part], weight_sems.at[3 + part])
        )
    for load in loads:
        load.start()
    tokens = tokens_ref[...]
    row_mean = jnp.mean(tokens, axis=1, keepdims=True)
    centred = tokens - row_mean
    variance = jnp.mean(centred * centred, axis=1, keepdims=True)
    normed = centred * lax.rsqrt(variance + epsilon) * gain_ref[...] + bias_ref[...]
    held[team] = normed.astype(jnp.bfloat16)
    greet(["team", "lane"])

    def hop(side, distance, start=True):
        block = team - distance if side == 0 else team + distance
        target = me + lanes if side == 0 else me - lanes
        return push(
            held.at[block],
            held.at[block],
            hop_send.at[side, distance],
            hop_recv.at[side, distance],
            {"seq": target},
            start,
        )

    @pl.when(team < TEAMS - 1)
    def _():
        hop(0, 0)

    @pl.when(team > 0)
    def _():
        hop(1, 0)

    for load in loads:
        load.wait()
    odd = lax.rem(team, 2) == 1
    pieces = []
    for part in range(3):
        window = windows[part]
        pieces.append(
            jnp.where(odd, window[:, wide - TEAM_WIDTH :], window[:, :TEAM_WIDTH])
        )
        if part < 2:
            pieces.append(firsts[part][:, :HEAD_DIM])
    weight_ref[...] = jnp.concatenate(pieces, axis=1)

    def block_copies(block, start):
        copies = []
        for k in range(1, lanes):
            target = {"seq": team * lanes + lax.rem(lane + k, lanes)}
            copies.append(
                push(
                    ready.at[block],
                    query_ref.at[lane, block],
                    team_send.at[block, k],
                    team_recv.at[block, k],
                    target,
                    start,
                )
            )
        for n, (source, destination) in enumerate(
            ((ready.at[block], query_ref.at[lane, block]), (held.at[block], lane_ref.at[block]))
        ):
            copy = pltpu.make_async_copy(source, destination, local_sems.at[n, block])
            if start:
                copy.start()
            copies.append(copy)
        return copies

    def project(block):
        result = dot(held[block], weight_ref[...]).astype(jnp.bfloat16)
        ready[block] = result[:, :QUERY_WIDTH] * jnp.bfloat16(HEAD_DIM ** (-0.5))
        block_copies(block, True)
        key_ref[block] = result[:, QUERY_WIDTH : 2 * QUERY_WIDTH]
        value_ref[block] = result[:, 2 * QUERY_WIDTH :]

    project(team)

    def arrive(step, _):
        distance, side = step // 2 + 1, lax.rem(step, 2)
        for which in range(2):
            block = team - distance if which == 0 else team + distance
            there = (block >= 0) if which == 0 else (block < TEAMS)
            further = (team < TEAMS - 1) if which == 0 else (team > 0)

            @pl.when((side == which) & there)
            def _():
                hop(which, distance - 1, False).wait_recv()

                @pl.when(further)
                def _():
                    hop(which, distance)

                project(block)

        return 0

    lax.fori_loop(0, 2 * (TEAMS - 1), arrive, 0)
    for distance in range(TEAMS - 1):

        @pl.when((team < TEAMS - 1) & (team >= distance))
        def _():
            hop(0, distance, False).wait_send()

        @pl.when((team > 0) & (team + distance < TEAMS))
        def _():
            hop(1, distance, False).wait_send()

    for block in range(TEAMS):
        for copy in block_copies(block, False):
            copy.wait()


def project(tokens, gain, bias, weight, collective):
    lanes = lax.axis_size("seq") // TEAMS
    rows, width = tokens.shape
    inside = pl.BlockSpec(memory_space=pltpu.VMEM)
    anywhere = pl.BlockSpec(memory_space=pl.ANY)
    columns = 2 * QUERY_WIDTH + TEAM_WIDTH
    low = jnp.bfloat16
    dma = pltpu.SemaphoreType.DMA
    return pl.pallas_call(
        project_body,
        out_shape=[
            jax.ShapeDtypeStruct((TEAMS, rows, width), low),
            jax.ShapeDtypeStruct((width, columns), low),
            jax.ShapeDtypeStruct((lanes, TEAMS, rows, QUERY_WIDTH), low),
            jax.ShapeDtypeStruct((TEAMS, rows, QUERY_WIDTH), low),
            jax.ShapeDtypeStruct((TEAMS, rows, TEAM_WIDTH), low),
        ],
        in_specs=[inside, inside, inside, anywhere],
        out_specs=[anywhere, inside, anywhere, inside, inside],
        scratch_shapes=[
            pltpu.VMEM((TEAMS, rows, width), low),
            pltpu.VMEM((TEAMS, rows, QUERY_WIDTH), low),
            pltpu.VMEM((3, width, 256), low),
            pltpu.VMEM((2, width, 128), low),
            dma((2, TEAMS)),
            dma((2, TEAMS)),
            dma((TEAMS, lanes)),
            dma((TEAMS, lanes)),
            dma((5,)),
            dma((2, TEAMS)),
        ],
        compiler_params=pltpu.CompilerParams(
            collective_id=collective, has_side_effects=True, vmem_limit_bytes=VMEM_BYTES
        ),
    )(tokens, gain[None], bias[None], weight)


def fold(tile):
    return jnp.sum(tile.reshape(tile.shape[0] // 8, 8, tile.shape[1]), axis=0)


def attend_body(
    length_ref,
    threshold_ref,
    q_ref,
    kk_ref,
    vv_ref,
    out_ref,
    mass_ref,
    carried_ref,
    excess_ref,
    key_heads,
    value_rows,
    running,
    logits,
    out_all,
    mass_all,
    lane_out,
    lane_mass,
    joined_out,
    joined_mass,
    home_out,
    home_mass,
    lane_send,
    lane_recv,
    home_send,
    home_recv,
    *,
    blocks,
    rows,
):
    lanes = blocks // TEAMS
    me = lax.axis_index("seq")
    team, lane = me // lanes, lax.rem(me, lanes)
    i = pl.program_id(0)
    scale = select_scale / (blocks * rows)
    key_iota = lax.broadcasted_iota(jnp.int32, (rows, rows), 0)
    query_iota = lax.broadcasted_iota(jnp.int32, (rows, rows), 1)

    def part_copies(j, start):
        z, owner = j // lanes, lax.rem(j, lanes)
        return [
            push(
                source.at[j],
                destination.at[z, lane],
                lane_send.at[n, j],
                lane_recv.at[n, z, lane],
                {"seq": team * lanes + owner},
                start,
            )
            for n, (source, destination) in enumerate(
                ((out_all, lane_out), (mass_all, lane_mass))
            )
        ]

    def home_copies(z, start):
        return [
            push(
                source.at[z],
                destination.at[team],
                home_send.at[n, z],
                home_recv.at[n, team],
                {"seq": z * lanes + lane},
                start,
            )
            for n, (source, destination) in enumerate(
                ((joined_out, home_out), (joined_mass, home_mass))
            )
        ]

    def join(z):
        for k in range(1, lanes):
            other = lax.rem(lane + k, lanes)
            for n, buffer in enumerate((lane_out, lane_mass)):
                pltpu.make_async_copy(
                    buffer.at[z, other], buffer.at[z, other], lane_recv.at[n, z, other]
                ).wait()
        masses = [lane_mass[z, p] for p in range(lanes)]
        peak = masses[0]
        for p in range(1, lanes):
            peak = jnp.maximum(peak, masses[p])
        shares = [jnp.exp(mass - peak) for mass in masses]
        whole = shares[0]
        for p in range(1, lanes):
            whole = whole + shares[p]
        joined_mass[z] = peak + jnp.log(whole)
        inverse = 1.0 / whole
        for h in range(TEAM_HEADS):
            span = slice(h * HEAD_DIM, (h + 1) * HEAD_DIM)
            mixed = None
            for p in range(lanes):
                share = (shares[p] * inverse)[h : h + 1, :]
                part = lane_out[z, p, span, :].astype(jnp.float32) * share
                mixed = part if p == 0 else mixed + part
            joined_out[z, span, :] = mixed.astype(jnp.bfloat16)

        @pl.when(team != z)
        def _():
            home_copies(z, True)

        @pl.when(team == z)
        def _():
            home_out[team] = joined_out[z]
            home_mass[team] = joined_mass[z]

    @pl.when(i == 0)
    def _():
        greet(["team", "lane"])
        running[...] = jnp.zeros_like(running)
        excess_ref[...] = jnp.zeros_like(excess_ref)
        for z in range(TEAMS):
            for h in range(TEAM_HEADS):
                key_heads[h, z] = kk_ref[z, :, h * HEAD_DIM : (h + 1) * HEAD_DIM]
            first = kk_ref[z, :, TEAM_WIDTH:]
            if z == 0:
                slot = lax.broadcasted_iota(jnp.int32, first.shape, 0) + lane * rows
                first = jnp.where(slot >= 1, first, jnp.zeros_like(first))
            key_heads[TEAM_HEADS, z] = first
            value_rows[z] = vv_ref[z].T

    active = jnp.where(i >= lane, (i - lane) // lanes + 1, 0)
    threshold = threshold_ref[0]

    @pl.when(active == 0)
    def _():
        out_all[i] = jnp.zeros((TEAM_WIDTH, rows), jnp.bfloat16)
        mass_all[i] = jnp.full((8, rows), negative, jnp.float32)

    def work(count):
        q_rows = q_ref[0, 0].T
        heads = [q_rows[h * HEAD_DIM : (h + 1) * HEAD_DIM] for h in range(TEAM_HEADS + 1)]
        earlier = jnp.where(key_iota < query_iota, scale, 0.0).astype(jnp.bfloat16)
        every = jnp.full((rows, rows), scale, jnp.bfloat16)
        last = ((count - 1) * lanes + lane) * rows + key_iota
        query_pos = i * rows + query_iota
        peaks = [None] * TEAM_HEADS
        for z in range(count):
            first = jnp.maximum(dot(key_heads[TEAM_HEADS, z], heads[TEAM_HEADS]), 0.0)
            if z == count - 1:
                first = jnp.where(last < query_pos, first, 0.0)
            first = first.astype(jnp.bfloat16)
            carried = running[z] + dot(first, earlier)
            running[z] = running[z] + dot(first, every)

            if z == count - 1:
                carried = jnp.where(last <= query_pos, carried, -negative)
            carried_ref[0, z] = carried
            for h in range(TEAM_HEADS):
                logit = dot(key_heads[h, z], heads[h]) - carried
                logits[h, z] = logit
                peak = jnp.max(logit.reshape(rows // 8, 8, rows), axis=0)
                peaks[h] = peak if z == 0 else jnp.maximum(peaks[h], peak)
        mass_all[i] = jnp.zeros((8, rows), jnp.float32)
        for h in range(TEAM_HEADS):
            peak = jnp.max(peaks[h], axis=0, keepdims=True)
            mass, mixed = None, None
            for z in range(count):
                terms = jnp.exp(logits[h, z] - peak)
                part = fold(terms)
                values = value_rows[z, h * HEAD_DIM : (h + 1) * HEAD_DIM, :]
                product = dot(values, terms.astype(jnp.bfloat16))
                mass = part if z == 0 else mass + part
                mixed = product if z == 0 else mixed + product
            mass = jnp.sum(mass, axis=0, keepdims=True)
            out_all[i, h * HEAD_DIM : (h + 1) * HEAD_DIM, :] = (mixed * (1.0 / mass)).astype(
                jnp.bfloat16
            )
            mass_all[i, h : h + 1, :] = peak + jnp.log(mass)

        @pl.when(lax.rem(i, TEAMS) == team)
        def _():
            total = None
            for z in range(count):
                carried = carried_ref[0, z]
                if z == count - 1:
                    carried = jnp.where(last < query_pos, carried, 0.0)
                part = fold(jnp.clip(carried - threshold, 0.0, 1.0))
                total = part if z == 0 else total + part
            valid = i * rows + lax.broadcasted_iota(jnp.int32, (8, rows), 1) < length_ref[0]
            excess_ref[...] += jnp.where(valid, total, 0.0)

    for count in range(1, TEAMS + 1):
        pl.when(active == count)(functools.partial(work, count))

    @pl.when(lax.rem(i, lanes) != lane)
    def _():
        part_copies(i, True)

    @pl.when(lax.rem(i, lanes) == lane)
    def _():
        lane_out[i // lanes, lane] = out_all[i]
        lane_mass[i // lanes, lane] = mass_all[i]

    for z in range(TEAMS - 1):
        pl.when(i == (z + 1) * lanes + 1)(functools.partial(join, z))

    @pl.when(i == blocks - 1)
    def _():
        join(TEAMS - 1)

        def drain(j, _):
            @pl.when(lax.rem(j, lanes) != lane)
            def _():
                for copy in part_copies(j, False):
                    copy.wait_send()

            return 0

        lax.fori_loop(0, blocks, drain, 0)
        for z in range(TEAMS):

            @pl.when(team != z)
            def _():
                for copy in home_copies(z, False):
                    copy.wait_send()
                for n, buffer in enumerate((home_out, home_mass)):
                    pltpu.make_async_copy(
                        buffer.at[z], buffer.at[z], home_recv.at[n, z]
                    ).wait()

        out_ref[...] = home_out[...]
        mass_ref[...] = home_mass[...]

def attend(length, threshold, queries, keys, values, blocks, rows, collective):
    lanes = blocks // TEAMS
    smem = pl.BlockSpec(memory_space=pltpu.SMEM)
    whole = pl.BlockSpec((TEAMS, rows, QUERY_WIDTH), lambda i: (0, 0, 0))
    return pl.pallas_call(
        functools.partial(attend_body, blocks=blocks, rows=rows),
        grid=(blocks,),
        in_specs=[
            smem,
            smem,
            pl.BlockSpec(
                (1, 1, rows, QUERY_WIDTH), lambda i: (lax.rem(i, lanes), i // lanes, 0, 0)
            ),
            whole,
            pl.BlockSpec((TEAMS, rows, TEAM_WIDTH), lambda i: (0, 0, 0)),
        ],
        out_specs=[
            pl.BlockSpec((TEAMS, TEAM_WIDTH, rows), lambda i: (0, 0, 0)),
            pl.BlockSpec((TEAMS, 8, rows), lambda i: (0, 0, 0)),
            pl.BlockSpec((1, TEAMS, rows, rows), lambda i: (i, 0, 0, 0)),
            pl.BlockSpec((8, rows), lambda i: (0, 0)),
        ],
        out_shape=[
            jax.ShapeDtypeStruct((TEAMS, TEAM_WIDTH, rows), jnp.bfloat16),
            jax.ShapeDtypeStruct((TEAMS, 8, rows), jnp.float32),
            jax.ShapeDtypeStruct((blocks, TEAMS, rows, rows), jnp.float32),
            jax.ShapeDtypeStruct((8, rows), jnp.float32),
        ],
        scratch_shapes=[
            pltpu.VMEM((TEAM_HEADS + 1, TEAMS, rows, HEAD_DIM), jnp.bfloat16),
            pltpu.VMEM((TEAMS, TEAM_WIDTH, rows), jnp.bfloat16),
            pltpu.VMEM((TEAMS, rows, rows), jnp.float32),
            pltpu.VMEM((TEAM_HEADS, TEAMS, rows, rows), jnp.float32),
            pltpu.VMEM((blocks, TEAM_WIDTH, rows), jnp.bfloat16),
            pltpu.VMEM((blocks, 8, rows), jnp.float32),
            pltpu.VMEM((TEAMS, lanes, TEAM_WIDTH, rows), jnp.bfloat16),
            pltpu.VMEM((TEAMS, lanes, 8, rows), jnp.float32),
            pltpu.VMEM((TEAMS, TEAM_WIDTH, rows), jnp.bfloat16),
            pltpu.VMEM((TEAMS, 8, rows), jnp.float32),
            pltpu.VMEM((TEAMS, TEAM_WIDTH, rows), jnp.bfloat16),
            pltpu.VMEM((TEAMS, 8, rows), jnp.float32),
            pltpu.SemaphoreType.DMA((2, blocks)),
            pltpu.SemaphoreType.DMA((2, TEAMS, lanes)),
            pltpu.SemaphoreType.DMA((2, TEAMS)),
            pltpu.SemaphoreType.DMA((2, TEAMS)),
        ],
        compiler_params=pltpu.CompilerParams(
            collective_id=collective, has_side_effects=True, vmem_limit_bytes=VMEM_BYTES
        ),
    )(length, threshold, queries, keys, values)


reduce_plan = [("lane", "second"), ("team", "spread"), ("team", "spread")]


def attend_back_body(
    q_ref,
    grad_ref,
    stat_ref,
    carried_ref,
    kk_ref,
    vv_ref,
    *refs,
    blocks,
    rows,
):
    plan = reduce_plan
    sources, refs = refs[:3], refs[3:]
    (query_grad_ref, key_grad_ref, value_grad_ref), targets, refs = refs[:3], refs[3:6], refs[6:]
    key_heads, key_rows, value_heads, running, key_sum, value_sum = refs[:6]
    grad_all, stat_all, grad_send, grad_recv, send, receive, local = refs[6:13]
    through = refs[13:]
    lanes = blocks // TEAMS
    me = lax.axis_index("seq")
    team, lane = me // lanes, lax.rem(me, lanes)
    step = pl.program_id(0)
    i = blocks - 1 - step
    scale = select_scale / (blocks * rows)
    span = [slice(h * HEAD_DIM, (h + 1) * HEAD_DIM) for h in range(TEAM_HEADS + 1)]
    key_iota = lax.broadcasted_iota(jnp.int32, (rows, rows), 0)
    query_iota = lax.broadcasted_iota(jnp.int32, (rows, rows), 1)

    place, owner = i // lanes, lax.rem(i, lanes)

    def grad_copies(z, start):
        return [
            push(
                buffer.at[lane, z],
                buffer.at[lane, z],
                grad_send.at[n, z, k],
                grad_recv.at[n, z, lane],
                {"seq": team * lanes + lax.rem(lane + k, lanes)},
                start,
            )
            for k in range(1, lanes)
            for n, buffer in enumerate((grad_all, stat_all))
        ]

    def own_copies(n, inward):
        scope, kind = plan[n]
        mine = peers_of(scope)[0]
        if inward:
            return pltpu.make_async_copy(part_of(kind, sources[n], mine), through[n], local.at[n])
        return pltpu.make_async_copy(through[n], targets[n].at[mine], local.at[n])

    def plan_copies(scope, start):
        chosen = [n for n in range(len(plan)) if plan[n][0] == scope]
        copies = []
        for n in chosen:
            copies += remote_copies(
                plan[n : n + 1],
                sources[n : n + 1],
                targets[n : n + 1],
                send.at[n : n + 1],
                receive.at[n : n + 1],
                start,
            )
        return copies

    @pl.when(step == 0)
    def _():
        greet(["team", "lane"])
        grad_all[lane] = grad_ref[...]
        stat_all[lane] = stat_ref[...]
        for z in reversed(range(TEAMS)):
            grad_copies(z, True)
        plan_copies("lane", True)
        for n in range(len(plan)):
            own_copies(n, True).start()
        running[...] = jnp.zeros_like(running)
        key_sum[...] = jnp.zeros_like(key_sum)
        value_sum[...] = jnp.zeros_like(value_sum)
        for z in range(TEAMS):
            for h in range(TEAM_HEADS + 1):
                key_heads[h, z] = kk_ref[z, :, span[h]]
            for h in range(TEAM_HEADS):
                value_heads[h, z] = vv_ref[z, :, span[h]]
            key_rows[z] = kk_ref[z].T
        first = kk_ref[0, :, span[TEAM_HEADS]]
        slot = lax.broadcasted_iota(jnp.int32, first.shape, 0) + lane * rows
        key_heads[TEAM_HEADS, 0] = jnp.where(slot >= 1, first, jnp.zeros_like(first))

    @pl.when(step == 2)
    def _():
        plan_copies("team", True)
        for n in range(len(plan)):
            own_copies(n, True).wait()
            own_copies(n, False).start()

    @pl.when(owner != lane)
    def _():
        for n, buffer in enumerate((grad_all, stat_all)):
            at = buffer.at[owner, place]
            pltpu.make_async_copy(at, at, grad_recv.at[n, place, owner]).wait()

    active = jnp.where(i >= lane, (i - lane) // lanes + 1, 0)

    @pl.when(active == 0)
    def _():
        query_grad_ref[...] = jnp.zeros_like(query_grad_ref)

    def work(count):
        q_rows = q_ref[0, 0].T
        grad_rows = grad_all[owner, place].T
        q_row = [q_rows[span[h]] for h in range(TEAM_HEADS + 1)]
        q_col = [q_ref[0, 0, :, span[h]] for h in range(TEAM_HEADS + 1)]
        grad_row = [grad_rows[span[h]] for h in range(TEAM_HEADS)]
        grad_col = [grad_all[owner, place, :, span[h]] for h in range(TEAM_HEADS)]
        mass = [stat_all[owner, place, h : h + 1, :] for h in range(TEAM_HEADS)]
        inner = [stat_all[owner, place, TEAM_HEADS + h : TEAM_HEADS + h + 1, :] for h in range(TEAM_HEADS)]
        later = jnp.where(key_iota > query_iota, -scale, 0.0).astype(jnp.bfloat16)
        every = jnp.full((rows, rows), -scale, jnp.bfloat16)
        last = ((count - 1) * lanes + lane) * rows + key_iota
        query_pos = i * rows + query_iota
        sums = [None] * (TEAM_HEADS + 1)
        for z in range(count):
            carried = carried_ref[0, z]
            total = None
            for h in range(TEAM_HEADS):
                probs = jnp.exp(dot(key_heads[h, z], q_row[h]) - carried - mass[h])
                value_sum[h, z] += dot(probs.astype(jnp.bfloat16), grad_col[h])
                grad_logit = probs * (dot(value_heads[h, z], grad_row[h]) - inner[h])
                total = grad_logit if h == 0 else total + grad_logit
                low = grad_logit.astype(jnp.bfloat16)
                key_sum[h, z] += dot(low, q_col[h])
                part = dot(key_rows[z, span[h], :], low)
                sums[h] = part if z == 0 else sums[h] + part
            total = total.astype(jnp.bfloat16)
            select_grad = running[z] + dot(total, later)
            running[z] = running[z] + dot(total, every)
            first = dot(key_heads[TEAM_HEADS, z], q_row[TEAM_HEADS])
            live = first > 0.0
            if z == count - 1:
                live = live & (last < query_pos)
            low = jnp.where(live, select_grad, 0.0).astype(jnp.bfloat16)
            key_sum[TEAM_HEADS, z] += dot(low, q_col[TEAM_HEADS])
            part = dot(key_rows[z, span[TEAM_HEADS], :], low)
            sums[TEAM_HEADS] = part if z == 0 else sums[TEAM_HEADS] + part
        for h in range(TEAM_HEADS + 1):
            query_grad_ref[0, 0, span[h], :] = sums[h].astype(jnp.bfloat16)

    for count in range(1, TEAMS + 1):
        pl.when(active == count)(functools.partial(work, count))

    @pl.when(step == blocks - 1)
    def _():
        for h in range(TEAM_HEADS + 1):
            key_grad_ref[:, :, span[h]] = key_sum[h].astype(jnp.bfloat16)
        for h in range(TEAM_HEADS):
            value_grad_ref[:, :, span[h]] = value_sum[h].astype(jnp.bfloat16)
        for z in range(TEAMS):
            for copy in grad_copies(z, False):
                copy.wait_send()
        for n in range(len(plan)):
            own_copies(n, False).wait()
        for scope in ("lane", "team"):
            for copy in plan_copies(scope, False):
                copy.wait()


def attend_back(queries, grads, stats, carried, keys, values, halves, blocks, rows, collective):
    lanes = blocks // TEAMS
    plan = reduce_plan
    shapes = exchange_shapes(plan, halves)

    def place(step):
        i = blocks - 1 - step
        return (lax.rem(i, lanes), i // lanes, 0, 0)

    return pl.pallas_call(
        functools.partial(attend_back_body, blocks=blocks, rows=rows),
        grid=(blocks,),
        in_specs=[
            pl.BlockSpec((1, 1, rows, QUERY_WIDTH), place),
            pl.BlockSpec((TEAMS, rows, TEAM_WIDTH), lambda step: (0, 0, 0)),
            pl.BlockSpec((TEAMS, 8, rows), lambda step: (0, 0, 0)),
            pl.BlockSpec((1, TEAMS, rows, rows), lambda step: (blocks - 1 - step, 0, 0, 0)),
            pl.BlockSpec((TEAMS, rows, QUERY_WIDTH), lambda step: (0, 0, 0)),
            pl.BlockSpec((TEAMS, rows, TEAM_WIDTH), lambda step: (0, 0, 0)),
        ]
        + [pl.BlockSpec(memory_space=pl.ANY)] * 3,
        out_specs=[
            pl.BlockSpec((1, 1, QUERY_WIDTH, rows), place),
            pl.BlockSpec((TEAMS, rows, QUERY_WIDTH), lambda step: (0, 0, 0)),
            pl.BlockSpec((TEAMS, rows, TEAM_WIDTH), lambda step: (0, 0, 0)),
        ]
        + [pl.BlockSpec(memory_space=pl.ANY)] * 3,
        out_shape=[
            jax.ShapeDtypeStruct((lanes, TEAMS, QUERY_WIDTH, rows), jnp.bfloat16),
            jax.ShapeDtypeStruct((TEAMS, rows, QUERY_WIDTH), jnp.bfloat16),
            jax.ShapeDtypeStruct((TEAMS, rows, TEAM_WIDTH), jnp.bfloat16),
        ]
        + shapes,
        scratch_shapes=[
            pltpu.VMEM((TEAM_HEADS + 1, TEAMS, rows, HEAD_DIM), jnp.bfloat16),
            pltpu.VMEM((TEAMS, QUERY_WIDTH, rows), jnp.bfloat16),
            pltpu.VMEM((TEAM_HEADS, TEAMS, rows, HEAD_DIM), jnp.bfloat16),
            pltpu.VMEM((TEAMS, rows, rows), jnp.float32),
            pltpu.VMEM((TEAM_HEADS + 1, TEAMS, rows, HEAD_DIM), jnp.float32),
            pltpu.VMEM((TEAM_HEADS, TEAMS, rows, HEAD_DIM), jnp.float32),
            pltpu.VMEM((lanes, TEAMS, rows, TEAM_WIDTH), jnp.bfloat16),
            pltpu.VMEM((lanes, TEAMS, 8, rows), jnp.float32),
            pltpu.SemaphoreType.DMA((2, TEAMS, lanes)),
            pltpu.SemaphoreType.DMA((2, TEAMS, lanes)),
        ]
        + exchange_sems(plan)
        + [pltpu.VMEM(x.shape[1:], x.dtype) for x in shapes],
        compiler_params=pltpu.CompilerParams(
            collective_id=collective, has_side_effects=True, vmem_limit_bytes=VMEM_BYTES
        ),
    )(queries, grads, stats, carried, keys, values, *halves)


def finish_body(
    main_ref,
    rows_ref,
    vector_ref,
    down_ref,
    up_ref,
    out_ref,
    whole_ref,
    home_ref,
    total_ref,
    whole_down,
    whole_up,
    whole_out,
    core_main,
    send_main,
    lane_main,
    team_send_main,
    team_main,
    assembled,
    vectors,
    ready,
    core_sems,
    lane_sems,
    team_sems,
    home_sems,
    vector_sems,
    out_lane_sems,
    out_core_sems,
    local_sems,
    early_team,
    early_lane,
    early_core,
    early_local,
):
    lanes = lax.axis_size("seq") // TEAMS
    me = lax.axis_index("seq")
    core = lax.axis_index("batch")
    team, lane = me // lanes, lax.rem(me, lanes)

    def lane_peer(k):
        other = lax.rem(lane + k, lanes)
        return other, {"seq": team * lanes + other}

    def team_peer(k):
        other = lax.rem(team + k, TEAMS)
        return other, {"seq": other * lanes + lane}

    sibling = {"batch": 1 - core}
    greet(["core", "team", "lane"])

    def place(n, p, t):
        if n == 0:
            return whole_down.at[core, p, t]
        ref = (None, whole_up, whole_out)[n]
        half = ref.shape[3] // 2
        return ref.at[p, t, :, pl.ds(pl.multiple_of(core * half, 128), half)]

    early = (down_ref, up_ref, out_ref)
    number = len(early)
    early_z = [[None] * TEAMS for _ in range(number)]
    for k in range(1, TEAMS):
        _, target = team_peer(k)
        for n in range(number):
            early_z[n][k] = push(
                early[n],
                place(n, lane, team),
                early_team.at[0, n, k],
                early_team.at[1, n, k],
                target,
            )
    early_kept = []
    for n in range(number):
        copy = pltpu.make_async_copy(early[n], place(n, lane, team), early_local.at[n])
        copy.start()
        early_kept.append(copy)
    theirs = pl.ds((1 - core) * lanes, lanes)
    core_copies = [
        push(main_ref.at[theirs], core_main, core_sems.at[0, 0], core_sems.at[1, 0], sibling),
        push(vector_ref, vectors.at[0], vector_sems.at[0, 0], vector_sems.at[1, 0], sibling),
    ]
    early_out = []
    early_sib = []

    def forward(j):
        t = lax.rem(team - j + TEAMS, TEAMS)
        for n in range(number):
            if j == 0:
                source = early[n]
            else:
                early_z[n][j].wait_recv()
                source = place(n, lane, t)
            for k in range(1, lanes):
                _, target = lane_peer(k)
                early_out.append(
                    push(
                        source,
                        place(n, lane, t),
                        early_lane.at[0, n, j, k],
                        early_lane.at[1, n, j, k],
                        target,
                    )
                )
            early_sib.append(
                push(
                    source,
                    place(n, lane, t),
                    early_core.at[0, n, j, 0],
                    early_core.at[1, n, j, 0],
                    sibling,
                )
            )

    forward(0)
    for copy in core_copies:
        copy.wait()

    both = vector_ref[...] + vectors[0]
    vectors[1 + lane] = both
    ready[0] = both
    for j in range(lanes):
        send_main[j] = (
            main_ref[core * lanes + j].astype(jnp.float32) + core_main[j].astype(jnp.float32)
        ).astype(jnp.bfloat16)
    lane_copies = []
    for k in range(1, lanes):
        other, target = lane_peer(k)
        lane_copies += [
            push(send_main.at[other], lane_main.at[lane], lane_sems.at[0, 0, k], lane_sems.at[1, 0, k], target),
            push(ready.at[0], vectors.at[1 + lane], vector_sems.at[0, k], vector_sems.at[1, k], target),
        ]
    lane_main[lane] = send_main[lane]
    for copy in lane_copies:
        copy.wait()

    def total(ref, start, number):
        result = ref[start].astype(jnp.float32)
        for j in range(1, number):
            result = result + ref[start + j].astype(jnp.float32)
        return result

    whole_vector = total(vectors, 1, lanes)
    ready[1] = whole_vector
    vectors[1 + lanes + team] = whole_vector
    low_main = total(lane_main, 0, lanes).astype(jnp.bfloat16)
    team_send_main[...] = low_main
    team_main[team] = low_main
    team_copies = []
    for k in range(1, TEAMS):
        other, target = team_peer(k)
        at = lanes + k
        team_copies += [
            push(team_send_main, team_main.at[team], team_sems.at[0, 0, k], team_sems.at[1, 0, k], target),
            push(ready.at[1], vectors.at[1 + lanes + team], vector_sems.at[0, at], vector_sems.at[1, at], target),
        ]
    home_copies = []
    for k in range(1, TEAMS):
        other, target = team_peer(k)
        home_copies.append(
            push(rows_ref.at[other], home_ref.at[team], home_sems.at[0, k], home_sems.at[1, k], target)
        )
    own = pltpu.make_async_copy(rows_ref.at[team], home_ref.at[team], local_sems.at[0])
    own.start()
    for j in range(1, TEAMS):
        forward(j)
    for copy in team_copies:
        copy.wait()
    total_ref[...] = total(vectors, 1 + lanes, TEAMS)
    pieces = []
    for part in range(3):
        first = part * QUERY_WIDTH
        for g in range(TEAMS):
            piece = team_main[g, :, first : first + TEAM_WIDTH]
            if g == 0 and part < 2:
                more = piece[:, :HEAD_DIM].astype(jnp.float32)
                for other in range(TEAMS):
                    more = more + team_main[
                        other, :, first + TEAM_WIDTH : first + QUERY_WIDTH
                    ].astype(jnp.float32)
                pieces += [more.astype(jnp.bfloat16), piece[:, HEAD_DIM:]]
            else:
                pieces.append(piece)
    assembled[...] = jnp.concatenate(pieces, axis=1)

    mine = core * lanes + lane
    out_copies = []
    for k in range(1, lanes):
        _, target = lane_peer(k)
        out_copies.append(
            push(assembled, whole_ref.at[mine], out_lane_sems.at[0, k], out_lane_sems.at[1, k], target)
        )
    core_out = [
        push(assembled, whole_ref.at[mine], out_core_sems.at[0, 0], out_core_sems.at[1, 0], sibling)
    ]
    kept = pltpu.make_async_copy(assembled, whole_ref.at[mine], local_sems.at[1])
    kept.start()
    for j in range(TEAMS):
        for n in range(number):
            for k in range(1, lanes):
                early_out[(j * number + n) * (lanes - 1) + k - 1].wait_recv()
                p = lax.rem(lane - k + lanes, lanes)
                at = place(n, p, lax.rem(team - j + TEAMS, TEAMS))
                early_sib.append(
                    push(at, at, early_core.at[0, n, j, k], early_core.at[1, n, j, k], sibling)
                )
    for k in range(1, lanes):
        source = core * lanes + lax.rem(lane - k + lanes, lanes)
        out_copies[k - 1].wait_recv()
        core_out.append(
            push(
                whole_ref.at[source],
                whole_ref.at[source],
                out_core_sems.at[0, k],
                out_core_sems.at[1, k],
                sibling,
            )
        )
    for copy in out_copies + early_out:
        copy.wait_send()
    for n in range(number):
        for k in range(1, TEAMS):
            early_z[n][k].wait_send()
    for copy in core_out + home_copies + early_sib + early_kept:
        copy.wait()
    own.wait()
    kept.wait()


def finish(main, rows_out, vector, quarters, collective):
    lanes = lax.axis_size("seq") // TEAMS
    chunks, depth, main_width = main.shape
    low = jnp.bfloat16
    dma = pltpu.SemaphoreType.DMA
    down, up, out = quarters
    wholes = [
        (2, lanes, TEAMS) + down.shape,
        (lanes, TEAMS, up.shape[0], 2 * up.shape[1]),
        (lanes, TEAMS, out.shape[0], 2 * out.shape[1]),
    ]
    anywhere = pl.BlockSpec(memory_space=pl.ANY)
    inside = pl.BlockSpec(memory_space=pltpu.VMEM)
    return pl.pallas_call(
        finish_body,
        out_shape=[
            jax.ShapeDtypeStruct((chunks, depth, TEAMS * 3 * TEAM_WIDTH), low),
            jax.ShapeDtypeStruct(rows_out.shape, low),
            jax.ShapeDtypeStruct(vector.shape, jnp.float32),
        ]
        + [jax.ShapeDtypeStruct(shape, low) for shape in wholes],
        in_specs=[inside, anywhere, inside] + [anywhere] * 3,
        out_specs=[anywhere, anywhere, inside] + [anywhere] * 3,
        scratch_shapes=[
            pltpu.VMEM((lanes, depth, main_width), low),
            pltpu.VMEM((lanes, depth, main_width), low),
            pltpu.VMEM((lanes, depth, main_width), low),
            pltpu.VMEM((depth, main_width), low),
            pltpu.VMEM((TEAMS, depth, main_width), low),
            pltpu.VMEM((depth, TEAMS * 3 * TEAM_WIDTH), low),
            pltpu.VMEM((1 + lanes + TEAMS,) + vector.shape, jnp.float32),
            pltpu.VMEM((2,) + vector.shape, jnp.float32),
            dma((2, 2)),
            dma((2, 2, lanes)),
            dma((2, 2, TEAMS)),
            dma((2, TEAMS)),
            dma((2, lanes + TEAMS)),
            dma((2, lanes)),
            dma((2, lanes)),
            dma((2,)),
            dma((2, 3, TEAMS)),
            dma((2, 3, TEAMS, lanes)),
            dma((2, 3, TEAMS, lanes)),
            dma((3,)),
        ],
        compiler_params=pltpu.CompilerParams(
            collective_id=collective, has_side_effects=True, vmem_limit_bytes=VMEM_BYTES
        ),
    )(main, rows_out, vector, *quarters)


def layer_norm(values, norm_gain, norm_bias):
    row_mean = jnp.mean(values, axis=-1, keepdims=True)
    centred = values - row_mean
    variance = jnp.mean(centred * centred, axis=-1, keepdims=True)
    return centred * lax.rsqrt(variance + epsilon) * norm_gain + norm_bias


def gelu_tanh(values):
    return jax.nn.gelu(values, approximate=True)


def contract_rows(left_op, right_op):
    return lax.dot_general(
        left_op, right_op, (((0,), (0,)), ((), ())), preferred_element_type=jnp.float32
    )


def contract_cols(left_op, right_op):
    return lax.dot_general(
        left_op, right_op, (((1,), (1,)), ((), ())), preferred_element_type=jnp.float32
    )


def per_device(
    block_input,
    ln1_gain,
    ln1_bias,
    w_qkv,
    w_out,
    ln2_gain,
    ln2_bias,
    w_up,
    w_down,
    length_draw,
    threshold_index,
    grad_out,
):
    rows = block_input.shape[1]
    width = block_input.shape[2]
    blocks = lax.axis_size("seq")
    lanes = blocks // TEAMS
    group_len = blocks * rows
    me = lax.axis_index("seq")
    team = me // lanes
    score_scale = HEAD_DIM ** (-0.5)
    length = group_len - rows + 1 + length_draw % rows
    row_valid = (me * rows + jnp.arange(rows, dtype=jnp.int32) < length[0])[:, None]
    threshold = threshold_index.astype(jnp.float32) / 128.0
    tokens = block_input[0]
    grad_top = grad_out[0]
    grad_top_low = grad_top.astype(jnp.bfloat16)

    ln1_pull = jax.vjp(layer_norm, tokens, ln1_gain, ln1_bias)[1]
    lane_rows, team_weight, queries, keys, values = project(tokens, ln1_gain, ln1_bias, w_qkv, 0)
    lane_rows = lane_rows.reshape(TEAMS * rows, width)

    head_out, masses, carried, excess = attend(
        length, threshold, queries, keys, values, blocks, rows, 1
    )
    head_out = head_out.reshape(TEAMS, TEAM_HEADS, HEAD_DIM, rows)
    log_mass = masses[:, :TEAM_HEADS]
    attn_mixed = jnp.where(row_valid, head_out.reshape(width, rows).T, jnp.zeros((), jnp.bfloat16))

    residual = tokens + dot(attn_mixed, w_out)
    normed_two, ln2_pull = jax.vjp(layer_norm, residual, ln2_gain, ln2_bias)
    normed_two_low = normed_two.astype(jnp.bfloat16)
    hidden = dot(normed_two_low, w_up)
    activated, gelu_pull = jax.vjp(gelu_tanh, hidden)
    activated_low = activated.astype(jnp.bfloat16)
    layer_out = residual + dot(activated_low, w_down)
    grad_hidden_low = gelu_pull(contract_cols(grad_top_low, w_down))[0].astype(jnp.bfloat16)
    grad_resid_norm, grad_ln2_gain, grad_ln2_bias = ln2_pull(contract_cols(grad_hidden_low, w_up))
    grad_resid = grad_top + grad_resid_norm
    grad_attn_low = grad_resid.astype(jnp.bfloat16)
    grad_mixed = jnp.where(
        row_valid,
        contract_cols(grad_attn_low, w_out).astype(jnp.bfloat16),
        jnp.zeros((), jnp.bfloat16),
    )
    grad_rows = grad_mixed.T.reshape(TEAMS, TEAM_HEADS, HEAD_DIM, rows).astype(jnp.float32)
    inner = jnp.sum(grad_rows * head_out.astype(jnp.float32), axis=2)
    stats = jnp.concatenate(
        [log_mass, inner, jnp.zeros((TEAMS, 8 - 2 * TEAM_HEADS, rows), jnp.float32)], axis=1
    )
    grad_cols = jnp.moveaxis(grad_mixed.reshape(rows, TEAMS, TEAM_WIDTH), 1, 0)
    grad_cols, stats, *pairs_of = exchange(
        [("lane", "spread"), ("lane", "spread")]
        + [("core", kind) for kind in ("half", "gather", "gather", "half", "gather", "half")],
        [
            grad_cols,
            stats,
            activated_low,
            grad_top_low,
            normed_two_low,
            grad_hidden_low,
            attn_mixed,
            grad_attn_low,
        ],
        3,
    )
    pairs_of = [x.reshape(2 * rows, -1) for x in pairs_of]
    down_half = contract_rows(pairs_of[0], pairs_of[1]).astype(jnp.bfloat16)
    up_half = contract_rows(pairs_of[2], pairs_of[3]).astype(jnp.bfloat16)
    out_half = contract_rows(pairs_of[4], pairs_of[5]).astype(jnp.bfloat16)
    halves = [x.reshape(lanes, TEAMS, -1, x.shape[1]) for x in (down_half, up_half, out_half)]
    query_grads, key_grads, value_grads, *halves = attend_back(
        queries, grad_cols, stats, carried, keys, values, halves, blocks, rows, 7
    )

    def summed(x):
        return jnp.sum(x.astype(jnp.float32), axis=0).astype(jnp.bfloat16)

    query_grads, *quarters = exchange(
        [("team", "spread"), ("team", "spread"), ("lane", "spread"), ("lane", "spread")],
        [query_grads] + [summed(x) for x in halves],
        5,
    )
    quarters = [summed(x) for x in quarters]
    query_grads = jnp.sum(query_grads.astype(jnp.float32), axis=0) * score_scale
    query_grads = jnp.swapaxes(query_grads.astype(jnp.bfloat16), 1, 2)
    grad_projected = jnp.concatenate([query_grads, key_grads, value_grads], axis=2)
    grad_projected = grad_projected.reshape(TEAMS * rows, -1)
    chunks = 2 * lanes
    grad_main = contract_rows(lane_rows, grad_projected)
    grad_lane_rows = contract_cols(grad_projected, team_weight)
    grad_ln1_bias = jnp.sum(grad_lane_rows, axis=0)
    grad_ln1_gain = (
        jnp.sum(grad_lane_rows * (lane_rows.astype(jnp.float32) - ln1_bias), axis=0) / ln1_gain
    )
    pairs = (length[0] - 1).astype(jnp.float32) * (length[0] - 2).astype(jnp.float32) / 2.0
    vectors = jnp.stack(
        [
            grad_ln1_gain,
            grad_ln1_bias,
            grad_ln2_gain,
            grad_ln2_bias,
            jnp.full((width,), jnp.sum(excess)),
            jnp.full((width,), pairs / blocks),
            jnp.zeros((width,), jnp.float32),
            jnp.zeros((width,), jnp.float32),
        ]
    )
    grad_w_qkv, home_rows, vectors, grad_w_down, grad_w_up, grad_w_out = finish(
        grad_main.astype(jnp.bfloat16).reshape(chunks, width // chunks, -1),
        grad_lane_rows.astype(jnp.bfloat16).reshape(TEAMS, rows, width),
        vectors,
        quarters,
        6,
    )
    grad_w_down = grad_w_down.reshape(w_down.shape)
    grad_w_up = grad_w_up.reshape(w_up.shape)
    grad_w_out = grad_w_out.reshape(w_out.shape)
    grad_w_qkv = grad_w_qkv.reshape(width, 3 * width)
    grad_normed = jnp.sum(home_rows.astype(jnp.float32), axis=0)
    grad_x = grad_resid + ln1_pull(grad_normed)[0]
    pruned_share = (vectors[4, 0] / vectors[5, 0]).reshape(1)
    return (
        layer_out[None],
        grad_x[None],
        vectors[0],
        vectors[1],
        grad_w_qkv.astype(jnp.float32),
        grad_w_out.astype(jnp.float32),
        vectors[2],
        vectors[3],
        grad_w_up.astype(jnp.float32),
        grad_w_down.astype(jnp.float32),
        pruned_share,
    )


def solution(mesh):
    placed = (
        P("batch", "seq", None),
        P(),
        P(),
        P(),
        P(),
        P(),
        P(),
        P(),
        P(),
        P("batch"),
        P(),
        P("batch", "seq", None),
    )
    return jax.shard_map(
        per_device,
        mesh=mesh,
        in_specs=placed,
        out_specs=(
            P("batch", "seq", None),
            P("batch", "seq", None),
            P(),
            P(),
            P(),
            P(),
            P(),
            P(),
            P(),
            P(),
            P(),
        ),
        check_vma=False,
    )
```

```python
import functools

import jax
import jax.numpy as jnp
from jax import lax
from jax.experimental import pallas as pl
from jax.experimental.pallas import tpu as pltpu
from jax.sharding import PartitionSpec as P

HEADS = 12
HEAD_DIM = 64
TEAMS = 4
TEAM_HEADS = HEADS // TEAMS
TEAM_WIDTH = TEAM_HEADS * HEAD_DIM
QUERY_WIDTH = TEAM_WIDTH + HEAD_DIM

epsilon = 1e-05
negative = -1e30
select_scale = 3.0
VMEM_BYTES = 60 * 2**20
MESH = pl.DeviceIdType.MESH


def peers_of(scope):
    lanes = lax.axis_size("seq") // TEAMS
    me = lax.axis_index("seq")
    team, lane = me // lanes, lax.rem(me, lanes)
    if scope == "team":
        return lane, lanes, lambda k: {"seq": team * lanes + k}
    if scope == "lane":
        return team, TEAMS, lambda k: {"seq": k * lanes + lane}
    if scope == "core":
        return lax.axis_index("batch"), 2, lambda k: {"batch": k}
    return me, lanes * TEAMS, lambda k: {"seq": k}


def scope_size(scope):
    count = lax.axis_size("seq")
    return {"team": count // TEAMS, "lane": TEAMS, "core": 2, "all": count}[scope]


def greet(scopes):
    barrier = pltpu.get_barrier_semaphore()
    number = 0
    for scope in scopes:
        mine, peers, device_of = peers_of(scope)
        for k in range(1, peers):
            pl.semaphore_signal(
                barrier, inc=1, device_id=device_of(lax.rem(mine + k, peers)), device_id_type=MESH
            )
        number += peers - 1
    pl.semaphore_wait(barrier, number)


def push(source, destination, send, receive, target, start=True):
    copy = pltpu.make_async_remote_copy(
        src_ref=source,
        dst_ref=destination,
        send_sem=send,
        recv_sem=receive,
        device_id=target,
        device_id_type=MESH,
    )
    if start:
        copy.start()
    return copy


def part_of(kind, ref, k):
    if kind == "gather":
        return ref
    if kind == "spread":
        return ref.at[k]
    if kind == "second":
        return ref.at[:, k]
    half = ref.shape[1] // 2
    return ref.at[:, pl.ds(pl.multiple_of(k * half, 128), half)]


def remote_copies(plan, sources, targets, send, receive, start=True):
    copies = []
    for n, (scope, kind) in enumerate(plan):
        mine, peers, device_of = peers_of(scope)
        for k in range(1, peers):
            peer = lax.rem(mine + k, peers)
            copies.append(
                push(
                    part_of(kind, sources[n], peer),
                    targets[n].at[mine],
                    send.at[n, k],
                    receive.at[n, k],
                    device_of(peer),
                    start,
                )
            )
    return copies


def exchange_shapes(plan, arrays):
    shapes = []
    for (scope, kind), x in zip(plan, arrays):
        shape = x.shape
        if kind == "gather":
            shape = (scope_size(scope),) + shape
        if kind == "half":
            shape = (2, shape[0], shape[1] // 2)
        if kind == "second":
            shape = (shape[1], shape[0]) + shape[2:]
        shapes.append(jax.ShapeDtypeStruct(shape, x.dtype))
    return shapes


def exchange_sems(plan):
    number, most = len(plan), max(scope_size(scope) for scope, _ in plan)
    return [
        pltpu.SemaphoreType.DMA((number, most)),
        pltpu.SemaphoreType.DMA((number, most)),
        pltpu.SemaphoreType.DMA((number,)),
    ]


def scopes_of(plan):
    return [x for x in ("core", "team", "lane", "all") if x in [scope for scope, _ in plan]]


def exchange(plan, arrays, collective):
    number = len(arrays)
    shapes = exchange_shapes(plan, arrays)

    def body(*refs):
        sources, targets = refs[:number], refs[number : 2 * number]
        send, receive, local = refs[2 * number : 2 * number + 3]
        through = refs[2 * number + 3 :]
        greet(scopes_of(plan))
        copies = remote_copies(plan, sources, targets, send, receive)
        inward = []
        for n, (scope, kind) in enumerate(plan):
            mine = peers_of(scope)[0]
            copy = pltpu.make_async_copy(part_of(kind, sources[n], mine), through[n], local.at[n])
            copy.start()
            inward.append(copy)
        for n, (scope, kind) in enumerate(plan):
            mine = peers_of(scope)[0]
            inward[n].wait()
            copy = pltpu.make_async_copy(through[n], targets[n].at[mine], local.at[n])
            copy.start()
            copies.append(copy)
        for copy in copies:
            copy.wait()

    return pl.pallas_call(
        body,
        out_shape=shapes,
        in_specs=[pl.BlockSpec(memory_space=pl.ANY)] * number,
        out_specs=[pl.BlockSpec(memory_space=pl.ANY)] * number,
        scratch_shapes=exchange_sems(plan) + [pltpu.VMEM(x.shape[1:], x.dtype) for x in shapes],
        compiler_params=pltpu.CompilerParams(
            collective_id=collective, has_side_effects=True, vmem_limit_bytes=VMEM_BYTES
        ),
    )(*arrays)


def dot(left, right):
    return jnp.dot(left, right, preferred_element_type=jnp.float32)


def project_body(
    tokens_ref,
    gain_ref,
    bias_ref,
    w_ref,
    lane_ref,
    weight_ref,
    query_ref,
    key_ref,
    value_ref,
    held,
    ready,
    windows,
    firsts,
    hop_send,
    hop_recv,
    team_send,
    team_recv,
    weight_sems,
    local_sems,
):
    lanes = lax.axis_size("seq") // TEAMS
    me = lax.axis_index("seq")
    team, lane = me // lanes, lax.rem(me, lanes)
    width = tokens_ref.shape[1]
    wide = windows.shape[2]
    start = (3 * team // 2) * 128
    loads = []
    for part in range(3):
        at = pl.ds(pl.multiple_of(part * width + start, 128), wide)
        loads.append(pltpu.make_async_copy(w_ref.at[:, at], windows.at[part], weight_sems.at[part]))
    for part in range(2):
        at = pl.ds(part * width, 128)
        loads.append(
            pltpu.make_async_copy(w_ref.at[:, at], firsts.at[part], weight_sems.at[3 + part])
        )
    for load in loads:
        load.start()
    tokens = tokens_ref[...]
    row_mean = jnp.mean(tokens, axis=1, keepdims=True)
    centred = tokens - row_mean
    variance = jnp.mean(centred * centred, axis=1, keepdims=True)
    normed = centred * lax.rsqrt(variance + epsilon) * gain_ref[...] + bias_ref[...]
    held[team] = normed.astype(jnp.bfloat16)
    greet(["team", "lane"])

    def hop(side, distance, start=True):
        block = team - distance if side == 0 else team + distance
        target = me + lanes if side == 0 else me - lanes
        return push(
            held.at[block],
            held.at[block],
            hop_send.at[side, distance],
            hop_recv.at[side, distance],
            {"seq": target},
            start,
        )

    @pl.when(team < TEAMS - 1)
    def _():
        hop(0, 0)

    @pl.when(team > 0)
    def _():
        hop(1, 0)

    for load in loads:
        load.wait()
    odd = lax.rem(team, 2) == 1
    pieces = []
    for part in range(3):
        window = windows[part]
        pieces.append(
            jnp.where(odd, window[:, wide - TEAM_WIDTH :], window[:, :TEAM_WIDTH])
        )
        if part < 2:
            pieces.append(firsts[part][:, :HEAD_DIM])
    weight_ref[...] = jnp.concatenate(pieces, axis=1)

    def block_copies(block, start):
        copies = []
        for k in range(1, lanes):
            target = {"seq": team * lanes + lax.rem(lane + k, lanes)}
            copies.append(
                push(
                    ready.at[block],
                    query_ref.at[lane, block],
                    team_send.at[block, k],
                    team_recv.at[block, k],
                    target,
                    start,
                )
            )
        for n, (source, destination) in enumerate(
            ((ready.at[block], query_ref.at[lane, block]), (held.at[block], lane_ref.at[block]))
        ):
            copy = pltpu.make_async_copy(source, destination, local_sems.at[n, block])
            if start:
                copy.start()
            copies.append(copy)
        return copies

    def project(block):
        result = dot(held[block], weight_ref[...]).astype(jnp.bfloat16)
        ready[block] = result[:, :QUERY_WIDTH] * jnp.bfloat16(HEAD_DIM ** (-0.5))
        block_copies(block, True)
        key_ref[block] = result[:, QUERY_WIDTH : 2 * QUERY_WIDTH]
        value_ref[block] = result[:, 2 * QUERY_WIDTH :]

    project(team)

    def arrive(step, _):
        distance, side = step // 2 + 1, lax.rem(step, 2)
        for which in range(2):
            block = team - distance if which == 0 else team + distance
            there = (block >= 0) if which == 0 else (block < TEAMS)
            further = (team < TEAMS - 1) if which == 0 else (team > 0)

            @pl.when((side == which) & there)
            def _():
                hop(which, distance - 1, False).wait_recv()

                @pl.when(further)
                def _():
                    hop(which, distance)

                project(block)

        return 0

    lax.fori_loop(0, 2 * (TEAMS - 1), arrive, 0)
    for distance in range(TEAMS - 1):

        @pl.when((team < TEAMS - 1) & (team >= distance))
        def _():
            hop(0, distance, False).wait_send()

        @pl.when((team > 0) & (team + distance < TEAMS))
        def _():
            hop(1, distance, False).wait_send()

    for block in range(TEAMS):
        for copy in block_copies(block, False):
            copy.wait()


def project(tokens, gain, bias, weight, collective):
    lanes = lax.axis_size("seq") // TEAMS
    rows, width = tokens.shape
    inside = pl.BlockSpec(memory_space=pltpu.VMEM)
    anywhere = pl.BlockSpec(memory_space=pl.ANY)
    columns = 2 * QUERY_WIDTH + TEAM_WIDTH
    low = jnp.bfloat16
    dma = pltpu.SemaphoreType.DMA
    return pl.pallas_call(
        project_body,
        out_shape=[
            jax.ShapeDtypeStruct((TEAMS, rows, width), low),
            jax.ShapeDtypeStruct((width, columns), low),
            jax.ShapeDtypeStruct((lanes, TEAMS, rows, QUERY_WIDTH), low),
            jax.ShapeDtypeStruct((TEAMS, rows, QUERY_WIDTH), low),
            jax.ShapeDtypeStruct((TEAMS, rows, TEAM_WIDTH), low),
        ],
        in_specs=[inside, inside, inside, anywhere],
        out_specs=[anywhere, inside, anywhere, inside, inside],
        scratch_shapes=[
            pltpu.VMEM((TEAMS, rows, width), low),
            pltpu.VMEM((TEAMS, rows, QUERY_WIDTH), low),
            pltpu.VMEM((3, width, 256), low),
            pltpu.VMEM((2, width, 128), low),
            dma((2, TEAMS)),
            dma((2, TEAMS)),
            dma((TEAMS, lanes)),
            dma((TEAMS, lanes)),
            dma((5,)),
            dma((2, TEAMS)),
        ],
        compiler_params=pltpu.CompilerParams(
            collective_id=collective, has_side_effects=True, vmem_limit_bytes=VMEM_BYTES
        ),
    )(tokens, gain[None], bias[None], weight)


def fold(tile):
    return jnp.sum(tile.reshape(tile.shape[0] // 8, 8, tile.shape[1]), axis=0)


def attend_body(
    length_ref,
    threshold_ref,
    q_ref,
    kk_ref,
    vv_ref,
    out_ref,
    mass_ref,
    carried_ref,
    excess_ref,
    key_heads,
    value_rows,
    running,
    logits,
    out_all,
    mass_all,
    lane_out,
    lane_mass,
    joined_out,
    joined_mass,
    home_out,
    home_mass,
    lane_send,
    lane_recv,
    home_send,
    home_recv,
    *,
    blocks,
    rows,
):
    lanes = blocks // TEAMS
    me = lax.axis_index("seq")
    team, lane = me // lanes, lax.rem(me, lanes)
    i = pl.program_id(0)
    scale = select_scale / (blocks * rows)
    key_iota = lax.broadcasted_iota(jnp.int32, (rows, rows), 0)
    query_iota = lax.broadcasted_iota(jnp.int32, (rows, rows), 1)

    def part_copies(j, start):
        z, owner = j // lanes, lax.rem(j, lanes)
        return [
            push(
                source.at[j],
                destination.at[z, lane],
                lane_send.at[n, j],
                lane_recv.at[n, z, lane],
                {"seq": team * lanes + owner},
                start,
            )
            for n, (source, destination) in enumerate(
                ((out_all, lane_out), (mass_all, lane_mass))
            )
        ]

    def home_copies(z, start):
        return [
            push(
                source.at[z],
                destination.at[team],
                home_send.at[n, z],
                home_recv.at[n, team],
                {"seq": z * lanes + lane},
                start,
            )
            for n, (source, destination) in enumerate(
                ((joined_out, home_out), (joined_mass, home_mass))
            )
        ]

    def join(z):
        for k in range(1, lanes):
            other = lax.rem(lane + k, lanes)
            for n, buffer in enumerate((lane_out, lane_mass)):
                pltpu.make_async_copy(
                    buffer.at[z, other], buffer.at[z, other], lane_recv.at[n, z, other]
                ).wait()
        masses = [lane_mass[z, p] for p in range(lanes)]
        peak = masses[0]
        for p in range(1, lanes):
            peak = jnp.maximum(peak, masses[p])
        shares = [jnp.exp(mass - peak) for mass in masses]
        whole = shares[0]
        for p in range(1, lanes):
            whole = whole + shares[p]
        joined_mass[z] = peak + jnp.log(whole)
        inverse = 1.0 / whole
        for h in range(TEAM_HEADS):
            span = slice(h * HEAD_DIM, (h + 1) * HEAD_DIM)
            mixed = None
            for p in range(lanes):
                share = (shares[p] * inverse)[h : h + 1, :]
                part = lane_out[z, p, span, :].astype(jnp.float32) * share
                mixed = part if p == 0 else mixed + part
            joined_out[z, span, :] = mixed.astype(jnp.bfloat16)

        @pl.when(team != z)
        def _():
            home_copies(z, True)

        @pl.when(team == z)
        def _():
            home_out[team] = joined_out[z]
            home_mass[team] = joined_mass[z]

    @pl.when(i == 0)
    def _():
        greet(["team", "lane"])
        running[...] = jnp.zeros_like(running)
        excess_ref[...] = jnp.zeros_like(excess_ref)
        for z in range(TEAMS):
            for h in range(TEAM_HEADS):
                key_heads[h, z] = kk_ref[z, :, h * HEAD_DIM : (h + 1) * HEAD_DIM]
            first = kk_ref[z, :, TEAM_WIDTH:]
            if z == 0:
                slot = lax.broadcasted_iota(jnp.int32, first.shape, 0) + lane * rows
                first = jnp.where(slot >= 1, first, jnp.zeros_like(first))
            key_heads[TEAM_HEADS, z] = first
            value_rows[z] = vv_ref[z].T

    active = jnp.where(i >= lane, (i - lane) // lanes + 1, 0)
    threshold = threshold_ref[0]

    @pl.when(active == 0)
    def _():
        out_all[i] = jnp.zeros((TEAM_WIDTH, rows), jnp.bfloat16)
        mass_all[i] = jnp.full((8, rows), negative, jnp.float32)

    def work(count):
        q_rows = q_ref[0, 0].T
        heads = [q_rows[h * HEAD_DIM : (h + 1) * HEAD_DIM] for h in range(TEAM_HEADS + 1)]
        earlier = jnp.where(key_iota < query_iota, scale, 0.0).astype(jnp.bfloat16)
        every = jnp.full((rows, rows), scale, jnp.bfloat16)
        last = ((count - 1) * lanes + lane) * rows + key_iota
        query_pos = i * rows + query_iota
        peaks = [None] * TEAM_HEADS
        for z in range(count):
            first = jnp.maximum(dot(key_heads[TEAM_HEADS, z], heads[TEAM_HEADS]), 0.0)
            if z == count - 1:
                first = jnp.where(last < query_pos, first, 0.0)
            first = first.astype(jnp.bfloat16)
            carried = running[z] + dot(first, earlier)
            running[z] = running[z] + dot(first, every)

            if z == count - 1:
                carried = jnp.where(last <= query_pos, carried, -negative)
            carried_ref[0, z] = carried
            for h in range(TEAM_HEADS):
                logit = dot(key_heads[h, z], heads[h]) - carried
                logits[h, z] = logit
                peak = jnp.max(logit.reshape(rows // 8, 8, rows), axis=0)
                peaks[h] = peak if z == 0 else jnp.maximum(peaks[h], peak)
        mass_all[i] = jnp.zeros((8, rows), jnp.float32)
        for h in range(TEAM_HEADS):
            peak = jnp.max(peaks[h], axis=0, keepdims=True)
            mass, mixed = None, None
            for z in range(count):
                terms = jnp.exp(logits[h, z] - peak)
                part = fold(terms)
                values = value_rows[z, h * HEAD_DIM : (h + 1) * HEAD_DIM, :]
                product = dot(values, terms.astype(jnp.bfloat16))
                mass = part if z == 0 else mass + part
                mixed = product if z == 0 else mixed + product
            mass = jnp.sum(mass, axis=0, keepdims=True)
            out_all[i, h * HEAD_DIM : (h + 1) * HEAD_DIM, :] = (mixed * (1.0 / mass)).astype(
                jnp.bfloat16
            )
            mass_all[i, h : h + 1, :] = peak + jnp.log(mass)

        @pl.when(lax.rem(i, TEAMS) == team)
        def _():
            total = None
            for z in range(count):
                carried = carried_ref[0, z]
                if z == count - 1:
                    carried = jnp.where(last < query_pos, carried, 0.0)
                part = fold(jnp.clip(carried - threshold, 0.0, 1.0))
                total = part if z == 0 else total + part
            valid = i * rows + lax.broadcasted_iota(jnp.int32, (8, rows), 1) < length_ref[0]
            excess_ref[...] += jnp.where(valid, total, 0.0)

    for count in range(1, TEAMS + 1):
        pl.when(active == count)(functools.partial(work, count))

    @pl.when(lax.rem(i, lanes) != lane)
    def _():
        part_copies(i, True)

    @pl.when(lax.rem(i, lanes) == lane)
    def _():
        lane_out[i // lanes, lane] = out_all[i]
        lane_mass[i // lanes, lane] = mass_all[i]

    for z in range(TEAMS - 1):
        pl.when(i == (z + 1) * lanes + 1)(functools.partial(join, z))

    @pl.when(i == blocks - 1)
    def _():
        join(TEAMS - 1)

        def drain(j, _):
            @pl.when(lax.rem(j, lanes) != lane)
            def _():
                for copy in part_copies(j, False):
                    copy.wait_send()

            return 0

        lax.fori_loop(0, blocks, drain, 0)
        for z in range(TEAMS):

            @pl.when(team != z)
            def _():
                for copy in home_copies(z, False):
                    copy.wait_send()
                for n, buffer in enumerate((home_out, home_mass)):
                    pltpu.make_async_copy(
                        buffer.at[z], buffer.at[z], home_recv.at[n, z]
                    ).wait()

        out_ref[...] = home_out[...]
        mass_ref[...] = home_mass[...]

def attend(length, threshold, queries, keys, values, blocks, rows, collective):
    lanes = blocks // TEAMS
    smem = pl.BlockSpec(memory_space=pltpu.SMEM)
    whole = pl.BlockSpec((TEAMS, rows, QUERY_WIDTH), lambda i: (0, 0, 0))
    return pl.pallas_call(
        functools.partial(attend_body, blocks=blocks, rows=rows),
        grid=(blocks,),
        in_specs=[
            smem,
            smem,
            pl.BlockSpec(
                (1, 1, rows, QUERY_WIDTH), lambda i: (lax.rem(i, lanes), i // lanes, 0, 0)
            ),
            whole,
            pl.BlockSpec((TEAMS, rows, TEAM_WIDTH), lambda i: (0, 0, 0)),
        ],
        out_specs=[
            pl.BlockSpec((TEAMS, TEAM_WIDTH, rows), lambda i: (0, 0, 0)),
            pl.BlockSpec((TEAMS, 8, rows), lambda i: (0, 0, 0)),
            pl.BlockSpec((1, TEAMS, rows, rows), lambda i: (i, 0, 0, 0)),
            pl.BlockSpec((8, rows), lambda i: (0, 0)),
        ],
        out_shape=[
            jax.ShapeDtypeStruct((TEAMS, TEAM_WIDTH, rows), jnp.bfloat16),
            jax.ShapeDtypeStruct((TEAMS, 8, rows), jnp.float32),
            jax.ShapeDtypeStruct((blocks, TEAMS, rows, rows), jnp.float32),
            jax.ShapeDtypeStruct((8, rows), jnp.float32),
        ],
        scratch_shapes=[
            pltpu.VMEM((TEAM_HEADS + 1, TEAMS, rows, HEAD_DIM), jnp.bfloat16),
            pltpu.VMEM((TEAMS, TEAM_WIDTH, rows), jnp.bfloat16),
            pltpu.VMEM((TEAMS, rows, rows), jnp.float32),
            pltpu.VMEM((TEAM_HEADS, TEAMS, rows, rows), jnp.float32),
            pltpu.VMEM((blocks, TEAM_WIDTH, rows), jnp.bfloat16),
            pltpu.VMEM((blocks, 8, rows), jnp.float32),
            pltpu.VMEM((TEAMS, lanes, TEAM_WIDTH, rows), jnp.bfloat16),
            pltpu.VMEM((TEAMS, lanes, 8, rows), jnp.float32),
            pltpu.VMEM((TEAMS, TEAM_WIDTH, rows), jnp.bfloat16),
            pltpu.VMEM((TEAMS, 8, rows), jnp.float32),
            pltpu.VMEM((TEAMS, TEAM_WIDTH, rows), jnp.bfloat16),
            pltpu.VMEM((TEAMS, 8, rows), jnp.float32),
            pltpu.SemaphoreType.DMA((2, blocks)),
            pltpu.SemaphoreType.DMA((2, TEAMS, lanes)),
            pltpu.SemaphoreType.DMA((2, TEAMS)),
            pltpu.SemaphoreType.DMA((2, TEAMS)),
        ],
        compiler_params=pltpu.CompilerParams(
            collective_id=collective, has_side_effects=True, vmem_limit_bytes=VMEM_BYTES
        ),
    )(length, threshold, queries, keys, values)


reduce_plan = [("lane", "second"), ("team", "spread"), ("team", "spread")]


def added(parts):
    total = parts[0].astype(jnp.float32)
    for part in parts[1:]:
        total = total + part.astype(jnp.float32)
    return total.astype(jnp.bfloat16)


def attend_back_body(
    q_ref,
    grad_ref,
    stat_ref,
    carried_ref,
    kk_ref,
    vv_ref,
    *refs,
    blocks,
    rows,
):
    plan = reduce_plan
    sources, refs = refs[:3], refs[3:]
    (query_grad_ref, key_grad_ref, value_grad_ref), reduced, refs = refs[:3], refs[3:6], refs[6:]
    key_heads, key_rows, value_heads, running, key_sum, value_sum = refs[:6]
    grad_all, stat_all, grad_send, grad_recv, send, receive, local = refs[6:13]
    targets = refs[13:]
    lanes = blocks // TEAMS
    me = lax.axis_index("seq")
    team, lane = me // lanes, lax.rem(me, lanes)
    step = pl.program_id(0)
    i = blocks - 1 - step
    scale = select_scale / (blocks * rows)
    span = [slice(h * HEAD_DIM, (h + 1) * HEAD_DIM) for h in range(TEAM_HEADS + 1)]
    key_iota = lax.broadcasted_iota(jnp.int32, (rows, rows), 0)
    query_iota = lax.broadcasted_iota(jnp.int32, (rows, rows), 1)

    place, owner = i // lanes, lax.rem(i, lanes)

    def grad_copies(z, start):
        return [
            push(
                buffer.at[lane, z],
                buffer.at[lane, z],
                grad_send.at[n, z, k],
                grad_recv.at[n, z, lane],
                {"seq": team * lanes + lax.rem(lane + k, lanes)},
                start,
            )
            for k in range(1, lanes)
            for n, buffer in enumerate((grad_all, stat_all))
        ]

    def own_copy(n):
        scope, kind = plan[n]
        mine = peers_of(scope)[0]
        return pltpu.make_async_copy(
            part_of(kind, sources[n], mine), targets[n].at[mine], local.at[n]
        )

    def plan_copies(scope, start):
        chosen = [n for n in range(len(plan)) if plan[n][0] == scope]
        copies = []
        for n in chosen:
            copies += remote_copies(
                plan[n : n + 1],
                sources[n : n + 1],
                targets[n : n + 1],
                send.at[n : n + 1],
                receive.at[n : n + 1],
                start,
            )
        return copies

    @pl.when(step == 0)
    def _():
        greet(["team", "lane"])
        grad_all[lane] = grad_ref[...]
        stat_all[lane] = stat_ref[...]
        for z in reversed(range(TEAMS)):
            grad_copies(z, True)
        plan_copies("lane", True)
        for n in range(len(plan)):
            own_copy(n).start()
        running[...] = jnp.zeros_like(running)
        key_sum[...] = jnp.zeros_like(key_sum)
        value_sum[...] = jnp.zeros_like(value_sum)
        for z in range(TEAMS):
            for h in range(TEAM_HEADS + 1):
                key_heads[h, z] = kk_ref[z, :, span[h]]
            for h in range(TEAM_HEADS):
                value_heads[h, z] = vv_ref[z, :, span[h]]
            key_rows[z] = kk_ref[z].T
        first = kk_ref[0, :, span[TEAM_HEADS]]
        slot = lax.broadcasted_iota(jnp.int32, first.shape, 0) + lane * rows
        key_heads[TEAM_HEADS, 0] = jnp.where(slot >= 1, first, jnp.zeros_like(first))

    @pl.when(step == 2)
    def _():
        plan_copies("team", True)

    @pl.when(owner != lane)
    def _():
        for n, buffer in enumerate((grad_all, stat_all)):
            at = buffer.at[owner, place]
            pltpu.make_async_copy(at, at, grad_recv.at[n, place, owner]).wait()

    active = jnp.where(i >= lane, (i - lane) // lanes + 1, 0)

    @pl.when(active == 0)
    def _():
        query_grad_ref[...] = jnp.zeros_like(query_grad_ref)

    def work(count):
        q_rows = q_ref[0, 0].T
        grad_rows = grad_all[owner, place].T
        q_row = [q_rows[span[h]] for h in range(TEAM_HEADS + 1)]
        q_col = [q_ref[0, 0, :, span[h]] for h in range(TEAM_HEADS + 1)]
        grad_row = [grad_rows[span[h]] for h in range(TEAM_HEADS)]
        grad_col = [grad_all[owner, place, :, span[h]] for h in range(TEAM_HEADS)]
        mass = [stat_all[owner, place, h : h + 1, :] for h in range(TEAM_HEADS)]
        inner = [stat_all[owner, place, TEAM_HEADS + h : TEAM_HEADS + h + 1, :] for h in range(TEAM_HEADS)]
        later = jnp.where(key_iota > query_iota, -scale, 0.0).astype(jnp.bfloat16)
        every = jnp.full((rows, rows), -scale, jnp.bfloat16)
        last = ((count - 1) * lanes + lane) * rows + key_iota
        query_pos = i * rows + query_iota
        sums = [None] * (TEAM_HEADS + 1)
        for z in range(count):
            carried = carried_ref[0, z]
            total = None
            for h in range(TEAM_HEADS):
                probs = jnp.exp(dot(key_heads[h, z], q_row[h]) - carried - mass[h])
                value_sum[h, z] += dot(probs.astype(jnp.bfloat16), grad_col[h])
                grad_logit = probs * (dot(value_heads[h, z], grad_row[h]) - inner[h])
                total = grad_logit if h == 0 else total + grad_logit
                low = grad_logit.astype(jnp.bfloat16)
                key_sum[h, z] += dot(low, q_col[h])
                part = dot(key_rows[z, span[h], :], low)
                sums[h] = part if z == 0 else sums[h] + part
            total = total.astype(jnp.bfloat16)
            select_grad = running[z] + dot(total, later)
            running[z] = running[z] + dot(total, every)
            first = dot(key_heads[TEAM_HEADS, z], q_row[TEAM_HEADS])
            live = first > 0.0
            if z == count - 1:
                live = live & (last < query_pos)
            low = jnp.where(live, select_grad, 0.0).astype(jnp.bfloat16)
            key_sum[TEAM_HEADS, z] += dot(low, q_col[TEAM_HEADS])
            part = dot(key_rows[z, span[TEAM_HEADS], :], low)
            sums[TEAM_HEADS] = part if z == 0 else sums[TEAM_HEADS] + part
        for h in range(TEAM_HEADS + 1):
            query_grad_ref[0, 0, span[h], :] = sums[h].astype(jnp.bfloat16)

    for count in range(1, TEAMS + 1):
        pl.when(active == count)(functools.partial(work, count))

    @pl.when(step == blocks - 1)
    def _():
        for h in range(TEAM_HEADS + 1):
            key_grad_ref[:, :, span[h]] = key_sum[h].astype(jnp.bfloat16)
        for h in range(TEAM_HEADS):
            value_grad_ref[:, :, span[h]] = value_sum[h].astype(jnp.bfloat16)
        for z in range(TEAMS):
            for copy in grad_copies(z, False):
                copy.wait_send()
        for n in range(len(plan)):
            own_copy(n).wait()
        for scope in ("lane", "team"):
            for copy in plan_copies(scope, False):
                copy.wait()
        for n in range(len(plan)):
            for j in range(reduced[n].shape[0]):
                reduced[n][j] = added([targets[n][k, j] for k in range(targets[n].shape[0])])


def attend_back(queries, grads, stats, carried, keys, values, halves, blocks, rows, collective):
    lanes = blocks // TEAMS
    plan = reduce_plan
    shapes = exchange_shapes(plan, halves)

    def place(step):
        i = blocks - 1 - step
        return (lax.rem(i, lanes), i // lanes, 0, 0)

    return pl.pallas_call(
        functools.partial(attend_back_body, blocks=blocks, rows=rows),
        grid=(blocks,),
        in_specs=[
            pl.BlockSpec((1, 1, rows, QUERY_WIDTH), place),
            pl.BlockSpec((TEAMS, rows, TEAM_WIDTH), lambda step: (0, 0, 0)),
            pl.BlockSpec((TEAMS, 8, rows), lambda step: (0, 0, 0)),
            pl.BlockSpec((1, TEAMS, rows, rows), lambda step: (blocks - 1 - step, 0, 0, 0)),
            pl.BlockSpec((TEAMS, rows, QUERY_WIDTH), lambda step: (0, 0, 0)),
            pl.BlockSpec((TEAMS, rows, TEAM_WIDTH), lambda step: (0, 0, 0)),
        ]
        + [pl.BlockSpec(memory_space=pl.ANY)] * 3,
        out_specs=[
            pl.BlockSpec((1, 1, QUERY_WIDTH, rows), place),
            pl.BlockSpec((TEAMS, rows, QUERY_WIDTH), lambda step: (0, 0, 0)),
            pl.BlockSpec((TEAMS, rows, TEAM_WIDTH), lambda step: (0, 0, 0)),
        ]
        + [pl.BlockSpec(x.shape[1:], lambda step: (0, 0, 0)) for x in shapes],
        out_shape=[
            jax.ShapeDtypeStruct((lanes, TEAMS, QUERY_WIDTH, rows), jnp.bfloat16),
            jax.ShapeDtypeStruct((TEAMS, rows, QUERY_WIDTH), jnp.bfloat16),
            jax.ShapeDtypeStruct((TEAMS, rows, TEAM_WIDTH), jnp.bfloat16),
        ]
        + [jax.ShapeDtypeStruct(x.shape[1:], x.dtype) for x in shapes],
        scratch_shapes=[
            pltpu.VMEM((TEAM_HEADS + 1, TEAMS, rows, HEAD_DIM), jnp.bfloat16),
            pltpu.VMEM((TEAMS, QUERY_WIDTH, rows), jnp.bfloat16),
            pltpu.VMEM((TEAM_HEADS, TEAMS, rows, HEAD_DIM), jnp.bfloat16),
            pltpu.VMEM((TEAMS, rows, rows), jnp.float32),
            pltpu.VMEM((TEAM_HEADS + 1, TEAMS, rows, HEAD_DIM), jnp.float32),
            pltpu.VMEM((TEAM_HEADS, TEAMS, rows, HEAD_DIM), jnp.float32),
            pltpu.VMEM((lanes, TEAMS, rows, TEAM_WIDTH), jnp.bfloat16),
            pltpu.VMEM((lanes, TEAMS, 8, rows), jnp.float32),
            pltpu.SemaphoreType.DMA((2, TEAMS, lanes)),
            pltpu.SemaphoreType.DMA((2, TEAMS, lanes)),
        ]
        + exchange_sems(plan)
        + [pltpu.VMEM(x.shape, x.dtype) for x in shapes],
        compiler_params=pltpu.CompilerParams(
            collective_id=collective, has_side_effects=True, vmem_limit_bytes=VMEM_BYTES
        ),
    )(queries, grads, stats, carried, keys, values, *halves)


def finish_body(
    query_ref,
    key_ref,
    value_ref,
    lane_ref,
    weight_ref,
    gain_ref,
    bias_ref,
    base_ref,
    down_in,
    up_in,
    out_in,
    whole_ref,
    home_ref,
    total_ref,
    whole_down,
    whole_up,
    whole_out,
    query_parts,
    down_parts,
    up_parts,
    out_parts,
    down_ref,
    up_ref,
    out_ref,
    turned,
    weight_rows,
    weight_grad,
    rows_sum,
    rows_ref,
    main_ref,
    vector_ref,
    core_main,
    send_main,
    lane_main,
    team_send_main,
    team_main,
    assembled,
    vectors,
    ready,
    core_sems,
    lane_sems,
    team_sems,
    home_sems,
    vector_sems,
    out_lane_sems,
    out_core_sems,
    local_sems,
    early_team,
    early_lane,
    early_core,
    early_local,
    first_send,
    first_recv,
    first_local,
):
    lanes = lax.axis_size("seq") // TEAMS
    me = lax.axis_index("seq")
    core = lax.axis_index("batch")
    team, lane = me // lanes, lax.rem(me, lanes)

    def lane_peer(k):
        other = lax.rem(lane + k, lanes)
        return other, {"seq": team * lanes + other}

    def team_peer(k):
        other = lax.rem(team + k, TEAMS)
        return other, {"seq": other * lanes + lane}

    sibling = {"batch": 1 - core}
    greet(["core", "team", "lane"])
    first_sources = (query_ref, down_in, up_in, out_in)
    first_targets = (query_parts, down_parts, up_parts, out_parts)
    first_plan = [("team", "spread"), ("team", "spread"), ("lane", "spread"), ("lane", "spread")]
    first_copies = [[], []]
    for n in (1, 2, 3, 0):
        mine = peers_of(first_plan[n][0])[0]
        own = pltpu.make_async_copy(first_sources[n].at[mine], first_targets[n].at[mine], first_local.at[n])
        own.start()
        first_copies[n == 0].append(own)
        first_copies[n == 0] += remote_copies(
            first_plan[n : n + 1],
            first_sources[n : n + 1],
            first_targets[n : n + 1],
            first_send.at[n : n + 1],
            first_recv.at[n : n + 1],
        )
    spans = (slice(0, QUERY_WIDTH), slice(QUERY_WIDTH, 2 * QUERY_WIDTH), slice(2 * QUERY_WIDTH, None))
    for span in spans:
        weight_rows[span, :] = weight_ref[:, span].T
    weight_grad[...] = jnp.zeros_like(weight_grad)

    def known(b, _):
        rows_low = lane_ref[b].T
        turned[b] = rows_low
        total = None
        for span, grads in ((spans[1], key_ref[b]), (spans[2], value_ref[b])):
            weight_grad[:, span] += dot(rows_low, grads)
            part = dot(grads, weight_rows[span, :])
            total = part if total is None else total + part
        rows_sum[b] = total
        return 0

    lax.fori_loop(0, TEAMS, known, 0)
    for copy in first_copies[0]:
        copy.wait()
    down_ref[...] = added([down_parts[k] for k in range(lanes)])
    up_ref[...] = added([up_parts[k] for k in range(TEAMS)])
    out_ref[...] = added([out_parts[k] for k in range(TEAMS)])

    def place(n, p, t):
        if n == 0:
            return whole_down.at[core, p, t]
        ref = (None, whole_up, whole_out)[n]
        half = ref.shape[3] // 2
        return ref.at[p, t, :, pl.ds(pl.multiple_of(core * half, 128), half)]

    early = (down_ref, up_ref, out_ref)
    number = len(early)
    early_z = [[None] * TEAMS for _ in range(number)]
    for k in range(1, TEAMS):
        _, target = team_peer(k)
        for n in range(number):
            early_z[n][k] = push(
                early[n],
                place(n, lane, team),
                early_team.at[0, n, k],
                early_team.at[1, n, k],
                target,
            )
    early_kept = []
    for n in range(number):
        copy = pltpu.make_async_copy(early[n], place(n, lane, team), early_local.at[n])
        copy.start()
        early_kept.append(copy)
    early_out = []
    early_sib = []

    def forward(j):
        t = lax.rem(team - j + TEAMS, TEAMS)
        for n in range(number):
            if j == 0:
                source = early[n]
            else:
                early_z[n][j].wait_recv()
                source = place(n, lane, t)
            for k in range(1, lanes):
                _, target = lane_peer(k)
                early_out.append(
                    push(
                        source,
                        place(n, lane, t),
                        early_lane.at[0, n, j, k],
                        early_lane.at[1, n, j, k],
                        target,
                    )
                )
            early_sib.append(
                push(
                    source,
                    place(n, lane, t),
                    early_core.at[0, n, j, 0],
                    early_core.at[1, n, j, 0],
                    sibling,
                )
            )

    forward(0)
    for copy in first_copies[1]:
        copy.wait()
    gain = gain_ref[...]
    bias = bias_ref[...]

    def last(b, sums):
        query_rows = query_parts[0, b].astype(jnp.float32)
        for p in range(1, lanes):
            query_rows = query_rows + query_parts[p, b].astype(jnp.float32)
        grads = (query_rows * HEAD_DIM ** (-0.5)).astype(jnp.bfloat16).T
        weight_grad[:, spans[0]] += dot(turned[b], grads)
        total = rows_sum[b] + dot(grads, weight_rows[spans[0], :])
        rows_ref[b] = total.astype(jnp.bfloat16)
        shifted = lane_ref[b].astype(jnp.float32) - bias
        return (
            sums[0] + jnp.sum(total * shifted, axis=0, keepdims=True),
            sums[1] + jnp.sum(total, axis=0, keepdims=True),
        )

    nothing = jnp.zeros_like(gain)
    gain_sum, bias_sum = lax.fori_loop(0, TEAMS, last, (nothing, nothing))
    vector_ref[...] = base_ref[...]
    vector_ref[0:1, :] = gain_sum / gain
    vector_ref[1:2, :] = bias_sum
    depth = main_ref.shape[1]
    for chunk in range(2 * lanes):
        main_ref[chunk] = weight_grad[chunk * depth : (chunk + 1) * depth, :].astype(jnp.bfloat16)
    theirs = pl.ds((1 - core) * lanes, lanes)
    core_copies = [
        push(main_ref.at[theirs], core_main, core_sems.at[0, 0], core_sems.at[1, 0], sibling),
        push(vector_ref, vectors.at[0], vector_sems.at[0, 0], vector_sems.at[1, 0], sibling),
    ]
    for copy in core_copies:
        copy.wait()

    both = vector_ref[...] + vectors[0]
    vectors[1 + lane] = both
    ready[0] = both
    for j in range(lanes):
        send_main[j] = (
            main_ref[core * lanes + j].astype(jnp.float32) + core_main[j].astype(jnp.float32)
        ).astype(jnp.bfloat16)
    lane_copies = []
    for k in range(1, lanes):
        other, target = lane_peer(k)
        lane_copies += [
            push(send_main.at[other], lane_main.at[lane], lane_sems.at[0, 0, k], lane_sems.at[1, 0, k], target),
            push(ready.at[0], vectors.at[1 + lane], vector_sems.at[0, k], vector_sems.at[1, k], target),
        ]
    lane_main[lane] = send_main[lane]
    for copy in lane_copies:
        copy.wait()

    def total(ref, start, number):
        result = ref[start].astype(jnp.float32)
        for j in range(1, number):
            result = result + ref[start + j].astype(jnp.float32)
        return result

    whole_vector = total(vectors, 1, lanes)
    ready[1] = whole_vector
    vectors[1 + lanes + team] = whole_vector
    low_main = total(lane_main, 0, lanes).astype(jnp.bfloat16)
    team_send_main[...] = low_main
    team_main[team] = low_main
    team_copies = []
    for k in range(1, TEAMS):
        other, target = team_peer(k)
        at = lanes + k
        team_copies += [
            push(team_send_main, team_main.at[team], team_sems.at[0, 0, k], team_sems.at[1, 0, k], target),
            push(ready.at[1], vectors.at[1 + lanes + team], vector_sems.at[0, at], vector_sems.at[1, at], target),
        ]
    home_copies = []
    for k in range(1, TEAMS):
        other, target = team_peer(k)
        home_copies.append(
            push(rows_ref.at[other], home_ref.at[team], home_sems.at[0, k], home_sems.at[1, k], target)
        )
    own = pltpu.make_async_copy(rows_ref.at[team], home_ref.at[team], local_sems.at[0])
    own.start()
    for j in range(1, TEAMS):
        forward(j)
    for copy in team_copies:
        copy.wait()
    total_ref[...] = total(vectors, 1 + lanes, TEAMS)
    pieces = []
    for part in range(3):
        first = part * QUERY_WIDTH
        for g in range(TEAMS):
            piece = team_main[g, :, first : first + TEAM_WIDTH]
            if g == 0 and part < 2:
                more = piece[:, :HEAD_DIM].astype(jnp.float32)
                for other in range(TEAMS):
                    more = more + team_main[
                        other, :, first + TEAM_WIDTH : first + QUERY_WIDTH
                    ].astype(jnp.float32)
                pieces += [more.astype(jnp.bfloat16), piece[:, HEAD_DIM:]]
            else:
                pieces.append(piece)
    assembled[...] = jnp.concatenate(pieces, axis=1)

    mine = core * lanes + lane
    out_copies = []
    for k in range(1, lanes):
        _, target = lane_peer(k)
        out_copies.append(
            push(assembled, whole_ref.at[mine], out_lane_sems.at[0, k], out_lane_sems.at[1, k], target)
        )
    core_out = [
        push(assembled, whole_ref.at[mine], out_core_sems.at[0, 0], out_core_sems.at[1, 0], sibling)
    ]
    kept = pltpu.make_async_copy(assembled, whole_ref.at[mine], local_sems.at[1])
    kept.start()
    for j in range(TEAMS):
        for n in range(number):
            for k in range(1, lanes):
                early_out[(j * number + n) * (lanes - 1) + k - 1].wait_recv()
                p = lax.rem(lane - k + lanes, lanes)
                at = place(n, p, lax.rem(team - j + TEAMS, TEAMS))
                early_sib.append(
                    push(at, at, early_core.at[0, n, j, k], early_core.at[1, n, j, k], sibling)
                )
    for k in range(1, lanes):
        source = core * lanes + lax.rem(lane - k + lanes, lanes)
        out_copies[k - 1].wait_recv()
        core_out.append(
            push(
                whole_ref.at[source],
                whole_ref.at[source],
                out_core_sems.at[0, k],
                out_core_sems.at[1, k],
                sibling,
            )
        )
    for copy in out_copies + early_out:
        copy.wait_send()
    for n in range(number):
        for k in range(1, TEAMS):
            early_z[n][k].wait_send()
    for copy in core_out + home_copies + early_sib + early_kept:
        copy.wait()
    own.wait()
    kept.wait()


def finish(queries, keys, values, lane_rows, weight, gain, bias, base, reduced, collective):
    lanes = lax.axis_size("seq") // TEAMS
    width, columns = weight.shape
    rows = lane_rows.shape[1]
    chunks, depth = 2 * lanes, width // (2 * lanes)
    low = jnp.bfloat16
    dma = pltpu.SemaphoreType.DMA
    down, up, out = (x.shape[1:] for x in reduced)
    wholes = [
        (2, lanes, TEAMS) + down,
        (lanes, TEAMS, up[0], 2 * up[1]),
        (lanes, TEAMS, out[0], 2 * out[1]),
    ]
    anywhere = pl.BlockSpec(memory_space=pl.ANY)
    inside = pl.BlockSpec(memory_space=pltpu.VMEM)
    return pl.pallas_call(
        finish_body,
        out_shape=[
            jax.ShapeDtypeStruct((chunks, depth, 3 * width), low),
            jax.ShapeDtypeStruct(lane_rows.shape, low),
            jax.ShapeDtypeStruct(base.shape, jnp.float32),
        ]
        + [jax.ShapeDtypeStruct(shape, low) for shape in wholes],
        in_specs=[anywhere] + [inside] * 7 + [anywhere] * 3,
        out_specs=[anywhere, anywhere, inside] + [anywhere] * 3,
        scratch_shapes=[
            pltpu.VMEM(queries.shape, low),
            pltpu.VMEM((lanes,) + down, low),
            pltpu.VMEM((TEAMS,) + up, low),
            pltpu.VMEM((TEAMS,) + out, low),
            pltpu.VMEM(down, low),
            pltpu.VMEM(up, low),
            pltpu.VMEM(out, low),
            pltpu.VMEM((TEAMS, width, rows), low),
            pltpu.VMEM((columns, width), low),
            pltpu.VMEM((width, columns), jnp.float32),
            pltpu.VMEM((TEAMS, rows, width), jnp.float32),
            pltpu.VMEM((TEAMS, rows, width), low),
            pltpu.VMEM((chunks, depth, columns), low),
            pltpu.VMEM(base.shape, jnp.float32),
            pltpu.VMEM((lanes, depth, columns), low),
            pltpu.VMEM((lanes, depth, columns), low),
            pltpu.VMEM((lanes, depth, columns), low),
            pltpu.VMEM((depth, columns), low),
            pltpu.VMEM((TEAMS, depth, columns), low),
            pltpu.VMEM((depth, 3 * width), low),
            pltpu.VMEM((1 + lanes + TEAMS,) + base.shape, jnp.float32),
            pltpu.VMEM((2,) + base.shape, jnp.float32),
            dma((2, 2)),
            dma((2, 2, lanes)),
            dma((2, 2, TEAMS)),
            dma((2, TEAMS)),
            dma((2, lanes + TEAMS)),
            dma((2, lanes)),
            dma((2, lanes)),
            dma((2,)),
            dma((2, 3, TEAMS)),
            dma((2, 3, TEAMS, lanes)),
            dma((2, 3, TEAMS, lanes)),
            dma((3,)),
            dma((4, max(lanes, TEAMS))),
            dma((4, max(lanes, TEAMS))),
            dma((4,)),
        ],
        compiler_params=pltpu.CompilerParams(
            collective_id=collective, has_side_effects=True, vmem_limit_bytes=VMEM_BYTES
        ),
    )(queries, keys, values, lane_rows, weight, gain[None], bias[None], base, *reduced)


def layer_norm(values, norm_gain, norm_bias):
    row_mean = jnp.mean(values, axis=-1, keepdims=True)
    centred = values - row_mean
    variance = jnp.mean(centred * centred, axis=-1, keepdims=True)
    return centred * lax.rsqrt(variance + epsilon) * norm_gain + norm_bias


def gelu_tanh(values):
    return jax.nn.gelu(values, approximate=True)


def contract_rows(left_op, right_op):
    return lax.dot_general(
        left_op, right_op, (((0,), (0,)), ((), ())), preferred_element_type=jnp.float32
    )


def contract_cols(left_op, right_op):
    return lax.dot_general(
        left_op, right_op, (((1,), (1,)), ((), ())), preferred_element_type=jnp.float32
    )


def per_device(
    block_input,
    ln1_gain,
    ln1_bias,
    w_qkv,
    w_out,
    ln2_gain,
    ln2_bias,
    w_up,
    w_down,
    length_draw,
    threshold_index,
    grad_out,
):
    rows = block_input.shape[1]
    width = block_input.shape[2]
    blocks = lax.axis_size("seq")
    lanes = blocks // TEAMS
    group_len = blocks * rows
    me = lax.axis_index("seq")
    team = me // lanes
    score_scale = HEAD_DIM ** (-0.5)
    length = group_len - rows + 1 + length_draw % rows
    row_valid = (me * rows + jnp.arange(rows, dtype=jnp.int32) < length[0])[:, None]
    threshold = threshold_index.astype(jnp.float32) / 128.0
    tokens = block_input[0]
    grad_top = grad_out[0]
    grad_top_low = grad_top.astype(jnp.bfloat16)

    ln1_pull = jax.vjp(layer_norm, tokens, ln1_gain, ln1_bias)[1]
    lane_rows, team_weight, queries, keys, values = project(tokens, ln1_gain, ln1_bias, w_qkv, 0)

    head_out, masses, carried, excess = attend(
        length, threshold, queries, keys, values, blocks, rows, 1
    )
    head_out = head_out.reshape(TEAMS, TEAM_HEADS, HEAD_DIM, rows)
    log_mass = masses[:, :TEAM_HEADS]
    attn_mixed = jnp.where(row_valid, head_out.reshape(width, rows).T, jnp.zeros((), jnp.bfloat16))

    residual = tokens + dot(attn_mixed, w_out)
    normed_two, ln2_pull = jax.vjp(layer_norm, residual, ln2_gain, ln2_bias)
    normed_two_low = normed_two.astype(jnp.bfloat16)
    hidden = dot(normed_two_low, w_up)
    activated, gelu_pull = jax.vjp(gelu_tanh, hidden)
    activated_low = activated.astype(jnp.bfloat16)
    layer_out = residual + dot(activated_low, w_down)
    grad_hidden_low = gelu_pull(contract_cols(grad_top_low, w_down))[0].astype(jnp.bfloat16)
    grad_resid_norm, grad_ln2_gain, grad_ln2_bias = ln2_pull(contract_cols(grad_hidden_low, w_up))
    grad_resid = grad_top + grad_resid_norm
    grad_attn_low = grad_resid.astype(jnp.bfloat16)
    grad_mixed = jnp.where(
        row_valid,
        contract_cols(grad_attn_low, w_out).astype(jnp.bfloat16),
        jnp.zeros((), jnp.bfloat16),
    )
    grad_rows = grad_mixed.T.reshape(TEAMS, TEAM_HEADS, HEAD_DIM, rows).astype(jnp.float32)
    inner = jnp.sum(grad_rows * head_out.astype(jnp.float32), axis=2)
    stats = jnp.concatenate(
        [log_mass, inner, jnp.zeros((TEAMS, 8 - 2 * TEAM_HEADS, rows), jnp.float32)], axis=1
    )
    grad_cols = jnp.moveaxis(grad_mixed.reshape(rows, TEAMS, TEAM_WIDTH), 1, 0)
    grad_cols, stats, *pairs_of = exchange(
        [("lane", "spread"), ("lane", "spread")]
        + [("core", kind) for kind in ("half", "gather", "gather", "half", "gather", "half")],
        [
            grad_cols,
            stats,
            activated_low,
            grad_top_low,
            normed_two_low,
            grad_hidden_low,
            attn_mixed,
            grad_attn_low,
        ],
        3,
    )
    pairs_of = [x.reshape(2 * rows, -1) for x in pairs_of]
    down_half = contract_rows(pairs_of[0], pairs_of[1]).astype(jnp.bfloat16)
    up_half = contract_rows(pairs_of[2], pairs_of[3]).astype(jnp.bfloat16)
    out_half = contract_rows(pairs_of[4], pairs_of[5]).astype(jnp.bfloat16)
    halves = [x.reshape(lanes, TEAMS, -1, x.shape[1]) for x in (down_half, up_half, out_half)]
    query_grads, key_grads, value_grads, *halves = attend_back(
        queries, grad_cols, stats, carried, keys, values, halves, blocks, rows, 7
    )

    pairs = (length[0] - 1).astype(jnp.float32) * (length[0] - 2).astype(jnp.float32) / 2.0
    nothing = jnp.zeros((width,), jnp.float32)
    base = jnp.stack(
        [
            nothing,
            nothing,
            grad_ln2_gain,
            grad_ln2_bias,
            jnp.full((width,), jnp.sum(excess)),
            jnp.full((width,), pairs / blocks),
            nothing,
            nothing,
        ]
    )
    grad_w_qkv, home_rows, vectors, grad_w_down, grad_w_up, grad_w_out = finish(
        query_grads,
        key_grads,
        value_grads,
        lane_rows,
        team_weight,
        ln1_gain,
        ln1_bias,
        base,
        halves,
        6,
    )
    grad_w_down = grad_w_down.reshape(w_down.shape)
    grad_w_up = grad_w_up.reshape(w_up.shape)
    grad_w_out = grad_w_out.reshape(w_out.shape)
    grad_w_qkv = grad_w_qkv.reshape(width, 3 * width)
    grad_normed = jnp.sum(home_rows.astype(jnp.float32), axis=0)
    grad_x = grad_resid + ln1_pull(grad_normed)[0]
    pruned_share = (vectors[4, 0] / vectors[5, 0]).reshape(1)
    return (
        layer_out[None],
        grad_x[None],
        vectors[0],
        vectors[1],
        grad_w_qkv.astype(jnp.float32),
        grad_w_out.astype(jnp.float32),
        vectors[2],
        vectors[3],
        grad_w_up.astype(jnp.float32),
        grad_w_down.astype(jnp.float32),
        pruned_share,
    )


def solution(mesh):
    placed = (
        P("batch", "seq", None),
        P(),
        P(),
        P(),
        P(),
        P(),
        P(),
        P(),
        P(),
        P("batch"),
        P(),
        P("batch", "seq", None),
    )
    return jax.shard_map(
        per_device,
        mesh=mesh,
        in_specs=placed,
        out_specs=(
            P("batch", "seq", None),
            P("batch", "seq", None),
            P(),
            P(),
            P(),
            P(),
            P(),
            P(),
            P(),
            P(),
            P(),
        ),
        check_vma=False,
    )
```

```python
import functools

import jax
import jax.numpy as jnp
from jax import lax
from jax.experimental import pallas as pl
from jax.experimental.pallas import tpu as pltpu
from jax.sharding import PartitionSpec as P

HEADS = 12
HEAD_DIM = 64
TEAMS = 4
TEAM_HEADS = HEADS // TEAMS
TEAM_WIDTH = TEAM_HEADS * HEAD_DIM
QUERY_WIDTH = TEAM_WIDTH + HEAD_DIM

epsilon = 1e-05
negative = -1e30
select_scale = 3.0
VMEM_BYTES = 60 * 2**20
MESH = pl.DeviceIdType.MESH


def peers_of(scope):
    lanes = lax.axis_size("seq") // TEAMS
    me = lax.axis_index("seq")
    team, lane = me // lanes, lax.rem(me, lanes)
    if scope == "team":
        return lane, lanes, lambda k: {"seq": team * lanes + k}
    if scope == "lane":
        return team, TEAMS, lambda k: {"seq": k * lanes + lane}
    if scope == "core":
        return lax.axis_index("batch"), 2, lambda k: {"batch": k}
    return me, lanes * TEAMS, lambda k: {"seq": k}


def scope_size(scope):
    count = lax.axis_size("seq")
    return {"team": count // TEAMS, "lane": TEAMS, "core": 2, "all": count}[scope]


def greet(scopes):
    barrier = pltpu.get_barrier_semaphore()
    number = 0
    for scope in scopes:
        mine, peers, device_of = peers_of(scope)
        for k in range(1, peers):
            pl.semaphore_signal(
                barrier, inc=1, device_id=device_of(lax.rem(mine + k, peers)), device_id_type=MESH
            )
        number += peers - 1
    pl.semaphore_wait(barrier, number)


def push(source, destination, send, receive, target, start=True):
    copy = pltpu.make_async_remote_copy(
        src_ref=source,
        dst_ref=destination,
        send_sem=send,
        recv_sem=receive,
        device_id=target,
        device_id_type=MESH,
    )
    if start:
        copy.start()
    return copy


def part_of(kind, ref, k):
    if kind == "gather":
        return ref
    if kind == "spread":
        return ref.at[k]
    if kind == "second":
        return ref.at[:, k]
    half = ref.shape[1] // 2
    return ref.at[:, pl.ds(pl.multiple_of(k * half, 128), half)]


def remote_copies(plan, sources, targets, send, receive, start=True):
    copies = []
    for n, (scope, kind) in enumerate(plan):
        mine, peers, device_of = peers_of(scope)
        for k in range(1, peers):
            peer = lax.rem(mine + k, peers)
            copies.append(
                push(
                    part_of(kind, sources[n], peer),
                    targets[n].at[mine],
                    send.at[n, k],
                    receive.at[n, k],
                    device_of(peer),
                    start,
                )
            )
    return copies


def exchange_shapes(plan, arrays):
    shapes = []
    for (scope, kind), x in zip(plan, arrays):
        shape = x.shape
        if kind == "gather":
            shape = (scope_size(scope),) + shape
        if kind == "half":
            shape = (2, shape[0], shape[1] // 2)
        if kind == "second":
            shape = (shape[1], shape[0]) + shape[2:]
        shapes.append(jax.ShapeDtypeStruct(shape, x.dtype))
    return shapes


def exchange_sems(plan):
    number, most = len(plan), max(scope_size(scope) for scope, _ in plan)
    return [
        pltpu.SemaphoreType.DMA((number, most)),
        pltpu.SemaphoreType.DMA((number, most)),
        pltpu.SemaphoreType.DMA((number,)),
    ]


def scopes_of(plan):
    return [x for x in ("core", "team", "lane", "all") if x in [scope for scope, _ in plan]]


def exchange(plan, arrays, collective):
    number = len(arrays)
    shapes = exchange_shapes(plan, arrays)

    def body(*refs):
        sources, targets = refs[:number], refs[number : 2 * number]
        send, receive, local = refs[2 * number : 2 * number + 3]
        through = refs[2 * number + 3 :]
        greet(scopes_of(plan))
        copies = remote_copies(plan, sources, targets, send, receive)
        inward = []
        for n, (scope, kind) in enumerate(plan):
            mine = peers_of(scope)[0]
            copy = pltpu.make_async_copy(part_of(kind, sources[n], mine), through[n], local.at[n])
            copy.start()
            inward.append(copy)
        for n, (scope, kind) in enumerate(plan):
            mine = peers_of(scope)[0]
            inward[n].wait()
            copy = pltpu.make_async_copy(through[n], targets[n].at[mine], local.at[n])
            copy.start()
            copies.append(copy)
        for copy in copies:
            copy.wait()

    return pl.pallas_call(
        body,
        out_shape=shapes,
        in_specs=[pl.BlockSpec(memory_space=pl.ANY)] * number,
        out_specs=[pl.BlockSpec(memory_space=pl.ANY)] * number,
        scratch_shapes=exchange_sems(plan) + [pltpu.VMEM(x.shape[1:], x.dtype) for x in shapes],
        compiler_params=pltpu.CompilerParams(
            collective_id=collective, has_side_effects=True, vmem_limit_bytes=VMEM_BYTES
        ),
    )(*arrays)


def dot(left, right):
    return jnp.dot(left, right, preferred_element_type=jnp.float32)


def project_body(
    tokens_ref,
    gain_ref,
    bias_ref,
    w_ref,
    lane_ref,
    weight_ref,
    query_ref,
    key_ref,
    value_ref,
    held,
    ready,
    windows,
    firsts,
    hop_send,
    hop_recv,
    team_send,
    team_recv,
    weight_sems,
    local_sems,
):
    lanes = lax.axis_size("seq") // TEAMS
    me = lax.axis_index("seq")
    team, lane = me // lanes, lax.rem(me, lanes)
    width = tokens_ref.shape[1]
    wide = windows.shape[2]
    start = (3 * team // 2) * 128
    loads = []
    for part in range(3):
        at = pl.ds(pl.multiple_of(part * width + start, 128), wide)
        loads.append(pltpu.make_async_copy(w_ref.at[:, at], windows.at[part], weight_sems.at[part]))
    for part in range(2):
        at = pl.ds(part * width, 128)
        loads.append(
            pltpu.make_async_copy(w_ref.at[:, at], firsts.at[part], weight_sems.at[3 + part])
        )
    for load in loads:
        load.start()
    tokens = tokens_ref[...]
    row_mean = jnp.mean(tokens, axis=1, keepdims=True)
    centred = tokens - row_mean
    variance = jnp.mean(centred * centred, axis=1, keepdims=True)
    normed = centred * lax.rsqrt(variance + epsilon) * gain_ref[...] + bias_ref[...]
    held[team] = normed.astype(jnp.bfloat16)
    greet(["team", "lane"])

    def hop(side, distance, start=True):
        block = team - distance if side == 0 else team + distance
        target = me + lanes if side == 0 else me - lanes
        return push(
            held.at[block],
            held.at[block],
            hop_send.at[side, distance],
            hop_recv.at[side, distance],
            {"seq": target},
            start,
        )

    @pl.when(team < TEAMS - 1)
    def _():
        hop(0, 0)

    @pl.when(team > 0)
    def _():
        hop(1, 0)

    for load in loads:
        load.wait()
    odd = lax.rem(team, 2) == 1
    pieces = []
    for part in range(3):
        window = windows[part]
        pieces.append(
            jnp.where(odd, window[:, wide - TEAM_WIDTH :], window[:, :TEAM_WIDTH])
        )
        if part < 2:
            pieces.append(firsts[part][:, :HEAD_DIM])
    weight_ref[...] = jnp.concatenate(pieces, axis=1)

    def block_copies(block, start):
        copies = []
        for k in range(1, lanes):
            target = {"seq": team * lanes + lax.rem(lane + k, lanes)}
            copies.append(
                push(
                    ready.at[block],
                    query_ref.at[lane, block],
                    team_send.at[block, k],
                    team_recv.at[block, k],
                    target,
                    start,
                )
            )
        for n, (source, destination) in enumerate(
            ((ready.at[block], query_ref.at[lane, block]), (held.at[block], lane_ref.at[block]))
        ):
            copy = pltpu.make_async_copy(source, destination, local_sems.at[n, block])
            if start:
                copy.start()
            copies.append(copy)
        return copies

    def project(block):
        result = dot(held[block], weight_ref[...]).astype(jnp.bfloat16)
        ready[block] = result[:, :QUERY_WIDTH] * jnp.bfloat16(HEAD_DIM ** (-0.5))
        block_copies(block, True)
        key_ref[block] = result[:, QUERY_WIDTH : 2 * QUERY_WIDTH]
        value_ref[block] = result[:, 2 * QUERY_WIDTH :]

    project(team)

    def arrive(step, _):
        distance, side = step // 2 + 1, lax.rem(step, 2)
        for which in range(2):
            block = team - distance if which == 0 else team + distance
            there = (block >= 0) if which == 0 else (block < TEAMS)
            further = (team < TEAMS - 1) if which == 0 else (team > 0)

            @pl.when((side == which) & there)
            def _():
                hop(which, distance - 1, False).wait_recv()

                @pl.when(further)
                def _():
                    hop(which, distance)

                project(block)

        return 0

    lax.fori_loop(0, 2 * (TEAMS - 1), arrive, 0)
    for distance in range(TEAMS - 1):

        @pl.when((team < TEAMS - 1) & (team >= distance))
        def _():
            hop(0, distance, False).wait_send()

        @pl.when((team > 0) & (team + distance < TEAMS))
        def _():
            hop(1, distance, False).wait_send()

    for block in range(TEAMS):
        for copy in block_copies(block, False):
            copy.wait()


def project(tokens, gain, bias, weight, collective):
    lanes = lax.axis_size("seq") // TEAMS
    rows, width = tokens.shape
    inside = pl.BlockSpec(memory_space=pltpu.VMEM)
    anywhere = pl.BlockSpec(memory_space=pl.ANY)
    columns = 2 * QUERY_WIDTH + TEAM_WIDTH
    low = jnp.bfloat16
    dma = pltpu.SemaphoreType.DMA
    return pl.pallas_call(
        project_body,
        out_shape=[
            jax.ShapeDtypeStruct((TEAMS, rows, width), low),
            jax.ShapeDtypeStruct((width, columns), low),
            jax.ShapeDtypeStruct((lanes, TEAMS, rows, QUERY_WIDTH), low),
            jax.ShapeDtypeStruct((TEAMS, rows, QUERY_WIDTH), low),
            jax.ShapeDtypeStruct((TEAMS, rows, TEAM_WIDTH), low),
        ],
        in_specs=[inside, inside, inside, anywhere],
        out_specs=[anywhere, inside, anywhere, inside, inside],
        scratch_shapes=[
            pltpu.VMEM((TEAMS, rows, width), low),
            pltpu.VMEM((TEAMS, rows, QUERY_WIDTH), low),
            pltpu.VMEM((3, width, 256), low),
            pltpu.VMEM((2, width, 128), low),
            dma((2, TEAMS)),
            dma((2, TEAMS)),
            dma((TEAMS, lanes)),
            dma((TEAMS, lanes)),
            dma((5,)),
            dma((2, TEAMS)),
        ],
        compiler_params=pltpu.CompilerParams(
            collective_id=collective, has_side_effects=True, vmem_limit_bytes=VMEM_BYTES
        ),
    )(tokens, gain[None], bias[None], weight)


def fold(tile):
    return jnp.sum(tile.reshape(tile.shape[0] // 8, 8, tile.shape[1]), axis=0)


def attend_body(
    length_ref,
    threshold_ref,
    q_ref,
    kk_ref,
    vv_ref,
    out_ref,
    mass_ref,
    carried_ref,
    excess_ref,
    key_heads,
    value_rows,
    running,
    logits,
    out_all,
    mass_all,
    lane_out,
    lane_mass,
    joined_out,
    joined_mass,
    home_out,
    home_mass,
    lane_send,
    lane_recv,
    home_send,
    home_recv,
    *,
    blocks,
    rows,
):
    lanes = blocks // TEAMS
    me = lax.axis_index("seq")
    team, lane = me // lanes, lax.rem(me, lanes)
    i = pl.program_id(0)
    scale = select_scale / (blocks * rows)
    key_iota = lax.broadcasted_iota(jnp.int32, (rows, rows), 0)
    query_iota = lax.broadcasted_iota(jnp.int32, (rows, rows), 1)

    def part_copies(j, start):
        z, owner = j // lanes, lax.rem(j, lanes)
        return [
            push(
                source.at[j],
                destination.at[z, lane],
                lane_send.at[n, j],
                lane_recv.at[n, z, lane],
                {"seq": team * lanes + owner},
                start,
            )
            for n, (source, destination) in enumerate(
                ((out_all, lane_out), (mass_all, lane_mass))
            )
        ]

    def home_copies(z, start):
        return [
            push(
                source.at[z],
                destination.at[team],
                home_send.at[n, z],
                home_recv.at[n, team],
                {"seq": z * lanes + lane},
                start,
            )
            for n, (source, destination) in enumerate(
                ((joined_out, home_out), (joined_mass, home_mass))
            )
        ]

    def join(z):
        for k in range(1, lanes):
            other = lax.rem(lane + k, lanes)
            for n, buffer in enumerate((lane_out, lane_mass)):
                pltpu.make_async_copy(
                    buffer.at[z, other], buffer.at[z, other], lane_recv.at[n, z, other]
                ).wait()
        masses = [lane_mass[z, p] for p in range(lanes)]
        peak = masses[0]
        for p in range(1, lanes):
            peak = jnp.maximum(peak, masses[p])
        shares = [jnp.exp(mass - peak) for mass in masses]
        whole = shares[0]
        for p in range(1, lanes):
            whole = whole + shares[p]
        joined_mass[z] = peak + jnp.log(whole)
        inverse = 1.0 / whole
        for h in range(TEAM_HEADS):
            span = slice(h * HEAD_DIM, (h + 1) * HEAD_DIM)
            mixed = None
            for p in range(lanes):
                share = (shares[p] * inverse)[h : h + 1, :]
                part = lane_out[z, p, span, :].astype(jnp.float32) * share
                mixed = part if p == 0 else mixed + part
            joined_out[z, span, :] = mixed.astype(jnp.bfloat16)

        @pl.when(team != z)
        def _():
            home_copies(z, True)

        @pl.when(team == z)
        def _():
            home_out[team] = joined_out[z]
            home_mass[team] = joined_mass[z]

    @pl.when(i == 0)
    def _():
        greet(["team", "lane"])
        running[...] = jnp.zeros_like(running)
        excess_ref[...] = jnp.zeros_like(excess_ref)
        for z in range(TEAMS):
            for h in range(TEAM_HEADS):
                key_heads[h, z] = kk_ref[z, :, h * HEAD_DIM : (h + 1) * HEAD_DIM]
            first = kk_ref[z, :, TEAM_WIDTH:]
            if z == 0:
                slot = lax.broadcasted_iota(jnp.int32, first.shape, 0) + lane * rows
                first = jnp.where(slot >= 1, first, jnp.zeros_like(first))
            key_heads[TEAM_HEADS, z] = first
            value_rows[z] = vv_ref[z].T

    active = jnp.where(i >= lane, (i - lane) // lanes + 1, 0)
    threshold = threshold_ref[0]

    @pl.when(active == 0)
    def _():
        out_all[i] = jnp.zeros((TEAM_WIDTH, rows), jnp.bfloat16)
        mass_all[i] = jnp.full((8, rows), negative, jnp.float32)

    def work(count):
        q_rows = q_ref[0, 0].T
        heads = [q_rows[h * HEAD_DIM : (h + 1) * HEAD_DIM] for h in range(TEAM_HEADS + 1)]
        earlier = jnp.where(key_iota < query_iota, scale, 0.0).astype(jnp.bfloat16)
        every = jnp.full((rows, rows), scale, jnp.bfloat16)
        last = ((count - 1) * lanes + lane) * rows + key_iota
        query_pos = i * rows + query_iota
        peaks = [None] * TEAM_HEADS
        for z in range(count):
            first = jnp.maximum(dot(key_heads[TEAM_HEADS, z], heads[TEAM_HEADS]), 0.0)
            if z == count - 1:
                first = jnp.where(last < query_pos, first, 0.0)
            first = first.astype(jnp.bfloat16)
            carried = running[z] + dot(first, earlier)
            running[z] = running[z] + dot(first, every)

            if z == count - 1:
                carried = jnp.where(last <= query_pos, carried, -negative)
            carried_ref[0, z] = carried
            for h in range(TEAM_HEADS):
                logit = dot(key_heads[h, z], heads[h]) - carried
                logits[h, z] = logit
                peak = jnp.max(logit.reshape(rows // 8, 8, rows), axis=0)
                peaks[h] = peak if z == 0 else jnp.maximum(peaks[h], peak)
        mass_all[i] = jnp.zeros((8, rows), jnp.float32)
        for h in range(TEAM_HEADS):
            peak = jnp.max(peaks[h], axis=0, keepdims=True)
            mass, mixed = None, None
            for z in range(count):
                terms = jnp.exp(logits[h, z] - peak)
                part = fold(terms)
                values = value_rows[z, h * HEAD_DIM : (h + 1) * HEAD_DIM, :]
                product = dot(values, terms.astype(jnp.bfloat16))
                mass = part if z == 0 else mass + part
                mixed = product if z == 0 else mixed + product
            mass = jnp.sum(mass, axis=0, keepdims=True)
            out_all[i, h * HEAD_DIM : (h + 1) * HEAD_DIM, :] = (mixed * (1.0 / mass)).astype(
                jnp.bfloat16
            )
            mass_all[i, h : h + 1, :] = peak + jnp.log(mass)

        @pl.when(lax.rem(i, TEAMS) == team)
        def _():
            total = None
            for z in range(count):
                carried = carried_ref[0, z]
                if z == count - 1:
                    carried = jnp.where(last < query_pos, carried, 0.0)
                part = fold(jnp.clip(carried - threshold, 0.0, 1.0))
                total = part if z == 0 else total + part
            valid = i * rows + lax.broadcasted_iota(jnp.int32, (8, rows), 1) < length_ref[0]
            excess_ref[...] += jnp.where(valid, total, 0.0)

    for count in range(1, TEAMS + 1):
        pl.when(active == count)(functools.partial(work, count))

    @pl.when(lax.rem(i, lanes) != lane)
    def _():
        part_copies(i, True)

    @pl.when(lax.rem(i, lanes) == lane)
    def _():
        lane_out[i // lanes, lane] = out_all[i]
        lane_mass[i // lanes, lane] = mass_all[i]

    for z in range(TEAMS - 1):
        pl.when(i == (z + 1) * lanes + 1)(functools.partial(join, z))

    @pl.when(i == blocks - 1)
    def _():
        join(TEAMS - 1)

        def drain(j, _):
            @pl.when(lax.rem(j, lanes) != lane)
            def _():
                for copy in part_copies(j, False):
                    copy.wait_send()

            return 0

        lax.fori_loop(0, blocks, drain, 0)
        for z in range(TEAMS):

            @pl.when(team != z)
            def _():
                for copy in home_copies(z, False):
                    copy.wait_send()
                for n, buffer in enumerate((home_out, home_mass)):
                    pltpu.make_async_copy(
                        buffer.at[z], buffer.at[z], home_recv.at[n, z]
                    ).wait()

        out_ref[...] = home_out[...]
        mass_ref[...] = home_mass[...]

def attend(length, threshold, queries, keys, values, blocks, rows, collective):
    lanes = blocks // TEAMS
    smem = pl.BlockSpec(memory_space=pltpu.SMEM)
    whole = pl.BlockSpec((TEAMS, rows, QUERY_WIDTH), lambda i: (0, 0, 0))
    return pl.pallas_call(
        functools.partial(attend_body, blocks=blocks, rows=rows),
        grid=(blocks,),
        in_specs=[
            smem,
            smem,
            pl.BlockSpec(
                (1, 1, rows, QUERY_WIDTH), lambda i: (lax.rem(i, lanes), i // lanes, 0, 0)
            ),
            whole,
            pl.BlockSpec((TEAMS, rows, TEAM_WIDTH), lambda i: (0, 0, 0)),
        ],
        out_specs=[
            pl.BlockSpec((TEAMS, TEAM_WIDTH, rows), lambda i: (0, 0, 0)),
            pl.BlockSpec((TEAMS, 8, rows), lambda i: (0, 0, 0)),
            pl.BlockSpec((1, TEAMS, rows, rows), lambda i: (i, 0, 0, 0)),
            pl.BlockSpec((8, rows), lambda i: (0, 0)),
        ],
        out_shape=[
            jax.ShapeDtypeStruct((TEAMS, TEAM_WIDTH, rows), jnp.bfloat16),
            jax.ShapeDtypeStruct((TEAMS, 8, rows), jnp.float32),
            jax.ShapeDtypeStruct((blocks, TEAMS, rows, rows), jnp.float32),
            jax.ShapeDtypeStruct((8, rows), jnp.float32),
        ],
        scratch_shapes=[
            pltpu.VMEM((TEAM_HEADS + 1, TEAMS, rows, HEAD_DIM), jnp.bfloat16),
            pltpu.VMEM((TEAMS, TEAM_WIDTH, rows), jnp.bfloat16),
            pltpu.VMEM((TEAMS, rows, rows), jnp.float32),
            pltpu.VMEM((TEAM_HEADS, TEAMS, rows, rows), jnp.float32),
            pltpu.VMEM((blocks, TEAM_WIDTH, rows), jnp.bfloat16),
            pltpu.VMEM((blocks, 8, rows), jnp.float32),
            pltpu.VMEM((TEAMS, lanes, TEAM_WIDTH, rows), jnp.bfloat16),
            pltpu.VMEM((TEAMS, lanes, 8, rows), jnp.float32),
            pltpu.VMEM((TEAMS, TEAM_WIDTH, rows), jnp.bfloat16),
            pltpu.VMEM((TEAMS, 8, rows), jnp.float32),
            pltpu.VMEM((TEAMS, TEAM_WIDTH, rows), jnp.bfloat16),
            pltpu.VMEM((TEAMS, 8, rows), jnp.float32),
            pltpu.SemaphoreType.DMA((2, blocks)),
            pltpu.SemaphoreType.DMA((2, TEAMS, lanes)),
            pltpu.SemaphoreType.DMA((2, TEAMS)),
            pltpu.SemaphoreType.DMA((2, TEAMS)),
        ],
        compiler_params=pltpu.CompilerParams(
            collective_id=collective, has_side_effects=True, vmem_limit_bytes=VMEM_BYTES
        ),
    )(length, threshold, queries, keys, values)


reduce_plan = [("lane", "second"), ("team", "spread"), ("team", "spread")]


def added(parts):
    total = parts[0].astype(jnp.float32)
    for part in parts[1:]:
        total = total + part.astype(jnp.float32)
    return total.astype(jnp.bfloat16)


def attend_back_body(
    q_ref,
    grad_ref,
    stat_ref,
    carried_ref,
    kk_ref,
    vv_ref,
    *refs,
    blocks,
    rows,
):
    plan = reduce_plan
    sources, refs = refs[:3], refs[3:]
    (query_grad_ref, key_grad_ref, value_grad_ref), reduced, refs = refs[:3], refs[3:6], refs[6:]
    key_heads, key_rows, value_heads, running, key_sum, value_sum = refs[:6]
    grad_all, stat_all, grad_send, grad_recv, send, receive, local = refs[6:13]
    targets = refs[13:]
    lanes = blocks // TEAMS
    me = lax.axis_index("seq")
    team, lane = me // lanes, lax.rem(me, lanes)
    step = pl.program_id(0)
    i = blocks - 1 - step
    scale = select_scale / (blocks * rows)
    span = [slice(h * HEAD_DIM, (h + 1) * HEAD_DIM) for h in range(TEAM_HEADS + 1)]
    key_iota = lax.broadcasted_iota(jnp.int32, (rows, rows), 0)
    query_iota = lax.broadcasted_iota(jnp.int32, (rows, rows), 1)

    place, owner = i // lanes, lax.rem(i, lanes)

    def grad_copies(z, start):
        return [
            push(
                buffer.at[lane, z],
                buffer.at[lane, z],
                grad_send.at[n, z, k],
                grad_recv.at[n, z, lane],
                {"seq": team * lanes + lax.rem(lane + k, lanes)},
                start,
            )
            for k in range(1, lanes)
            for n, buffer in enumerate((grad_all, stat_all))
        ]

    def own_copy(n):
        scope, kind = plan[n]
        mine = peers_of(scope)[0]
        return pltpu.make_async_copy(
            part_of(kind, sources[n], mine), targets[n].at[mine], local.at[n]
        )

    def plan_copies(scope, start):
        chosen = [n for n in range(len(plan)) if plan[n][0] == scope]
        copies = []
        for n in chosen:
            copies += remote_copies(
                plan[n : n + 1],
                sources[n : n + 1],
                targets[n : n + 1],
                send.at[n : n + 1],
                receive.at[n : n + 1],
                start,
            )
        return copies

    @pl.when(step == 0)
    def _():
        greet(["team", "lane"])
        grad_all[lane] = grad_ref[...]
        stat_all[lane] = stat_ref[...]
        for z in reversed(range(TEAMS)):
            grad_copies(z, True)
        plan_copies("lane", True)
        for n in range(len(plan)):
            own_copy(n).start()
        running[...] = jnp.zeros_like(running)
        key_sum[...] = jnp.zeros_like(key_sum)
        value_sum[...] = jnp.zeros_like(value_sum)
        for z in range(TEAMS):
            for h in range(TEAM_HEADS + 1):
                key_heads[h, z] = kk_ref[z, :, span[h]]
            for h in range(TEAM_HEADS):
                value_heads[h, z] = vv_ref[z, :, span[h]]
            key_rows[z] = kk_ref[z].T
        first = kk_ref[0, :, span[TEAM_HEADS]]
        slot = lax.broadcasted_iota(jnp.int32, first.shape, 0) + lane * rows
        key_heads[TEAM_HEADS, 0] = jnp.where(slot >= 1, first, jnp.zeros_like(first))

    @pl.when(step == 2)
    def _():
        plan_copies("team", True)

    @pl.when(owner != lane)
    def _():
        for n, buffer in enumerate((grad_all, stat_all)):
            at = buffer.at[owner, place]
            pltpu.make_async_copy(at, at, grad_recv.at[n, place, owner]).wait()

    active = jnp.where(i >= lane, (i - lane) // lanes + 1, 0)

    @pl.when(active == 0)
    def _():
        query_grad_ref[...] = jnp.zeros_like(query_grad_ref)

    def work(count):
        q_rows = q_ref[0, 0].T
        grad_rows = grad_all[owner, place].T
        q_row = [q_rows[span[h]] for h in range(TEAM_HEADS + 1)]
        q_col = [q_ref[0, 0, :, span[h]] for h in range(TEAM_HEADS + 1)]
        grad_row = [grad_rows[span[h]] for h in range(TEAM_HEADS)]
        grad_col = [grad_all[owner, place, :, span[h]] for h in range(TEAM_HEADS)]
        mass = [stat_all[owner, place, h : h + 1, :] for h in range(TEAM_HEADS)]
        inner = [stat_all[owner, place, TEAM_HEADS + h : TEAM_HEADS + h + 1, :] for h in range(TEAM_HEADS)]
        later = jnp.where(key_iota > query_iota, -scale, 0.0).astype(jnp.bfloat16)
        every = jnp.full((rows, rows), -scale, jnp.bfloat16)
        last = ((count - 1) * lanes + lane) * rows + key_iota
        query_pos = i * rows + query_iota
        sums = [None] * (TEAM_HEADS + 1)
        for z in range(count):
            carried = carried_ref[0, z]
            total = None
            for h in range(TEAM_HEADS):
                probs = jnp.exp(dot(key_heads[h, z], q_row[h]) - carried - mass[h])
                value_sum[h, z] += dot(probs.astype(jnp.bfloat16), grad_col[h])
                grad_logit = probs * (dot(value_heads[h, z], grad_row[h]) - inner[h])
                total = grad_logit if h == 0 else total + grad_logit
                low = grad_logit.astype(jnp.bfloat16)
                key_sum[h, z] += dot(low, q_col[h])
                part = dot(key_rows[z, span[h], :], low)
                sums[h] = part if z == 0 else sums[h] + part
            total = total.astype(jnp.bfloat16)
            select_grad = running[z] + dot(total, later)
            running[z] = running[z] + dot(total, every)
            first = dot(key_heads[TEAM_HEADS, z], q_row[TEAM_HEADS])
            live = first > 0.0
            if z == count - 1:
                live = live & (last < query_pos)
            low = jnp.where(live, select_grad, 0.0).astype(jnp.bfloat16)
            key_sum[TEAM_HEADS, z] += dot(low, q_col[TEAM_HEADS])
            part = dot(key_rows[z, span[TEAM_HEADS], :], low)
            sums[TEAM_HEADS] = part if z == 0 else sums[TEAM_HEADS] + part
        for h in range(TEAM_HEADS + 1):
            query_grad_ref[0, 0, span[h], :] = sums[h].astype(jnp.bfloat16)

    for count in range(1, TEAMS + 1):
        pl.when(active == count)(functools.partial(work, count))

    @pl.when(step == blocks - 1)
    def _():
        for h in range(TEAM_HEADS + 1):
            key_grad_ref[:, :, span[h]] = key_sum[h].astype(jnp.bfloat16)
        for h in range(TEAM_HEADS):
            value_grad_ref[:, :, span[h]] = value_sum[h].astype(jnp.bfloat16)
        for z in range(TEAMS):
            for copy in grad_copies(z, False):
                copy.wait_send()
        for n in range(len(plan)):
            own_copy(n).wait()
        for scope in ("lane", "team"):
            for copy in plan_copies(scope, False):
                copy.wait()
        for n in range(len(plan)):
            for j in range(reduced[n].shape[0]):
                reduced[n][j] = added([targets[n][k, j] for k in range(targets[n].shape[0])])


def attend_back(queries, grads, stats, carried, keys, values, halves, blocks, rows, collective):
    lanes = blocks // TEAMS
    plan = reduce_plan
    shapes = exchange_shapes(plan, halves)

    def place(step):
        i = blocks - 1 - step
        return (lax.rem(i, lanes), i // lanes, 0, 0)

    return pl.pallas_call(
        functools.partial(attend_back_body, blocks=blocks, rows=rows),
        grid=(blocks,),
        in_specs=[
            pl.BlockSpec((1, 1, rows, QUERY_WIDTH), place),
            pl.BlockSpec((TEAMS, rows, TEAM_WIDTH), lambda step: (0, 0, 0)),
            pl.BlockSpec((TEAMS, 8, rows), lambda step: (0, 0, 0)),
            pl.BlockSpec((1, TEAMS, rows, rows), lambda step: (blocks - 1 - step, 0, 0, 0)),
            pl.BlockSpec((TEAMS, rows, QUERY_WIDTH), lambda step: (0, 0, 0)),
            pl.BlockSpec((TEAMS, rows, TEAM_WIDTH), lambda step: (0, 0, 0)),
        ]
        + [pl.BlockSpec(memory_space=pl.ANY)] * 3,
        out_specs=[
            pl.BlockSpec((1, 1, QUERY_WIDTH, rows), place),
            pl.BlockSpec((TEAMS, rows, QUERY_WIDTH), lambda step: (0, 0, 0)),
            pl.BlockSpec((TEAMS, rows, TEAM_WIDTH), lambda step: (0, 0, 0)),
        ]
        + [pl.BlockSpec(x.shape[1:], lambda step: (0, 0, 0)) for x in shapes],
        out_shape=[
            jax.ShapeDtypeStruct((lanes, TEAMS, QUERY_WIDTH, rows), jnp.bfloat16),
            jax.ShapeDtypeStruct((TEAMS, rows, QUERY_WIDTH), jnp.bfloat16),
            jax.ShapeDtypeStruct((TEAMS, rows, TEAM_WIDTH), jnp.bfloat16),
        ]
        + [jax.ShapeDtypeStruct(x.shape[1:], x.dtype) for x in shapes],
        scratch_shapes=[
            pltpu.VMEM((TEAM_HEADS + 1, TEAMS, rows, HEAD_DIM), jnp.bfloat16),
            pltpu.VMEM((TEAMS, QUERY_WIDTH, rows), jnp.bfloat16),
            pltpu.VMEM((TEAM_HEADS, TEAMS, rows, HEAD_DIM), jnp.bfloat16),
            pltpu.VMEM((TEAMS, rows, rows), jnp.float32),
            pltpu.VMEM((TEAM_HEADS + 1, TEAMS, rows, HEAD_DIM), jnp.float32),
            pltpu.VMEM((TEAM_HEADS, TEAMS, rows, HEAD_DIM), jnp.float32),
            pltpu.VMEM((lanes, TEAMS, rows, TEAM_WIDTH), jnp.bfloat16),
            pltpu.VMEM((lanes, TEAMS, 8, rows), jnp.float32),
            pltpu.SemaphoreType.DMA((2, TEAMS, lanes)),
            pltpu.SemaphoreType.DMA((2, TEAMS, lanes)),
        ]
        + exchange_sems(plan)
        + [pltpu.VMEM(x.shape, x.dtype) for x in shapes],
        compiler_params=pltpu.CompilerParams(
            collective_id=collective, has_side_effects=True, vmem_limit_bytes=VMEM_BYTES
        ),
    )(queries, grads, stats, carried, keys, values, *halves)


def finish_body(
    query_ref,
    key_ref,
    value_ref,
    lane_ref,
    weight_ref,
    gain_ref,
    bias_ref,
    base_ref,
    down_in,
    up_in,
    out_in,
    whole_ref,
    home_ref,
    total_ref,
    whole_down,
    whole_up,
    whole_out,
    query_parts,
    down_parts,
    up_parts,
    out_parts,
    down_ref,
    up_ref,
    out_ref,
    turned,
    weight_rows,
    weight_grad,
    rows_sum,
    rows_ref,
    main_ref,
    vector_ref,
    core_main,
    send_main,
    lane_main,
    team_send_main,
    team_main,
    assembled,
    vectors,
    ready,
    core_sems,
    lane_sems,
    team_sems,
    home_sems,
    vector_sems,
    out_lane_sems,
    out_core_sems,
    local_sems,
    early_team,
    early_lane,
    early_core,
    early_local,
    first_send,
    first_recv,
    first_local,
):
    lanes = lax.axis_size("seq") // TEAMS
    me = lax.axis_index("seq")
    core = lax.axis_index("batch")
    team, lane = me // lanes, lax.rem(me, lanes)

    def lane_peer(k):
        other = lax.rem(lane + k, lanes)
        return other, {"seq": team * lanes + other}

    def team_peer(k):
        other = lax.rem(team + k, TEAMS)
        return other, {"seq": other * lanes + lane}

    sibling = {"batch": 1 - core}
    greet(["core", "team", "lane"])
    first_sources = (query_ref, down_in, up_in, out_in)
    first_targets = (query_parts, down_parts, up_parts, out_parts)
    first_plan = [("team", "spread"), ("team", "spread"), ("lane", "spread"), ("lane", "spread")]
    first_copies = [[], []]
    for n in (1, 2, 3, 0):
        mine = peers_of(first_plan[n][0])[0]
        own = pltpu.make_async_copy(first_sources[n].at[mine], first_targets[n].at[mine], first_local.at[n])
        own.start()
        first_copies[n == 0].append(own)
        first_copies[n == 0] += remote_copies(
            first_plan[n : n + 1],
            first_sources[n : n + 1],
            first_targets[n : n + 1],
            first_send.at[n : n + 1],
            first_recv.at[n : n + 1],
        )
    spans = (slice(0, QUERY_WIDTH), slice(QUERY_WIDTH, 2 * QUERY_WIDTH), slice(2 * QUERY_WIDTH, None))
    for span in spans:
        weight_rows[span, :] = weight_ref[:, span].T
    weight_grad[...] = jnp.zeros_like(weight_grad)

    def known(b, _):
        rows_low = lane_ref[b].T
        turned[b] = rows_low
        total = None
        for span, grads in ((spans[1], key_ref[b]), (spans[2], value_ref[b])):
            weight_grad[:, span] += dot(rows_low, grads)
            part = dot(grads, weight_rows[span, :])
            total = part if total is None else total + part
        rows_sum[b] = total
        return 0

    lax.fori_loop(0, TEAMS, known, 0)
    for copy in first_copies[0]:
        copy.wait()
    down_ref[...] = added([down_parts[k] for k in range(lanes)])
    up_ref[...] = added([up_parts[k] for k in range(TEAMS)])
    out_ref[...] = added([out_parts[k] for k in range(TEAMS)])

    def place(n, p, t):
        if n == 0:
            return whole_down.at[core, p, t]
        ref = (None, whole_up, whole_out)[n]
        half = ref.shape[3] // 2
        return ref.at[p, t, :, pl.ds(pl.multiple_of(core * half, 128), half)]

    early = (down_ref, up_ref, out_ref)
    number = len(early)
    early_z = [[None] * TEAMS for _ in range(number)]
    for k in range(1, TEAMS):
        _, target = team_peer(k)
        for n in range(number):
            early_z[n][k] = push(
                early[n],
                place(n, lane, team),
                early_team.at[0, n, k],
                early_team.at[1, n, k],
                target,
            )
    early_kept = []
    for n in range(number):
        copy = pltpu.make_async_copy(early[n], place(n, lane, team), early_local.at[n])
        copy.start()
        early_kept.append(copy)
    early_out = []
    early_sib = []

    def forward(j):
        t = lax.rem(team - j + TEAMS, TEAMS)
        for n in range(number):
            if j == 0:
                source = early[n]
            else:
                early_z[n][j].wait_recv()
                source = place(n, lane, t)
            for k in range(1, lanes):
                _, target = lane_peer(k)
                early_out.append(
                    push(
                        source,
                        place(n, lane, t),
                        early_lane.at[0, n, j, k],
                        early_lane.at[1, n, j, k],
                        target,
                    )
                )
            early_sib.append(
                push(
                    source,
                    place(n, lane, t),
                    early_core.at[0, n, j, 0],
                    early_core.at[1, n, j, 0],
                    sibling,
                )
            )

    forward(0)
    for copy in first_copies[1]:
        copy.wait()
    gain = gain_ref[...]
    bias = bias_ref[...]

    def last(b, sums):
        query_rows = query_parts[0, b].astype(jnp.float32)
        for p in range(1, lanes):
            query_rows = query_rows + query_parts[p, b].astype(jnp.float32)
        grads = (query_rows * HEAD_DIM ** (-0.5)).astype(jnp.bfloat16).T
        weight_grad[:, spans[0]] += dot(turned[b], grads)
        total = rows_sum[b] + dot(grads, weight_rows[spans[0], :])
        rows_ref[b] = total.astype(jnp.bfloat16)
        shifted = lane_ref[b].astype(jnp.float32) - bias
        return (
            sums[0] + jnp.sum(total * shifted, axis=0, keepdims=True),
            sums[1] + jnp.sum(total, axis=0, keepdims=True),
        )

    nothing = jnp.zeros_like(gain)
    gain_sum, bias_sum = lax.fori_loop(0, TEAMS, last, (nothing, nothing))
    vector_ref[...] = base_ref[...]
    vector_ref[0:1, :] = gain_sum / gain
    vector_ref[1:2, :] = bias_sum
    depth = main_ref.shape[1]
    for chunk in range(2 * lanes):
        main_ref[chunk] = weight_grad[chunk * depth : (chunk + 1) * depth, :].astype(jnp.bfloat16)
    theirs = pl.ds((1 - core) * lanes, lanes)
    core_copies = [
        push(main_ref.at[theirs], core_main, core_sems.at[0, 0], core_sems.at[1, 0], sibling),
        push(vector_ref, vectors.at[0], vector_sems.at[0, 0], vector_sems.at[1, 0], sibling),
    ]
    for copy in core_copies:
        copy.wait()

    both = vector_ref[...] + vectors[0]
    vectors[1 + lane] = both
    ready[0] = both
    for j in range(lanes):
        send_main[j] = (
            main_ref[core * lanes + j].astype(jnp.float32) + core_main[j].astype(jnp.float32)
        ).astype(jnp.bfloat16)
    lane_copies = []
    for k in range(1, lanes):
        other, target = lane_peer(k)
        lane_copies += [
            push(send_main.at[other], lane_main.at[lane], lane_sems.at[0, 0, k], lane_sems.at[1, 0, k], target),
            push(ready.at[0], vectors.at[1 + lane], vector_sems.at[0, k], vector_sems.at[1, k], target),
        ]
    lane_main[lane] = send_main[lane]
    for copy in lane_copies:
        copy.wait()

    def total(ref, start, number):
        result = ref[start].astype(jnp.float32)
        for j in range(1, number):
            result = result + ref[start + j].astype(jnp.float32)
        return result

    whole_vector = total(vectors, 1, lanes)
    ready[1] = whole_vector
    vectors[1 + lanes + team] = whole_vector
    low_main = total(lane_main, 0, lanes).astype(jnp.bfloat16)
    team_send_main[...] = low_main
    team_main[team] = low_main
    team_copies = []
    for k in range(1, TEAMS):
        other, target = team_peer(k)
        at = lanes + k
        team_copies += [
            push(team_send_main, team_main.at[team], team_sems.at[0, 0, k], team_sems.at[1, 0, k], target),
            push(ready.at[1], vectors.at[1 + lanes + team], vector_sems.at[0, at], vector_sems.at[1, at], target),
        ]
    home_copies = []
    for k in range(1, TEAMS):
        other, target = team_peer(k)
        home_copies.append(
            push(rows_ref.at[other], home_ref.at[team], home_sems.at[0, k], home_sems.at[1, k], target)
        )
    own = pltpu.make_async_copy(rows_ref.at[team], home_ref.at[team], local_sems.at[0])
    own.start()
    for j in range(1, TEAMS):
        forward(j)
    for copy in team_copies:
        copy.wait()
    total_ref[...] = total(vectors, 1 + lanes, TEAMS)
    pieces = []
    for part in range(3):
        first = part * QUERY_WIDTH
        for g in range(TEAMS):
            piece = team_main[g, :, first : first + TEAM_WIDTH]
            if g == 0 and part < 2:
                more = piece[:, :HEAD_DIM].astype(jnp.float32)
                for other in range(TEAMS):
                    more = more + team_main[
                        other, :, first + TEAM_WIDTH : first + QUERY_WIDTH
                    ].astype(jnp.float32)
                pieces += [more.astype(jnp.bfloat16), piece[:, HEAD_DIM:]]
            else:
                pieces.append(piece)
    assembled[...] = jnp.concatenate(pieces, axis=1)

    mine = core * lanes + lane
    out_copies = []
    for k in range(1, lanes):
        _, target = lane_peer(k)
        out_copies.append(
            push(assembled, whole_ref.at[mine], out_lane_sems.at[0, k], out_lane_sems.at[1, k], target)
        )
    core_out = [
        push(assembled, whole_ref.at[mine], out_core_sems.at[0, 0], out_core_sems.at[1, 0], sibling)
    ]
    kept = pltpu.make_async_copy(assembled, whole_ref.at[mine], local_sems.at[1])
    kept.start()
    for j in range(TEAMS):
        for n in range(number):
            for k in range(1, lanes):
                early_out[(j * number + n) * (lanes - 1) + k - 1].wait_recv()
                p = lax.rem(lane - k + lanes, lanes)
                at = place(n, p, lax.rem(team - j + TEAMS, TEAMS))
                early_sib.append(
                    push(at, at, early_core.at[0, n, j, k], early_core.at[1, n, j, k], sibling)
                )
    for k in range(1, lanes):
        source = core * lanes + lax.rem(lane - k + lanes, lanes)
        out_copies[k - 1].wait_recv()
        core_out.append(
            push(
                whole_ref.at[source],
                whole_ref.at[source],
                out_core_sems.at[0, k],
                out_core_sems.at[1, k],
                sibling,
            )
        )
    for copy in out_copies + early_out:
        copy.wait_send()
    for n in range(number):
        for k in range(1, TEAMS):
            early_z[n][k].wait_send()
    for copy in core_out + home_copies + early_sib + early_kept:
        copy.wait()
    own.wait()
    kept.wait()


def finish(queries, keys, values, lane_rows, weight, gain, bias, base, reduced, collective):
    lanes = lax.axis_size("seq") // TEAMS
    width, columns = weight.shape
    rows = lane_rows.shape[1]
    chunks, depth = 2 * lanes, width // (2 * lanes)
    low = jnp.bfloat16
    dma = pltpu.SemaphoreType.DMA
    down, up, out = (x.shape[1:] for x in reduced)
    wholes = [
        (2, lanes, TEAMS) + down,
        (lanes, TEAMS, up[0], 2 * up[1]),
        (lanes, TEAMS, out[0], 2 * out[1]),
    ]
    anywhere = pl.BlockSpec(memory_space=pl.ANY)
    inside = pl.BlockSpec(memory_space=pltpu.VMEM)
    return pl.pallas_call(
        finish_body,
        out_shape=[
            jax.ShapeDtypeStruct((chunks, depth, 3 * width), low),
            jax.ShapeDtypeStruct(lane_rows.shape, low),
            jax.ShapeDtypeStruct(base.shape, jnp.float32),
        ]
        + [jax.ShapeDtypeStruct(shape, low) for shape in wholes],
        in_specs=[anywhere] + [inside] * 7 + [anywhere] * 3,
        out_specs=[anywhere, anywhere, inside] + [anywhere] * 3,
        scratch_shapes=[
            pltpu.VMEM(queries.shape, low),
            pltpu.VMEM((lanes,) + down, low),
            pltpu.VMEM((TEAMS,) + up, low),
            pltpu.VMEM((TEAMS,) + out, low),
            pltpu.VMEM(down, low),
            pltpu.VMEM(up, low),
            pltpu.VMEM(out, low),
            pltpu.VMEM((TEAMS, width, rows), low),
            pltpu.VMEM((columns, width), low),
            pltpu.VMEM((width, columns), jnp.float32),
            pltpu.VMEM((TEAMS, rows, width), jnp.float32),
            pltpu.VMEM((TEAMS, rows, width), low),
            pltpu.VMEM((chunks, depth, columns), low),
            pltpu.VMEM(base.shape, jnp.float32),
            pltpu.VMEM((lanes, depth, columns), low),
            pltpu.VMEM((lanes, depth, columns), low),
            pltpu.VMEM((lanes, depth, columns), low),
            pltpu.VMEM((depth, columns), low),
            pltpu.VMEM((TEAMS, depth, columns), low),
            pltpu.VMEM((depth, 3 * width), low),
            pltpu.VMEM((1 + lanes + TEAMS,) + base.shape, jnp.float32),
            pltpu.VMEM((2,) + base.shape, jnp.float32),
            dma((2, 2)),
            dma((2, 2, lanes)),
            dma((2, 2, TEAMS)),
            dma((2, TEAMS)),
            dma((2, lanes + TEAMS)),
            dma((2, lanes)),
            dma((2, lanes)),
            dma((2,)),
            dma((2, 3, TEAMS)),
            dma((2, 3, TEAMS, lanes)),
            dma((2, 3, TEAMS, lanes)),
            dma((3,)),
            dma((4, max(lanes, TEAMS))),
            dma((4, max(lanes, TEAMS))),
            dma((4,)),
        ],
        compiler_params=pltpu.CompilerParams(
            collective_id=collective, has_side_effects=True, vmem_limit_bytes=VMEM_BYTES
        ),
    )(queries, keys, values, lane_rows, weight, gain[None], bias[None], base, *reduced)


def contract_cols(left, right):
    return lax.dot_general(left, right, (((1,), (1,)), ((), ())), preferred_element_type=jnp.float32)


def dense_body(
    length_ref,
    mixed_ref,
    mass_ref,
    tokens_ref,
    grad_ref,
    gain_ref,
    bias_ref,
    w_out_hbm,
    w_up_hbm,
    w_down_hbm,
    layer_ref,
    resid_ref,
    norm_ref,
    cols_ref,
    stats_ref,
    down_hbm,
    up_hbm,
    out_hbm,
    w_out,
    w_up,
    w_down,
    active,
    slope,
    top,
    normed,
    mixed,
    slant,
    active_other,
    slope_other,
    top_other,
    normed_other,
    mixed_other,
    slant_other,
    total,
    back,
    cols,
    stats,
    down_half,
    up_half,
    out_half,
    load_sems,
    core_sems,
    lane_sems,
    keep_sems,
    store_sems,
):
    rows, width = tokens_ref.shape
    hidden = w_up.shape[1]
    step = width
    count = lax.axis_size("seq")
    lanes = count // TEAMS
    me = lax.axis_index("seq")
    core = lax.axis_index("batch")
    team, lane = me // lanes, lax.rem(me, lanes)
    sibling = {"batch": 1 - core}
    loads = [
        pltpu.make_async_copy(source, target, load_sems.at[n])
        for n, (source, target) in enumerate(
            ((w_out_hbm, w_out), (w_up_hbm, w_up), (w_down_hbm, w_down))
        )
    ]
    for load in loads:
        load.start()
    greet(["core", "lane"])

    def half_of(ref, which):
        half = ref.shape[1] // 2
        return ref.at[:, pl.ds(pl.multiple_of(which * half, 128), half)]

    pairs = (
        (active, active_other, True),
        (top, top_other, False),
        (normed, normed_other, False),
        (slope, slope_other, True),
        (mixed, mixed_other, False),
        (slant, slant_other, True),
    )

    def swap(n, start):
        source, target, halved = pairs[n]
        return push(
            half_of(source, 1 - core) if halved else source,
            target,
            core_sems.at[0, n],
            core_sems.at[1, n],
            sibling,
            start,
        )

    grad_top = grad_ref[...]
    top[...] = grad_top.astype(jnp.bfloat16)
    swap(1, True)
    valid = me * rows + lax.broadcasted_iota(jnp.int32, (rows, width), 0) < length_ref[0]
    mixed_rows = mixed_ref[...]
    mixed[...] = jnp.where(valid, mixed_rows.T, jnp.zeros((), jnp.bfloat16))
    swap(4, True)
    loads[0].wait()
    residual = tokens_ref[...] + dot(mixed[...], w_out[...])
    row_mean = jnp.mean(residual, axis=1, keepdims=True)
    centred = residual - row_mean
    variance = jnp.mean(centred * centred, axis=1, keepdims=True)
    spread = lax.rsqrt(variance + epsilon)
    scaled = centred * spread
    gain = gain_ref[...]
    normed[...] = (scaled * gain + bias_ref[...]).astype(jnp.bfloat16)
    swap(2, True)
    total[...] = residual
    back[...] = jnp.zeros_like(back)
    loads[1].wait()
    loads[2].wait()

    def chunk(c, _):
        at = pl.ds(pl.multiple_of(c * step, 128), step)
        up = w_up[:, at]
        down = w_down[at, :]
        u = dot(normed[...], up)
        squared = u * u
        bend = jnp.tanh(0.7978845608028654 * u * (1.0 + 0.044715 * squared))
        lift = 0.5 * (1.0 + bend)
        low = (u * lift).astype(jnp.bfloat16)
        active[:, at] = low
        turn = lift + (0.5 * 0.7978845608028654) * u * (1.0 - bend * bend) * (
            1.0 + (3.0 * 0.044715) * squared
        )
        grad_low = (contract_cols(top[...], down) * turn).astype(jnp.bfloat16)
        slope[:, at] = grad_low
        total[...] += dot(low, down)
        back[...] += contract_cols(grad_low, up)
        return 0

    lax.fori_loop(0, hidden // step, chunk, 0)
    swap(0, True)
    swap(3, True)
    layer_ref[...] = total[...]
    grad_normed = back[...]
    norm_ref[0:1, :] = jnp.sum(grad_normed * scaled, axis=0, keepdims=True)
    norm_ref[1:2, :] = jnp.sum(grad_normed, axis=0, keepdims=True)
    inner = grad_normed * gain
    resid = grad_top + spread * (
        inner
        - jnp.mean(inner, axis=1, keepdims=True)
        - scaled * jnp.mean(inner * scaled, axis=1, keepdims=True)
    )
    resid_ref[...] = resid
    slant[...] = resid.astype(jnp.bfloat16)
    swap(5, True)
    grad_mixed = contract_cols(slant[...], w_out[...]).astype(jnp.bfloat16)
    grad_mixed = jnp.where(valid, grad_mixed, jnp.zeros((), jnp.bfloat16))
    products = grad_mixed.T.astype(jnp.float32) * mixed_rows.astype(jnp.float32)
    for t in range(TEAMS):
        cols[t] = grad_mixed[:, t * TEAM_WIDTH : (t + 1) * TEAM_WIDTH]
        stats[t] = mass_ref[t]
        for h in range(TEAM_HEADS):
            first = t * TEAM_WIDTH + h * HEAD_DIM
            stats[t, TEAM_HEADS + h : TEAM_HEADS + h + 1, :] = jnp.sum(
                products[first : first + HEAD_DIM], axis=0, keepdims=True
            )
    copies = []
    for k in range(1, TEAMS):
        other = lax.rem(team + k, TEAMS)
        for n, (source, target) in enumerate(((cols, cols_ref), (stats, stats_ref))):
            copies.append(
                push(
                    source.at[other],
                    target.at[team],
                    lane_sems.at[0, n, k],
                    lane_sems.at[1, n, k],
                    {"seq": other * lanes + lane},
                )
            )
    for n, (source, target) in enumerate(((cols, cols_ref), (stats, stats_ref))):
        copy = pltpu.make_async_copy(source.at[team], target.at[team], keep_sems.at[n])
        copy.start()
        copies.append(copy)

    def pair_dot(left, left_other, right, right_other, at):
        return (
            dot(left[:, at].T, right[...]) + dot(left_other[:, at].T, right_other[...])
        ).astype(jnp.bfloat16)

    for n in range(len(pairs)):
        swap(n, False).wait()
    block = 384
    own_active = half_of(active, core)
    own_slope = half_of(slope, core)
    own_slant = half_of(slant, core)

    def down_rows(c, _):
        at = pl.ds(pl.multiple_of(c * block, 128), block)
        down_half[at, :] = pair_dot(own_active, active_other, top, top_other, at)
        return 0

    lax.fori_loop(0, down_half.shape[0] // block, down_rows, 0)
    stores = [pltpu.make_async_copy(down_half, down_hbm, store_sems.at[0])]
    stores[0].start()

    def up_rows(c, _):
        at = pl.ds(pl.multiple_of(c * block, 128), block)
        up_half[at, :] = pair_dot(normed, normed_other, own_slope, slope_other, at)
        out_half[at, :] = pair_dot(mixed, mixed_other, own_slant, slant_other, at)
        return 0

    lax.fori_loop(0, width // block, up_rows, 0)
    for n, (source, target) in enumerate(((up_half, up_hbm), (out_half, out_hbm))):
        copy = pltpu.make_async_copy(source, target, store_sems.at[1 + n])
        copy.start()
        stores.append(copy)
    for copy in copies + stores:
        copy.wait()


def dense(length, mixed, masses, tokens, grad, gain, bias, w_out, w_up, w_down, collective):
    rows, width = tokens.shape
    hidden = w_up.shape[1]
    low, full = jnp.bfloat16, jnp.float32
    inside = pl.BlockSpec(memory_space=pltpu.VMEM)
    anywhere = pl.BlockSpec(memory_space=pl.ANY)
    dma = pltpu.SemaphoreType.DMA
    half = hidden // 2
    return pl.pallas_call(
        dense_body,
        out_shape=[
            jax.ShapeDtypeStruct((rows, width), full),
            jax.ShapeDtypeStruct((rows, width), full),
            jax.ShapeDtypeStruct((2, width), full),
            jax.ShapeDtypeStruct((TEAMS, rows, TEAM_WIDTH), low),
            jax.ShapeDtypeStruct((TEAMS, 8, rows), full),
            jax.ShapeDtypeStruct((half, width), low),
            jax.ShapeDtypeStruct((width, half), low),
            jax.ShapeDtypeStruct((width, width // 2), low),
        ],
        in_specs=[pl.BlockSpec(memory_space=pltpu.SMEM)] + [inside] * 6 + [anywhere] * 3,
        out_specs=[inside] * 3 + [anywhere] * 5,
        scratch_shapes=[
            pltpu.VMEM((width, width), low),
            pltpu.VMEM((width, hidden), low),
            pltpu.VMEM((hidden, width), low),
            pltpu.VMEM((rows, hidden), low),
            pltpu.VMEM((rows, hidden), low),
            pltpu.VMEM((rows, width), low),
            pltpu.VMEM((rows, width), low),
            pltpu.VMEM((rows, width), low),
            pltpu.VMEM((rows, width), low),
            pltpu.VMEM((rows, half), low),
            pltpu.VMEM((rows, half), low),
            pltpu.VMEM((rows, width), low),
            pltpu.VMEM((rows, width), low),
            pltpu.VMEM((rows, width), low),
            pltpu.VMEM((rows, width // 2), low),
            pltpu.VMEM((rows, width), full),
            pltpu.VMEM((rows, width), full),
            pltpu.VMEM((TEAMS, rows, TEAM_WIDTH), low),
            pltpu.VMEM((TEAMS, 8, rows), full),
            pltpu.VMEM((half, width), low),
            pltpu.VMEM((width, half), low),
            pltpu.VMEM((width, width // 2), low),
            dma((3,)),
            dma((2, 6)),
            dma((2, 2, TEAMS)),
            dma((2,)),
            dma((3,)),
        ],
        compiler_params=pltpu.CompilerParams(
            collective_id=collective, has_side_effects=True, vmem_limit_bytes=VMEM_BYTES
        ),
    )(length, mixed, masses, tokens, grad, gain[None], bias[None], w_out, w_up, w_down)


def layer_norm(values, norm_gain, norm_bias):
    row_mean = jnp.mean(values, axis=-1, keepdims=True)
    centred = values - row_mean
    variance = jnp.mean(centred * centred, axis=-1, keepdims=True)
    return centred * lax.rsqrt(variance + epsilon) * norm_gain + norm_bias


def per_device(
    block_input,
    ln1_gain,
    ln1_bias,
    w_qkv,
    w_out,
    ln2_gain,
    ln2_bias,
    w_up,
    w_down,
    length_draw,
    threshold_index,
    grad_out,
):
    rows = block_input.shape[1]
    width = block_input.shape[2]
    blocks = lax.axis_size("seq")
    lanes = blocks // TEAMS
    group_len = blocks * rows
    me = lax.axis_index("seq")
    team = me // lanes
    length = group_len - rows + 1 + length_draw % rows
    threshold = threshold_index.astype(jnp.float32) / 128.0
    tokens = block_input[0]
    grad_top = grad_out[0]

    ln1_pull = jax.vjp(layer_norm, tokens, ln1_gain, ln1_bias)[1]
    lane_rows, team_weight, queries, keys, values = project(tokens, ln1_gain, ln1_bias, w_qkv, 0)

    head_out, masses, carried, excess = attend(
        length, threshold, queries, keys, values, blocks, rows, 1
    )
    layer_out, grad_resid, grad_ln2, grad_cols, stats, down_half, up_half, out_half = dense(
        length,
        head_out.reshape(width, rows),
        masses,
        tokens,
        grad_top,
        ln2_gain,
        ln2_bias,
        w_out,
        w_up,
        w_down,
        3,
    )
    halves = [x.reshape(lanes, TEAMS, -1, x.shape[1]) for x in (down_half, up_half, out_half)]
    query_grads, key_grads, value_grads, *halves = attend_back(
        queries, grad_cols, stats, carried, keys, values, halves, blocks, rows, 7
    )

    pairs = (length[0] - 1).astype(jnp.float32) * (length[0] - 2).astype(jnp.float32) / 2.0
    nothing = jnp.zeros((width,), jnp.float32)
    base = jnp.stack(
        [
            nothing,
            nothing,
            grad_ln2[0],
            grad_ln2[1],
            jnp.full((width,), jnp.sum(excess)),
            jnp.full((width,), pairs / blocks),
            nothing,
            nothing,
        ]
    )
    grad_w_qkv, home_rows, vectors, grad_w_down, grad_w_up, grad_w_out = finish(
        query_grads,
        key_grads,
        value_grads,
        lane_rows,
        team_weight,
        ln1_gain,
        ln1_bias,
        base,
        halves,
        6,
    )
    grad_w_down = grad_w_down.reshape(w_down.shape)
    grad_w_up = grad_w_up.reshape(w_up.shape)
    grad_w_out = grad_w_out.reshape(w_out.shape)
    grad_w_qkv = grad_w_qkv.reshape(width, 3 * width)
    grad_normed = jnp.sum(home_rows.astype(jnp.float32), axis=0)
    grad_x = grad_resid + ln1_pull(grad_normed)[0]
    pruned_share = (vectors[4, 0] / vectors[5, 0]).reshape(1)
    return (
        layer_out[None],
        grad_x[None],
        vectors[0],
        vectors[1],
        grad_w_qkv.astype(jnp.float32),
        grad_w_out.astype(jnp.float32),
        vectors[2],
        vectors[3],
        grad_w_up.astype(jnp.float32),
        grad_w_down.astype(jnp.float32),
        pruned_share,
    )


def solution(mesh):
    placed = (
        P("batch", "seq", None),
        P(),
        P(),
        P(),
        P(),
        P(),
        P(),
        P(),
        P(),
        P("batch"),
        P(),
        P("batch", "seq", None),
    )
    return jax.shard_map(
        per_device,
        mesh=mesh,
        in_specs=placed,
        out_specs=(
            P("batch", "seq", None),
            P("batch", "seq", None),
            P(),
            P(),
            P(),
            P(),
            P(),
            P(),
            P(),
            P(),
            P(),
        ),
        check_vma=False,
    )
```

```python
import functools

import jax
import jax.numpy as jnp
from jax import lax
from jax.experimental import pallas as pl
from jax.experimental.pallas import tpu as pltpu
from jax.sharding import PartitionSpec as P

HEADS = 12
HEAD_DIM = 64
TEAMS = 4
TEAM_HEADS = HEADS // TEAMS
TEAM_WIDTH = TEAM_HEADS * HEAD_DIM
QUERY_WIDTH = TEAM_WIDTH + HEAD_DIM

epsilon = 1e-05
negative = -1e30
select_scale = 3.0
VMEM_BYTES = 60 * 2**20
MESH = pl.DeviceIdType.MESH


def peers_of(scope):
    lanes = lax.axis_size("seq") // TEAMS
    me = lax.axis_index("seq")
    team, lane = me // lanes, lax.rem(me, lanes)
    if scope == "team":
        return lane, lanes, lambda k: {"seq": team * lanes + k}
    if scope == "lane":
        return team, TEAMS, lambda k: {"seq": k * lanes + lane}
    if scope == "core":
        return lax.axis_index("batch"), 2, lambda k: {"batch": k}
    return me, lanes * TEAMS, lambda k: {"seq": k}


def scope_size(scope):
    count = lax.axis_size("seq")
    return {"team": count // TEAMS, "lane": TEAMS, "core": 2, "all": count}[scope]


def greet(scopes):
    barrier = pltpu.get_barrier_semaphore()
    number = 0
    for scope in scopes:
        mine, peers, device_of = peers_of(scope)
        for k in range(1, peers):
            pl.semaphore_signal(
                barrier, inc=1, device_id=device_of(lax.rem(mine + k, peers)), device_id_type=MESH
            )
        number += peers - 1
    pl.semaphore_wait(barrier, number)


def push(source, destination, send, receive, target, start=True):
    copy = pltpu.make_async_remote_copy(
        src_ref=source,
        dst_ref=destination,
        send_sem=send,
        recv_sem=receive,
        device_id=target,
        device_id_type=MESH,
    )
    if start:
        copy.start()
    return copy


def part_of(kind, ref, k):
    if kind == "gather":
        return ref
    if kind == "spread":
        return ref.at[k]
    if kind == "second":
        return ref.at[:, k]
    half = ref.shape[1] // 2
    return ref.at[:, pl.ds(pl.multiple_of(k * half, 128), half)]


def remote_copies(plan, sources, targets, send, receive, start=True):
    copies = []
    for n, (scope, kind) in enumerate(plan):
        mine, peers, device_of = peers_of(scope)
        for k in range(1, peers):
            peer = lax.rem(mine + k, peers)
            copies.append(
                push(
                    part_of(kind, sources[n], peer),
                    targets[n].at[mine],
                    send.at[n, k],
                    receive.at[n, k],
                    device_of(peer),
                    start,
                )
            )
    return copies


def exchange_shapes(plan, arrays):
    shapes = []
    for (scope, kind), x in zip(plan, arrays):
        shape = x.shape
        if kind == "gather":
            shape = (scope_size(scope),) + shape
        if kind == "half":
            shape = (2, shape[0], shape[1] // 2)
        if kind == "second":
            shape = (shape[1], shape[0]) + shape[2:]
        shapes.append(jax.ShapeDtypeStruct(shape, x.dtype))
    return shapes


def exchange_sems(plan):
    number, most = len(plan), max(scope_size(scope) for scope, _ in plan)
    return [
        pltpu.SemaphoreType.DMA((number, most)),
        pltpu.SemaphoreType.DMA((number, most)),
        pltpu.SemaphoreType.DMA((number,)),
    ]


def scopes_of(plan):
    return [x for x in ("core", "team", "lane", "all") if x in [scope for scope, _ in plan]]


def exchange(plan, arrays, collective):
    number = len(arrays)
    shapes = exchange_shapes(plan, arrays)

    def body(*refs):
        sources, targets = refs[:number], refs[number : 2 * number]
        send, receive, local = refs[2 * number : 2 * number + 3]
        through = refs[2 * number + 3 :]
        greet(scopes_of(plan))
        copies = remote_copies(plan, sources, targets, send, receive)
        inward = []
        for n, (scope, kind) in enumerate(plan):
            mine = peers_of(scope)[0]
            copy = pltpu.make_async_copy(part_of(kind, sources[n], mine), through[n], local.at[n])
            copy.start()
            inward.append(copy)
        for n, (scope, kind) in enumerate(plan):
            mine = peers_of(scope)[0]
            inward[n].wait()
            copy = pltpu.make_async_copy(through[n], targets[n].at[mine], local.at[n])
            copy.start()
            copies.append(copy)
        for copy in copies:
            copy.wait()

    return pl.pallas_call(
        body,
        out_shape=shapes,
        in_specs=[pl.BlockSpec(memory_space=pl.ANY)] * number,
        out_specs=[pl.BlockSpec(memory_space=pl.ANY)] * number,
        scratch_shapes=exchange_sems(plan) + [pltpu.VMEM(x.shape[1:], x.dtype) for x in shapes],
        compiler_params=pltpu.CompilerParams(
            collective_id=collective, has_side_effects=True, vmem_limit_bytes=VMEM_BYTES
        ),
    )(*arrays)


def dot(left, right):
    return jnp.dot(left, right, preferred_element_type=jnp.float32)


def project_body(
    tokens_ref,
    gain_ref,
    bias_ref,
    w_ref,
    lane_ref,
    weight_ref,
    query_ref,
    key_ref,
    value_ref,
    held,
    ready,
    windows,
    firsts,
    hop_send,
    hop_recv,
    team_send,
    team_recv,
    weight_sems,
    local_sems,
):
    lanes = lax.axis_size("seq") // TEAMS
    me = lax.axis_index("seq")
    team, lane = me // lanes, lax.rem(me, lanes)
    width = tokens_ref.shape[1]
    wide = windows.shape[2]
    start = (3 * team // 2) * 128
    loads = []
    for part in range(3):
        at = pl.ds(pl.multiple_of(part * width + start, 128), wide)
        loads.append(pltpu.make_async_copy(w_ref.at[:, at], windows.at[part], weight_sems.at[part]))
    for part in range(2):
        at = pl.ds(part * width, 128)
        loads.append(
            pltpu.make_async_copy(w_ref.at[:, at], firsts.at[part], weight_sems.at[3 + part])
        )
    for load in loads:
        load.start()
    tokens = tokens_ref[...]
    row_mean = jnp.mean(tokens, axis=1, keepdims=True)
    centred = tokens - row_mean
    variance = jnp.mean(centred * centred, axis=1, keepdims=True)
    normed = (
        centred * lax.rsqrt(variance + epsilon) * gain_ref[...][None, :] + bias_ref[...][None, :]
    )
    held[team] = normed.astype(jnp.bfloat16)
    greet(["team", "lane"])

    def hop(side, distance, start=True):
        block = team - distance if side == 0 else team + distance
        target = me + lanes if side == 0 else me - lanes
        return push(
            held.at[block],
            held.at[block],
            hop_send.at[side, distance],
            hop_recv.at[side, distance],
            {"seq": target},
            start,
        )

    @pl.when(team < TEAMS - 1)
    def _():
        hop(0, 0)

    @pl.when(team > 0)
    def _():
        hop(1, 0)

    for load in loads:
        load.wait()
    odd = lax.rem(team, 2) == 1
    pieces = []
    for part in range(3):
        window = windows[part]
        pieces.append(
            jnp.where(odd, window[:, wide - TEAM_WIDTH :], window[:, :TEAM_WIDTH])
        )
        if part < 2:
            pieces.append(firsts[part][:, :HEAD_DIM])
    weight_ref[...] = jnp.concatenate(pieces, axis=1)

    def block_copies(block, start):
        copies = []
        for k in range(1, lanes):
            target = {"seq": team * lanes + lax.rem(lane + k, lanes)}
            copies.append(
                push(
                    ready.at[block],
                    query_ref.at[lane, block],
                    team_send.at[block, k],
                    team_recv.at[block, k],
                    target,
                    start,
                )
            )
        for n, (source, destination) in enumerate(
            ((ready.at[block], query_ref.at[lane, block]), (held.at[block], lane_ref.at[block]))
        ):
            copy = pltpu.make_async_copy(source, destination, local_sems.at[n, block])
            if start:
                copy.start()
            copies.append(copy)
        return copies

    def project(block):
        result = dot(held[block], weight_ref[...]).astype(jnp.bfloat16)
        ready[block] = result[:, :QUERY_WIDTH] * jnp.bfloat16(HEAD_DIM ** (-0.5))
        block_copies(block, True)
        key_ref[block] = result[:, QUERY_WIDTH : 2 * QUERY_WIDTH]
        value_ref[block] = result[:, 2 * QUERY_WIDTH :]

    project(team)

    def arrive(step, _):
        distance, side = step // 2 + 1, lax.rem(step, 2)
        for which in range(2):
            block = team - distance if which == 0 else team + distance
            there = (block >= 0) if which == 0 else (block < TEAMS)
            further = (team < TEAMS - 1) if which == 0 else (team > 0)

            @pl.when((side == which) & there)
            def _():
                hop(which, distance - 1, False).wait_recv()

                @pl.when(further)
                def _():
                    hop(which, distance)

                project(block)

        return 0

    lax.fori_loop(0, 2 * (TEAMS - 1), arrive, 0)
    for distance in range(TEAMS - 1):

        @pl.when((team < TEAMS - 1) & (team >= distance))
        def _():
            hop(0, distance, False).wait_send()

        @pl.when((team > 0) & (team + distance < TEAMS))
        def _():
            hop(1, distance, False).wait_send()

    for block in range(TEAMS):
        for copy in block_copies(block, False):
            copy.wait()


def project(tokens, gain, bias, weight, collective):
    lanes = lax.axis_size("seq") // TEAMS
    rows, width = tokens.shape
    inside = pl.BlockSpec(memory_space=pltpu.VMEM)
    anywhere = pl.BlockSpec(memory_space=pl.ANY)
    columns = 2 * QUERY_WIDTH + TEAM_WIDTH
    low = jnp.bfloat16
    dma = pltpu.SemaphoreType.DMA
    return pl.pallas_call(
        project_body,
        out_shape=[
            jax.ShapeDtypeStruct((TEAMS, rows, width), low),
            jax.ShapeDtypeStruct((width, columns), low),
            jax.ShapeDtypeStruct((lanes, TEAMS, rows, QUERY_WIDTH), low),
            jax.ShapeDtypeStruct((TEAMS, rows, QUERY_WIDTH), low),
            jax.ShapeDtypeStruct((TEAMS, rows, TEAM_WIDTH), low),
        ],
        in_specs=[inside, inside, inside, anywhere],
        out_specs=[anywhere, inside, anywhere, inside, inside],
        scratch_shapes=[
            pltpu.VMEM((TEAMS, rows, width), low),
            pltpu.VMEM((TEAMS, rows, QUERY_WIDTH), low),
            pltpu.VMEM((3, width, 256), low),
            pltpu.VMEM((2, width, 128), low),
            dma((2, TEAMS)),
            dma((2, TEAMS)),
            dma((TEAMS, lanes)),
            dma((TEAMS, lanes)),
            dma((5,)),
            dma((2, TEAMS)),
        ],
        compiler_params=pltpu.CompilerParams(
            collective_id=collective, has_side_effects=True, vmem_limit_bytes=VMEM_BYTES
        ),
    )(tokens, gain, bias, weight)


def fold(tile):
    return jnp.sum(tile.reshape(tile.shape[0] // 8, 8, tile.shape[1]), axis=0)


def attend_body(
    length_ref,
    threshold_ref,
    q_ref,
    kk_ref,
    vv_ref,
    out_ref,
    mass_ref,
    carried_ref,
    excess_ref,
    key_heads,
    value_rows,
    running,
    logits,
    out_all,
    mass_all,
    lane_out,
    lane_mass,
    joined_out,
    joined_mass,
    home_out,
    home_mass,
    lane_send,
    lane_recv,
    home_send,
    home_recv,
    *,
    blocks,
    rows,
):
    lanes = blocks // TEAMS
    me = lax.axis_index("seq")
    team, lane = me // lanes, lax.rem(me, lanes)
    i = pl.program_id(0)
    scale = select_scale / (blocks * rows)
    key_iota = lax.broadcasted_iota(jnp.int32, (rows, rows), 0)
    query_iota = lax.broadcasted_iota(jnp.int32, (rows, rows), 1)

    def part_copies(j, start):
        z, owner = j // lanes, lax.rem(j, lanes)
        return [
            push(
                source.at[j],
                destination.at[z, lane],
                lane_send.at[n, j],
                lane_recv.at[n, z, lane],
                {"seq": team * lanes + owner},
                start,
            )
            for n, (source, destination) in enumerate(
                ((out_all, lane_out), (mass_all, lane_mass))
            )
        ]

    def home_copies(z, start):
        return [
            push(
                source.at[z],
                destination.at[team],
                home_send.at[n, z],
                home_recv.at[n, team],
                {"seq": z * lanes + lane},
                start,
            )
            for n, (source, destination) in enumerate(
                ((joined_out, home_out), (joined_mass, home_mass))
            )
        ]

    def join(z):
        for k in range(1, lanes):
            other = lax.rem(lane + k, lanes)
            for n, buffer in enumerate((lane_out, lane_mass)):
                pltpu.make_async_copy(
                    buffer.at[z, other], buffer.at[z, other], lane_recv.at[n, z, other]
                ).wait()
        masses = [lane_mass[z, p] for p in range(lanes)]
        peak = masses[0]
        for p in range(1, lanes):
            peak = jnp.maximum(peak, masses[p])
        shares = [jnp.exp(mass - peak) for mass in masses]
        whole = shares[0]
        for p in range(1, lanes):
            whole = whole + shares[p]
        joined_mass[z] = peak + jnp.log(whole)
        inverse = 1.0 / whole
        for h in range(TEAM_HEADS):
            span = slice(h * HEAD_DIM, (h + 1) * HEAD_DIM)
            mixed = None
            for p in range(lanes):
                share = (shares[p] * inverse)[h : h + 1, :]
                part = lane_out[z, p, span, :].astype(jnp.float32) * share
                mixed = part if p == 0 else mixed + part
            joined_out[z, span, :] = mixed.astype(jnp.bfloat16)

        @pl.when(team != z)
        def _():
            home_copies(z, True)

        @pl.when(team == z)
        def _():
            home_out[team] = joined_out[z]
            home_mass[team] = joined_mass[z]

    @pl.when(i == 0)
    def _():
        greet(["team", "lane"])
        running[...] = jnp.zeros_like(running)
        excess_ref[...] = jnp.zeros_like(excess_ref)
        for z in range(TEAMS):
            for h in range(TEAM_HEADS):
                key_heads[h, z] = kk_ref[z, :, h * HEAD_DIM : (h + 1) * HEAD_DIM]
            first = kk_ref[z, :, TEAM_WIDTH:]
            if z == 0:
                slot = lax.broadcasted_iota(jnp.int32, first.shape, 0) + lane * rows
                first = jnp.where(slot >= 1, first, jnp.zeros_like(first))
            key_heads[TEAM_HEADS, z] = first
            value_rows[z] = vv_ref[z].T

    active = jnp.where(i >= lane, (i - lane) // lanes + 1, 0)
    threshold = threshold_ref[0]

    @pl.when(active == 0)
    def _():
        out_all[i] = jnp.zeros((TEAM_WIDTH, rows), jnp.bfloat16)
        mass_all[i] = jnp.full((8, rows), negative, jnp.float32)

    def work(count):
        q_rows = q_ref[0, 0].T
        heads = [q_rows[h * HEAD_DIM : (h + 1) * HEAD_DIM] for h in range(TEAM_HEADS + 1)]
        earlier = jnp.where(key_iota < query_iota, scale, 0.0).astype(jnp.bfloat16)
        every = jnp.full((rows, rows), scale, jnp.bfloat16)
        last = ((count - 1) * lanes + lane) * rows + key_iota
        query_pos = i * rows + query_iota
        peaks = [None] * TEAM_HEADS
        for z in range(count):
            first = jnp.maximum(dot(key_heads[TEAM_HEADS, z], heads[TEAM_HEADS]), 0.0)
            if z == count - 1:
                first = jnp.where(last < query_pos, first, 0.0)
            first = first.astype(jnp.bfloat16)
            carried = running[z] + dot(first, earlier)
            running[z] = running[z] + dot(first, every)

            if z == count - 1:
                carried = jnp.where(last <= query_pos, carried, -negative)
            carried_ref[0, z] = carried
            for h in range(TEAM_HEADS):
                logit = dot(key_heads[h, z], heads[h]) - carried
                logits[h, z] = logit
                peak = jnp.max(logit.reshape(rows // 8, 8, rows), axis=0)
                peaks[h] = peak if z == 0 else jnp.maximum(peaks[h], peak)
        mass_all[i] = jnp.zeros((8, rows), jnp.float32)
        for h in range(TEAM_HEADS):
            peak = jnp.max(peaks[h], axis=0, keepdims=True)
            mass, mixed = None, None
            for z in range(count):
                terms = jnp.exp(logits[h, z] - peak)
                part = fold(terms)
                values = value_rows[z, h * HEAD_DIM : (h + 1) * HEAD_DIM, :]
                product = dot(values, terms.astype(jnp.bfloat16))
                mass = part if z == 0 else mass + part
                mixed = product if z == 0 else mixed + product
            mass = jnp.sum(mass, axis=0, keepdims=True)
            out_all[i, h * HEAD_DIM : (h + 1) * HEAD_DIM, :] = (mixed * (1.0 / mass)).astype(
                jnp.bfloat16
            )
            mass_all[i, h : h + 1, :] = peak + jnp.log(mass)

        @pl.when(lax.rem(i, TEAMS) == team)
        def _():
            total = None
            for z in range(count):
                carried = carried_ref[0, z]
                if z == count - 1:
                    carried = jnp.where(last < query_pos, carried, 0.0)
                part = fold(jnp.clip(carried - threshold, 0.0, 1.0))
                total = part if z == 0 else total + part
            valid = i * rows + lax.broadcasted_iota(jnp.int32, (8, rows), 1) < length_ref[0]
            excess_ref[...] += jnp.where(valid, total, 0.0)

    for count in range(1, TEAMS + 1):
        pl.when(active == count)(functools.partial(work, count))

    @pl.when(lax.rem(i, lanes) != lane)
    def _():
        part_copies(i, True)

    @pl.when(lax.rem(i, lanes) == lane)
    def _():
        lane_out[i // lanes, lane] = out_all[i]
        lane_mass[i // lanes, lane] = mass_all[i]

    for z in range(TEAMS - 1):
        pl.when(i == (z + 1) * lanes + 1)(functools.partial(join, z))

    @pl.when(i == blocks - 1)
    def _():
        join(TEAMS - 1)

        def drain(j, _):
            @pl.when(lax.rem(j, lanes) != lane)
            def _():
                for copy in part_copies(j, False):
                    copy.wait_send()

            return 0

        lax.fori_loop(0, blocks, drain, 0)
        for z in range(TEAMS):

            @pl.when(team != z)
            def _():
                for copy in home_copies(z, False):
                    copy.wait_send()
                for n, buffer in enumerate((home_out, home_mass)):
                    pltpu.make_async_copy(
                        buffer.at[z], buffer.at[z], home_recv.at[n, z]
                    ).wait()

        out_ref[...] = home_out[...]
        mass_ref[...] = home_mass[...]

def attend(length, threshold, queries, keys, values, blocks, rows, collective):
    lanes = blocks // TEAMS
    smem = pl.BlockSpec(memory_space=pltpu.SMEM)
    whole = pl.BlockSpec((TEAMS, rows, QUERY_WIDTH), lambda i: (0, 0, 0))
    return pl.pallas_call(
        functools.partial(attend_body, blocks=blocks, rows=rows),
        grid=(blocks,),
        in_specs=[
            smem,
            smem,
            pl.BlockSpec(
                (1, 1, rows, QUERY_WIDTH), lambda i: (lax.rem(i, lanes), i // lanes, 0, 0)
            ),
            whole,
            pl.BlockSpec((TEAMS, rows, TEAM_WIDTH), lambda i: (0, 0, 0)),
        ],
        out_specs=[
            pl.BlockSpec((TEAMS, TEAM_WIDTH, rows), lambda i: (0, 0, 0)),
            pl.BlockSpec((TEAMS, 8, rows), lambda i: (0, 0, 0)),
            pl.BlockSpec((1, TEAMS, rows, rows), lambda i: (i, 0, 0, 0)),
            pl.BlockSpec((8, rows), lambda i: (0, 0)),
        ],
        out_shape=[
            jax.ShapeDtypeStruct((TEAMS, TEAM_WIDTH, rows), jnp.bfloat16),
            jax.ShapeDtypeStruct((TEAMS, 8, rows), jnp.float32),
            jax.ShapeDtypeStruct((blocks, TEAMS, rows, rows), jnp.float32),
            jax.ShapeDtypeStruct((8, rows), jnp.float32),
        ],
        scratch_shapes=[
            pltpu.VMEM((TEAM_HEADS + 1, TEAMS, rows, HEAD_DIM), jnp.bfloat16),
            pltpu.VMEM((TEAMS, TEAM_WIDTH, rows), jnp.bfloat16),
            pltpu.VMEM((TEAMS, rows, rows), jnp.float32),
            pltpu.VMEM((TEAM_HEADS, TEAMS, rows, rows), jnp.float32),
            pltpu.VMEM((blocks, TEAM_WIDTH, rows), jnp.bfloat16),
            pltpu.VMEM((blocks, 8, rows), jnp.float32),
            pltpu.VMEM((TEAMS, lanes, TEAM_WIDTH, rows), jnp.bfloat16),
            pltpu.VMEM((TEAMS, lanes, 8, rows), jnp.float32),
            pltpu.VMEM((TEAMS, TEAM_WIDTH, rows), jnp.bfloat16),
            pltpu.VMEM((TEAMS, 8, rows), jnp.float32),
            pltpu.VMEM((TEAMS, TEAM_WIDTH, rows), jnp.bfloat16),
            pltpu.VMEM((TEAMS, 8, rows), jnp.float32),
            pltpu.SemaphoreType.DMA((2, blocks)),
            pltpu.SemaphoreType.DMA((2, TEAMS, lanes)),
            pltpu.SemaphoreType.DMA((2, TEAMS)),
            pltpu.SemaphoreType.DMA((2, TEAMS)),
        ],
        compiler_params=pltpu.CompilerParams(
            collective_id=collective, has_side_effects=True, vmem_limit_bytes=VMEM_BYTES
        ),
    )(length, threshold, queries, keys, values)


reduce_plan = [("lane", "second"), ("team", "spread"), ("team", "spread")]


def added(parts):
    total = parts[0].astype(jnp.float32)
    for part in parts[1:]:
        total = total + part.astype(jnp.float32)
    return total.astype(jnp.bfloat16)


def attend_back_body(
    q_ref,
    grad_ref,
    stat_ref,
    carried_ref,
    kk_ref,
    vv_ref,
    *refs,
    blocks,
    rows,
):
    plan = reduce_plan
    sources, refs = refs[:3], refs[3:]
    (query_grad_ref, key_grad_ref, value_grad_ref), reduced, refs = refs[:3], refs[3:6], refs[6:]
    key_heads, key_rows, value_heads, running, key_sum, value_sum = refs[:6]
    grad_all, stat_all, grad_send, grad_recv, send, receive, local = refs[6:13]
    targets = refs[13:]
    lanes = blocks // TEAMS
    me = lax.axis_index("seq")
    team, lane = me // lanes, lax.rem(me, lanes)
    step = pl.program_id(0)
    i = blocks - 1 - step
    scale = select_scale / (blocks * rows)
    span = [slice(h * HEAD_DIM, (h + 1) * HEAD_DIM) for h in range(TEAM_HEADS + 1)]
    key_iota = lax.broadcasted_iota(jnp.int32, (rows, rows), 0)
    query_iota = lax.broadcasted_iota(jnp.int32, (rows, rows), 1)

    place, owner = i // lanes, lax.rem(i, lanes)

    def grad_copies(z, start):
        return [
            push(
                buffer.at[lane, z],
                buffer.at[lane, z],
                grad_send.at[n, z, k],
                grad_recv.at[n, z, lane],
                {"seq": team * lanes + lax.rem(lane + k, lanes)},
                start,
            )
            for k in range(1, lanes)
            for n, buffer in enumerate((grad_all, stat_all))
        ]

    def own_copy(n):
        scope, kind = plan[n]
        mine = peers_of(scope)[0]
        return pltpu.make_async_copy(
            part_of(kind, sources[n], mine), targets[n].at[mine], local.at[n]
        )

    def plan_copies(scope, start):
        chosen = [n for n in range(len(plan)) if plan[n][0] == scope]
        copies = []
        for n in chosen:
            copies += remote_copies(
                plan[n : n + 1],
                sources[n : n + 1],
                targets[n : n + 1],
                send.at[n : n + 1],
                receive.at[n : n + 1],
                start,
            )
        return copies

    @pl.when(step == 0)
    def _():
        greet(["team", "lane"])
        grad_all[lane] = grad_ref[...]
        stat_all[lane] = stat_ref[...]
        for z in reversed(range(TEAMS)):
            grad_copies(z, True)
        plan_copies("lane", True)
        for n in range(len(plan)):
            own_copy(n).start()
        running[...] = jnp.zeros_like(running)
        key_sum[...] = jnp.zeros_like(key_sum)
        value_sum[...] = jnp.zeros_like(value_sum)
        for z in range(TEAMS):
            for h in range(TEAM_HEADS + 1):
                key_heads[h, z] = kk_ref[z, :, span[h]]
            for h in range(TEAM_HEADS):
                value_heads[h, z] = vv_ref[z, :, span[h]]
            key_rows[z] = kk_ref[z].T
        first = kk_ref[0, :, span[TEAM_HEADS]]
        slot = lax.broadcasted_iota(jnp.int32, first.shape, 0) + lane * rows
        key_heads[TEAM_HEADS, 0] = jnp.where(slot >= 1, first, jnp.zeros_like(first))

    @pl.when(step == 2)
    def _():
        plan_copies("team", True)

    @pl.when(owner != lane)
    def _():
        for n, buffer in enumerate((grad_all, stat_all)):
            at = buffer.at[owner, place]
            pltpu.make_async_copy(at, at, grad_recv.at[n, place, owner]).wait()

    active = jnp.where(i >= lane, (i - lane) // lanes + 1, 0)

    @pl.when(active == 0)
    def _():
        query_grad_ref[...] = jnp.zeros_like(query_grad_ref)

    def work(count):
        q_rows = q_ref[0, 0].T
        grad_rows = grad_all[owner, place].T
        q_row = [q_rows[span[h]] for h in range(TEAM_HEADS + 1)]
        q_col = [q_ref[0, 0, :, span[h]] for h in range(TEAM_HEADS + 1)]
        grad_row = [grad_rows[span[h]] for h in range(TEAM_HEADS)]
        grad_col = [grad_all[owner, place, :, span[h]] for h in range(TEAM_HEADS)]
        mass = [stat_all[owner, place, h : h + 1, :] for h in range(TEAM_HEADS)]
        inner = [stat_all[owner, place, TEAM_HEADS + h : TEAM_HEADS + h + 1, :] for h in range(TEAM_HEADS)]
        later = jnp.where(key_iota > query_iota, -scale, 0.0).astype(jnp.bfloat16)
        every = jnp.full((rows, rows), -scale, jnp.bfloat16)
        last = ((count - 1) * lanes + lane) * rows + key_iota
        query_pos = i * rows + query_iota
        sums = [None] * (TEAM_HEADS + 1)
        for z in range(count):
            carried = carried_ref[0, z]
            total = None
            for h in range(TEAM_HEADS):
                probs = jnp.exp(dot(key_heads[h, z], q_row[h]) - carried - mass[h])
                value_sum[h, z] += dot(probs.astype(jnp.bfloat16), grad_col[h])
                grad_logit = probs * (dot(value_heads[h, z], grad_row[h]) - inner[h])
                total = grad_logit if h == 0 else total + grad_logit
                low = grad_logit.astype(jnp.bfloat16)
                key_sum[h, z] += dot(low, q_col[h])
                part = dot(key_rows[z, span[h], :], low)
                sums[h] = part if z == 0 else sums[h] + part
            total = total.astype(jnp.bfloat16)
            select_grad = running[z] + dot(total, later)
            running[z] = running[z] + dot(total, every)
            first = dot(key_heads[TEAM_HEADS, z], q_row[TEAM_HEADS])
            live = first > 0.0
            if z == count - 1:
                live = live & (last < query_pos)
            low = jnp.where(live, select_grad, 0.0).astype(jnp.bfloat16)
            key_sum[TEAM_HEADS, z] += dot(low, q_col[TEAM_HEADS])
            part = dot(key_rows[z, span[TEAM_HEADS], :], low)
            sums[TEAM_HEADS] = part if z == 0 else sums[TEAM_HEADS] + part
        for h in range(TEAM_HEADS + 1):
            query_grad_ref[0, 0, span[h], :] = sums[h].astype(jnp.bfloat16)

    for count in range(1, TEAMS + 1):
        pl.when(active == count)(functools.partial(work, count))

    @pl.when(step == blocks - 1)
    def _():
        for h in range(TEAM_HEADS + 1):
            key_grad_ref[:, :, span[h]] = key_sum[h].astype(jnp.bfloat16)
        for h in range(TEAM_HEADS):
            value_grad_ref[:, :, span[h]] = value_sum[h].astype(jnp.bfloat16)
        for z in range(TEAMS):
            for copy in grad_copies(z, False):
                copy.wait_send()
        for n in range(len(plan)):
            own_copy(n).wait()
        for scope in ("lane", "team"):
            for copy in plan_copies(scope, False):
                copy.wait()
        for n in range(len(plan)):
            for j in range(reduced[n].shape[0]):
                reduced[n][j] = added([targets[n][k, j] for k in range(targets[n].shape[0])])


def attend_back(queries, grads, stats, carried, keys, values, halves, blocks, rows, collective):
    lanes = blocks // TEAMS
    plan = reduce_plan
    shapes = exchange_shapes(plan, halves)

    def place(step):
        i = blocks - 1 - step
        return (lax.rem(i, lanes), i // lanes, 0, 0)

    return pl.pallas_call(
        functools.partial(attend_back_body, blocks=blocks, rows=rows),
        grid=(blocks,),
        in_specs=[
            pl.BlockSpec((1, 1, rows, QUERY_WIDTH), place),
            pl.BlockSpec((TEAMS, rows, TEAM_WIDTH), lambda step: (0, 0, 0)),
            pl.BlockSpec((TEAMS, 8, rows), lambda step: (0, 0, 0)),
            pl.BlockSpec((1, TEAMS, rows, rows), lambda step: (blocks - 1 - step, 0, 0, 0)),
            pl.BlockSpec((TEAMS, rows, QUERY_WIDTH), lambda step: (0, 0, 0)),
            pl.BlockSpec((TEAMS, rows, TEAM_WIDTH), lambda step: (0, 0, 0)),
        ]
        + [pl.BlockSpec(memory_space=pl.ANY)] * 3,
        out_specs=[
            pl.BlockSpec((1, 1, QUERY_WIDTH, rows), place),
            pl.BlockSpec((TEAMS, rows, QUERY_WIDTH), lambda step: (0, 0, 0)),
            pl.BlockSpec((TEAMS, rows, TEAM_WIDTH), lambda step: (0, 0, 0)),
        ]
        + [pl.BlockSpec(x.shape[1:], lambda step: (0, 0, 0)) for x in shapes],
        out_shape=[
            jax.ShapeDtypeStruct((lanes, TEAMS, QUERY_WIDTH, rows), jnp.bfloat16),
            jax.ShapeDtypeStruct((TEAMS, rows, QUERY_WIDTH), jnp.bfloat16),
            jax.ShapeDtypeStruct((TEAMS, rows, TEAM_WIDTH), jnp.bfloat16),
        ]
        + [jax.ShapeDtypeStruct(x.shape[1:], x.dtype) for x in shapes],
        scratch_shapes=[
            pltpu.VMEM((TEAM_HEADS + 1, TEAMS, rows, HEAD_DIM), jnp.bfloat16),
            pltpu.VMEM((TEAMS, QUERY_WIDTH, rows), jnp.bfloat16),
            pltpu.VMEM((TEAM_HEADS, TEAMS, rows, HEAD_DIM), jnp.bfloat16),
            pltpu.VMEM((TEAMS, rows, rows), jnp.float32),
            pltpu.VMEM((TEAM_HEADS + 1, TEAMS, rows, HEAD_DIM), jnp.float32),
            pltpu.VMEM((TEAM_HEADS, TEAMS, rows, HEAD_DIM), jnp.float32),
            pltpu.VMEM((lanes, TEAMS, rows, TEAM_WIDTH), jnp.bfloat16),
            pltpu.VMEM((lanes, TEAMS, 8, rows), jnp.float32),
            pltpu.SemaphoreType.DMA((2, TEAMS, lanes)),
            pltpu.SemaphoreType.DMA((2, TEAMS, lanes)),
        ]
        + exchange_sems(plan)
        + [pltpu.VMEM(x.shape, x.dtype) for x in shapes],
        compiler_params=pltpu.CompilerParams(
            collective_id=collective, has_side_effects=True, vmem_limit_bytes=VMEM_BYTES
        ),
    )(queries, grads, stats, carried, keys, values, *halves)


def finish_body(
    query_ref,
    key_ref,
    value_ref,
    lane_ref,
    weight_ref,
    gain_ref,
    bias_ref,
    norm_ref,
    excess_ref,
    length_ref,
    down_in,
    up_in,
    out_in,
    whole_ref,
    home_ref,
    total_ref,
    whole_down,
    whole_up,
    whole_out,
    query_parts,
    down_parts,
    up_parts,
    out_parts,
    down_ref,
    up_ref,
    out_ref,
    turned,
    weight_rows,
    weight_grad,
    rows_sum,
    rows_ref,
    main_ref,
    vector_ref,
    core_main,
    send_main,
    lane_main,
    team_send_main,
    team_main,
    assembled,
    vectors,
    ready,
    core_sems,
    lane_sems,
    team_sems,
    home_sems,
    vector_sems,
    out_lane_sems,
    out_core_sems,
    local_sems,
    early_team,
    early_lane,
    early_core,
    early_local,
    first_send,
    first_recv,
    first_local,
):
    lanes = lax.axis_size("seq") // TEAMS
    me = lax.axis_index("seq")
    core = lax.axis_index("batch")
    team, lane = me // lanes, lax.rem(me, lanes)

    def lane_peer(k):
        other = lax.rem(lane + k, lanes)
        return other, {"seq": team * lanes + other}

    def team_peer(k):
        other = lax.rem(team + k, TEAMS)
        return other, {"seq": other * lanes + lane}

    sibling = {"batch": 1 - core}
    greet(["core", "team", "lane"])
    first_sources = (query_ref, down_in, up_in, out_in)
    first_targets = (query_parts, down_parts, up_parts, out_parts)
    first_plan = [("team", "spread"), ("team", "spread"), ("lane", "spread"), ("lane", "spread")]
    first_copies = [[], []]
    for n in (1, 2, 3, 0):
        mine = peers_of(first_plan[n][0])[0]
        own = pltpu.make_async_copy(first_sources[n].at[mine], first_targets[n].at[mine], first_local.at[n])
        own.start()
        first_copies[n == 0].append(own)
        first_copies[n == 0] += remote_copies(
            first_plan[n : n + 1],
            first_sources[n : n + 1],
            first_targets[n : n + 1],
            first_send.at[n : n + 1],
            first_recv.at[n : n + 1],
        )
    spans = (slice(0, QUERY_WIDTH), slice(QUERY_WIDTH, 2 * QUERY_WIDTH), slice(2 * QUERY_WIDTH, None))
    for span in spans:
        weight_rows[span, :] = weight_ref[:, span].T
    weight_grad[...] = jnp.zeros_like(weight_grad)

    def known(b, _):
        rows_low = lane_ref[b].T
        turned[b] = rows_low
        total = None
        for span, grads in ((spans[1], key_ref[b]), (spans[2], value_ref[b])):
            weight_grad[:, span] += dot(rows_low, grads)
            part = dot(grads, weight_rows[span, :])
            total = part if total is None else total + part
        rows_sum[b] = total
        return 0

    lax.fori_loop(0, TEAMS, known, 0)
    for copy in first_copies[0]:
        copy.wait()
    down_ref[...] = added([down_parts[k] for k in range(lanes)])
    up_ref[...] = added([up_parts[k] for k in range(TEAMS)])
    out_ref[...] = added([out_parts[k] for k in range(TEAMS)])

    def place(n, p, t, part=None):
        if n == 0:
            ref, start, wide = whole_down.at[core, p, t], 0, whole_down.shape[4]
        else:
            ref = (None, whole_up, whole_out)[n]
            wide = ref.shape[3] // 2
            ref, start = ref.at[p, t], core * wide
        cut = (wide // 128 + 1) // 2 * 128
        if part is not None:
            start, wide = ((start, cut), (start + cut, wide - cut))[part]
        return ref.at[:, pl.ds(pl.multiple_of(start, 128), wide)]

    square = lanes == 4
    if square:
        across, along = lax.rem(lane, 2), lane // 2
        direct = [2 * along + 1 - across, 2 * (1 - along) + across]
        origins = direct
    else:
        direct = [lax.rem(lane + k, lanes) for k in range(1, lanes)]
        origins = [lax.rem(lane - k + lanes, lanes) for k in range(1, lanes)]
    corner = lanes - 1 - lane

    def lane_of(p):
        return {"seq": team * lanes + p}

    def landed(ref, sem):
        pltpu.make_async_copy(ref, ref, sem).wait()

    early = (down_ref, up_ref, out_ref)
    number = len(early)
    early_z = [[None] * TEAMS for _ in range(number)]
    for k in range(1, TEAMS):
        _, target = team_peer(k)
        for n in range(number):
            early_z[n][k] = push(
                early[n],
                place(n, lane, team),
                early_team.at[0, n, k],
                early_team.at[1, n, k],
                target,
            )
    early_kept = []
    for n in range(number):
        copy = pltpu.make_async_copy(early[n], place(n, lane, team), early_local.at[n])
        copy.start()
        early_kept.append(copy)
    early_out = []
    early_sib = []

    def forward(j):
        t = lax.rem(team - j + TEAMS, TEAMS)
        for n in range(number):
            if j == 0:
                source = early[n]
            else:
                early_z[n][j].wait_recv()
                source = place(n, lane, t)
            target = place(n, lane, t)
            for m, p in enumerate(direct):
                sems = [early_lane.at[side, n, j, m] for side in range(2)]
                early_out.append(push(source, target, *sems, lane_of(p)))
            sems = [early_core.at[side, n, j, 0] for side in range(2)]
            early_sib.append(push(source, target, *sems, sibling))

    def relay(j):
        t = lax.rem(team - j + TEAMS, TEAMS)
        for n in range(number):
            for m, p in enumerate(origins):
                piece = place(n, p, t)
                landed(piece, early_lane.at[1, n, j, m])
                if square:
                    side = place(n, p, t, m)
                    sems = [early_lane.at[side_, n, j, 2 + m] for side_ in range(2)]
                    early_out.append(push(side, side, *sems, lane_of(direct[1 - m])))
                sems = [early_core.at[side_, n, j, 1 + m] for side_ in range(2)]
                early_sib.append(push(piece, piece, *sems, sibling))

    def settle(j):
        if not square:
            return
        t = lax.rem(team - j + TEAMS, TEAMS)
        for n in range(number):
            for m in range(2):
                landed(place(n, corner, t, m), early_lane.at[1, n, j, 2 + m])
            piece = place(n, corner, t)
            sems = [early_core.at[side, n, j, 3] for side in range(2)]
            early_sib.append(push(piece, piece, *sems, sibling))

    forward(0)
    for copy in first_copies[1]:
        copy.wait()
    gain = gain_ref[...][None, :]
    bias = bias_ref[...][None, :]

    def last(b, sums):
        query_rows = query_parts[0, b].astype(jnp.float32)
        for p in range(1, lanes):
            query_rows = query_rows + query_parts[p, b].astype(jnp.float32)
        grads = (query_rows * HEAD_DIM ** (-0.5)).astype(jnp.bfloat16).T
        weight_grad[:, spans[0]] += dot(turned[b], grads)
        total = rows_sum[b] + dot(grads, weight_rows[spans[0], :])
        rows_ref[b] = total.astype(jnp.bfloat16)
        shifted = lane_ref[b].astype(jnp.float32) - bias
        return (
            sums[0] + jnp.sum(total * shifted, axis=0, keepdims=True),
            sums[1] + jnp.sum(total, axis=0, keepdims=True),
        )

    nothing = jnp.zeros_like(gain)
    gain_sum, bias_sum = lax.fori_loop(0, TEAMS, last, (nothing, nothing))
    length = length_ref[0].astype(jnp.float32)
    pairs = (length - 1.0) * (length - 2.0) / (2.0 * TEAMS * lanes)
    excess = jnp.sum(jnp.sum(excess_ref[...], axis=0, keepdims=True), axis=1, keepdims=True)
    vector_ref[...] = jnp.zeros_like(vector_ref)
    vector_ref[0:1, :] = gain_sum / gain
    vector_ref[1:2, :] = bias_sum
    vector_ref[2:4, :] = norm_ref[...]
    vector_ref[4:5, :] = jnp.broadcast_to(excess, nothing.shape)
    vector_ref[5:6, :] = jnp.full(nothing.shape, pairs)
    depth = main_ref.shape[1]
    for chunk in range(2 * lanes):
        main_ref[chunk] = weight_grad[chunk * depth : (chunk + 1) * depth, :].astype(jnp.bfloat16)
    theirs = pl.ds((1 - core) * lanes, lanes)
    core_copies = [
        push(main_ref.at[theirs], core_main, core_sems.at[0, 0], core_sems.at[1, 0], sibling),
        push(vector_ref, vectors.at[0], vector_sems.at[0, 0], vector_sems.at[1, 0], sibling),
    ]
    for copy in core_copies:
        copy.wait()
    relay(0)

    both = vector_ref[...] + vectors[0]
    vectors[1 + lane] = both
    ready[0] = both
    for j in range(lanes):
        send_main[j] = (
            main_ref[core * lanes + j].astype(jnp.float32) + core_main[j].astype(jnp.float32)
        ).astype(jnp.bfloat16)
    lane_copies = []
    for k in range(1, lanes):
        other, target = lane_peer(k)
        lane_copies += [
            push(send_main.at[other], lane_main.at[lane], lane_sems.at[0, 0, k], lane_sems.at[1, 0, k], target),
            push(ready.at[0], vectors.at[1 + lane], vector_sems.at[0, k], vector_sems.at[1, k], target),
        ]
    lane_main[lane] = send_main[lane]
    for copy in lane_copies:
        copy.wait()

    def total(ref, start, number):
        result = ref[start].astype(jnp.float32)
        for j in range(1, number):
            result = result + ref[start + j].astype(jnp.float32)
        return result

    whole_vector = total(vectors, 1, lanes)
    ready[1] = whole_vector
    vectors[1 + lanes + team] = whole_vector
    low_main = total(lane_main, 0, lanes).astype(jnp.bfloat16)
    team_send_main[...] = low_main
    team_main[team] = low_main
    team_copies = []
    for k in range(1, TEAMS):
        other, target = team_peer(k)
        at = lanes + k
        team_copies += [
            push(team_send_main, team_main.at[team], team_sems.at[0, 0, k], team_sems.at[1, 0, k], target),
            push(ready.at[1], vectors.at[1 + lanes + team], vector_sems.at[0, at], vector_sems.at[1, at], target),
        ]
    home_copies = []
    for k in range(1, TEAMS):
        other, target = team_peer(k)
        home_copies.append(
            push(rows_ref.at[other], home_ref.at[team], home_sems.at[0, k], home_sems.at[1, k], target)
        )
    own = pltpu.make_async_copy(rows_ref.at[team], home_ref.at[team], local_sems.at[0])
    own.start()
    for j in range(1, TEAMS):
        forward(j)
        settle(j - 1)
        if j < TEAMS - 1:
            relay(j)
    for copy in team_copies:
        copy.wait()
    total_ref[...] = total(vectors, 1 + lanes, TEAMS)
    pieces = []
    for part in range(3):
        first = part * QUERY_WIDTH
        for g in range(TEAMS):
            piece = team_main[g, :, first : first + TEAM_WIDTH]
            if g == 0 and part < 2:
                more = piece[:, :HEAD_DIM].astype(jnp.float32)
                for other in range(TEAMS):
                    more = more + team_main[
                        other, :, first + TEAM_WIDTH : first + QUERY_WIDTH
                    ].astype(jnp.float32)
                pieces += [more.astype(jnp.bfloat16), piece[:, HEAD_DIM:]]
            else:
                pieces.append(piece)
    assembled[...] = jnp.concatenate(pieces, axis=1)

    def chunk_of(p, part=None):
        ref = whole_ref.at[core * lanes + p]
        half = whole_ref.shape[2] // 2
        return ref if part is None else ref.at[:, pl.ds(part * half, half)]

    out_copies, core_out = [], []
    for m, p in enumerate(direct):
        sems = [out_lane_sems.at[side, m] for side in range(2)]
        out_copies.append(push(assembled, chunk_of(lane), *sems, lane_of(p)))
    sems = [out_core_sems.at[side, 0] for side in range(2)]
    core_out.append(push(assembled, chunk_of(lane), *sems, sibling))
    kept = pltpu.make_async_copy(assembled, chunk_of(lane), local_sems.at[1])
    kept.start()
    relay(TEAMS - 1)
    for m, p in enumerate(origins):
        landed(chunk_of(p), out_lane_sems.at[1, m])
        if square:
            sems = [out_lane_sems.at[side, 2 + m] for side in range(2)]
            out_copies.append(push(chunk_of(p, m), chunk_of(p, m), *sems, lane_of(direct[1 - m])))
        sems = [out_core_sems.at[side, 1 + m] for side in range(2)]
        core_out.append(push(chunk_of(p), chunk_of(p), *sems, sibling))
    settle(TEAMS - 1)
    if square:
        for m in range(2):
            landed(chunk_of(corner, m), out_lane_sems.at[1, 2 + m])
        sems = [out_core_sems.at[side, 3] for side in range(2)]
        core_out.append(push(chunk_of(corner), chunk_of(corner), *sems, sibling))
    for copy in out_copies + early_out:
        copy.wait_send()
    for n in range(number):
        for k in range(1, TEAMS):
            early_z[n][k].wait_send()
    for copy in core_out + home_copies + early_sib + early_kept:
        copy.wait()
    own.wait()
    kept.wait()


def finish(
    queries, keys, values, lane_rows, weight, gain, bias, norm, excess, length, reduced, collective
):
    lanes = lax.axis_size("seq") // TEAMS
    width, columns = weight.shape
    rows = lane_rows.shape[1]
    vector = (8, width)
    chunks, depth = 2 * lanes, width // (2 * lanes)
    low = jnp.bfloat16
    dma = pltpu.SemaphoreType.DMA
    down, up, out = (x.shape[1:] for x in reduced)
    wholes = [
        (2, lanes, TEAMS) + down,
        (lanes, TEAMS, up[0], 2 * up[1]),
        (lanes, TEAMS, out[0], 2 * out[1]),
    ]
    anywhere = pl.BlockSpec(memory_space=pl.ANY)
    inside = pl.BlockSpec(memory_space=pltpu.VMEM)
    return pl.pallas_call(
        finish_body,
        out_shape=[
            jax.ShapeDtypeStruct((chunks, depth, 3 * width), low),
            jax.ShapeDtypeStruct(lane_rows.shape, low),
            jax.ShapeDtypeStruct(vector, jnp.float32),
        ]
        + [jax.ShapeDtypeStruct(shape, low) for shape in wholes],
        in_specs=[anywhere]
        + [inside] * 8
        + [pl.BlockSpec(memory_space=pltpu.SMEM)]
        + [anywhere] * 3,
        out_specs=[anywhere, anywhere, inside] + [anywhere] * 3,
        scratch_shapes=[
            pltpu.VMEM(queries.shape, low),
            pltpu.VMEM((lanes,) + down, low),
            pltpu.VMEM((TEAMS,) + up, low),
            pltpu.VMEM((TEAMS,) + out, low),
            pltpu.VMEM(down, low),
            pltpu.VMEM(up, low),
            pltpu.VMEM(out, low),
            pltpu.VMEM((TEAMS, width, rows), low),
            pltpu.VMEM((columns, width), low),
            pltpu.VMEM((width, columns), jnp.float32),
            pltpu.VMEM((TEAMS, rows, width), jnp.float32),
            pltpu.VMEM((TEAMS, rows, width), low),
            pltpu.VMEM((chunks, depth, columns), low),
            pltpu.VMEM(vector, jnp.float32),
            pltpu.VMEM((lanes, depth, columns), low),
            pltpu.VMEM((lanes, depth, columns), low),
            pltpu.VMEM((lanes, depth, columns), low),
            pltpu.VMEM((depth, columns), low),
            pltpu.VMEM((TEAMS, depth, columns), low),
            pltpu.VMEM((depth, 3 * width), low),
            pltpu.VMEM((1 + lanes + TEAMS,) + vector, jnp.float32),
            pltpu.VMEM((2,) + vector, jnp.float32),
            dma((2, 2)),
            dma((2, 2, lanes)),
            dma((2, 2, TEAMS)),
            dma((2, TEAMS)),
            dma((2, lanes + TEAMS)),
            dma((2, lanes)),
            dma((2, lanes)),
            dma((2,)),
            dma((2, 3, TEAMS)),
            dma((2, 3, TEAMS, lanes)),
            dma((2, 3, TEAMS, lanes)),
            dma((3,)),
            dma((4, max(lanes, TEAMS))),
            dma((4, max(lanes, TEAMS))),
            dma((4,)),
        ],
        compiler_params=pltpu.CompilerParams(
            collective_id=collective, has_side_effects=True, vmem_limit_bytes=VMEM_BYTES
        ),
    )(queries, keys, values, lane_rows, weight, gain, bias, norm, excess, length, *reduced)


def contract_cols(left, right):
    return lax.dot_general(left, right, (((1,), (1,)), ((), ())), preferred_element_type=jnp.float32)


def dense_body(
    length_ref,
    mixed_ref,
    mass_ref,
    tokens_ref,
    grad_ref,
    gain_ref,
    bias_ref,
    w_out_hbm,
    w_up_hbm,
    w_down_hbm,
    layer_ref,
    resid_ref,
    norm_ref,
    cols_ref,
    stats_ref,
    down_hbm,
    up_hbm,
    out_hbm,
    w_out,
    w_up,
    w_down,
    active,
    slope,
    top,
    normed,
    mixed,
    slant,
    active_other,
    slope_other,
    top_other,
    normed_other,
    mixed_other,
    slant_other,
    total,
    back,
    cols,
    stats,
    down_half,
    up_half,
    out_half,
    load_sems,
    core_sems,
    lane_sems,
    keep_sems,
    store_sems,
):
    rows, width = tokens_ref.shape
    hidden = w_up.shape[1]
    step = width
    count = lax.axis_size("seq")
    lanes = count // TEAMS
    me = lax.axis_index("seq")
    core = lax.axis_index("batch")
    team, lane = me // lanes, lax.rem(me, lanes)
    sibling = {"batch": 1 - core}
    loads = [
        pltpu.make_async_copy(source, target, load_sems.at[n])
        for n, (source, target) in enumerate(
            ((w_out_hbm, w_out), (w_up_hbm, w_up), (w_down_hbm, w_down))
        )
    ]
    for load in loads:
        load.start()
    greet(["core", "lane"])

    def half_of(ref, which):
        half = ref.shape[1] // 2
        return ref.at[:, pl.ds(pl.multiple_of(which * half, 128), half)]

    pairs = (
        (active, active_other, True),
        (top, top_other, False),
        (normed, normed_other, False),
        (slope, slope_other, True),
        (mixed, mixed_other, False),
        (slant, slant_other, True),
    )

    def swap(n, start):
        source, target, halved = pairs[n]
        return push(
            half_of(source, 1 - core) if halved else source,
            target,
            core_sems.at[0, n],
            core_sems.at[1, n],
            sibling,
            start,
        )

    grad_top = grad_ref[...]
    top[...] = grad_top.astype(jnp.bfloat16)
    swap(1, True)
    valid = me * rows + lax.broadcasted_iota(jnp.int32, (rows, width), 0) < length_ref[0]
    mixed_rows = mixed_ref[...]
    mixed[...] = jnp.where(valid, mixed_rows.T, jnp.zeros((), jnp.bfloat16))
    swap(4, True)
    loads[0].wait()
    residual = tokens_ref[...] + dot(mixed[...], w_out[...])
    row_mean = jnp.mean(residual, axis=1, keepdims=True)
    centred = residual - row_mean
    variance = jnp.mean(centred * centred, axis=1, keepdims=True)
    spread = lax.rsqrt(variance + epsilon)
    scaled = centred * spread
    gain = gain_ref[...][None, :]
    normed[...] = (scaled * gain + bias_ref[...][None, :]).astype(jnp.bfloat16)
    swap(2, True)
    total[...] = residual
    back[...] = jnp.zeros_like(back)
    loads[1].wait()
    loads[2].wait()

    def chunk(c, _):
        at = pl.ds(pl.multiple_of(c * step, 128), step)
        up = w_up[:, at]
        down = w_down[at, :]
        u = dot(normed[...], up)
        squared = u * u
        bend = jnp.tanh(0.7978845608028654 * u * (1.0 + 0.044715 * squared))
        lift = 0.5 * (1.0 + bend)
        low = (u * lift).astype(jnp.bfloat16)
        active[:, at] = low
        turn = lift + (0.5 * 0.7978845608028654) * u * (1.0 - bend * bend) * (
            1.0 + (3.0 * 0.044715) * squared
        )
        grad_low = (contract_cols(top[...], down) * turn).astype(jnp.bfloat16)
        slope[:, at] = grad_low
        total[...] += dot(low, down)
        back[...] += contract_cols(grad_low, up)
        return 0

    lax.fori_loop(0, hidden // step, chunk, 0)
    swap(0, True)
    swap(3, True)
    layer_ref[...] = total[...]
    grad_normed = back[...]
    norm_ref[0:1, :] = jnp.sum(grad_normed * scaled, axis=0, keepdims=True)
    norm_ref[1:2, :] = jnp.sum(grad_normed, axis=0, keepdims=True)
    inner = grad_normed * gain
    resid = grad_top + spread * (
        inner
        - jnp.mean(inner, axis=1, keepdims=True)
        - scaled * jnp.mean(inner * scaled, axis=1, keepdims=True)
    )
    resid_ref[...] = resid
    slant[...] = resid.astype(jnp.bfloat16)
    swap(5, True)
    grad_mixed = contract_cols(slant[...], w_out[...]).astype(jnp.bfloat16)
    grad_mixed = jnp.where(valid, grad_mixed, jnp.zeros((), jnp.bfloat16))
    products = grad_mixed.T.astype(jnp.float32) * mixed_rows.astype(jnp.float32)
    for t in range(TEAMS):
        cols[t] = grad_mixed[:, t * TEAM_WIDTH : (t + 1) * TEAM_WIDTH]
        stats[t] = mass_ref[t]
        for h in range(TEAM_HEADS):
            first = t * TEAM_WIDTH + h * HEAD_DIM
            stats[t, TEAM_HEADS + h : TEAM_HEADS + h + 1, :] = jnp.sum(
                products[first : first + HEAD_DIM], axis=0, keepdims=True
            )
    copies = []
    for k in range(1, TEAMS):
        other = lax.rem(team + k, TEAMS)
        for n, (source, target) in enumerate(((cols, cols_ref), (stats, stats_ref))):
            copies.append(
                push(
                    source.at[other],
                    target.at[team],
                    lane_sems.at[0, n, k],
                    lane_sems.at[1, n, k],
                    {"seq": other * lanes + lane},
                )
            )
    for n, (source, target) in enumerate(((cols, cols_ref), (stats, stats_ref))):
        copy = pltpu.make_async_copy(source.at[team], target.at[team], keep_sems.at[n])
        copy.start()
        copies.append(copy)

    def pair_dot(left, left_other, right, right_other, at):
        return (
            dot(left[:, at].T, right[...]) + dot(left_other[:, at].T, right_other[...])
        ).astype(jnp.bfloat16)

    for n in range(len(pairs)):
        swap(n, False).wait()
    block = 384
    own_active = half_of(active, core)
    own_slope = half_of(slope, core)
    own_slant = half_of(slant, core)

    def down_rows(c, _):
        at = pl.ds(pl.multiple_of(c * block, 128), block)
        down_half[at, :] = pair_dot(own_active, active_other, top, top_other, at)
        return 0

    lax.fori_loop(0, down_half.shape[0] // block, down_rows, 0)
    stores = [pltpu.make_async_copy(down_half, down_hbm, store_sems.at[0])]
    stores[0].start()

    def up_rows(c, _):
        at = pl.ds(pl.multiple_of(c * block, 128), block)
        up_half[at, :] = pair_dot(normed, normed_other, own_slope, slope_other, at)
        out_half[at, :] = pair_dot(mixed, mixed_other, own_slant, slant_other, at)
        return 0

    lax.fori_loop(0, width // block, up_rows, 0)
    for n, (source, target) in enumerate(((up_half, up_hbm), (out_half, out_hbm))):
        copy = pltpu.make_async_copy(source, target, store_sems.at[1 + n])
        copy.start()
        stores.append(copy)
    for copy in copies + stores:
        copy.wait()


def dense(length, mixed, masses, tokens, grad, gain, bias, w_out, w_up, w_down, collective):
    rows, width = tokens.shape
    hidden = w_up.shape[1]
    low, full = jnp.bfloat16, jnp.float32
    inside = pl.BlockSpec(memory_space=pltpu.VMEM)
    anywhere = pl.BlockSpec(memory_space=pl.ANY)
    dma = pltpu.SemaphoreType.DMA
    half = hidden // 2
    return pl.pallas_call(
        dense_body,
        out_shape=[
            jax.ShapeDtypeStruct((rows, width), full),
            jax.ShapeDtypeStruct((rows, width), full),
            jax.ShapeDtypeStruct((2, width), full),
            jax.ShapeDtypeStruct((TEAMS, rows, TEAM_WIDTH), low),
            jax.ShapeDtypeStruct((TEAMS, 8, rows), full),
            jax.ShapeDtypeStruct((half, width), low),
            jax.ShapeDtypeStruct((width, half), low),
            jax.ShapeDtypeStruct((width, width // 2), low),
        ],
        in_specs=[pl.BlockSpec(memory_space=pltpu.SMEM)] + [inside] * 6 + [anywhere] * 3,
        out_specs=[inside] * 3 + [anywhere] * 5,
        scratch_shapes=[
            pltpu.VMEM((width, width), low),
            pltpu.VMEM((width, hidden), low),
            pltpu.VMEM((hidden, width), low),
            pltpu.VMEM((rows, hidden), low),
            pltpu.VMEM((rows, hidden), low),
            pltpu.VMEM((rows, width), low),
            pltpu.VMEM((rows, width), low),
            pltpu.VMEM((rows, width), low),
            pltpu.VMEM((rows, width), low),
            pltpu.VMEM((rows, half), low),
            pltpu.VMEM((rows, half), low),
            pltpu.VMEM((rows, width), low),
            pltpu.VMEM((rows, width), low),
            pltpu.VMEM((rows, width), low),
            pltpu.VMEM((rows, width // 2), low),
            pltpu.VMEM((rows, width), full),
            pltpu.VMEM((rows, width), full),
            pltpu.VMEM((TEAMS, rows, TEAM_WIDTH), low),
            pltpu.VMEM((TEAMS, 8, rows), full),
            pltpu.VMEM((half, width), low),
            pltpu.VMEM((width, half), low),
            pltpu.VMEM((width, width // 2), low),
            dma((3,)),
            dma((2, 6)),
            dma((2, 2, TEAMS)),
            dma((2,)),
            dma((3,)),
        ],
        compiler_params=pltpu.CompilerParams(
            collective_id=collective, has_side_effects=True, vmem_limit_bytes=VMEM_BYTES
        ),
    )(length, mixed, masses, tokens, grad, gain, bias, w_out, w_up, w_down)


def close_body(tokens_ref, gain_ref, resid_ref, home_ref, *refs):
    grad_ref, rest = refs[len(refs) // 2], refs[: len(refs) // 2] + refs[len(refs) // 2 + 1 :]
    for n in range(len(rest) // 2):
        rest[len(rest) // 2 + n][...] = rest[n][...].astype(jnp.float32)
    tokens = tokens_ref[...]
    centred = tokens - jnp.mean(tokens, axis=1, keepdims=True)
    spread = lax.rsqrt(jnp.mean(centred * centred, axis=1, keepdims=True) + epsilon)
    scaled = centred * spread
    total = home_ref[0].astype(jnp.float32)
    for t in range(1, TEAMS):
        total = total + home_ref[t].astype(jnp.float32)
    inner = total * gain_ref[...][None, :]
    grad_ref[...] = resid_ref[...] + spread * (
        inner
        - jnp.mean(inner, axis=1, keepdims=True)
        - scaled * jnp.mean(inner * scaled, axis=1, keepdims=True)
    )


def close(tokens, gain, resid, home, weights):
    steps = 8
    rows, width = tokens.shape

    def band(x):
        return pl.BlockSpec((x.shape[0] // steps, x.shape[1]), lambda i: (i, 0))

    return pl.pallas_call(
        close_body,
        grid=(steps,),
        in_specs=[
            band(tokens),
            pl.BlockSpec((width,), lambda i: (0,)),
            band(resid),
            pl.BlockSpec((TEAMS, rows // steps, width), lambda i: (0, i, 0)),
        ]
        + [band(x) for x in weights],
        out_specs=[band(tokens)] + [band(x) for x in weights],
        out_shape=[jax.ShapeDtypeStruct(x.shape, jnp.float32) for x in [tokens] + weights],
        compiler_params=pltpu.CompilerParams(vmem_limit_bytes=VMEM_BYTES),
    )(tokens, gain, resid, home, *weights)


def per_device(
    block_input,
    ln1_gain,
    ln1_bias,
    w_qkv,
    w_out,
    ln2_gain,
    ln2_bias,
    w_up,
    w_down,
    length_draw,
    threshold_index,
    grad_out,
):
    rows = block_input.shape[1]
    width = block_input.shape[2]
    blocks = lax.axis_size("seq")
    lanes = blocks // TEAMS
    group_len = blocks * rows
    me = lax.axis_index("seq")
    team = me // lanes
    length = group_len - rows + 1 + length_draw % rows
    threshold = threshold_index.astype(jnp.float32) / 128.0
    tokens = block_input[0]
    grad_top = grad_out[0]

    lane_rows, team_weight, queries, keys, values = project(tokens, ln1_gain, ln1_bias, w_qkv, 0)

    head_out, masses, carried, excess = attend(
        length, threshold, queries, keys, values, blocks, rows, 1
    )
    layer_out, grad_resid, grad_ln2, grad_cols, stats, down_half, up_half, out_half = dense(
        length,
        head_out.reshape(width, rows),
        masses,
        tokens,
        grad_top,
        ln2_gain,
        ln2_bias,
        w_out,
        w_up,
        w_down,
        3,
    )
    halves = [x.reshape(lanes, TEAMS, -1, x.shape[1]) for x in (down_half, up_half, out_half)]
    query_grads, key_grads, value_grads, *halves = attend_back(
        queries, grad_cols, stats, carried, keys, values, halves, blocks, rows, 7
    )

    grad_w_qkv, home_rows, vectors, grad_w_down, grad_w_up, grad_w_out = finish(
        query_grads,
        key_grads,
        value_grads,
        lane_rows,
        team_weight,
        ln1_gain,
        ln1_bias,
        grad_ln2,
        excess,
        length,
        halves,
        6,
    )
    grad_x, grad_w_qkv, grad_w_out, grad_w_up, grad_w_down = close(
        tokens,
        ln1_gain,
        grad_resid,
        home_rows,
        [
            grad_w_qkv.reshape(w_qkv.shape),
            grad_w_out.reshape(w_out.shape),
            grad_w_up.reshape(w_up.shape),
            grad_w_down.reshape(w_down.shape),
        ],
    )
    pruned_share = (vectors[4, 0] / vectors[5, 0]).reshape(1)
    return (
        layer_out[None],
        grad_x[None],
        vectors[0],
        vectors[1],
        grad_w_qkv,
        grad_w_out,
        vectors[2],
        vectors[3],
        grad_w_up,
        grad_w_down,
        pruned_share,
    )


def solution(mesh):
    placed = (
        P("batch", "seq", None),
        P(),
        P(),
        P(),
        P(),
        P(),
        P(),
        P(),
        P(),
        P("batch"),
        P(),
        P("batch", "seq", None),
    )
    return jax.shard_map(
        per_device,
        mesh=mesh,
        in_specs=placed,
        out_specs=(
            P("batch", "seq", None),
            P("batch", "seq", None),
            P(),
            P(),
            P(),
            P(),
            P(),
            P(),
            P(),
            P(),
            P(),
        ),
        check_vma=False,
    )
```

```python
import functools

import jax
import jax.numpy as jnp
from jax import lax
from jax.experimental import pallas as pl
from jax.experimental.pallas import tpu as pltpu
from jax.sharding import PartitionSpec as P

HEADS = 12
HEAD_DIM = 64
TEAMS = 4
TEAM_HEADS = HEADS // TEAMS
TEAM_WIDTH = TEAM_HEADS * HEAD_DIM
QUERY_WIDTH = TEAM_WIDTH + HEAD_DIM

epsilon = 1e-05
negative = -1e30
select_scale = 3.0
VMEM_BYTES = 60 * 2**20
MESH = pl.DeviceIdType.MESH


def peers_of(scope):
    lanes = lax.axis_size("seq") // TEAMS
    me = lax.axis_index("seq")
    team, lane = me // lanes, lax.rem(me, lanes)
    if scope == "team":
        return lane, lanes, lambda k: {"seq": team * lanes + k}
    if scope == "lane":
        return team, TEAMS, lambda k: {"seq": k * lanes + lane}
    if scope == "core":
        return lax.axis_index("batch"), 2, lambda k: {"batch": k}
    return me, lanes * TEAMS, lambda k: {"seq": k}


def scope_size(scope):
    count = lax.axis_size("seq")
    return {"team": count // TEAMS, "lane": TEAMS, "core": 2, "all": count}[scope]


def greet(scopes, meanwhile=None):
    barrier = pltpu.get_barrier_semaphore()
    number = 0
    for scope in scopes:
        mine, peers, device_of = peers_of(scope)
        for k in range(1, peers):
            pl.semaphore_signal(
                barrier, inc=1, device_id=device_of(lax.rem(mine + k, peers)), device_id_type=MESH
            )
        number += peers - 1
    if meanwhile is not None:
        meanwhile()
    pl.semaphore_wait(barrier, number)


def push(source, destination, send, receive, target, start=True):
    copy = pltpu.make_async_remote_copy(
        src_ref=source,
        dst_ref=destination,
        send_sem=send,
        recv_sem=receive,
        device_id=target,
        device_id_type=MESH,
    )
    if start:
        copy.start()
    return copy


def part_of(kind, ref, k):
    if kind == "gather":
        return ref
    if kind == "spread":
        return ref.at[k]
    if kind == "second":
        return ref.at[:, k]
    half = ref.shape[1] // 2
    return ref.at[:, pl.ds(pl.multiple_of(k * half, 128), half)]


def remote_copies(plan, sources, targets, send, receive, start=True):
    copies = []
    for n, (scope, kind) in enumerate(plan):
        mine, peers, device_of = peers_of(scope)
        for k in range(1, peers):
            peer = lax.rem(mine + k, peers)
            copies.append(
                push(
                    part_of(kind, sources[n], peer),
                    targets[n].at[mine],
                    send.at[n, k],
                    receive.at[n, k],
                    device_of(peer),
                    start,
                )
            )
    return copies


def exchange_shapes(plan, arrays):
    shapes = []
    for (scope, kind), x in zip(plan, arrays):
        shape = x.shape
        if kind == "gather":
            shape = (scope_size(scope),) + shape
        if kind == "half":
            shape = (2, shape[0], shape[1] // 2)
        if kind == "second":
            shape = (shape[1], shape[0]) + shape[2:]
        shapes.append(jax.ShapeDtypeStruct(shape, x.dtype))
    return shapes


def exchange_sems(plan):
    number, most = len(plan), max(scope_size(scope) for scope, _ in plan)
    return [
        pltpu.SemaphoreType.DMA((number, most)),
        pltpu.SemaphoreType.DMA((number, most)),
        pltpu.SemaphoreType.DMA((number,)),
    ]


def scopes_of(plan):
    return [x for x in ("core", "team", "lane", "all") if x in [scope for scope, _ in plan]]


def exchange(plan, arrays, collective):
    number = len(arrays)
    shapes = exchange_shapes(plan, arrays)

    def body(*refs):
        sources, targets = refs[:number], refs[number : 2 * number]
        send, receive, local = refs[2 * number : 2 * number + 3]
        through = refs[2 * number + 3 :]
        greet(scopes_of(plan))
        copies = remote_copies(plan, sources, targets, send, receive)
        inward = []
        for n, (scope, kind) in enumerate(plan):
            mine = peers_of(scope)[0]
            copy = pltpu.make_async_copy(part_of(kind, sources[n], mine), through[n], local.at[n])
            copy.start()
            inward.append(copy)
        for n, (scope, kind) in enumerate(plan):
            mine = peers_of(scope)[0]
            inward[n].wait()
            copy = pltpu.make_async_copy(through[n], targets[n].at[mine], local.at[n])
            copy.start()
            copies.append(copy)
        for copy in copies:
            copy.wait()

    return pl.pallas_call(
        body,
        out_shape=shapes,
        in_specs=[pl.BlockSpec(memory_space=pl.ANY)] * number,
        out_specs=[pl.BlockSpec(memory_space=pl.ANY)] * number,
        scratch_shapes=exchange_sems(plan) + [pltpu.VMEM(x.shape[1:], x.dtype) for x in shapes],
        compiler_params=pltpu.CompilerParams(
            collective_id=collective, has_side_effects=True, vmem_limit_bytes=VMEM_BYTES
        ),
    )(*arrays)


def dot(left, right):
    return jnp.dot(left, right, preferred_element_type=jnp.float32)


def project_body(
    tokens_ref,
    gain_ref,
    bias_ref,
    w_ref,
    lane_ref,
    weight_ref,
    query_ref,
    key_ref,
    value_ref,
    held,
    ready,
    windows,
    firsts,
    hop_send,
    hop_recv,
    team_send,
    team_recv,
    weight_sems,
    local_sems,
):
    lanes = lax.axis_size("seq") // TEAMS
    me = lax.axis_index("seq")
    team, lane = me // lanes, lax.rem(me, lanes)
    width = tokens_ref.shape[1]
    wide = windows.shape[2]
    start = (3 * team // 2) * 128
    loads = []
    for part in range(3):
        at = pl.ds(pl.multiple_of(part * width + start, 128), wide)
        loads.append(pltpu.make_async_copy(w_ref.at[:, at], windows.at[part], weight_sems.at[part]))
    for part in range(2):
        at = pl.ds(part * width, 128)
        loads.append(
            pltpu.make_async_copy(w_ref.at[:, at], firsts.at[part], weight_sems.at[3 + part])
        )
    for load in loads:
        load.start()
    def norm():
        tokens = tokens_ref[...]
        row_mean = jnp.mean(tokens, axis=1, keepdims=True)
        centred = tokens - row_mean
        variance = jnp.mean(centred * centred, axis=1, keepdims=True)
        normed = (
            centred * lax.rsqrt(variance + epsilon) * gain_ref[...][None, :] + bias_ref[...][None, :]
        )
        held[team] = normed.astype(jnp.bfloat16)

    greet(["team", "lane"], norm)

    def hop(side, distance, start=True):
        block = team - distance if side == 0 else team + distance
        target = me + lanes if side == 0 else me - lanes
        return push(
            held.at[block],
            held.at[block],
            hop_send.at[side, distance],
            hop_recv.at[side, distance],
            {"seq": target},
            start,
        )

    @pl.when(team < TEAMS - 1)
    def _():
        hop(0, 0)

    @pl.when(team > 0)
    def _():
        hop(1, 0)

    for load in loads:
        load.wait()
    odd = lax.rem(team, 2) == 1
    pieces = []
    for part in range(3):
        window = windows[part]
        pieces.append(
            jnp.where(odd, window[:, wide - TEAM_WIDTH :], window[:, :TEAM_WIDTH])
        )
        if part < 2:
            pieces.append(firsts[part][:, :HEAD_DIM])
    weight_ref[...] = jnp.concatenate(pieces, axis=1)

    def block_copies(block, start):
        copies = []
        for k in range(1, lanes):
            target = {"seq": team * lanes + lax.rem(lane + k, lanes)}
            copies.append(
                push(
                    ready.at[block],
                    query_ref.at[lane, block],
                    team_send.at[block, k],
                    team_recv.at[block, k],
                    target,
                    start,
                )
            )
        for n, (source, destination) in enumerate(
            ((ready.at[block], query_ref.at[lane, block]), (held.at[block], lane_ref.at[block]))
        ):
            copy = pltpu.make_async_copy(source, destination, local_sems.at[n, block])
            if start:
                copy.start()
            copies.append(copy)
        return copies

    def project(block):
        result = dot(held[block], weight_ref[...]).astype(jnp.bfloat16)
        ready[block] = result[:, :QUERY_WIDTH] * jnp.bfloat16(HEAD_DIM ** (-0.5))
        block_copies(block, True)
        key_ref[block] = result[:, QUERY_WIDTH : 2 * QUERY_WIDTH]
        value_ref[block] = result[:, 2 * QUERY_WIDTH :]

    project(team)

    def arrive(step, _):
        distance, side = step // 2 + 1, lax.rem(step, 2)
        for which in range(2):
            block = team - distance if which == 0 else team + distance
            there = (block >= 0) if which == 0 else (block < TEAMS)
            further = (team < TEAMS - 1) if which == 0 else (team > 0)

            @pl.when((side == which) & there)
            def _():
                hop(which, distance - 1, False).wait_recv()

                @pl.when(further)
                def _():
                    hop(which, distance)

                project(block)

        return 0

    lax.fori_loop(0, 2 * (TEAMS - 1), arrive, 0)
    for distance in range(TEAMS - 1):

        @pl.when((team < TEAMS - 1) & (team >= distance))
        def _():
            hop(0, distance, False).wait_send()

        @pl.when((team > 0) & (team + distance < TEAMS))
        def _():
            hop(1, distance, False).wait_send()

    for block in range(TEAMS):
        for copy in block_copies(block, False):
            copy.wait()


def project(tokens, gain, bias, weight, collective):
    lanes = lax.axis_size("seq") // TEAMS
    rows, width = tokens.shape
    inside = pl.BlockSpec(memory_space=pltpu.VMEM)
    anywhere = pl.BlockSpec(memory_space=pl.ANY)
    columns = 2 * QUERY_WIDTH + TEAM_WIDTH
    low = jnp.bfloat16
    dma = pltpu.SemaphoreType.DMA
    return pl.pallas_call(
        project_body,
        out_shape=[
            jax.ShapeDtypeStruct((TEAMS, rows, width), low),
            jax.ShapeDtypeStruct((width, columns), low),
            jax.ShapeDtypeStruct((lanes, TEAMS, rows, QUERY_WIDTH), low),
            jax.ShapeDtypeStruct((TEAMS, rows, QUERY_WIDTH), low),
            jax.ShapeDtypeStruct((TEAMS, rows, TEAM_WIDTH), low),
        ],
        in_specs=[inside, inside, inside, anywhere],
        out_specs=[anywhere, inside, anywhere, inside, inside],
        scratch_shapes=[
            pltpu.VMEM((TEAMS, rows, width), low),
            pltpu.VMEM((TEAMS, rows, QUERY_WIDTH), low),
            pltpu.VMEM((3, width, 256), low),
            pltpu.VMEM((2, width, 128), low),
            dma((2, TEAMS)),
            dma((2, TEAMS)),
            dma((TEAMS, lanes)),
            dma((TEAMS, lanes)),
            dma((5,)),
            dma((2, TEAMS)),
        ],
        compiler_params=pltpu.CompilerParams(
            collective_id=collective, has_side_effects=True, vmem_limit_bytes=VMEM_BYTES
        ),
    )(tokens, gain, bias, weight)


def fold(tile):
    return jnp.sum(tile.reshape(tile.shape[0] // 8, 8, tile.shape[1]), axis=0)


def attend_body(
    length_ref,
    threshold_ref,
    q_ref,
    kk_ref,
    vv_ref,
    out_ref,
    mass_ref,
    carried_ref,
    excess_ref,
    key_heads,
    value_rows,
    running,
    logits,
    out_all,
    mass_all,
    lane_out,
    lane_mass,
    joined_out,
    joined_mass,
    home_out,
    home_mass,
    lane_send,
    lane_recv,
    home_send,
    home_recv,
    *,
    blocks,
    rows,
):
    lanes = blocks // TEAMS
    me = lax.axis_index("seq")
    team, lane = me // lanes, lax.rem(me, lanes)
    i = pl.program_id(0)
    scale = select_scale / (blocks * rows)
    key_iota = lax.broadcasted_iota(jnp.int32, (rows, rows), 0)
    query_iota = lax.broadcasted_iota(jnp.int32, (rows, rows), 1)

    def part_copies(j, start):
        z, owner = j // lanes, lax.rem(j, lanes)
        return [
            push(
                source.at[j],
                destination.at[z, lane],
                lane_send.at[n, j],
                lane_recv.at[n, z, lane],
                {"seq": team * lanes + owner},
                start,
            )
            for n, (source, destination) in enumerate(
                ((out_all, lane_out), (mass_all, lane_mass))
            )
        ]

    def home_copies(z, start):
        return [
            push(
                source.at[z],
                destination.at[team],
                home_send.at[n, z],
                home_recv.at[n, team],
                {"seq": z * lanes + lane},
                start,
            )
            for n, (source, destination) in enumerate(
                ((joined_out, home_out), (joined_mass, home_mass))
            )
        ]

    def join(z):
        for k in range(1, lanes):
            other = lax.rem(lane + k, lanes)
            for n, buffer in enumerate((lane_out, lane_mass)):
                pltpu.make_async_copy(
                    buffer.at[z, other], buffer.at[z, other], lane_recv.at[n, z, other]
                ).wait()
        masses = [lane_mass[z, p] for p in range(lanes)]
        peak = masses[0]
        for p in range(1, lanes):
            peak = jnp.maximum(peak, masses[p])
        shares = [jnp.exp(mass - peak) for mass in masses]
        whole = shares[0]
        for p in range(1, lanes):
            whole = whole + shares[p]
        joined_mass[z] = peak + jnp.log(whole)
        inverse = 1.0 / whole
        for h in range(TEAM_HEADS):
            span = slice(h * HEAD_DIM, (h + 1) * HEAD_DIM)
            mixed = None
            for p in range(lanes):
                share = (shares[p] * inverse)[h : h + 1, :]
                part = lane_out[z, p, span, :].astype(jnp.float32) * share
                mixed = part if p == 0 else mixed + part
            joined_out[z, span, :] = mixed.astype(jnp.bfloat16)

        @pl.when(team != z)
        def _():
            home_copies(z, True)

        @pl.when(team == z)
        def _():
            home_out[team] = joined_out[z]
            home_mass[team] = joined_mass[z]

    @pl.when(i == 0)
    def _():
        greet(["team", "lane"])
        running[...] = jnp.zeros_like(running)
        excess_ref[...] = jnp.zeros_like(excess_ref)
        for z in range(TEAMS):
            for h in range(TEAM_HEADS):
                key_heads[h, z] = kk_ref[z, :, h * HEAD_DIM : (h + 1) * HEAD_DIM]
            first = kk_ref[z, :, TEAM_WIDTH:]
            if z == 0:
                slot = lax.broadcasted_iota(jnp.int32, first.shape, 0) + lane * rows
                first = jnp.where(slot >= 1, first, jnp.zeros_like(first))
            key_heads[TEAM_HEADS, z] = first
            value_rows[z] = vv_ref[z].T

    active = jnp.where(i >= lane, (i - lane) // lanes + 1, 0)
    threshold = threshold_ref[0]

    @pl.when(active == 0)
    def _():
        out_all[i] = jnp.zeros((TEAM_WIDTH, rows), jnp.bfloat16)
        mass_all[i] = jnp.full((8, rows), negative, jnp.float32)

    def work(count):
        q_rows = q_ref[0, 0].T
        heads = [q_rows[h * HEAD_DIM : (h + 1) * HEAD_DIM] for h in range(TEAM_HEADS + 1)]
        earlier = jnp.where(key_iota < query_iota, scale, 0.0).astype(jnp.bfloat16)
        every = jnp.full((rows, rows), scale, jnp.bfloat16)
        last = ((count - 1) * lanes + lane) * rows + key_iota
        query_pos = i * rows + query_iota
        peaks = [None] * TEAM_HEADS
        for z in range(count):
            first = jnp.maximum(dot(key_heads[TEAM_HEADS, z], heads[TEAM_HEADS]), 0.0)
            if z == count - 1:
                first = jnp.where(last < query_pos, first, 0.0)
            first = first.astype(jnp.bfloat16)
            carried = running[z] + dot(first, earlier)
            running[z] = running[z] + dot(first, every)

            if z == count - 1:
                carried = jnp.where(last <= query_pos, carried, -negative)
            carried_ref[0, z] = carried
            for h in range(TEAM_HEADS):
                logit = dot(key_heads[h, z], heads[h]) - carried
                logits[h, z] = logit
                peak = jnp.max(logit.reshape(rows // 8, 8, rows), axis=0)
                peaks[h] = peak if z == 0 else jnp.maximum(peaks[h], peak)
        mass_all[i] = jnp.zeros((8, rows), jnp.float32)
        for h in range(TEAM_HEADS):
            peak = jnp.max(peaks[h], axis=0, keepdims=True)
            mass, mixed = None, None
            for z in range(count):
                terms = jnp.exp(logits[h, z] - peak)
                part = fold(terms)
                values = value_rows[z, h * HEAD_DIM : (h + 1) * HEAD_DIM, :]
                product = dot(values, terms.astype(jnp.bfloat16))
                mass = part if z == 0 else mass + part
                mixed = product if z == 0 else mixed + product
            mass = jnp.sum(mass, axis=0, keepdims=True)
            out_all[i, h * HEAD_DIM : (h + 1) * HEAD_DIM, :] = (mixed * (1.0 / mass)).astype(
                jnp.bfloat16
            )
            mass_all[i, h : h + 1, :] = peak + jnp.log(mass)

        @pl.when(lax.rem(i, TEAMS) == team)
        def _():
            total = None
            for z in range(count):
                carried = carried_ref[0, z]
                if z == count - 1:
                    carried = jnp.where(last < query_pos, carried, 0.0)
                part = fold(jnp.clip(carried - threshold, 0.0, 1.0))
                total = part if z == 0 else total + part
            valid = i * rows + lax.broadcasted_iota(jnp.int32, (8, rows), 1) < length_ref[0]
            excess_ref[...] += jnp.where(valid, total, 0.0)

    for count in range(1, TEAMS + 1):
        pl.when(active == count)(functools.partial(work, count))

    @pl.when(lax.rem(i, lanes) != lane)
    def _():
        part_copies(i, True)

    @pl.when(lax.rem(i, lanes) == lane)
    def _():
        lane_out[i // lanes, lane] = out_all[i]
        lane_mass[i // lanes, lane] = mass_all[i]

    for z in range(TEAMS - 1):
        pl.when(i == (z + 1) * lanes + 1)(functools.partial(join, z))

    @pl.when(i == blocks - 1)
    def _():
        join(TEAMS - 1)

        def drain(j, _):
            @pl.when(lax.rem(j, lanes) != lane)
            def _():
                for copy in part_copies(j, False):
                    copy.wait_send()

            return 0

        lax.fori_loop(0, blocks, drain, 0)
        for z in range(TEAMS):

            @pl.when(team != z)
            def _():
                for copy in home_copies(z, False):
                    copy.wait_send()
                for n, buffer in enumerate((home_out, home_mass)):
                    pltpu.make_async_copy(
                        buffer.at[z], buffer.at[z], home_recv.at[n, z]
                    ).wait()

        out_ref[...] = home_out[...]
        mass_ref[...] = home_mass[...]

def attend(length, threshold, queries, keys, values, blocks, rows, collective):
    lanes = blocks // TEAMS
    smem = pl.BlockSpec(memory_space=pltpu.SMEM)
    whole = pl.BlockSpec((TEAMS, rows, QUERY_WIDTH), lambda i: (0, 0, 0))
    return pl.pallas_call(
        functools.partial(attend_body, blocks=blocks, rows=rows),
        grid=(blocks,),
        in_specs=[
            smem,
            smem,
            pl.BlockSpec(
                (1, 1, rows, QUERY_WIDTH), lambda i: (lax.rem(i, lanes), i // lanes, 0, 0)
            ),
            whole,
            pl.BlockSpec((TEAMS, rows, TEAM_WIDTH), lambda i: (0, 0, 0)),
        ],
        out_specs=[
            pl.BlockSpec((TEAMS, TEAM_WIDTH, rows), lambda i: (0, 0, 0)),
            pl.BlockSpec((TEAMS, 8, rows), lambda i: (0, 0, 0)),
            pl.BlockSpec((1, TEAMS, rows, rows), lambda i: (i, 0, 0, 0)),
            pl.BlockSpec((8, rows), lambda i: (0, 0)),
        ],
        out_shape=[
            jax.ShapeDtypeStruct((TEAMS, TEAM_WIDTH, rows), jnp.bfloat16),
            jax.ShapeDtypeStruct((TEAMS, 8, rows), jnp.float32),
            jax.ShapeDtypeStruct((blocks, TEAMS, rows, rows), jnp.float32),
            jax.ShapeDtypeStruct((8, rows), jnp.float32),
        ],
        scratch_shapes=[
            pltpu.VMEM((TEAM_HEADS + 1, TEAMS, rows, HEAD_DIM), jnp.bfloat16),
            pltpu.VMEM((TEAMS, TEAM_WIDTH, rows), jnp.bfloat16),
            pltpu.VMEM((TEAMS, rows, rows), jnp.float32),
            pltpu.VMEM((TEAM_HEADS, TEAMS, rows, rows), jnp.float32),
            pltpu.VMEM((blocks, TEAM_WIDTH, rows), jnp.bfloat16),
            pltpu.VMEM((blocks, 8, rows), jnp.float32),
            pltpu.VMEM((TEAMS, lanes, TEAM_WIDTH, rows), jnp.bfloat16),
            pltpu.VMEM((TEAMS, lanes, 8, rows), jnp.float32),
            pltpu.VMEM((TEAMS, TEAM_WIDTH, rows), jnp.bfloat16),
            pltpu.VMEM((TEAMS, 8, rows), jnp.float32),
            pltpu.VMEM((TEAMS, TEAM_WIDTH, rows), jnp.bfloat16),
            pltpu.VMEM((TEAMS, 8, rows), jnp.float32),
            pltpu.SemaphoreType.DMA((2, blocks)),
            pltpu.SemaphoreType.DMA((2, TEAMS, lanes)),
            pltpu.SemaphoreType.DMA((2, TEAMS)),
            pltpu.SemaphoreType.DMA((2, TEAMS)),
        ],
        compiler_params=pltpu.CompilerParams(
            collective_id=collective, has_side_effects=True, vmem_limit_bytes=VMEM_BYTES
        ),
    )(length, threshold, queries, keys, values)


reduce_plan = [("lane", "second"), ("team", "spread"), ("team", "spread")]


def added(parts):
    total = parts[0].astype(jnp.float32)
    for part in parts[1:]:
        total = total + part.astype(jnp.float32)
    return total.astype(jnp.bfloat16)


def attend_back_body(
    q_ref,
    grad_ref,
    stat_ref,
    carried_ref,
    kk_ref,
    vv_ref,
    *refs,
    blocks,
    rows,
):
    plan = reduce_plan
    sources, refs = refs[:3], refs[3:]
    (query_grad_ref, key_grad_ref, value_grad_ref), reduced, refs = refs[:3], refs[3:6], refs[6:]
    key_heads, key_rows, value_heads, running, key_sum, value_sum = refs[:6]
    grad_all, stat_all, grad_send, grad_recv, send, receive, local = refs[6:13]
    targets = refs[13:]
    lanes = blocks // TEAMS
    me = lax.axis_index("seq")
    team, lane = me // lanes, lax.rem(me, lanes)
    step = pl.program_id(0)
    i = blocks - 1 - step
    scale = select_scale / (blocks * rows)
    span = [slice(h * HEAD_DIM, (h + 1) * HEAD_DIM) for h in range(TEAM_HEADS + 1)]
    key_iota = lax.broadcasted_iota(jnp.int32, (rows, rows), 0)
    query_iota = lax.broadcasted_iota(jnp.int32, (rows, rows), 1)

    place, owner = i // lanes, lax.rem(i, lanes)

    def grad_copies(z, start):
        return [
            push(
                buffer.at[lane, z],
                buffer.at[lane, z],
                grad_send.at[n, z, k],
                grad_recv.at[n, z, lane],
                {"seq": team * lanes + lax.rem(lane + k, lanes)},
                start,
            )
            for k in range(1, lanes)
            for n, buffer in enumerate((grad_all, stat_all))
        ]

    def own_copy(n):
        scope, kind = plan[n]
        mine = peers_of(scope)[0]
        return pltpu.make_async_copy(
            part_of(kind, sources[n], mine), targets[n].at[mine], local.at[n]
        )

    def plan_copies(scope, start):
        chosen = [n for n in range(len(plan)) if plan[n][0] == scope]
        copies = []
        for n in chosen:
            copies += remote_copies(
                plan[n : n + 1],
                sources[n : n + 1],
                targets[n : n + 1],
                send.at[n : n + 1],
                receive.at[n : n + 1],
                start,
            )
        return copies

    @pl.when(step == 0)
    def _():
        greet(["team", "lane"])
        grad_all[lane] = grad_ref[...]
        stat_all[lane] = stat_ref[...]
        for z in reversed(range(TEAMS)):
            grad_copies(z, True)
        plan_copies("lane", True)
        for n in range(len(plan)):
            own_copy(n).start()
        running[...] = jnp.zeros_like(running)
        key_sum[...] = jnp.zeros_like(key_sum)
        value_sum[...] = jnp.zeros_like(value_sum)
        for z in range(TEAMS):
            for h in range(TEAM_HEADS + 1):
                key_heads[h, z] = kk_ref[z, :, span[h]]
            for h in range(TEAM_HEADS):
                value_heads[h, z] = vv_ref[z, :, span[h]]
            key_rows[z] = kk_ref[z].T
        first = kk_ref[0, :, span[TEAM_HEADS]]
        slot = lax.broadcasted_iota(jnp.int32, first.shape, 0) + lane * rows
        key_heads[TEAM_HEADS, 0] = jnp.where(slot >= 1, first, jnp.zeros_like(first))

    @pl.when(step == 2)
    def _():
        plan_copies("team", True)

    @pl.when(owner != lane)
    def _():
        for n, buffer in enumerate((grad_all, stat_all)):
            at = buffer.at[owner, place]
            pltpu.make_async_copy(at, at, grad_recv.at[n, place, owner]).wait()

    active = jnp.where(i >= lane, (i - lane) // lanes + 1, 0)

    @pl.when(active == 0)
    def _():
        query_grad_ref[...] = jnp.zeros_like(query_grad_ref)

    def work(count):
        q_rows = q_ref[0, 0].T
        grad_rows = grad_all[owner, place].T
        q_row = [q_rows[span[h]] for h in range(TEAM_HEADS + 1)]
        q_col = [q_ref[0, 0, :, span[h]] for h in range(TEAM_HEADS + 1)]
        grad_row = [grad_rows[span[h]] for h in range(TEAM_HEADS)]
        grad_col = [grad_all[owner, place, :, span[h]] for h in range(TEAM_HEADS)]
        mass = [stat_all[owner, place, h : h + 1, :] for h in range(TEAM_HEADS)]
        inner = [stat_all[owner, place, TEAM_HEADS + h : TEAM_HEADS + h + 1, :] for h in range(TEAM_HEADS)]
        later = jnp.where(key_iota > query_iota, -scale, 0.0).astype(jnp.bfloat16)
        every = jnp.full((rows, rows), -scale, jnp.bfloat16)
        last = ((count - 1) * lanes + lane) * rows + key_iota
        query_pos = i * rows + query_iota
        lows = [[] for _ in range(TEAM_HEADS + 1)]
        totals = [None] * count
        for h in range(TEAM_HEADS):
            for z in range(count):
                probs = jnp.exp(dot(key_heads[h, z], q_row[h]) - carried_ref[0, z] - mass[h])
                value_sum[h, z] += dot(probs.astype(jnp.bfloat16), grad_col[h])
                grad_logit = probs * (dot(value_heads[h, z], grad_row[h]) - inner[h])
                totals[z] = grad_logit if h == 0 else totals[z] + grad_logit
                low = grad_logit.astype(jnp.bfloat16)
                key_sum[h, z] += dot(low, q_col[h])
                lows[h].append(low)
        for z in range(count):
            total = totals[z].astype(jnp.bfloat16)
            select_grad = running[z] + dot(total, later)
            running[z] = running[z] + dot(total, every)
            first = dot(key_heads[TEAM_HEADS, z], q_row[TEAM_HEADS])
            live = first > 0.0
            if z == count - 1:
                live = live & (last < query_pos)
            low = jnp.where(live, select_grad, 0.0).astype(jnp.bfloat16)
            key_sum[TEAM_HEADS, z] += dot(low, q_col[TEAM_HEADS])
            lows[TEAM_HEADS].append(low)
        for h in range(TEAM_HEADS + 1):
            left = jnp.concatenate([key_rows[z, span[h], :] for z in range(count)], axis=1)
            result = dot(left, jnp.concatenate(lows[h], axis=0))
            query_grad_ref[0, 0, span[h], :] = result.astype(jnp.bfloat16)

    for count in range(1, TEAMS + 1):
        pl.when(active == count)(functools.partial(work, count))

    @pl.when(step == blocks - 1)
    def _():
        for h in range(TEAM_HEADS + 1):
            key_grad_ref[:, :, span[h]] = key_sum[h].astype(jnp.bfloat16)
        for h in range(TEAM_HEADS):
            value_grad_ref[:, :, span[h]] = value_sum[h].astype(jnp.bfloat16)
        for z in range(TEAMS):
            for copy in grad_copies(z, False):
                copy.wait_send()
        for n in range(len(plan)):
            own_copy(n).wait()
        for scope in ("lane", "team"):
            for copy in plan_copies(scope, False):
                copy.wait()
        for n in range(len(plan)):
            for j in range(reduced[n].shape[0]):
                reduced[n][j] = added([targets[n][k, j] for k in range(targets[n].shape[0])])


def attend_back(queries, grads, stats, carried, keys, values, halves, blocks, rows, collective):
    lanes = blocks // TEAMS
    plan = reduce_plan
    shapes = exchange_shapes(plan, halves)

    def place(step):
        i = blocks - 1 - step
        return (lax.rem(i, lanes), i // lanes, 0, 0)

    return pl.pallas_call(
        functools.partial(attend_back_body, blocks=blocks, rows=rows),
        grid=(blocks,),
        in_specs=[
            pl.BlockSpec((1, 1, rows, QUERY_WIDTH), place),
            pl.BlockSpec((TEAMS, rows, TEAM_WIDTH), lambda step: (0, 0, 0)),
            pl.BlockSpec((TEAMS, 8, rows), lambda step: (0, 0, 0)),
            pl.BlockSpec((1, TEAMS, rows, rows), lambda step: (blocks - 1 - step, 0, 0, 0)),
            pl.BlockSpec((TEAMS, rows, QUERY_WIDTH), lambda step: (0, 0, 0)),
            pl.BlockSpec((TEAMS, rows, TEAM_WIDTH), lambda step: (0, 0, 0)),
        ]
        + [pl.BlockSpec(memory_space=pl.ANY)] * 3,
        out_specs=[
            pl.BlockSpec((1, 1, QUERY_WIDTH, rows), place),
            pl.BlockSpec((TEAMS, rows, QUERY_WIDTH), lambda step: (0, 0, 0)),
            pl.BlockSpec((TEAMS, rows, TEAM_WIDTH), lambda step: (0, 0, 0)),
        ]
        + [pl.BlockSpec(x.shape[1:], lambda step: (0, 0, 0)) for x in shapes],
        out_shape=[
            jax.ShapeDtypeStruct((lanes, TEAMS, QUERY_WIDTH, rows), jnp.bfloat16),
            jax.ShapeDtypeStruct((TEAMS, rows, QUERY_WIDTH), jnp.bfloat16),
            jax.ShapeDtypeStruct((TEAMS, rows, TEAM_WIDTH), jnp.bfloat16),
        ]
        + [jax.ShapeDtypeStruct(x.shape[1:], x.dtype) for x in shapes],
        scratch_shapes=[
            pltpu.VMEM((TEAM_HEADS + 1, TEAMS, rows, HEAD_DIM), jnp.bfloat16),
            pltpu.VMEM((TEAMS, QUERY_WIDTH, rows), jnp.bfloat16),
            pltpu.VMEM((TEAM_HEADS, TEAMS, rows, HEAD_DIM), jnp.bfloat16),
            pltpu.VMEM((TEAMS, rows, rows), jnp.float32),
            pltpu.VMEM((TEAM_HEADS + 1, TEAMS, rows, HEAD_DIM), jnp.float32),
            pltpu.VMEM((TEAM_HEADS, TEAMS, rows, HEAD_DIM), jnp.float32),
            pltpu.VMEM((lanes, TEAMS, rows, TEAM_WIDTH), jnp.bfloat16),
            pltpu.VMEM((lanes, TEAMS, 8, rows), jnp.float32),
            pltpu.SemaphoreType.DMA((2, TEAMS, lanes)),
            pltpu.SemaphoreType.DMA((2, TEAMS, lanes)),
        ]
        + exchange_sems(plan)
        + [pltpu.VMEM(x.shape, x.dtype) for x in shapes],
        compiler_params=pltpu.CompilerParams(
            collective_id=collective, has_side_effects=True, vmem_limit_bytes=VMEM_BYTES
        ),
    )(queries, grads, stats, carried, keys, values, *halves)


def finish_body(
    query_ref,
    key_ref,
    value_ref,
    lane_ref,
    weight_ref,
    gain_ref,
    bias_ref,
    norm_ref,
    excess_ref,
    length_ref,
    down_in,
    up_in,
    out_in,
    whole_ref,
    home_ref,
    total_ref,
    whole_down,
    whole_up,
    whole_out,
    query_parts,
    down_parts,
    up_parts,
    out_parts,
    down_ref,
    up_ref,
    out_ref,
    turned,
    weight_rows,
    weight_grad,
    rows_sum,
    rows_ref,
    main_ref,
    vector_ref,
    core_main,
    send_main,
    lane_main,
    team_send_main,
    team_main,
    assembled,
    vectors,
    ready,
    core_sems,
    lane_sems,
    team_sems,
    home_sems,
    vector_sems,
    out_lane_sems,
    out_core_sems,
    local_sems,
    early_team,
    early_lane,
    early_core,
    early_local,
    first_send,
    first_recv,
    first_local,
):
    lanes = lax.axis_size("seq") // TEAMS
    me = lax.axis_index("seq")
    core = lax.axis_index("batch")
    team, lane = me // lanes, lax.rem(me, lanes)

    def lane_peer(k):
        other = lax.rem(lane + k, lanes)
        return other, {"seq": team * lanes + other}

    def team_peer(k):
        other = lax.rem(team + k, TEAMS)
        return other, {"seq": other * lanes + lane}

    sibling = {"batch": 1 - core}
    spans = (slice(0, QUERY_WIDTH), slice(QUERY_WIDTH, 2 * QUERY_WIDTH), slice(2 * QUERY_WIDTH, None))

    def turn():
        for span in spans:
            weight_rows[span, :] = weight_ref[:, span].T
        weight_grad[...] = jnp.zeros_like(weight_grad)

    greet(["core", "team", "lane"], turn)
    first_sources = (query_ref, down_in, up_in, out_in)
    first_targets = (query_parts, down_parts, up_parts, out_parts)
    first_plan = [("team", "spread"), ("team", "spread"), ("lane", "spread"), ("lane", "spread")]
    first_copies = [[], [], []]
    for n in (1, 2, 3, 0):
        mine = peers_of(first_plan[n][0])[0]
        own = pltpu.make_async_copy(first_sources[n].at[mine], first_targets[n].at[mine], first_local.at[n])
        own.start()
        group = (2, 0, 1, 1)[n]
        first_copies[group].append(own)
        first_copies[group] += remote_copies(
            first_plan[n : n + 1],
            first_sources[n : n + 1],
            first_targets[n : n + 1],
            first_send.at[n : n + 1],
            first_recv.at[n : n + 1],
        )
    def place(n, p, t, part=None):
        if n == 0:
            ref, start, wide = whole_down.at[core, p, t], 0, whole_down.shape[4]
        else:
            ref = (None, whole_up, whole_out)[n]
            wide = ref.shape[3] // 2
            ref, start = ref.at[p, t], core * wide
        cut = (wide // 128 + 1) // 2 * 128
        if part is not None:
            start, wide = ((start, cut), (start + cut, wide - cut))[part]
        return ref.at[:, pl.ds(pl.multiple_of(start, 128), wide)]

    square = lanes == 4
    if square:
        across, along = lax.rem(lane, 2), lane // 2
        direct = [2 * along + 1 - across, 2 * (1 - along) + across]
        origins = direct
    else:
        direct = [lax.rem(lane + k, lanes) for k in range(1, lanes)]
        origins = [lax.rem(lane - k + lanes, lanes) for k in range(1, lanes)]
    corner = lanes - 1 - lane

    def lane_of(p):
        return {"seq": team * lanes + p}

    def landed(ref, sem):
        pltpu.make_async_copy(ref, ref, sem).wait()

    early = (down_ref, up_ref, out_ref)
    number = len(early)
    early_z = [[None] * TEAMS for _ in range(number)]
    early_kept = []

    def publish(n):
        for k in range(1, TEAMS):
            _, target = team_peer(k)
            sems = [early_team.at[side, n, k] for side in range(2)]
            early_z[n][k] = push(early[n], place(n, lane, team), *sems, target)
        copy = pltpu.make_async_copy(early[n], place(n, lane, team), early_local.at[n])
        copy.start()
        early_kept.append(copy)

    early_out = []
    early_sib = []

    def forward(j, chosen=(0, 1, 2)):
        t = lax.rem(team - j + TEAMS, TEAMS)
        for n in chosen:
            if j == 0:
                source = early[n]
            else:
                early_z[n][j].wait_recv()
                source = place(n, lane, t)
            target = place(n, lane, t)
            for m, p in enumerate(direct):
                sems = [early_lane.at[side, n, j, m] for side in range(2)]
                early_out.append(push(source, target, *sems, lane_of(p)))
            sems = [early_core.at[side, n, j, 0] for side in range(2)]
            early_sib.append(push(source, target, *sems, sibling))

    def relay(j):
        t = lax.rem(team - j + TEAMS, TEAMS)
        for n in range(number):
            for m, p in enumerate(origins):
                piece = place(n, p, t)
                landed(piece, early_lane.at[1, n, j, m])
                if square:
                    side = place(n, p, t, m)
                    sems = [early_lane.at[side_, n, j, 2 + m] for side_ in range(2)]
                    early_out.append(push(side, side, *sems, lane_of(direct[1 - m])))
                sems = [early_core.at[side_, n, j, 1 + m] for side_ in range(2)]
                early_sib.append(push(piece, piece, *sems, sibling))

    def settle(j):
        if not square:
            return
        t = lax.rem(team - j + TEAMS, TEAMS)
        for n in range(number):
            for m in range(2):
                landed(place(n, corner, t, m), early_lane.at[1, n, j, 2 + m])
            piece = place(n, corner, t)
            sems = [early_core.at[side, n, j, 3] for side in range(2)]
            early_sib.append(push(piece, piece, *sems, sibling))

    for copy in first_copies[0]:
        copy.wait()
    down_ref[...] = added([down_parts[k] for k in range(lanes)])
    publish(0)
    forward(0, (0,))

    def known(b, _):
        rows_low = lane_ref[b].T
        turned[b] = rows_low
        total = None
        for span, grads in ((spans[1], key_ref[b]), (spans[2], value_ref[b])):
            weight_grad[:, span] += dot(rows_low, grads)
            part = dot(grads, weight_rows[span, :])
            total = part if total is None else total + part
        rows_sum[b] = total
        return 0

    lax.fori_loop(0, TEAMS, known, 0)
    for copy in first_copies[1]:
        copy.wait()
    up_ref[...] = added([up_parts[k] for k in range(TEAMS)])
    out_ref[...] = added([out_parts[k] for k in range(TEAMS)])
    publish(1)
    publish(2)
    forward(0, (1, 2))
    for copy in first_copies[2]:
        copy.wait()
    gain = gain_ref[...][None, :]
    bias = bias_ref[...][None, :]

    def last(b, sums):
        query_rows = query_parts[0, b].astype(jnp.float32)
        for p in range(1, lanes):
            query_rows = query_rows + query_parts[p, b].astype(jnp.float32)
        grads = (query_rows * HEAD_DIM ** (-0.5)).astype(jnp.bfloat16).T
        weight_grad[:, spans[0]] += dot(turned[b], grads)
        total = rows_sum[b] + dot(grads, weight_rows[spans[0], :])
        rows_ref[b] = total.astype(jnp.bfloat16)
        shifted = lane_ref[b].astype(jnp.float32) - bias
        return (
            sums[0] + jnp.sum(total * shifted, axis=0, keepdims=True),
            sums[1] + jnp.sum(total, axis=0, keepdims=True),
        )

    nothing = jnp.zeros_like(gain)
    gain_sum, bias_sum = lax.fori_loop(0, TEAMS, last, (nothing, nothing))
    length = length_ref[0].astype(jnp.float32)
    pairs = (length - 1.0) * (length - 2.0) / (2.0 * TEAMS * lanes)
    excess = jnp.sum(jnp.sum(excess_ref[...], axis=0, keepdims=True), axis=1, keepdims=True)
    vector_ref[...] = jnp.zeros_like(vector_ref)
    vector_ref[0:1, :] = gain_sum / gain
    vector_ref[1:2, :] = bias_sum
    vector_ref[2:4, :] = norm_ref[...]
    vector_ref[4:5, :] = jnp.broadcast_to(excess, nothing.shape)
    vector_ref[5:6, :] = jnp.full(nothing.shape, pairs)
    depth = main_ref.shape[1]
    for chunk in range(2 * lanes):
        main_ref[chunk] = weight_grad[chunk * depth : (chunk + 1) * depth, :].astype(jnp.bfloat16)
    theirs = pl.ds((1 - core) * lanes, lanes)
    core_copies = [
        push(main_ref.at[theirs], core_main, core_sems.at[0, 0], core_sems.at[1, 0], sibling),
        push(vector_ref, vectors.at[0], vector_sems.at[0, 0], vector_sems.at[1, 0], sibling),
    ]
    for copy in core_copies:
        copy.wait()
    relay(0)

    both = vector_ref[...] + vectors[0]
    vectors[1 + lane] = both
    ready[0] = both
    for j in range(lanes):
        send_main[j] = (
            main_ref[core * lanes + j].astype(jnp.float32) + core_main[j].astype(jnp.float32)
        ).astype(jnp.bfloat16)
    lane_copies = []
    for k in range(1, lanes):
        other, target = lane_peer(k)
        lane_copies += [
            push(send_main.at[other], lane_main.at[lane], lane_sems.at[0, 0, k], lane_sems.at[1, 0, k], target),
            push(ready.at[0], vectors.at[1 + lane], vector_sems.at[0, k], vector_sems.at[1, k], target),
        ]
    lane_main[lane] = send_main[lane]
    for copy in lane_copies:
        copy.wait()

    def total(ref, start, number):
        result = ref[start].astype(jnp.float32)
        for j in range(1, number):
            result = result + ref[start + j].astype(jnp.float32)
        return result

    whole_vector = total(vectors, 1, lanes)
    ready[1] = whole_vector
    vectors[1 + lanes + team] = whole_vector
    low_main = total(lane_main, 0, lanes).astype(jnp.bfloat16)
    team_send_main[...] = low_main
    team_main[team] = low_main
    team_copies = []
    for k in range(1, TEAMS):
        other, target = team_peer(k)
        at = lanes + k
        team_copies += [
            push(team_send_main, team_main.at[team], team_sems.at[0, 0, k], team_sems.at[1, 0, k], target),
            push(ready.at[1], vectors.at[1 + lanes + team], vector_sems.at[0, at], vector_sems.at[1, at], target),
        ]
    home_copies = []
    for k in range(1, TEAMS):
        other, target = team_peer(k)
        home_copies.append(
            push(rows_ref.at[other], home_ref.at[team], home_sems.at[0, k], home_sems.at[1, k], target)
        )
    own = pltpu.make_async_copy(rows_ref.at[team], home_ref.at[team], local_sems.at[0])
    own.start()
    for j in range(1, TEAMS):
        forward(j)
        settle(j - 1)
        if j < TEAMS - 1:
            relay(j)
    for copy in team_copies:
        copy.wait()
    total_ref[...] = total(vectors, 1 + lanes, TEAMS)
    pieces = []
    for part in range(3):
        first = part * QUERY_WIDTH
        for g in range(TEAMS):
            piece = team_main[g, :, first : first + TEAM_WIDTH]
            if g == 0 and part < 2:
                more = piece[:, :HEAD_DIM].astype(jnp.float32)
                for other in range(TEAMS):
                    more = more + team_main[
                        other, :, first + TEAM_WIDTH : first + QUERY_WIDTH
                    ].astype(jnp.float32)
                pieces += [more.astype(jnp.bfloat16), piece[:, HEAD_DIM:]]
            else:
                pieces.append(piece)
    assembled[...] = jnp.concatenate(pieces, axis=1)

    def chunk_of(p, part=None):
        ref = whole_ref.at[core * lanes + p]
        half = whole_ref.shape[2] // 2
        return ref if part is None else ref.at[:, pl.ds(part * half, half)]

    out_copies, core_out = [], []
    for m, p in enumerate(direct):
        sems = [out_lane_sems.at[side, m] for side in range(2)]
        out_copies.append(push(assembled, chunk_of(lane), *sems, lane_of(p)))
    sems = [out_core_sems.at[side, 0] for side in range(2)]
    core_out.append(push(assembled, chunk_of(lane), *sems, sibling))
    kept = pltpu.make_async_copy(assembled, chunk_of(lane), local_sems.at[1])
    kept.start()
    relay(TEAMS - 1)
    for m, p in enumerate(origins):
        landed(chunk_of(p), out_lane_sems.at[1, m])
        if square:
            sems = [out_lane_sems.at[side, 2 + m] for side in range(2)]
            out_copies.append(push(chunk_of(p, m), chunk_of(p, m), *sems, lane_of(direct[1 - m])))
        sems = [out_core_sems.at[side, 1 + m] for side in range(2)]
        core_out.append(push(chunk_of(p), chunk_of(p), *sems, sibling))
    settle(TEAMS - 1)
    if square:
        for m in range(2):
            landed(chunk_of(corner, m), out_lane_sems.at[1, 2 + m])
        sems = [out_core_sems.at[side, 3] for side in range(2)]
        core_out.append(push(chunk_of(corner), chunk_of(corner), *sems, sibling))
    for copy in out_copies + early_out:
        copy.wait_send()
    for n in range(number):
        for k in range(1, TEAMS):
            early_z[n][k].wait_send()
    for copy in core_out + home_copies + early_sib + early_kept:
        copy.wait()
    own.wait()
    kept.wait()


def finish(
    queries, keys, values, lane_rows, weight, gain, bias, norm, excess, length, reduced, collective
):
    lanes = lax.axis_size("seq") // TEAMS
    width, columns = weight.shape
    rows = lane_rows.shape[1]
    vector = (8, width)
    chunks, depth = 2 * lanes, width // (2 * lanes)
    low = jnp.bfloat16
    dma = pltpu.SemaphoreType.DMA
    down, up, out = (x.shape[1:] for x in reduced)
    wholes = [
        (2, lanes, TEAMS) + down,
        (lanes, TEAMS, up[0], 2 * up[1]),
        (lanes, TEAMS, out[0], 2 * out[1]),
    ]
    anywhere = pl.BlockSpec(memory_space=pl.ANY)
    inside = pl.BlockSpec(memory_space=pltpu.VMEM)
    return pl.pallas_call(
        finish_body,
        out_shape=[
            jax.ShapeDtypeStruct((chunks, depth, 3 * width), low),
            jax.ShapeDtypeStruct(lane_rows.shape, low),
            jax.ShapeDtypeStruct(vector, jnp.float32),
        ]
        + [jax.ShapeDtypeStruct(shape, low) for shape in wholes],
        in_specs=[anywhere]
        + [inside] * 8
        + [pl.BlockSpec(memory_space=pltpu.SMEM)]
        + [anywhere] * 3,
        out_specs=[anywhere, anywhere, inside] + [anywhere] * 3,
        scratch_shapes=[
            pltpu.VMEM(queries.shape, low),
            pltpu.VMEM((lanes,) + down, low),
            pltpu.VMEM((TEAMS,) + up, low),
            pltpu.VMEM((TEAMS,) + out, low),
            pltpu.VMEM(down, low),
            pltpu.VMEM(up, low),
            pltpu.VMEM(out, low),
            pltpu.VMEM((TEAMS, width, rows), low),
            pltpu.VMEM((columns, width), low),
            pltpu.VMEM((width, columns), jnp.float32),
            pltpu.VMEM((TEAMS, rows, width), jnp.float32),
            pltpu.VMEM((TEAMS, rows, width), low),
            pltpu.VMEM((chunks, depth, columns), low),
            pltpu.VMEM(vector, jnp.float32),
            pltpu.VMEM((lanes, depth, columns), low),
            pltpu.VMEM((lanes, depth, columns), low),
            pltpu.VMEM((lanes, depth, columns), low),
            pltpu.VMEM((depth, columns), low),
            pltpu.VMEM((TEAMS, depth, columns), low),
            pltpu.VMEM((depth, 3 * width), low),
            pltpu.VMEM((1 + lanes + TEAMS,) + vector, jnp.float32),
            pltpu.VMEM((2,) + vector, jnp.float32),
            dma((2, 2)),
            dma((2, 2, lanes)),
            dma((2, 2, TEAMS)),
            dma((2, TEAMS)),
            dma((2, lanes + TEAMS)),
            dma((2, lanes)),
            dma((2, lanes)),
            dma((2,)),
            dma((2, 3, TEAMS)),
            dma((2, 3, TEAMS, lanes)),
            dma((2, 3, TEAMS, lanes)),
            dma((3,)),
            dma((4, max(lanes, TEAMS))),
            dma((4, max(lanes, TEAMS))),
            dma((4,)),
        ],
        compiler_params=pltpu.CompilerParams(
            collective_id=collective, has_side_effects=True, vmem_limit_bytes=VMEM_BYTES
        ),
    )(queries, keys, values, lane_rows, weight, gain, bias, norm, excess, length, *reduced)


def contract_cols(left, right):
    return lax.dot_general(left, right, (((1,), (1,)), ((), ())), preferred_element_type=jnp.float32)


def dense_body(
    length_ref,
    mixed_ref,
    mass_ref,
    tokens_ref,
    grad_ref,
    gain_ref,
    bias_ref,
    w_out_hbm,
    w_up_hbm,
    w_down_hbm,
    layer_ref,
    resid_ref,
    norm_ref,
    cols_ref,
    stats_ref,
    down_hbm,
    up_hbm,
    out_hbm,
    w_out,
    w_up,
    w_down,
    active,
    slope,
    top,
    normed,
    mixed,
    slant,
    active_other,
    slope_other,
    top_other,
    normed_other,
    mixed_other,
    slant_other,
    total,
    back,
    cols,
    stats,
    down_half,
    up_half,
    out_half,
    load_sems,
    core_sems,
    lane_sems,
    keep_sems,
    store_sems,
):
    rows, width = tokens_ref.shape
    hidden = w_up.shape[1]
    step = width
    count = lax.axis_size("seq")
    lanes = count // TEAMS
    me = lax.axis_index("seq")
    core = lax.axis_index("batch")
    team, lane = me // lanes, lax.rem(me, lanes)
    sibling = {"batch": 1 - core}
    loads = [
        pltpu.make_async_copy(source, target, load_sems.at[n])
        for n, (source, target) in enumerate(
            ((w_out_hbm, w_out), (w_up_hbm, w_up), (w_down_hbm, w_down))
        )
    ]
    for load in loads:
        load.start()
    greet(["core", "lane"])

    def half_of(ref, which):
        half = ref.shape[1] // 2
        return ref.at[:, pl.ds(pl.multiple_of(which * half, 128), half)]

    pairs = (
        (active, active_other, True),
        (top, top_other, False),
        (normed, normed_other, False),
        (slope, slope_other, True),
        (mixed, mixed_other, False),
        (slant, slant_other, True),
    )

    def swap(n, start):
        source, target, halved = pairs[n]
        return push(
            half_of(source, 1 - core) if halved else source,
            target,
            core_sems.at[0, n],
            core_sems.at[1, n],
            sibling,
            start,
        )

    grad_top = grad_ref[...]
    top[...] = grad_top.astype(jnp.bfloat16)
    swap(1, True)
    valid = me * rows + lax.broadcasted_iota(jnp.int32, (rows, width), 0) < length_ref[0]
    mixed_rows = mixed_ref[...]
    mixed[...] = jnp.where(valid, mixed_rows.T, jnp.zeros((), jnp.bfloat16))
    swap(4, True)
    loads[0].wait()
    residual = tokens_ref[...] + dot(mixed[...], w_out[...])
    row_mean = jnp.mean(residual, axis=1, keepdims=True)
    centred = residual - row_mean
    variance = jnp.mean(centred * centred, axis=1, keepdims=True)
    spread = lax.rsqrt(variance + epsilon)
    scaled = centred * spread
    gain = gain_ref[...][None, :]
    normed[...] = (scaled * gain + bias_ref[...][None, :]).astype(jnp.bfloat16)
    swap(2, True)
    total[...] = residual
    back[...] = jnp.zeros_like(back)
    loads[1].wait()
    loads[2].wait()

    def chunk(c, _):
        at = pl.ds(pl.multiple_of(c * step, 128), step)
        up = w_up[:, at]
        down = w_down[at, :]
        u = dot(normed[...], up)
        squared = u * u
        bend = jnp.tanh(0.7978845608028654 * u * (1.0 + 0.044715 * squared))
        lift = 0.5 * (1.0 + bend)
        low = (u * lift).astype(jnp.bfloat16)
        active[:, at] = low
        turn = lift + (0.5 * 0.7978845608028654) * u * (1.0 - bend * bend) * (
            1.0 + (3.0 * 0.044715) * squared
        )
        grad_low = (contract_cols(top[...], down) * turn).astype(jnp.bfloat16)
        slope[:, at] = grad_low
        total[...] += dot(low, down)
        back[...] += contract_cols(grad_low, up)
        return 0

    lax.fori_loop(0, hidden // step, chunk, 0)
    swap(0, True)
    swap(3, True)
    layer_ref[...] = total[...]
    grad_normed = back[...]
    norm_ref[0:1, :] = jnp.sum(grad_normed * scaled, axis=0, keepdims=True)
    norm_ref[1:2, :] = jnp.sum(grad_normed, axis=0, keepdims=True)
    inner = grad_normed * gain
    resid = grad_top + spread * (
        inner
        - jnp.mean(inner, axis=1, keepdims=True)
        - scaled * jnp.mean(inner * scaled, axis=1, keepdims=True)
    )
    resid_ref[...] = resid
    slant[...] = resid.astype(jnp.bfloat16)
    swap(5, True)
    grad_mixed = contract_cols(slant[...], w_out[...]).astype(jnp.bfloat16)
    grad_mixed = jnp.where(valid, grad_mixed, jnp.zeros((), jnp.bfloat16))
    products = grad_mixed.T.astype(jnp.float32) * mixed_rows.astype(jnp.float32)
    for t in range(TEAMS):
        cols[t] = grad_mixed[:, t * TEAM_WIDTH : (t + 1) * TEAM_WIDTH]
        stats[t] = mass_ref[t]
        for h in range(TEAM_HEADS):
            first = t * TEAM_WIDTH + h * HEAD_DIM
            stats[t, TEAM_HEADS + h : TEAM_HEADS + h + 1, :] = jnp.sum(
                products[first : first + HEAD_DIM], axis=0, keepdims=True
            )
    copies = []
    for k in range(1, TEAMS):
        other = lax.rem(team + k, TEAMS)
        for n, (source, target) in enumerate(((cols, cols_ref), (stats, stats_ref))):
            copies.append(
                push(
                    source.at[other],
                    target.at[team],
                    lane_sems.at[0, n, k],
                    lane_sems.at[1, n, k],
                    {"seq": other * lanes + lane},
                )
            )
    for n, (source, target) in enumerate(((cols, cols_ref), (stats, stats_ref))):
        copy = pltpu.make_async_copy(source.at[team], target.at[team], keep_sems.at[n])
        copy.start()
        copies.append(copy)

    def pair_dot(left, left_other, right, right_other, at):
        return (
            dot(left[:, at].T, right[...]) + dot(left_other[:, at].T, right_other[...])
        ).astype(jnp.bfloat16)

    for n in range(len(pairs)):
        swap(n, False).wait()
    block = 384
    own_active = half_of(active, core)
    own_slope = half_of(slope, core)
    own_slant = half_of(slant, core)

    def down_rows(c, _):
        at = pl.ds(pl.multiple_of(c * block, 128), block)
        down_half[at, :] = pair_dot(own_active, active_other, top, top_other, at)
        return 0

    lax.fori_loop(0, down_half.shape[0] // block, down_rows, 0)
    stores = [pltpu.make_async_copy(down_half, down_hbm, store_sems.at[0])]
    stores[0].start()

    def up_rows(c, _):
        at = pl.ds(pl.multiple_of(c * block, 128), block)
        up_half[at, :] = pair_dot(normed, normed_other, own_slope, slope_other, at)
        out_half[at, :] = pair_dot(mixed, mixed_other, own_slant, slant_other, at)
        return 0

    lax.fori_loop(0, width // block, up_rows, 0)
    for n, (source, target) in enumerate(((up_half, up_hbm), (out_half, out_hbm))):
        copy = pltpu.make_async_copy(source, target, store_sems.at[1 + n])
        copy.start()
        stores.append(copy)
    for copy in copies + stores:
        copy.wait()


def dense(length, mixed, masses, tokens, grad, gain, bias, w_out, w_up, w_down, collective):
    rows, width = tokens.shape
    hidden = w_up.shape[1]
    low, full = jnp.bfloat16, jnp.float32
    inside = pl.BlockSpec(memory_space=pltpu.VMEM)
    anywhere = pl.BlockSpec(memory_space=pl.ANY)
    dma = pltpu.SemaphoreType.DMA
    half = hidden // 2
    return pl.pallas_call(
        dense_body,
        out_shape=[
            jax.ShapeDtypeStruct((rows, width), full),
            jax.ShapeDtypeStruct((rows, width), full),
            jax.ShapeDtypeStruct((2, width), full),
            jax.ShapeDtypeStruct((TEAMS, rows, TEAM_WIDTH), low),
            jax.ShapeDtypeStruct((TEAMS, 8, rows), full),
            jax.ShapeDtypeStruct((half, width), low),
            jax.ShapeDtypeStruct((width, half), low),
            jax.ShapeDtypeStruct((width, width // 2), low),
        ],
        in_specs=[pl.BlockSpec(memory_space=pltpu.SMEM)] + [inside] * 6 + [anywhere] * 3,
        out_specs=[inside] * 3 + [anywhere] * 5,
        scratch_shapes=[
            pltpu.VMEM((width, width), low),
            pltpu.VMEM((width, hidden), low),
            pltpu.VMEM((hidden, width), low),
            pltpu.VMEM((rows, hidden), low),
            pltpu.VMEM((rows, hidden), low),
            pltpu.VMEM((rows, width), low),
            pltpu.VMEM((rows, width), low),
            pltpu.VMEM((rows, width), low),
            pltpu.VMEM((rows, width), low),
            pltpu.VMEM((rows, half), low),
            pltpu.VMEM((rows, half), low),
            pltpu.VMEM((rows, width), low),
            pltpu.VMEM((rows, width), low),
            pltpu.VMEM((rows, width), low),
            pltpu.VMEM((rows, width // 2), low),
            pltpu.VMEM((rows, width), full),
            pltpu.VMEM((rows, width), full),
            pltpu.VMEM((TEAMS, rows, TEAM_WIDTH), low),
            pltpu.VMEM((TEAMS, 8, rows), full),
            pltpu.VMEM((half, width), low),
            pltpu.VMEM((width, half), low),
            pltpu.VMEM((width, width // 2), low),
            dma((3,)),
            dma((2, 6)),
            dma((2, 2, TEAMS)),
            dma((2,)),
            dma((3,)),
        ],
        compiler_params=pltpu.CompilerParams(
            collective_id=collective, has_side_effects=True, vmem_limit_bytes=VMEM_BYTES
        ),
    )(length, mixed, masses, tokens, grad, gain, bias, w_out, w_up, w_down)


def close_body(
    tokens_ref,
    gain_ref,
    resid_ref,
    home_ref,
    layer_ref,
    vector_ref,
    *refs,
):
    count = (len(refs) - 6) // 2
    weights, refs = refs[:count], refs[count:]
    grad_ref, layer_out, *refs = refs
    for source, target in zip(weights, refs[:count]):
        target[...] = source[...].astype(jnp.float32)
    layer_out[...] = layer_ref[...]
    tokens = tokens_ref[...]
    centred = tokens - jnp.mean(tokens, axis=1, keepdims=True)
    spread = lax.rsqrt(jnp.mean(centred * centred, axis=1, keepdims=True) + epsilon)
    scaled = centred * spread
    total = home_ref[0].astype(jnp.float32)
    for t in range(1, TEAMS):
        total = total + home_ref[t].astype(jnp.float32)
    inner = total * gain_ref[...][None, :]
    grad_ref[...] = resid_ref[...] + spread * (
        inner
        - jnp.mean(inner, axis=1, keepdims=True)
        - scaled * jnp.mean(inner * scaled, axis=1, keepdims=True)
    )

    @pl.when(pl.program_id(0) == 0)
    def _():
        for n in range(4):
            refs[count + n][...] = vector_ref[n]


def close(tokens, gain, resid, home, layer, vectors, weights):
    steps = 4
    rows, width = tokens.shape

    def band(x):
        return pl.BlockSpec((x.shape[0] // steps, x.shape[1]), lambda i: (i, 0))

    line = pl.BlockSpec((width,), lambda i: (0,))
    large = [tokens, layer] + weights
    return pl.pallas_call(
        close_body,
        grid=(steps,),
        in_specs=[
            band(tokens),
            line,
            band(resid),
            pl.BlockSpec((TEAMS, rows // steps, width), lambda i: (0, i, 0)),
            band(layer),
            pl.BlockSpec(vectors.shape, lambda i: (0, 0)),
        ]
        + [band(x) for x in weights],
        out_specs=[band(x) for x in large] + [line] * 4,
        out_shape=[jax.ShapeDtypeStruct(x.shape, jnp.float32) for x in large]
        + [jax.ShapeDtypeStruct((width,), jnp.float32)] * 4,
        compiler_params=pltpu.CompilerParams(vmem_limit_bytes=VMEM_BYTES),
    )(tokens, gain, resid, home, layer, vectors, *weights)


def per_device(
    block_input,
    ln1_gain,
    ln1_bias,
    w_qkv,
    w_out,
    ln2_gain,
    ln2_bias,
    w_up,
    w_down,
    length_draw,
    threshold_index,
    grad_out,
):
    rows = block_input.shape[1]
    width = block_input.shape[2]
    blocks = lax.axis_size("seq")
    lanes = blocks // TEAMS
    group_len = blocks * rows
    me = lax.axis_index("seq")
    team = me // lanes
    length = group_len - rows + 1 + length_draw % rows
    threshold = threshold_index.astype(jnp.float32) / 128.0
    tokens = block_input[0]
    grad_top = grad_out[0]

    lane_rows, team_weight, queries, keys, values = project(tokens, ln1_gain, ln1_bias, w_qkv, 0)

    head_out, masses, carried, excess = attend(
        length, threshold, queries, keys, values, blocks, rows, 1
    )
    layer_out, grad_resid, grad_ln2, grad_cols, stats, down_half, up_half, out_half = dense(
        length,
        head_out.reshape(width, rows),
        masses,
        tokens,
        grad_top,
        ln2_gain,
        ln2_bias,
        w_out,
        w_up,
        w_down,
        3,
    )
    halves = [x.reshape(lanes, TEAMS, -1, x.shape[1]) for x in (down_half, up_half, out_half)]
    query_grads, key_grads, value_grads, *halves = attend_back(
        queries, grad_cols, stats, carried, keys, values, halves, blocks, rows, 7
    )

    grad_w_qkv, home_rows, vectors, grad_w_down, grad_w_up, grad_w_out = finish(
        query_grads,
        key_grads,
        value_grads,
        lane_rows,
        team_weight,
        ln1_gain,
        ln1_bias,
        grad_ln2,
        excess,
        length,
        halves,
        6,
    )
    pruned_share = (vectors[4, 0] / vectors[5, 0]).reshape(1)
    grad_x, layer_out, grad_w_qkv, grad_w_out, grad_w_up, grad_w_down, *lines = close(
        tokens,
        ln1_gain,
        grad_resid,
        home_rows,
        layer_out,
        vectors,
        [
            grad_w_qkv.reshape(w_qkv.shape),
            grad_w_out.reshape(w_out.shape),
            grad_w_up.reshape(w_up.shape),
            grad_w_down.reshape(w_down.shape),
        ],
    )
    return (
        layer_out[None],
        grad_x[None],
        lines[0],
        lines[1],
        grad_w_qkv,
        grad_w_out,
        lines[2],
        lines[3],
        grad_w_up,
        grad_w_down,
        pruned_share,
    )


def solution(mesh):
    placed = (
        P("batch", "seq", None),
        P(),
        P(),
        P(),
        P(),
        P(),
        P(),
        P(),
        P(),
        P("batch"),
        P(),
        P("batch", "seq", None),
    )
    return jax.shard_map(
        per_device,
        mesh=mesh,
        in_specs=placed,
        out_specs=(
            P("batch", "seq", None),
            P("batch", "seq", None),
            P(),
            P(),
            P(),
            P(),
            P(),
            P(),
            P(),
            P(),
            P(),
        ),
        check_vma=False,
    )
```

```python
import functools

import jax
import jax.numpy as jnp
from jax import lax
from jax.experimental import pallas as pl
from jax.experimental.pallas import tpu as pltpu
from jax.sharding import PartitionSpec as P

HEADS = 12
HEAD_DIM = 64
TEAMS = 4
TEAM_HEADS = HEADS // TEAMS
TEAM_WIDTH = TEAM_HEADS * HEAD_DIM
QUERY_WIDTH = TEAM_WIDTH + HEAD_DIM

epsilon = 1e-05
negative = -1e30
select_scale = 3.0
VMEM_BYTES = 60 * 2**20
MESH = pl.DeviceIdType.MESH


def peers_of(scope):
    lanes = lax.axis_size("seq") // TEAMS
    me = lax.axis_index("seq")
    team, lane = me // lanes, lax.rem(me, lanes)
    if scope == "team":
        return lane, lanes, lambda k: {"seq": team * lanes + k}
    if scope == "lane":
        return team, TEAMS, lambda k: {"seq": k * lanes + lane}
    if scope == "core":
        return lax.axis_index("batch"), 2, lambda k: {"batch": k}
    return me, lanes * TEAMS, lambda k: {"seq": k}


def scope_size(scope):
    count = lax.axis_size("seq")
    return {"team": count // TEAMS, "lane": TEAMS, "core": 2, "all": count}[scope]


def greet(scopes, meanwhile=None):
    barrier = pltpu.get_barrier_semaphore()
    number = 0
    for scope in scopes:
        mine, peers, device_of = peers_of(scope)
        for k in range(1, peers):
            pl.semaphore_signal(
                barrier, inc=1, device_id=device_of(lax.rem(mine + k, peers)), device_id_type=MESH
            )
        number += peers - 1
    if meanwhile is not None:
        meanwhile()
    pl.semaphore_wait(barrier, number)


def push(source, destination, send, receive, target, start=True):
    copy = pltpu.make_async_remote_copy(
        src_ref=source,
        dst_ref=destination,
        send_sem=send,
        recv_sem=receive,
        device_id=target,
        device_id_type=MESH,
    )
    if start:
        copy.start()
    return copy


def part_of(kind, ref, k):
    if kind == "gather":
        return ref
    if kind == "spread":
        return ref.at[k]
    if kind == "second":
        return ref.at[:, k]
    half = ref.shape[1] // 2
    return ref.at[:, pl.ds(pl.multiple_of(k * half, 128), half)]


def remote_copies(plan, sources, targets, send, receive, start=True):
    copies = []
    for n, (scope, kind) in enumerate(plan):
        mine, peers, device_of = peers_of(scope)
        for k in range(1, peers):
            peer = lax.rem(mine + k, peers)
            copies.append(
                push(
                    part_of(kind, sources[n], peer),
                    targets[n].at[mine],
                    send.at[n, k],
                    receive.at[n, k],
                    device_of(peer),
                    start,
                )
            )
    return copies


def exchange_shapes(plan, arrays):
    shapes = []
    for (scope, kind), x in zip(plan, arrays):
        shape = x.shape
        if kind == "gather":
            shape = (scope_size(scope),) + shape
        if kind == "half":
            shape = (2, shape[0], shape[1] // 2)
        if kind == "second":
            shape = (shape[1], shape[0]) + shape[2:]
        shapes.append(jax.ShapeDtypeStruct(shape, x.dtype))
    return shapes


def exchange_sems(plan):
    number, most = len(plan), max(scope_size(scope) for scope, _ in plan)
    return [
        pltpu.SemaphoreType.DMA((number, most)),
        pltpu.SemaphoreType.DMA((number, most)),
        pltpu.SemaphoreType.DMA((number,)),
    ]


def scopes_of(plan):
    return [x for x in ("core", "team", "lane", "all") if x in [scope for scope, _ in plan]]


def exchange(plan, arrays, collective):
    number = len(arrays)
    shapes = exchange_shapes(plan, arrays)

    def body(*refs):
        sources, targets = refs[:number], refs[number : 2 * number]
        send, receive, local = refs[2 * number : 2 * number + 3]
        through = refs[2 * number + 3 :]
        greet(scopes_of(plan))
        copies = remote_copies(plan, sources, targets, send, receive)
        inward = []
        for n, (scope, kind) in enumerate(plan):
            mine = peers_of(scope)[0]
            copy = pltpu.make_async_copy(part_of(kind, sources[n], mine), through[n], local.at[n])
            copy.start()
            inward.append(copy)
        for n, (scope, kind) in enumerate(plan):
            mine = peers_of(scope)[0]
            inward[n].wait()
            copy = pltpu.make_async_copy(through[n], targets[n].at[mine], local.at[n])
            copy.start()
            copies.append(copy)
        for copy in copies:
            copy.wait()

    return pl.pallas_call(
        body,
        out_shape=shapes,
        in_specs=[pl.BlockSpec(memory_space=pl.ANY)] * number,
        out_specs=[pl.BlockSpec(memory_space=pl.ANY)] * number,
        scratch_shapes=exchange_sems(plan) + [pltpu.VMEM(x.shape[1:], x.dtype) for x in shapes],
        compiler_params=pltpu.CompilerParams(
            collective_id=collective, has_side_effects=True, vmem_limit_bytes=VMEM_BYTES
        ),
    )(*arrays)


def dot(left, right):
    return jnp.dot(left, right, preferred_element_type=jnp.float32)


def project_body(
    tokens_ref,
    gain_ref,
    bias_ref,
    w_ref,
    lane_ref,
    weight_ref,
    query_ref,
    key_ref,
    value_ref,
    held,
    ready,
    windows,
    firsts,
    hop_send,
    hop_recv,
    team_send,
    team_recv,
    weight_sems,
    local_sems,
):
    lanes = lax.axis_size("seq") // TEAMS
    me = lax.axis_index("seq")
    team, lane = me // lanes, lax.rem(me, lanes)
    width = tokens_ref.shape[1]
    wide = windows.shape[2]
    start = (3 * team // 2) * 128
    loads = []
    for part in range(3):
        at = pl.ds(pl.multiple_of(part * width + start, 128), wide)
        loads.append(pltpu.make_async_copy(w_ref.at[:, at], windows.at[part], weight_sems.at[part]))
    for part in range(2):
        at = pl.ds(part * width, 128)
        loads.append(
            pltpu.make_async_copy(w_ref.at[:, at], firsts.at[part], weight_sems.at[3 + part])
        )
    for load in loads:
        load.start()
    def norm():
        tokens = tokens_ref[...]
        row_mean = jnp.mean(tokens, axis=1, keepdims=True)
        centred = tokens - row_mean
        variance = jnp.mean(centred * centred, axis=1, keepdims=True)
        normed = (
            centred * lax.rsqrt(variance + epsilon) * gain_ref[...][None, :] + bias_ref[...][None, :]
        )
        held[team] = normed.astype(jnp.bfloat16)

    greet(["team", "lane"], norm)

    def hop(side, distance, start=True):
        block = team - distance if side == 0 else team + distance
        target = me + lanes if side == 0 else me - lanes
        return push(
            held.at[block],
            held.at[block],
            hop_send.at[side, distance],
            hop_recv.at[side, distance],
            {"seq": target},
            start,
        )

    @pl.when(team < TEAMS - 1)
    def _():
        hop(0, 0)

    @pl.when(team > 0)
    def _():
        hop(1, 0)

    for load in loads:
        load.wait()
    odd = lax.rem(team, 2) == 1
    pieces = []
    for part in range(3):
        window = windows[part]
        pieces.append(
            jnp.where(odd, window[:, wide - TEAM_WIDTH :], window[:, :TEAM_WIDTH])
        )
        if part < 2:
            pieces.append(firsts[part][:, :HEAD_DIM])
    weight_ref[...] = jnp.concatenate(pieces, axis=1)

    def block_copies(block, start):
        copies = []
        for k in range(1, lanes):
            target = {"seq": team * lanes + lax.rem(lane + k, lanes)}
            copies.append(
                push(
                    ready.at[block],
                    query_ref.at[lane, block],
                    team_send.at[block, k],
                    team_recv.at[block, k],
                    target,
                    start,
                )
            )
        for n, (source, destination) in enumerate(
            ((ready.at[block], query_ref.at[lane, block]), (held.at[block], lane_ref.at[block]))
        ):
            copy = pltpu.make_async_copy(source, destination, local_sems.at[n, block])
            if start:
                copy.start()
            copies.append(copy)
        return copies

    def project(block):
        result = dot(held[block], weight_ref[...]).astype(jnp.bfloat16)
        ready[block] = result[:, :QUERY_WIDTH] * jnp.bfloat16(HEAD_DIM ** (-0.5))
        block_copies(block, True)
        key_ref[block] = result[:, QUERY_WIDTH : 2 * QUERY_WIDTH]
        value_ref[block] = result[:, 2 * QUERY_WIDTH :]

    project(team)

    def arrive(step, _):
        distance, side = step // 2 + 1, lax.rem(step, 2)
        for which in range(2):
            block = team - distance if which == 0 else team + distance
            there = (block >= 0) if which == 0 else (block < TEAMS)
            further = (team < TEAMS - 1) if which == 0 else (team > 0)

            @pl.when((side == which) & there)
            def _():
                hop(which, distance - 1, False).wait_recv()

                @pl.when(further)
                def _():
                    hop(which, distance)

                project(block)

        return 0

    lax.fori_loop(0, 2 * (TEAMS - 1), arrive, 0)
    for distance in range(TEAMS - 1):

        @pl.when((team < TEAMS - 1) & (team >= distance))
        def _():
            hop(0, distance, False).wait_send()

        @pl.when((team > 0) & (team + distance < TEAMS))
        def _():
            hop(1, distance, False).wait_send()

    for block in range(TEAMS):
        for copy in block_copies(block, False):
            copy.wait()


def project(tokens, gain, bias, weight, collective):
    lanes = lax.axis_size("seq") // TEAMS
    rows, width = tokens.shape
    inside = pl.BlockSpec(memory_space=pltpu.VMEM)
    anywhere = pl.BlockSpec(memory_space=pl.ANY)
    columns = 2 * QUERY_WIDTH + TEAM_WIDTH
    low = jnp.bfloat16
    dma = pltpu.SemaphoreType.DMA
    return pl.pallas_call(
        project_body,
        out_shape=[
            jax.ShapeDtypeStruct((TEAMS, rows, width), low),
            jax.ShapeDtypeStruct((width, columns), low),
            jax.ShapeDtypeStruct((lanes, TEAMS, rows, QUERY_WIDTH), low),
            jax.ShapeDtypeStruct((TEAMS, rows, QUERY_WIDTH), low),
            jax.ShapeDtypeStruct((TEAMS, rows, TEAM_WIDTH), low),
        ],
        in_specs=[inside, inside, inside, anywhere],
        out_specs=[anywhere, inside, anywhere, inside, inside],
        scratch_shapes=[
            pltpu.VMEM((TEAMS, rows, width), low),
            pltpu.VMEM((TEAMS, rows, QUERY_WIDTH), low),
            pltpu.VMEM((3, width, 256), low),
            pltpu.VMEM((2, width, 128), low),
            dma((2, TEAMS)),
            dma((2, TEAMS)),
            dma((TEAMS, lanes)),
            dma((TEAMS, lanes)),
            dma((5,)),
            dma((2, TEAMS)),
        ],
        compiler_params=pltpu.CompilerParams(
            collective_id=collective, has_side_effects=True, vmem_limit_bytes=VMEM_BYTES
        ),
    )(tokens, gain, bias, weight)


def fold(tile):
    return jnp.sum(tile.reshape(tile.shape[0] // 8, 8, tile.shape[1]), axis=0)


def attend_body(
    length_ref,
    threshold_ref,
    q_ref,
    kk_ref,
    vv_ref,
    out_ref,
    mass_ref,
    carried_ref,
    excess_ref,
    key_heads,
    value_rows,
    running,
    logits,
    out_all,
    mass_all,
    lane_out,
    lane_mass,
    joined_out,
    joined_mass,
    home_out,
    home_mass,
    lane_send,
    lane_recv,
    home_send,
    home_recv,
    *,
    blocks,
    rows,
):
    lanes = blocks // TEAMS
    me = lax.axis_index("seq")
    team, lane = me // lanes, lax.rem(me, lanes)
    i = pl.program_id(0)
    scale = select_scale / (blocks * rows)
    key_iota = lax.broadcasted_iota(jnp.int32, (rows, rows), 0)
    query_iota = lax.broadcasted_iota(jnp.int32, (rows, rows), 1)

    def part_copies(j, start):
        z, owner = j // lanes, lax.rem(j, lanes)
        return [
            push(
                source.at[j],
                destination.at[z, lane],
                lane_send.at[n, j],
                lane_recv.at[n, z, lane],
                {"seq": team * lanes + owner},
                start,
            )
            for n, (source, destination) in enumerate(
                ((out_all, lane_out), (mass_all, lane_mass))
            )
        ]

    def home_copies(z, start):
        return [
            push(
                source.at[z],
                destination.at[team],
                home_send.at[n, z],
                home_recv.at[n, team],
                {"seq": z * lanes + lane},
                start,
            )
            for n, (source, destination) in enumerate(
                ((joined_out, home_out), (joined_mass, home_mass))
            )
        ]

    def join(z):
        for k in range(1, lanes):
            other = lax.rem(lane + k, lanes)
            for n, buffer in enumerate((lane_out, lane_mass)):
                pltpu.make_async_copy(
                    buffer.at[z, other], buffer.at[z, other], lane_recv.at[n, z, other]
                ).wait()
        masses = [lane_mass[z, p] for p in range(lanes)]
        peak = masses[0]
        for p in range(1, lanes):
            peak = jnp.maximum(peak, masses[p])
        shares = [jnp.exp(mass - peak) for mass in masses]
        whole = shares[0]
        for p in range(1, lanes):
            whole = whole + shares[p]
        joined_mass[z] = peak + jnp.log(whole)
        inverse = 1.0 / whole
        for h in range(TEAM_HEADS):
            span = slice(h * HEAD_DIM, (h + 1) * HEAD_DIM)
            mixed = None
            for p in range(lanes):
                share = (shares[p] * inverse)[h : h + 1, :]
                part = lane_out[z, p, span, :].astype(jnp.float32) * share
                mixed = part if p == 0 else mixed + part
            joined_out[z, span, :] = mixed.astype(jnp.bfloat16)

        @pl.when(team != z)
        def _():
            home_copies(z, True)

        @pl.when(team == z)
        def _():
            home_out[team] = joined_out[z]
            home_mass[team] = joined_mass[z]

    @pl.when(i == 0)
    def _():
        greet(["team", "lane"])
        running[...] = jnp.zeros_like(running)
        excess_ref[...] = jnp.zeros_like(excess_ref)
        for z in range(TEAMS):
            for h in range(TEAM_HEADS):
                key_heads[h, z] = kk_ref[z, :, h * HEAD_DIM : (h + 1) * HEAD_DIM]
            first = kk_ref[z, :, TEAM_WIDTH:]
            if z == 0:
                slot = lax.broadcasted_iota(jnp.int32, first.shape, 0) + lane * rows
                first = jnp.where(slot >= 1, first, jnp.zeros_like(first))
            key_heads[TEAM_HEADS, z] = first
            value_rows[z] = vv_ref[z].T

    active = jnp.where(i >= lane, (i - lane) // lanes + 1, 0)
    threshold = threshold_ref[0]

    @pl.when(active == 0)
    def _():
        out_all[i] = jnp.zeros((TEAM_WIDTH, rows), jnp.bfloat16)
        mass_all[i] = jnp.full((8, rows), negative, jnp.float32)

    def work(count):
        q_rows = q_ref[0, 0].T
        heads = [q_rows[h * HEAD_DIM : (h + 1) * HEAD_DIM] for h in range(TEAM_HEADS + 1)]
        earlier = jnp.where(key_iota < query_iota, scale, 0.0).astype(jnp.bfloat16)
        every = jnp.full((rows, rows), scale, jnp.bfloat16)
        last = ((count - 1) * lanes + lane) * rows + key_iota
        query_pos = i * rows + query_iota
        peaks = [None] * TEAM_HEADS
        for z in range(count):
            first = jnp.maximum(dot(key_heads[TEAM_HEADS, z], heads[TEAM_HEADS]), 0.0)
            if z == count - 1:
                first = jnp.where(last < query_pos, first, 0.0)
            first = first.astype(jnp.bfloat16)
            carried = running[z] + dot(first, earlier)
            running[z] = running[z] + dot(first, every)

            if z == count - 1:
                carried = jnp.where(last <= query_pos, carried, -negative)
            carried_ref[0, z] = carried
            for h in range(TEAM_HEADS):
                logit = dot(key_heads[h, z], heads[h]) - carried
                logits[h, z] = logit
                peak = jnp.max(logit.reshape(rows // 8, 8, rows), axis=0)
                peaks[h] = peak if z == 0 else jnp.maximum(peaks[h], peak)
        mass_all[i] = jnp.zeros((8, rows), jnp.float32)
        for h in range(TEAM_HEADS):
            peak = jnp.max(peaks[h], axis=0, keepdims=True)
            mass, mixed = None, None
            for z in range(count):
                terms = jnp.exp(logits[h, z] - peak)
                part = fold(terms)
                values = value_rows[z, h * HEAD_DIM : (h + 1) * HEAD_DIM, :]
                product = dot(values, terms.astype(jnp.bfloat16))
                mass = part if z == 0 else mass + part
                mixed = product if z == 0 else mixed + product
            mass = jnp.sum(mass, axis=0, keepdims=True)
            out_all[i, h * HEAD_DIM : (h + 1) * HEAD_DIM, :] = (mixed * (1.0 / mass)).astype(
                jnp.bfloat16
            )
            mass_all[i, h : h + 1, :] = peak + jnp.log(mass)

        @pl.when(lax.rem(i, TEAMS) == team)
        def _():
            total = None
            for z in range(count):
                carried = carried_ref[0, z]
                if z == count - 1:
                    carried = jnp.where(last < query_pos, carried, 0.0)
                part = fold(jnp.clip(carried - threshold, 0.0, 1.0))
                total = part if z == 0 else total + part
            valid = i * rows + lax.broadcasted_iota(jnp.int32, (8, rows), 1) < length_ref[0]
            excess_ref[...] += jnp.where(valid, total, 0.0)

    for count in range(1, TEAMS + 1):
        pl.when(active == count)(functools.partial(work, count))

    @pl.when(lax.rem(i, lanes) != lane)
    def _():
        part_copies(i, True)

    @pl.when(lax.rem(i, lanes) == lane)
    def _():
        lane_out[i // lanes, lane] = out_all[i]
        lane_mass[i // lanes, lane] = mass_all[i]

    for z in range(TEAMS - 1):
        pl.when(i == (z + 1) * lanes + 1)(functools.partial(join, z))

    @pl.when(i == blocks - 1)
    def _():
        join(TEAMS - 1)

        def drain(j, _):
            @pl.when(lax.rem(j, lanes) != lane)
            def _():
                for copy in part_copies(j, False):
                    copy.wait_send()

            return 0

        lax.fori_loop(0, blocks, drain, 0)
        for z in range(TEAMS):

            @pl.when(team != z)
            def _():
                for copy in home_copies(z, False):
                    copy.wait_send()
                for n, buffer in enumerate((home_out, home_mass)):
                    pltpu.make_async_copy(
                        buffer.at[z], buffer.at[z], home_recv.at[n, z]
                    ).wait()

        out_ref[...] = home_out[...]
        mass_ref[...] = home_mass[...]

def attend(length, threshold, queries, keys, values, blocks, rows, collective):
    lanes = blocks // TEAMS
    smem = pl.BlockSpec(memory_space=pltpu.SMEM)
    whole = pl.BlockSpec((TEAMS, rows, QUERY_WIDTH), lambda i: (0, 0, 0))
    return pl.pallas_call(
        functools.partial(attend_body, blocks=blocks, rows=rows),
        grid=(blocks,),
        in_specs=[
            smem,
            smem,
            pl.BlockSpec(
                (1, 1, rows, QUERY_WIDTH), lambda i: (lax.rem(i, lanes), i // lanes, 0, 0)
            ),
            whole,
            pl.BlockSpec((TEAMS, rows, TEAM_WIDTH), lambda i: (0, 0, 0)),
        ],
        out_specs=[
            pl.BlockSpec((TEAMS, TEAM_WIDTH, rows), lambda i: (0, 0, 0)),
            pl.BlockSpec((TEAMS, 8, rows), lambda i: (0, 0, 0)),
            pl.BlockSpec((1, TEAMS, rows, rows), lambda i: (i, 0, 0, 0)),
            pl.BlockSpec((8, rows), lambda i: (0, 0)),
        ],
        out_shape=[
            jax.ShapeDtypeStruct((TEAMS, TEAM_WIDTH, rows), jnp.bfloat16),
            jax.ShapeDtypeStruct((TEAMS, 8, rows), jnp.float32),
            jax.ShapeDtypeStruct((blocks, TEAMS, rows, rows), jnp.float32),
            jax.ShapeDtypeStruct((8, rows), jnp.float32),
        ],
        scratch_shapes=[
            pltpu.VMEM((TEAM_HEADS + 1, TEAMS, rows, HEAD_DIM), jnp.bfloat16),
            pltpu.VMEM((TEAMS, TEAM_WIDTH, rows), jnp.bfloat16),
            pltpu.VMEM((TEAMS, rows, rows), jnp.float32),
            pltpu.VMEM((TEAM_HEADS, TEAMS, rows, rows), jnp.float32),
            pltpu.VMEM((blocks, TEAM_WIDTH, rows), jnp.bfloat16),
            pltpu.VMEM((blocks, 8, rows), jnp.float32),
            pltpu.VMEM((TEAMS, lanes, TEAM_WIDTH, rows), jnp.bfloat16),
            pltpu.VMEM((TEAMS, lanes, 8, rows), jnp.float32),
            pltpu.VMEM((TEAMS, TEAM_WIDTH, rows), jnp.bfloat16),
            pltpu.VMEM((TEAMS, 8, rows), jnp.float32),
            pltpu.VMEM((TEAMS, TEAM_WIDTH, rows), jnp.bfloat16),
            pltpu.VMEM((TEAMS, 8, rows), jnp.float32),
            pltpu.SemaphoreType.DMA((2, blocks)),
            pltpu.SemaphoreType.DMA((2, TEAMS, lanes)),
            pltpu.SemaphoreType.DMA((2, TEAMS)),
            pltpu.SemaphoreType.DMA((2, TEAMS)),
        ],
        compiler_params=pltpu.CompilerParams(
            collective_id=collective, has_side_effects=True, vmem_limit_bytes=VMEM_BYTES
        ),
    )(length, threshold, queries, keys, values)


reduce_plan = [("lane", "second"), ("team", "spread"), ("team", "spread")]


def added(parts):
    total = parts[0].astype(jnp.float32)
    for part in parts[1:]:
        total = total + part.astype(jnp.float32)
    return total.astype(jnp.bfloat16)


def attend_back_body(
    q_ref,
    grad_ref,
    stat_ref,
    carried_ref,
    kk_ref,
    vv_ref,
    *refs,
    blocks,
    rows,
):
    plan = reduce_plan
    sources, refs = refs[:3], refs[3:]
    (query_grad_ref, key_grad_ref, value_grad_ref), reduced, refs = refs[:3], refs[3:6], refs[6:]
    key_heads, key_rows, value_heads, running, key_sum, value_sum = refs[:6]
    grad_all, stat_all, grad_send, grad_recv, send, receive, local = refs[6:13]
    targets = refs[13:]
    lanes = blocks // TEAMS
    me = lax.axis_index("seq")
    team, lane = me // lanes, lax.rem(me, lanes)
    step = pl.program_id(0)
    i = blocks - 1 - step
    scale = select_scale / (blocks * rows)
    span = [slice(h * HEAD_DIM, (h + 1) * HEAD_DIM) for h in range(TEAM_HEADS + 1)]
    key_iota = lax.broadcasted_iota(jnp.int32, (rows, rows), 0)
    query_iota = lax.broadcasted_iota(jnp.int32, (rows, rows), 1)

    place, owner = i // lanes, lax.rem(i, lanes)

    def grad_copies(z, start):
        return [
            push(
                buffer.at[lane, z],
                buffer.at[lane, z],
                grad_send.at[n, z, k],
                grad_recv.at[n, z, lane],
                {"seq": team * lanes + lax.rem(lane + k, lanes)},
                start,
            )
            for k in range(1, lanes)
            for n, buffer in enumerate((grad_all, stat_all))
        ]

    def own_copy(n):
        scope, kind = plan[n]
        mine = peers_of(scope)[0]
        return pltpu.make_async_copy(
            part_of(kind, sources[n], mine), targets[n].at[mine], local.at[n]
        )

    def plan_copies(scope, start):
        chosen = [n for n in range(len(plan)) if plan[n][0] == scope]
        copies = []
        for n in chosen:
            copies += remote_copies(
                plan[n : n + 1],
                sources[n : n + 1],
                targets[n : n + 1],
                send.at[n : n + 1],
                receive.at[n : n + 1],
                start,
            )
        return copies

    @pl.when(step == 0)
    def _():
        greet(["team", "lane"])
        grad_all[lane] = grad_ref[...]
        stat_all[lane] = stat_ref[...]
        for z in reversed(range(TEAMS)):
            grad_copies(z, True)
        plan_copies("lane", True)
        for n in range(len(plan)):
            own_copy(n).start()
        running[...] = jnp.zeros_like(running)
        key_sum[...] = jnp.zeros_like(key_sum)
        value_sum[...] = jnp.zeros_like(value_sum)
        for z in range(TEAMS):
            for h in range(TEAM_HEADS + 1):
                key_heads[h, z] = kk_ref[z, :, span[h]]
            for h in range(TEAM_HEADS):
                value_heads[h, z] = vv_ref[z, :, span[h]]
            key_rows[z] = kk_ref[z].T
        first = kk_ref[0, :, span[TEAM_HEADS]]
        slot = lax.broadcasted_iota(jnp.int32, first.shape, 0) + lane * rows
        key_heads[TEAM_HEADS, 0] = jnp.where(slot >= 1, first, jnp.zeros_like(first))

    @pl.when(step == 2)
    def _():
        plan_copies("team", True)

    @pl.when(owner != lane)
    def _():
        for n, buffer in enumerate((grad_all, stat_all)):
            at = buffer.at[owner, place]
            pltpu.make_async_copy(at, at, grad_recv.at[n, place, owner]).wait()

    active = jnp.where(i >= lane, (i - lane) // lanes + 1, 0)

    @pl.when(active == 0)
    def _():
        query_grad_ref[...] = jnp.zeros_like(query_grad_ref)

    def work(count):
        q_rows = q_ref[0, 0].T
        grad_rows = grad_all[owner, place].T
        q_row = [q_rows[span[h]] for h in range(TEAM_HEADS + 1)]
        q_col = [q_ref[0, 0, :, span[h]] for h in range(TEAM_HEADS + 1)]
        grad_row = [grad_rows[span[h]] for h in range(TEAM_HEADS)]
        grad_col = [grad_all[owner, place, :, span[h]] for h in range(TEAM_HEADS)]
        mass = [stat_all[owner, place, h : h + 1, :] for h in range(TEAM_HEADS)]
        inner = [stat_all[owner, place, TEAM_HEADS + h : TEAM_HEADS + h + 1, :] for h in range(TEAM_HEADS)]
        later = jnp.where(key_iota > query_iota, -scale, 0.0).astype(jnp.bfloat16)
        every = jnp.full((rows, rows), -scale, jnp.bfloat16)
        last = ((count - 1) * lanes + lane) * rows + key_iota
        query_pos = i * rows + query_iota
        lows = [[] for _ in range(TEAM_HEADS + 1)]
        totals = [None] * count
        for h in range(TEAM_HEADS):
            for z in range(count):
                probs = jnp.exp(dot(key_heads[h, z], q_row[h]) - carried_ref[0, z] - mass[h])
                value_sum[h, z] += dot(probs.astype(jnp.bfloat16), grad_col[h])
                grad_logit = probs * (dot(value_heads[h, z], grad_row[h]) - inner[h])
                totals[z] = grad_logit if h == 0 else totals[z] + grad_logit
                low = grad_logit.astype(jnp.bfloat16)
                key_sum[h, z] += dot(low, q_col[h])
                lows[h].append(low)
        for z in range(count):
            total = totals[z].astype(jnp.bfloat16)
            select_grad = running[z] + dot(total, later)
            running[z] = running[z] + dot(total, every)
            first = dot(key_heads[TEAM_HEADS, z], q_row[TEAM_HEADS])
            live = first > 0.0
            if z == count - 1:
                live = live & (last < query_pos)
            low = jnp.where(live, select_grad, 0.0).astype(jnp.bfloat16)
            key_sum[TEAM_HEADS, z] += dot(low, q_col[TEAM_HEADS])
            lows[TEAM_HEADS].append(low)
        for h in range(TEAM_HEADS + 1):
            left = jnp.concatenate([key_rows[z, span[h], :] for z in range(count)], axis=1)
            result = dot(left, jnp.concatenate(lows[h], axis=0))
            query_grad_ref[0, 0, span[h], :] = result.astype(jnp.bfloat16)

    for count in range(1, TEAMS + 1):
        pl.when(active == count)(functools.partial(work, count))

    @pl.when(step == blocks - 1)
    def _():
        for h in range(TEAM_HEADS + 1):
            key_grad_ref[:, :, span[h]] = key_sum[h].astype(jnp.bfloat16)
        for h in range(TEAM_HEADS):
            value_grad_ref[:, :, span[h]] = value_sum[h].astype(jnp.bfloat16)
        for z in range(TEAMS):
            for copy in grad_copies(z, False):
                copy.wait_send()
        for n in range(len(plan)):
            own_copy(n).wait()
        for scope in ("lane", "team"):
            for copy in plan_copies(scope, False):
                copy.wait()
        for n in range(len(plan)):
            for j in range(reduced[n].shape[0]):
                reduced[n][j] = added([targets[n][k, j] for k in range(targets[n].shape[0])])


def attend_back(queries, grads, stats, carried, keys, values, halves, blocks, rows, collective):
    lanes = blocks // TEAMS
    plan = reduce_plan
    shapes = exchange_shapes(plan, halves)

    def place(step):
        i = blocks - 1 - step
        return (lax.rem(i, lanes), i // lanes, 0, 0)

    return pl.pallas_call(
        functools.partial(attend_back_body, blocks=blocks, rows=rows),
        grid=(blocks,),
        in_specs=[
            pl.BlockSpec((1, 1, rows, QUERY_WIDTH), place),
            pl.BlockSpec((TEAMS, rows, TEAM_WIDTH), lambda step: (0, 0, 0)),
            pl.BlockSpec((TEAMS, 8, rows), lambda step: (0, 0, 0)),
            pl.BlockSpec((1, TEAMS, rows, rows), lambda step: (blocks - 1 - step, 0, 0, 0)),
            pl.BlockSpec((TEAMS, rows, QUERY_WIDTH), lambda step: (0, 0, 0)),
            pl.BlockSpec((TEAMS, rows, TEAM_WIDTH), lambda step: (0, 0, 0)),
        ]
        + [pl.BlockSpec(memory_space=pl.ANY)] * 3,
        out_specs=[
            pl.BlockSpec((1, 1, QUERY_WIDTH, rows), place),
            pl.BlockSpec((TEAMS, rows, QUERY_WIDTH), lambda step: (0, 0, 0)),
            pl.BlockSpec((TEAMS, rows, TEAM_WIDTH), lambda step: (0, 0, 0)),
        ]
        + [pl.BlockSpec(x.shape[1:], lambda step: (0, 0, 0)) for x in shapes],
        out_shape=[
            jax.ShapeDtypeStruct((lanes, TEAMS, QUERY_WIDTH, rows), jnp.bfloat16),
            jax.ShapeDtypeStruct((TEAMS, rows, QUERY_WIDTH), jnp.bfloat16),
            jax.ShapeDtypeStruct((TEAMS, rows, TEAM_WIDTH), jnp.bfloat16),
        ]
        + [jax.ShapeDtypeStruct(x.shape[1:], x.dtype) for x in shapes],
        scratch_shapes=[
            pltpu.VMEM((TEAM_HEADS + 1, TEAMS, rows, HEAD_DIM), jnp.bfloat16),
            pltpu.VMEM((TEAMS, QUERY_WIDTH, rows), jnp.bfloat16),
            pltpu.VMEM((TEAM_HEADS, TEAMS, rows, HEAD_DIM), jnp.bfloat16),
            pltpu.VMEM((TEAMS, rows, rows), jnp.float32),
            pltpu.VMEM((TEAM_HEADS + 1, TEAMS, rows, HEAD_DIM), jnp.float32),
            pltpu.VMEM((TEAM_HEADS, TEAMS, rows, HEAD_DIM), jnp.float32),
            pltpu.VMEM((lanes, TEAMS, rows, TEAM_WIDTH), jnp.bfloat16),
            pltpu.VMEM((lanes, TEAMS, 8, rows), jnp.float32),
            pltpu.SemaphoreType.DMA((2, TEAMS, lanes)),
            pltpu.SemaphoreType.DMA((2, TEAMS, lanes)),
        ]
        + exchange_sems(plan)
        + [pltpu.VMEM(x.shape, x.dtype) for x in shapes],
        compiler_params=pltpu.CompilerParams(
            collective_id=collective, has_side_effects=True, vmem_limit_bytes=VMEM_BYTES
        ),
    )(queries, grads, stats, carried, keys, values, *halves)


def finish_body(
    query_ref,
    key_ref,
    value_ref,
    lane_ref,
    weight_ref,
    gain_ref,
    bias_ref,
    norm_ref,
    excess_ref,
    length_ref,
    down_in,
    up_in,
    out_in,
    whole_ref,
    home_ref,
    total_ref,
    whole_down,
    whole_up,
    whole_out,
    query_parts,
    down_parts,
    up_parts,
    out_parts,
    down_ref,
    up_ref,
    out_ref,
    turned,
    weight_rows,
    weight_grad,
    rows_sum,
    rows_ref,
    main_ref,
    vector_ref,
    core_main,
    send_main,
    lane_main,
    team_send_main,
    team_main,
    assembled,
    vectors,
    ready,
    core_sems,
    lane_sems,
    team_sems,
    home_sems,
    vector_sems,
    out_lane_sems,
    out_core_sems,
    local_sems,
    early_team,
    early_lane,
    early_core,
    early_local,
    first_send,
    first_recv,
    first_local,
):
    lanes = lax.axis_size("seq") // TEAMS
    me = lax.axis_index("seq")
    core = lax.axis_index("batch")
    team, lane = me // lanes, lax.rem(me, lanes)

    def lane_peer(k):
        other = lax.rem(lane + k, lanes)
        return other, {"seq": team * lanes + other}

    def team_peer(k):
        other = lax.rem(team + k, TEAMS)
        return other, {"seq": other * lanes + lane}

    sibling = {"batch": 1 - core}
    spans = (slice(0, QUERY_WIDTH), slice(QUERY_WIDTH, 2 * QUERY_WIDTH), slice(2 * QUERY_WIDTH, None))

    def turn():
        for span in spans:
            weight_rows[span, :] = weight_ref[:, span].T
        weight_grad[...] = jnp.zeros_like(weight_grad)

    greet(["core", "team", "lane"], turn)
    first_sources = (query_ref, down_in, up_in, out_in)
    first_targets = (query_parts, down_parts, up_parts, out_parts)
    first_plan = [("team", "spread"), ("team", "spread"), ("lane", "spread"), ("lane", "spread")]
    first_copies = [[], [], []]
    for n in (1, 2, 3, 0):
        mine = peers_of(first_plan[n][0])[0]
        own = pltpu.make_async_copy(first_sources[n].at[mine], first_targets[n].at[mine], first_local.at[n])
        own.start()
        group = (2, 0, 1, 1)[n]
        first_copies[group].append(own)
        first_copies[group] += remote_copies(
            first_plan[n : n + 1],
            first_sources[n : n + 1],
            first_targets[n : n + 1],
            first_send.at[n : n + 1],
            first_recv.at[n : n + 1],
        )
    def place(n, p, t, part=None):
        if n == 0:
            ref, start, wide = whole_down.at[core, p, t], 0, whole_down.shape[4]
        else:
            ref = (None, whole_up, whole_out)[n]
            wide = ref.shape[3] // 2
            ref, start = ref.at[p, t], core * wide
        cut = (wide // 128 + 1) // 2 * 128
        if part is not None:
            start, wide = ((start, cut), (start + cut, wide - cut))[part]
        return ref.at[:, pl.ds(pl.multiple_of(start, 128), wide)]

    square = lanes == 4
    if square:
        across, along = lax.rem(lane, 2), lane // 2
        direct = [2 * along + 1 - across, 2 * (1 - along) + across]
        origins = direct
    else:
        direct = [lax.rem(lane + k, lanes) for k in range(1, lanes)]
        origins = [lax.rem(lane - k + lanes, lanes) for k in range(1, lanes)]
    corner = lanes - 1 - lane

    def lane_of(p):
        return {"seq": team * lanes + p}

    def landed(ref, sem):
        pltpu.make_async_copy(ref, ref, sem).wait()

    early = (down_ref, up_ref, out_ref)
    number = len(early)
    early_z = [[None] * TEAMS for _ in range(number)]
    early_kept = []

    def publish(n):
        for k in range(1, TEAMS):
            _, target = team_peer(k)
            sems = [early_team.at[side, n, k] for side in range(2)]
            early_z[n][k] = push(early[n], place(n, lane, team), *sems, target)
        copy = pltpu.make_async_copy(early[n], place(n, lane, team), early_local.at[n])
        copy.start()
        early_kept.append(copy)

    early_out = []
    early_sib = []

    def forward(j, chosen=(0, 1, 2)):
        t = lax.rem(team - j + TEAMS, TEAMS)
        for n in chosen:
            if j == 0:
                source = early[n]
            else:
                early_z[n][j].wait_recv()
                source = place(n, lane, t)
            target = place(n, lane, t)
            for m, p in enumerate(direct):
                sems = [early_lane.at[side, n, j, m] for side in range(2)]
                early_out.append(push(source, target, *sems, lane_of(p)))
            sems = [early_core.at[side, n, j, 0] for side in range(2)]
            early_sib.append(push(source, target, *sems, sibling))

    def relay(j):
        t = lax.rem(team - j + TEAMS, TEAMS)
        for n in range(number):
            for m, p in enumerate(origins):
                piece = place(n, p, t)
                landed(piece, early_lane.at[1, n, j, m])
                if square:
                    side = place(n, p, t, m)
                    sems = [early_lane.at[side_, n, j, 2 + m] for side_ in range(2)]
                    early_out.append(push(side, side, *sems, lane_of(direct[1 - m])))
                sems = [early_core.at[side_, n, j, 1 + m] for side_ in range(2)]
                early_sib.append(push(piece, piece, *sems, sibling))

    def settle(j):
        if not square:
            return
        t = lax.rem(team - j + TEAMS, TEAMS)
        for n in range(number):
            for m in range(2):
                landed(place(n, corner, t, m), early_lane.at[1, n, j, 2 + m])
            piece = place(n, corner, t)
            sems = [early_core.at[side, n, j, 3] for side in range(2)]
            early_sib.append(push(piece, piece, *sems, sibling))

    for copy in first_copies[0]:
        copy.wait()
    down_ref[...] = added([down_parts[k] for k in range(lanes)])
    publish(0)
    forward(0, (0,))

    def known(b, _):
        rows_low = lane_ref[b].T
        turned[b] = rows_low
        total = None
        for span, grads in ((spans[1], key_ref[b]), (spans[2], value_ref[b])):
            weight_grad[:, span] += dot(rows_low, grads)
            part = dot(grads, weight_rows[span, :])
            total = part if total is None else total + part
        rows_sum[b] = total
        return 0

    lax.fori_loop(0, TEAMS, known, 0)
    for copy in first_copies[1]:
        copy.wait()
    up_ref[...] = added([up_parts[k] for k in range(TEAMS)])
    out_ref[...] = added([out_parts[k] for k in range(TEAMS)])
    publish(1)
    publish(2)
    forward(0, (1, 2))
    for copy in first_copies[2]:
        copy.wait()
    gain = gain_ref[...][None, :]
    bias = bias_ref[...][None, :]

    def last(b, sums):
        query_rows = query_parts[0, b].astype(jnp.float32)
        for p in range(1, lanes):
            query_rows = query_rows + query_parts[p, b].astype(jnp.float32)
        grads = (query_rows * HEAD_DIM ** (-0.5)).astype(jnp.bfloat16).T
        weight_grad[:, spans[0]] += dot(turned[b], grads)
        total = rows_sum[b] + dot(grads, weight_rows[spans[0], :])
        rows_ref[b] = total.astype(jnp.bfloat16)
        shifted = lane_ref[b].astype(jnp.float32) - bias
        return (
            sums[0] + jnp.sum(total * shifted, axis=0, keepdims=True),
            sums[1] + jnp.sum(total, axis=0, keepdims=True),
        )

    nothing = jnp.zeros_like(gain)
    gain_sum, bias_sum = lax.fori_loop(0, TEAMS, last, (nothing, nothing))
    length = length_ref[0].astype(jnp.float32)
    pairs = (length - 1.0) * (length - 2.0) / (2.0 * TEAMS * lanes)
    excess = jnp.sum(jnp.sum(excess_ref[...], axis=0, keepdims=True), axis=1, keepdims=True)
    vector_ref[...] = jnp.zeros_like(vector_ref)
    vector_ref[0:1, :] = gain_sum / gain
    vector_ref[1:2, :] = bias_sum
    vector_ref[2:4, :] = norm_ref[...]
    vector_ref[4:5, :] = jnp.broadcast_to(excess, nothing.shape)
    vector_ref[5:6, :] = jnp.full(nothing.shape, pairs)
    depth = main_ref.shape[1]
    for chunk in range(2 * lanes):
        main_ref[chunk] = weight_grad[chunk * depth : (chunk + 1) * depth, :].astype(jnp.bfloat16)
    theirs = pl.ds((1 - core) * lanes, lanes)
    core_copies = [
        push(main_ref.at[theirs], core_main, core_sems.at[0, 0], core_sems.at[1, 0], sibling),
        push(vector_ref, vectors.at[0], vector_sems.at[0, 0], vector_sems.at[1, 0], sibling),
    ]
    for copy in core_copies:
        copy.wait()

    both = vector_ref[...] + vectors[0]
    vectors[1 + lane] = both
    ready[0] = both
    for j in range(lanes):
        send_main[j] = (
            main_ref[core * lanes + j].astype(jnp.float32) + core_main[j].astype(jnp.float32)
        ).astype(jnp.bfloat16)
    lane_copies = []
    for k in range(1, lanes):
        other, target = lane_peer(k)
        lane_copies += [
            push(send_main.at[other], lane_main.at[lane], lane_sems.at[0, 0, k], lane_sems.at[1, 0, k], target),
            push(ready.at[0], vectors.at[1 + lane], vector_sems.at[0, k], vector_sems.at[1, k], target),
        ]
    lane_main[lane] = send_main[lane]
    for copy in lane_copies:
        copy.wait()

    def total(ref, start, number):
        result = ref[start].astype(jnp.float32)
        for j in range(1, number):
            result = result + ref[start + j].astype(jnp.float32)
        return result

    whole_vector = total(vectors, 1, lanes)
    ready[1] = whole_vector
    vectors[1 + lanes + team] = whole_vector
    low_main = total(lane_main, 0, lanes).astype(jnp.bfloat16)
    team_send_main[...] = low_main
    team_main[team] = low_main
    team_copies = []
    for k in range(1, TEAMS):
        other, target = team_peer(k)
        at = lanes + k
        team_copies += [
            push(team_send_main, team_main.at[team], team_sems.at[0, 0, k], team_sems.at[1, 0, k], target),
            push(ready.at[1], vectors.at[1 + lanes + team], vector_sems.at[0, at], vector_sems.at[1, at], target),
        ]
    relay(0)
    home_copies = []
    for k in range(1, TEAMS):
        other, target = team_peer(k)
        home_copies.append(
            push(rows_ref.at[other], home_ref.at[team], home_sems.at[0, k], home_sems.at[1, k], target)
        )
    own = pltpu.make_async_copy(rows_ref.at[team], home_ref.at[team], local_sems.at[0])
    own.start()
    for j in range(1, TEAMS):
        forward(j)
        settle(j - 1)
        if j < TEAMS - 1:
            relay(j)
    for copy in team_copies:
        copy.wait()
    total_ref[...] = total(vectors, 1 + lanes, TEAMS)
    pieces = []
    for part in range(3):
        first = part * QUERY_WIDTH
        for g in range(TEAMS):
            piece = team_main[g, :, first : first + TEAM_WIDTH]
            if g == 0 and part < 2:
                more = piece[:, :HEAD_DIM].astype(jnp.float32)
                for other in range(TEAMS):
                    more = more + team_main[
                        other, :, first + TEAM_WIDTH : first + QUERY_WIDTH
                    ].astype(jnp.float32)
                pieces += [more.astype(jnp.bfloat16), piece[:, HEAD_DIM:]]
            else:
                pieces.append(piece)
    assembled[...] = jnp.concatenate(pieces, axis=1)

    def chunk_of(p, part=None):
        ref = whole_ref.at[core * lanes + p]
        half = whole_ref.shape[2] // 2
        return ref if part is None else ref.at[:, pl.ds(part * half, half)]

    out_copies, core_out = [], []
    for m, p in enumerate(direct):
        sems = [out_lane_sems.at[side, m] for side in range(2)]
        out_copies.append(push(assembled, chunk_of(lane), *sems, lane_of(p)))
    sems = [out_core_sems.at[side, 0] for side in range(2)]
    core_out.append(push(assembled, chunk_of(lane), *sems, sibling))
    kept = pltpu.make_async_copy(assembled, chunk_of(lane), local_sems.at[1])
    kept.start()
    relay(TEAMS - 1)
    for m, p in enumerate(origins):
        landed(chunk_of(p), out_lane_sems.at[1, m])
        if square:
            sems = [out_lane_sems.at[side, 2 + m] for side in range(2)]
            out_copies.append(push(chunk_of(p, m), chunk_of(p, m), *sems, lane_of(direct[1 - m])))
        sems = [out_core_sems.at[side, 1 + m] for side in range(2)]
        core_out.append(push(chunk_of(p), chunk_of(p), *sems, sibling))
    settle(TEAMS - 1)
    if square:
        for m in range(2):
            landed(chunk_of(corner, m), out_lane_sems.at[1, 2 + m])
        sems = [out_core_sems.at[side, 3] for side in range(2)]
        core_out.append(push(chunk_of(corner), chunk_of(corner), *sems, sibling))
    for copy in out_copies + early_out:
        copy.wait_send()
    for n in range(number):
        for k in range(1, TEAMS):
            early_z[n][k].wait_send()
    for copy in core_out + home_copies + early_sib + early_kept:
        copy.wait()
    own.wait()
    kept.wait()


def finish(
    queries, keys, values, lane_rows, weight, gain, bias, norm, excess, length, reduced, collective
):
    lanes = lax.axis_size("seq") // TEAMS
    width, columns = weight.shape
    rows = lane_rows.shape[1]
    vector = (8, width)
    chunks, depth = 2 * lanes, width // (2 * lanes)
    low = jnp.bfloat16
    dma = pltpu.SemaphoreType.DMA
    down, up, out = (x.shape[1:] for x in reduced)
    wholes = [
        (2, lanes, TEAMS) + down,
        (lanes, TEAMS, up[0], 2 * up[1]),
        (lanes, TEAMS, out[0], 2 * out[1]),
    ]
    anywhere = pl.BlockSpec(memory_space=pl.ANY)
    inside = pl.BlockSpec(memory_space=pltpu.VMEM)
    return pl.pallas_call(
        finish_body,
        out_shape=[
            jax.ShapeDtypeStruct((chunks, depth, 3 * width), low),
            jax.ShapeDtypeStruct(lane_rows.shape, low),
            jax.ShapeDtypeStruct(vector, jnp.float32),
        ]
        + [jax.ShapeDtypeStruct(shape, low) for shape in wholes],
        in_specs=[anywhere]
        + [inside] * 8
        + [pl.BlockSpec(memory_space=pltpu.SMEM)]
        + [anywhere] * 3,
        out_specs=[anywhere, anywhere, inside] + [anywhere] * 3,
        scratch_shapes=[
            pltpu.VMEM(queries.shape, low),
            pltpu.VMEM((lanes,) + down, low),
            pltpu.VMEM((TEAMS,) + up, low),
            pltpu.VMEM((TEAMS,) + out, low),
            pltpu.VMEM(down, low),
            pltpu.VMEM(up, low),
            pltpu.VMEM(out, low),
            pltpu.VMEM((TEAMS, width, rows), low),
            pltpu.VMEM((columns, width), low),
            pltpu.VMEM((width, columns), jnp.float32),
            pltpu.VMEM((TEAMS, rows, width), jnp.float32),
            pltpu.VMEM((TEAMS, rows, width), low),
            pltpu.VMEM((chunks, depth, columns), low),
            pltpu.VMEM(vector, jnp.float32),
            pltpu.VMEM((lanes, depth, columns), low),
            pltpu.VMEM((lanes, depth, columns), low),
            pltpu.VMEM((lanes, depth, columns), low),
            pltpu.VMEM((depth, columns), low),
            pltpu.VMEM((TEAMS, depth, columns), low),
            pltpu.VMEM((depth, 3 * width), low),
            pltpu.VMEM((1 + lanes + TEAMS,) + vector, jnp.float32),
            pltpu.VMEM((2,) + vector, jnp.float32),
            dma((2, 2)),
            dma((2, 2, lanes)),
            dma((2, 2, TEAMS)),
            dma((2, TEAMS)),
            dma((2, lanes + TEAMS)),
            dma((2, lanes)),
            dma((2, lanes)),
            dma((2,)),
            dma((2, 3, TEAMS)),
            dma((2, 3, TEAMS, lanes)),
            dma((2, 3, TEAMS, lanes)),
            dma((3,)),
            dma((4, max(lanes, TEAMS))),
            dma((4, max(lanes, TEAMS))),
            dma((4,)),
        ],
        compiler_params=pltpu.CompilerParams(
            collective_id=collective, has_side_effects=True, vmem_limit_bytes=VMEM_BYTES
        ),
    )(queries, keys, values, lane_rows, weight, gain, bias, norm, excess, length, *reduced)


def contract_cols(left, right):
    return lax.dot_general(left, right, (((1,), (1,)), ((), ())), preferred_element_type=jnp.float32)


def dense_body(
    length_ref,
    mixed_ref,
    mass_ref,
    tokens_ref,
    grad_ref,
    gain_ref,
    bias_ref,
    w_out_hbm,
    w_up_hbm,
    w_down_hbm,
    layer_ref,
    resid_ref,
    norm_ref,
    cols_ref,
    stats_ref,
    down_hbm,
    up_hbm,
    out_hbm,
    w_out,
    w_up,
    w_down,
    active,
    slope,
    top,
    normed,
    mixed,
    slant,
    active_other,
    slope_other,
    top_other,
    normed_other,
    mixed_other,
    slant_other,
    total,
    back,
    cols,
    stats,
    down_half,
    up_half,
    out_half,
    load_sems,
    core_sems,
    lane_sems,
    keep_sems,
    store_sems,
):
    rows, width = tokens_ref.shape
    hidden = w_up.shape[1]
    step = width
    count = lax.axis_size("seq")
    lanes = count // TEAMS
    me = lax.axis_index("seq")
    core = lax.axis_index("batch")
    team, lane = me // lanes, lax.rem(me, lanes)
    sibling = {"batch": 1 - core}
    loads = [
        pltpu.make_async_copy(source, target, load_sems.at[n])
        for n, (source, target) in enumerate(
            ((w_out_hbm, w_out), (w_up_hbm, w_up), (w_down_hbm, w_down))
        )
    ]
    for load in loads:
        load.start()
    greet(["core", "lane"])

    def half_of(ref, which):
        half = ref.shape[1] // 2
        return ref.at[:, pl.ds(pl.multiple_of(which * half, 128), half)]

    pairs = (
        (active, active_other, True),
        (top, top_other, False),
        (normed, normed_other, False),
        (slope, slope_other, True),
        (mixed, mixed_other, False),
        (slant, slant_other, True),
    )

    def swap(n, start):
        source, target, halved = pairs[n]
        return push(
            half_of(source, 1 - core) if halved else source,
            target,
            core_sems.at[0, n],
            core_sems.at[1, n],
            sibling,
            start,
        )

    grad_top = grad_ref[...]
    top[...] = grad_top.astype(jnp.bfloat16)
    swap(1, True)
    valid = me * rows + lax.broadcasted_iota(jnp.int32, (rows, width), 0) < length_ref[0]
    mixed_rows = mixed_ref[...]
    mixed[...] = jnp.where(valid, mixed_rows.T, jnp.zeros((), jnp.bfloat16))
    swap(4, True)
    loads[0].wait()
    residual = tokens_ref[...] + dot(mixed[...], w_out[...])
    row_mean = jnp.mean(residual, axis=1, keepdims=True)
    centred = residual - row_mean
    variance = jnp.mean(centred * centred, axis=1, keepdims=True)
    spread = lax.rsqrt(variance + epsilon)
    scaled = centred * spread
    gain = gain_ref[...][None, :]
    normed[...] = (scaled * gain + bias_ref[...][None, :]).astype(jnp.bfloat16)
    swap(2, True)
    total[...] = residual
    back[...] = jnp.zeros_like(back)
    loads[1].wait()
    loads[2].wait()

    def chunk(c, _):
        at = pl.ds(pl.multiple_of(c * step, 128), step)
        up = w_up[:, at]
        down = w_down[at, :]
        u = dot(normed[...], up)
        squared = u * u
        bend = jnp.tanh(0.7978845608028654 * u * (1.0 + 0.044715 * squared))
        lift = 0.5 * (1.0 + bend)
        low = (u * lift).astype(jnp.bfloat16)
        active[:, at] = low
        turn = lift + (0.5 * 0.7978845608028654) * u * (1.0 - bend * bend) * (
            1.0 + (3.0 * 0.044715) * squared
        )
        grad_low = (contract_cols(top[...], down) * turn).astype(jnp.bfloat16)
        slope[:, at] = grad_low
        total[...] += dot(low, down)
        back[...] += contract_cols(grad_low, up)
        return 0

    lax.fori_loop(0, hidden // step, chunk, 0)
    swap(0, True)
    swap(3, True)
    layer_ref[...] = total[...]
    grad_normed = back[...]
    norm_ref[0:1, :] = jnp.sum(grad_normed * scaled, axis=0, keepdims=True)
    norm_ref[1:2, :] = jnp.sum(grad_normed, axis=0, keepdims=True)
    inner = grad_normed * gain
    resid = grad_top + spread * (
        inner
        - jnp.mean(inner, axis=1, keepdims=True)
        - scaled * jnp.mean(inner * scaled, axis=1, keepdims=True)
    )
    resid_ref[...] = resid
    slant[...] = resid.astype(jnp.bfloat16)
    swap(5, True)
    grad_mixed = contract_cols(slant[...], w_out[...]).astype(jnp.bfloat16)
    grad_mixed = jnp.where(valid, grad_mixed, jnp.zeros((), jnp.bfloat16))
    products = grad_mixed.T.astype(jnp.float32) * mixed_rows.astype(jnp.float32)
    for t in range(TEAMS):
        cols[t] = grad_mixed[:, t * TEAM_WIDTH : (t + 1) * TEAM_WIDTH]
        stats[t] = mass_ref[t]
        for h in range(TEAM_HEADS):
            first = t * TEAM_WIDTH + h * HEAD_DIM
            stats[t, TEAM_HEADS + h : TEAM_HEADS + h + 1, :] = jnp.sum(
                products[first : first + HEAD_DIM], axis=0, keepdims=True
            )
    copies = []
    for k in range(1, TEAMS):
        other = lax.rem(team + k, TEAMS)
        for n, (source, target) in enumerate(((cols, cols_ref), (stats, stats_ref))):
            copies.append(
                push(
                    source.at[other],
                    target.at[team],
                    lane_sems.at[0, n, k],
                    lane_sems.at[1, n, k],
                    {"seq": other * lanes + lane},
                )
            )
    for n, (source, target) in enumerate(((cols, cols_ref), (stats, stats_ref))):
        copy = pltpu.make_async_copy(source.at[team], target.at[team], keep_sems.at[n])
        copy.start()
        copies.append(copy)

    def pair_dot(left, left_other, right, right_other, at):
        return (
            dot(left[:, at].T, right[...]) + dot(left_other[:, at].T, right_other[...])
        ).astype(jnp.bfloat16)

    for n in range(len(pairs)):
        swap(n, False).wait()
    block = 384
    own_active = half_of(active, core)
    own_slope = half_of(slope, core)
    own_slant = half_of(slant, core)

    def down_rows(c, _):
        at = pl.ds(pl.multiple_of(c * block, 128), block)
        down_half[at, :] = pair_dot(own_active, active_other, top, top_other, at)
        return 0

    lax.fori_loop(0, down_half.shape[0] // block, down_rows, 0)
    stores = [pltpu.make_async_copy(down_half, down_hbm, store_sems.at[0])]
    stores[0].start()

    def up_rows(c, _):
        at = pl.ds(pl.multiple_of(c * block, 128), block)
        up_half[at, :] = pair_dot(normed, normed_other, own_slope, slope_other, at)
        out_half[at, :] = pair_dot(mixed, mixed_other, own_slant, slant_other, at)
        return 0

    lax.fori_loop(0, width // block, up_rows, 0)
    for n, (source, target) in enumerate(((up_half, up_hbm), (out_half, out_hbm))):
        copy = pltpu.make_async_copy(source, target, store_sems.at[1 + n])
        copy.start()
        stores.append(copy)
    for copy in copies + stores:
        copy.wait()


def dense(length, mixed, masses, tokens, grad, gain, bias, w_out, w_up, w_down, collective):
    rows, width = tokens.shape
    hidden = w_up.shape[1]
    low, full = jnp.bfloat16, jnp.float32
    inside = pl.BlockSpec(memory_space=pltpu.VMEM)
    anywhere = pl.BlockSpec(memory_space=pl.ANY)
    dma = pltpu.SemaphoreType.DMA
    half = hidden // 2
    return pl.pallas_call(
        dense_body,
        out_shape=[
            jax.ShapeDtypeStruct((rows, width), full),
            jax.ShapeDtypeStruct((rows, width), full),
            jax.ShapeDtypeStruct((2, width), full),
            jax.ShapeDtypeStruct((TEAMS, rows, TEAM_WIDTH), low),
            jax.ShapeDtypeStruct((TEAMS, 8, rows), full),
            jax.ShapeDtypeStruct((half, width), low),
            jax.ShapeDtypeStruct((width, half), low),
            jax.ShapeDtypeStruct((width, width // 2), low),
        ],
        in_specs=[pl.BlockSpec(memory_space=pltpu.SMEM)] + [inside] * 6 + [anywhere] * 3,
        out_specs=[inside] * 3 + [anywhere] * 5,
        scratch_shapes=[
            pltpu.VMEM((width, width), low),
            pltpu.VMEM((width, hidden), low),
            pltpu.VMEM((hidden, width), low),
            pltpu.VMEM((rows, hidden), low),
            pltpu.VMEM((rows, hidden), low),
            pltpu.VMEM((rows, width), low),
            pltpu.VMEM((rows, width), low),
            pltpu.VMEM((rows, width), low),
            pltpu.VMEM((rows, width), low),
            pltpu.VMEM((rows, half), low),
            pltpu.VMEM((rows, half), low),
            pltpu.VMEM((rows, width), low),
            pltpu.VMEM((rows, width), low),
            pltpu.VMEM((rows, width), low),
            pltpu.VMEM((rows, width // 2), low),
            pltpu.VMEM((rows, width), full),
            pltpu.VMEM((rows, width), full),
            pltpu.VMEM((TEAMS, rows, TEAM_WIDTH), low),
            pltpu.VMEM((TEAMS, 8, rows), full),
            pltpu.VMEM((half, width), low),
            pltpu.VMEM((width, half), low),
            pltpu.VMEM((width, width // 2), low),
            dma((3,)),
            dma((2, 6)),
            dma((2, 2, TEAMS)),
            dma((2,)),
            dma((3,)),
        ],
        compiler_params=pltpu.CompilerParams(
            collective_id=collective, has_side_effects=True, vmem_limit_bytes=VMEM_BYTES
        ),
    )(length, mixed, masses, tokens, grad, gain, bias, w_out, w_up, w_down)


def close_body(
    tokens_ref,
    gain_ref,
    resid_ref,
    home_ref,
    layer_ref,
    vector_ref,
    *refs,
):
    count = (len(refs) - 6) // 2
    weights, refs = refs[:count], refs[count:]
    grad_ref, layer_out, *refs = refs
    for source, target in zip(weights, refs[:count]):
        target[...] = source[...].astype(jnp.float32)
    layer_out[...] = layer_ref[...]
    tokens = tokens_ref[...]
    centred = tokens - jnp.mean(tokens, axis=1, keepdims=True)
    spread = lax.rsqrt(jnp.mean(centred * centred, axis=1, keepdims=True) + epsilon)
    scaled = centred * spread
    total = home_ref[0].astype(jnp.float32)
    for t in range(1, TEAMS):
        total = total + home_ref[t].astype(jnp.float32)
    inner = total * gain_ref[...][None, :]
    grad_ref[...] = resid_ref[...] + spread * (
        inner
        - jnp.mean(inner, axis=1, keepdims=True)
        - scaled * jnp.mean(inner * scaled, axis=1, keepdims=True)
    )

    @pl.when(pl.program_id(0) == 0)
    def _():
        for n in range(4):
            refs[count + n][...] = vector_ref[n]


def close(tokens, gain, resid, home, layer, vectors, weights):
    steps = 4
    rows, width = tokens.shape

    def band(x):
        return pl.BlockSpec((x.shape[0] // steps, x.shape[1]), lambda i: (i, 0))

    line = pl.BlockSpec((width,), lambda i: (0,))
    large = [tokens, layer] + weights
    return pl.pallas_call(
        close_body,
        grid=(steps,),
        in_specs=[
            band(tokens),
            line,
            band(resid),
            pl.BlockSpec((TEAMS, rows // steps, width), lambda i: (0, i, 0)),
            band(layer),
            pl.BlockSpec(vectors.shape, lambda i: (0, 0)),
        ]
        + [band(x) for x in weights],
        out_specs=[band(x) for x in large] + [line] * 4,
        out_shape=[jax.ShapeDtypeStruct(x.shape, jnp.float32) for x in large]
        + [jax.ShapeDtypeStruct((width,), jnp.float32)] * 4,
        compiler_params=pltpu.CompilerParams(vmem_limit_bytes=VMEM_BYTES),
    )(tokens, gain, resid, home, layer, vectors, *weights)


def per_device(
    block_input,
    ln1_gain,
    ln1_bias,
    w_qkv,
    w_out,
    ln2_gain,
    ln2_bias,
    w_up,
    w_down,
    length_draw,
    threshold_index,
    grad_out,
):
    rows = block_input.shape[1]
    width = block_input.shape[2]
    blocks = lax.axis_size("seq")
    lanes = blocks // TEAMS
    group_len = blocks * rows
    me = lax.axis_index("seq")
    team = me // lanes
    length = group_len - rows + 1 + length_draw % rows
    threshold = threshold_index.astype(jnp.float32) / 128.0
    tokens = block_input[0]
    grad_top = grad_out[0]

    lane_rows, team_weight, queries, keys, values = project(tokens, ln1_gain, ln1_bias, w_qkv, 0)

    head_out, masses, carried, excess = attend(
        length, threshold, queries, keys, values, blocks, rows, 1
    )
    layer_out, grad_resid, grad_ln2, grad_cols, stats, down_half, up_half, out_half = dense(
        length,
        head_out.reshape(width, rows),
        masses,
        tokens,
        grad_top,
        ln2_gain,
        ln2_bias,
        w_out,
        w_up,
        w_down,
        3,
    )
    halves = [x.reshape(lanes, TEAMS, -1, x.shape[1]) for x in (down_half, up_half, out_half)]
    query_grads, key_grads, value_grads, *halves = attend_back(
        queries, grad_cols, stats, carried, keys, values, halves, blocks, rows, 7
    )

    grad_w_qkv, home_rows, vectors, grad_w_down, grad_w_up, grad_w_out = finish(
        query_grads,
        key_grads,
        value_grads,
        lane_rows,
        team_weight,
        ln1_gain,
        ln1_bias,
        grad_ln2,
        excess,
        length,
        halves,
        6,
    )
    pruned_share = (vectors[4, 0] / vectors[5, 0]).reshape(1)
    grad_x, layer_out, grad_w_qkv, grad_w_out, grad_w_up, grad_w_down, *lines = close(
        tokens,
        ln1_gain,
        grad_resid,
        home_rows,
        layer_out,
        vectors,
        [
            grad_w_qkv.reshape(w_qkv.shape),
            grad_w_out.reshape(w_out.shape),
            grad_w_up.reshape(w_up.shape),
            grad_w_down.reshape(w_down.shape),
        ],
    )
    return (
        layer_out[None],
        grad_x[None],
        lines[0],
        lines[1],
        grad_w_qkv,
        grad_w_out,
        lines[2],
        lines[3],
        grad_w_up,
        grad_w_down,
        pruned_share,
    )


def solution(mesh):
    placed = (
        P("batch", "seq", None),
        P(),
        P(),
        P(),
        P(),
        P(),
        P(),
        P(),
        P(),
        P("batch"),
        P(),
        P("batch", "seq", None),
    )
    return jax.shard_map(
        per_device,
        mesh=mesh,
        in_specs=placed,
        out_specs=(
            P("batch", "seq", None),
            P("batch", "seq", None),
            P(),
            P(),
            P(),
            P(),
            P(),
            P(),
            P(),
            P(),
            P(),
        ),
        check_vma=False,
    )
```

```python
import functools

import jax
import jax.numpy as jnp
from jax import lax
from jax.experimental import pallas as pl
from jax.experimental.pallas import tpu as pltpu
from jax.sharding import PartitionSpec as P

HEADS = 12
HEAD_DIM = 64
TEAMS = 4
TEAM_HEADS = HEADS // TEAMS
TEAM_WIDTH = TEAM_HEADS * HEAD_DIM
QUERY_WIDTH = TEAM_WIDTH + HEAD_DIM

epsilon = 1e-05
negative = -1e30
select_scale = 3.0
VMEM_BYTES = 60 * 2**20
MESH = pl.DeviceIdType.MESH


def peers_of(scope):
    lanes = lax.axis_size("seq") // TEAMS
    me = lax.axis_index("seq")
    team, lane = me // lanes, lax.rem(me, lanes)
    if scope == "team":
        return lane, lanes, lambda k: {"seq": team * lanes + k}
    if scope == "lane":
        return team, TEAMS, lambda k: {"seq": k * lanes + lane}
    if scope == "core":
        return lax.axis_index("batch"), 2, lambda k: {"batch": k}
    return me, lanes * TEAMS, lambda k: {"seq": k}


def scope_size(scope):
    count = lax.axis_size("seq")
    return {"team": count // TEAMS, "lane": TEAMS, "core": 2, "all": count}[scope]


def greet(scopes, meanwhile=None):
    barrier = pltpu.get_barrier_semaphore()
    number = 0
    for scope in scopes:
        mine, peers, device_of = peers_of(scope)
        for k in range(1, peers):
            pl.semaphore_signal(
                barrier, inc=1, device_id=device_of(lax.rem(mine + k, peers)), device_id_type=MESH
            )
        number += peers - 1
    if meanwhile is not None:
        meanwhile()
    pl.semaphore_wait(barrier, number)


def push(source, destination, send, receive, target, start=True):
    copy = pltpu.make_async_remote_copy(
        src_ref=source,
        dst_ref=destination,
        send_sem=send,
        recv_sem=receive,
        device_id=target,
        device_id_type=MESH,
    )
    if start:
        copy.start()
    return copy


def part_of(kind, ref, k):
    if kind == "gather":
        return ref
    if kind == "spread":
        return ref.at[k]
    if kind == "second":
        return ref.at[:, k]
    half = ref.shape[1] // 2
    return ref.at[:, pl.ds(pl.multiple_of(k * half, 128), half)]


def remote_copies(plan, sources, targets, send, receive, start=True):
    copies = []
    for n, (scope, kind) in enumerate(plan):
        mine, peers, device_of = peers_of(scope)
        for k in range(1, peers):
            peer = lax.rem(mine + k, peers)
            copies.append(
                push(
                    part_of(kind, sources[n], peer),
                    targets[n].at[mine],
                    send.at[n, k],
                    receive.at[n, k],
                    device_of(peer),
                    start,
                )
            )
    return copies


def exchange_shapes(plan, arrays):
    shapes = []
    for (scope, kind), x in zip(plan, arrays):
        shape = x.shape
        if kind == "gather":
            shape = (scope_size(scope),) + shape
        if kind == "half":
            shape = (2, shape[0], shape[1] // 2)
        if kind == "second":
            shape = (shape[1], shape[0]) + shape[2:]
        shapes.append(jax.ShapeDtypeStruct(shape, x.dtype))
    return shapes


def exchange_sems(plan):
    number, most = len(plan), max(scope_size(scope) for scope, _ in plan)
    return [
        pltpu.SemaphoreType.DMA((number, most)),
        pltpu.SemaphoreType.DMA((number, most)),
        pltpu.SemaphoreType.DMA((number,)),
    ]


def scopes_of(plan):
    return [x for x in ("core", "team", "lane", "all") if x in [scope for scope, _ in plan]]


def exchange(plan, arrays, collective):
    number = len(arrays)
    shapes = exchange_shapes(plan, arrays)

    def body(*refs):
        sources, targets = refs[:number], refs[number : 2 * number]
        send, receive, local = refs[2 * number : 2 * number + 3]
        through = refs[2 * number + 3 :]
        greet(scopes_of(plan))
        copies = remote_copies(plan, sources, targets, send, receive)
        inward = []
        for n, (scope, kind) in enumerate(plan):
            mine = peers_of(scope)[0]
            copy = pltpu.make_async_copy(part_of(kind, sources[n], mine), through[n], local.at[n])
            copy.start()
            inward.append(copy)
        for n, (scope, kind) in enumerate(plan):
            mine = peers_of(scope)[0]
            inward[n].wait()
            copy = pltpu.make_async_copy(through[n], targets[n].at[mine], local.at[n])
            copy.start()
            copies.append(copy)
        for copy in copies:
            copy.wait()

    return pl.pallas_call(
        body,
        out_shape=shapes,
        in_specs=[pl.BlockSpec(memory_space=pl.ANY)] * number,
        out_specs=[pl.BlockSpec(memory_space=pl.ANY)] * number,
        scratch_shapes=exchange_sems(plan) + [pltpu.VMEM(x.shape[1:], x.dtype) for x in shapes],
        compiler_params=pltpu.CompilerParams(
            collective_id=collective, has_side_effects=True, vmem_limit_bytes=VMEM_BYTES
        ),
    )(*arrays)


def dot(left, right):
    return jnp.dot(left, right, preferred_element_type=jnp.float32)


def project_body(
    tokens_ref,
    gain_ref,
    bias_ref,
    w_ref,
    lane_ref,
    weight_ref,
    query_ref,
    key_ref,
    value_ref,
    held,
    ready,
    windows,
    firsts,
    hop_send,
    hop_recv,
    team_send,
    team_recv,
    weight_sems,
    local_sems,
):
    lanes = lax.axis_size("seq") // TEAMS
    me = lax.axis_index("seq")
    team, lane = me // lanes, lax.rem(me, lanes)
    width = tokens_ref.shape[1]
    wide = windows.shape[2]
    start = (3 * team // 2) * 128
    loads = []
    for part in range(3):
        at = pl.ds(pl.multiple_of(part * width + start, 128), wide)
        loads.append(pltpu.make_async_copy(w_ref.at[:, at], windows.at[part], weight_sems.at[part]))
    for part in range(2):
        at = pl.ds(part * width, 128)
        loads.append(
            pltpu.make_async_copy(w_ref.at[:, at], firsts.at[part], weight_sems.at[3 + part])
        )
    for load in loads:
        load.start()
    def norm():
        tokens = tokens_ref[...]
        row_mean = jnp.mean(tokens, axis=1, keepdims=True)
        centred = tokens - row_mean
        variance = jnp.mean(centred * centred, axis=1, keepdims=True)
        normed = (
            centred * lax.rsqrt(variance + epsilon) * gain_ref[...][None, :] + bias_ref[...][None, :]
        )
        held[team] = normed.astype(jnp.bfloat16)

    greet(["team", "lane"], norm)

    def hop(side, distance, start=True):
        block = team - distance if side == 0 else team + distance
        target = me + lanes if side == 0 else me - lanes
        return push(
            held.at[block],
            held.at[block],
            hop_send.at[side, distance],
            hop_recv.at[side, distance],
            {"seq": target},
            start,
        )

    @pl.when(team < TEAMS - 1)
    def _():
        hop(0, 0)

    @pl.when(team > 0)
    def _():
        hop(1, 0)

    for load in loads:
        load.wait()
    odd = lax.rem(team, 2) == 1
    pieces = []
    for part in range(3):
        window = windows[part]
        pieces.append(
            jnp.where(odd, window[:, wide - TEAM_WIDTH :], window[:, :TEAM_WIDTH])
        )
        if part < 2:
            pieces.append(firsts[part][:, :HEAD_DIM])
    weight_ref[...] = jnp.concatenate(pieces, axis=1)

    def block_copies(block, start):
        copies = []
        for k in range(1, lanes):
            target = {"seq": team * lanes + lax.rem(lane + k, lanes)}
            copies.append(
                push(
                    ready.at[block],
                    query_ref.at[lane, block],
                    team_send.at[block, k],
                    team_recv.at[block, k],
                    target,
                    start,
                )
            )
        for n, (source, destination) in enumerate(
            ((ready.at[block], query_ref.at[lane, block]), (held.at[block], lane_ref.at[block]))
        ):
            copy = pltpu.make_async_copy(source, destination, local_sems.at[n, block])
            if start:
                copy.start()
            copies.append(copy)
        return copies

    def project(block):
        result = dot(held[block], weight_ref[...]).astype(jnp.bfloat16)
        ready[block] = result[:, :QUERY_WIDTH] * jnp.bfloat16(HEAD_DIM ** (-0.5))
        block_copies(block, True)
        key_ref[block] = result[:, QUERY_WIDTH : 2 * QUERY_WIDTH]
        value_ref[block] = result[:, 2 * QUERY_WIDTH :]

    project(team)

    def arrive(step, _):
        distance, side = step // 2 + 1, lax.rem(step, 2)
        for which in range(2):
            block = team - distance if which == 0 else team + distance
            there = (block >= 0) if which == 0 else (block < TEAMS)
            further = (team < TEAMS - 1) if which == 0 else (team > 0)

            @pl.when((side == which) & there)
            def _():
                hop(which, distance - 1, False).wait_recv()

                @pl.when(further)
                def _():
                    hop(which, distance)

                project(block)

        return 0

    lax.fori_loop(0, 2 * (TEAMS - 1), arrive, 0)
    for distance in range(TEAMS - 1):

        @pl.when((team < TEAMS - 1) & (team >= distance))
        def _():
            hop(0, distance, False).wait_send()

        @pl.when((team > 0) & (team + distance < TEAMS))
        def _():
            hop(1, distance, False).wait_send()

    for block in range(TEAMS):
        for copy in block_copies(block, False):
            copy.wait()


def project(tokens, gain, bias, weight, collective):
    lanes = lax.axis_size("seq") // TEAMS
    rows, width = tokens.shape
    inside = pl.BlockSpec(memory_space=pltpu.VMEM)
    anywhere = pl.BlockSpec(memory_space=pl.ANY)
    columns = 2 * QUERY_WIDTH + TEAM_WIDTH
    low = jnp.bfloat16
    dma = pltpu.SemaphoreType.DMA
    return pl.pallas_call(
        project_body,
        out_shape=[
            jax.ShapeDtypeStruct((TEAMS, rows, width), low),
            jax.ShapeDtypeStruct((width, columns), low),
            jax.ShapeDtypeStruct((lanes, TEAMS, rows, QUERY_WIDTH), low),
            jax.ShapeDtypeStruct((TEAMS, rows, QUERY_WIDTH), low),
            jax.ShapeDtypeStruct((TEAMS, rows, TEAM_WIDTH), low),
        ],
        in_specs=[inside, inside, inside, anywhere],
        out_specs=[anywhere, inside, anywhere, inside, inside],
        scratch_shapes=[
            pltpu.VMEM((TEAMS, rows, width), low),
            pltpu.VMEM((TEAMS, rows, QUERY_WIDTH), low),
            pltpu.VMEM((3, width, 256), low),
            pltpu.VMEM((2, width, 128), low),
            dma((2, TEAMS)),
            dma((2, TEAMS)),
            dma((TEAMS, lanes)),
            dma((TEAMS, lanes)),
            dma((5,)),
            dma((2, TEAMS)),
        ],
        compiler_params=pltpu.CompilerParams(
            collective_id=collective, has_side_effects=True, vmem_limit_bytes=VMEM_BYTES
        ),
    )(tokens, gain, bias, weight)


def fold(tile):
    return jnp.sum(tile.reshape(tile.shape[0] // 8, 8, tile.shape[1]), axis=0)


def attend_body(
    length_ref,
    threshold_ref,
    q_ref,
    kk_ref,
    vv_ref,
    out_ref,
    mass_ref,
    carried_ref,
    excess_ref,
    key_heads,
    value_rows,
    running,
    logits,
    out_all,
    mass_all,
    lane_out,
    lane_mass,
    joined_out,
    joined_mass,
    home_out,
    home_mass,
    lane_send,
    lane_recv,
    home_send,
    home_recv,
    *,
    blocks,
    rows,
):
    lanes = blocks // TEAMS
    me = lax.axis_index("seq")
    team, lane = me // lanes, lax.rem(me, lanes)
    i = pl.program_id(0)
    scale = select_scale / (blocks * rows)
    key_iota = lax.broadcasted_iota(jnp.int32, (rows, rows), 0)
    query_iota = lax.broadcasted_iota(jnp.int32, (rows, rows), 1)

    def part_copies(j, start):
        z, owner = j // lanes, lax.rem(j, lanes)
        return [
            push(
                source.at[j],
                destination.at[z, lane],
                lane_send.at[n, j],
                lane_recv.at[n, z, lane],
                {"seq": team * lanes + owner},
                start,
            )
            for n, (source, destination) in enumerate(
                ((out_all, lane_out), (mass_all, lane_mass))
            )
        ]

    def home_copies(z, start):
        return [
            push(
                source.at[z],
                destination.at[team],
                home_send.at[n, z],
                home_recv.at[n, team],
                {"seq": z * lanes + lane},
                start,
            )
            for n, (source, destination) in enumerate(
                ((joined_out, home_out), (joined_mass, home_mass))
            )
        ]

    def join(z):
        for k in range(1, lanes):
            other = lax.rem(lane + k, lanes)
            for n, buffer in enumerate((lane_out, lane_mass)):
                pltpu.make_async_copy(
                    buffer.at[z, other], buffer.at[z, other], lane_recv.at[n, z, other]
                ).wait()
        masses = [lane_mass[z, p] for p in range(lanes)]
        peak = masses[0]
        for p in range(1, lanes):
            peak = jnp.maximum(peak, masses[p])
        shares = [jnp.exp(mass - peak) for mass in masses]
        whole = shares[0]
        for p in range(1, lanes):
            whole = whole + shares[p]
        joined_mass[z] = peak + jnp.log(whole)
        inverse = 1.0 / whole
        for h in range(TEAM_HEADS):
            span = slice(h * HEAD_DIM, (h + 1) * HEAD_DIM)
            mixed = None
            for p in range(lanes):
                share = (shares[p] * inverse)[h : h + 1, :]
                part = lane_out[z, p, span, :].astype(jnp.float32) * share
                mixed = part if p == 0 else mixed + part
            joined_out[z, span, :] = mixed.astype(jnp.bfloat16)

        @pl.when(team != z)
        def _():
            home_copies(z, True)

        @pl.when(team == z)
        def _():
            home_out[team] = joined_out[z]
            home_mass[team] = joined_mass[z]

    @pl.when(i == 0)
    def _():
        greet(["team", "lane"])
        running[...] = jnp.zeros_like(running)
        excess_ref[...] = jnp.zeros_like(excess_ref)
        for z in range(TEAMS):
            for h in range(TEAM_HEADS):
                key_heads[h, z] = kk_ref[z, :, h * HEAD_DIM : (h + 1) * HEAD_DIM]
            first = kk_ref[z, :, TEAM_WIDTH:]
            if z == 0:
                slot = lax.broadcasted_iota(jnp.int32, first.shape, 0) + lane * rows
                first = jnp.where(slot >= 1, first, jnp.zeros_like(first))
            key_heads[TEAM_HEADS, z] = first
            value_rows[z] = vv_ref[z].T

    active = jnp.where(i >= lane, (i - lane) // lanes + 1, 0)
    threshold = threshold_ref[0]

    @pl.when(active == 0)
    def _():
        out_all[i] = jnp.zeros((TEAM_WIDTH, rows), jnp.bfloat16)
        mass_all[i] = jnp.full((8, rows), negative, jnp.float32)

    def work(count):
        q_rows = q_ref[0, 0].T
        heads = [q_rows[h * HEAD_DIM : (h + 1) * HEAD_DIM] for h in range(TEAM_HEADS + 1)]
        earlier = jnp.where(key_iota < query_iota, scale, 0.0).astype(jnp.bfloat16)
        every = jnp.full((rows, rows), scale, jnp.bfloat16)
        last = ((count - 1) * lanes + lane) * rows + key_iota
        query_pos = i * rows + query_iota
        peaks = [None] * TEAM_HEADS
        for z in range(count):
            first = jnp.maximum(dot(key_heads[TEAM_HEADS, z], heads[TEAM_HEADS]), 0.0)
            if z == count - 1:
                first = jnp.where(last < query_pos, first, 0.0)
            first = first.astype(jnp.bfloat16)
            carried = running[z] + dot(first, earlier)
            running[z] = running[z] + dot(first, every)

            if z == count - 1:
                carried = jnp.where(last <= query_pos, carried, -negative)
            carried_ref[0, z] = carried
            for h in range(TEAM_HEADS):
                logit = dot(key_heads[h, z], heads[h]) - carried
                logits[h, z] = logit
                peak = jnp.max(logit.reshape(rows // 8, 8, rows), axis=0)
                peaks[h] = peak if z == 0 else jnp.maximum(peaks[h], peak)
        mass_all[i] = jnp.zeros((8, rows), jnp.float32)
        for h in range(TEAM_HEADS):
            peak = jnp.max(peaks[h], axis=0, keepdims=True)
            mass, mixed = None, None
            for z in range(count):
                terms = jnp.exp(logits[h, z] - peak)
                part = fold(terms)
                values = value_rows[z, h * HEAD_DIM : (h + 1) * HEAD_DIM, :]
                product = dot(values, terms.astype(jnp.bfloat16))
                mass = part if z == 0 else mass + part
                mixed = product if z == 0 else mixed + product
            mass = jnp.sum(mass, axis=0, keepdims=True)
            out_all[i, h * HEAD_DIM : (h + 1) * HEAD_DIM, :] = (mixed * (1.0 / mass)).astype(
                jnp.bfloat16
            )
            mass_all[i, h : h + 1, :] = peak + jnp.log(mass)

        @pl.when(lax.rem(i, TEAMS) == team)
        def _():
            total = None
            for z in range(count):
                carried = carried_ref[0, z]
                if z == count - 1:
                    carried = jnp.where(last < query_pos, carried, 0.0)
                part = fold(jnp.clip(carried - threshold, 0.0, 1.0))
                total = part if z == 0 else total + part
            valid = i * rows + lax.broadcasted_iota(jnp.int32, (8, rows), 1) < length_ref[0]
            excess_ref[...] += jnp.where(valid, total, 0.0)

    for count in range(1, TEAMS + 1):
        pl.when(active == count)(functools.partial(work, count))

    @pl.when(lax.rem(i, lanes) != lane)
    def _():
        part_copies(i, True)

    @pl.when(lax.rem(i, lanes) == lane)
    def _():
        lane_out[i // lanes, lane] = out_all[i]
        lane_mass[i // lanes, lane] = mass_all[i]

    for z in range(TEAMS - 1):
        pl.when(i == (z + 1) * lanes + 1)(functools.partial(join, z))

    @pl.when(i == blocks - 1)
    def _():
        join(TEAMS - 1)

        def drain(j, _):
            @pl.when(lax.rem(j, lanes) != lane)
            def _():
                for copy in part_copies(j, False):
                    copy.wait_send()

            return 0

        lax.fori_loop(0, blocks, drain, 0)
        for z in range(TEAMS):

            @pl.when(team != z)
            def _():
                for copy in home_copies(z, False):
                    copy.wait_send()
                for n, buffer in enumerate((home_out, home_mass)):
                    pltpu.make_async_copy(
                        buffer.at[z], buffer.at[z], home_recv.at[n, z]
                    ).wait()

        out_ref[...] = home_out[...]
        mass_ref[...] = home_mass[...]

def attend(length, threshold, queries, keys, values, blocks, rows, collective):
    lanes = blocks // TEAMS
    smem = pl.BlockSpec(memory_space=pltpu.SMEM)
    whole = pl.BlockSpec((TEAMS, rows, QUERY_WIDTH), lambda i: (0, 0, 0))
    return pl.pallas_call(
        functools.partial(attend_body, blocks=blocks, rows=rows),
        grid=(blocks,),
        in_specs=[
            smem,
            smem,
            pl.BlockSpec(
                (1, 1, rows, QUERY_WIDTH), lambda i: (lax.rem(i, lanes), i // lanes, 0, 0)
            ),
            whole,
            pl.BlockSpec((TEAMS, rows, TEAM_WIDTH), lambda i: (0, 0, 0)),
        ],
        out_specs=[
            pl.BlockSpec((TEAMS, TEAM_WIDTH, rows), lambda i: (0, 0, 0)),
            pl.BlockSpec((TEAMS, 8, rows), lambda i: (0, 0, 0)),
            pl.BlockSpec((1, TEAMS, rows, rows), lambda i: (i, 0, 0, 0)),
            pl.BlockSpec((8, rows), lambda i: (0, 0)),
        ],
        out_shape=[
            jax.ShapeDtypeStruct((TEAMS, TEAM_WIDTH, rows), jnp.bfloat16),
            jax.ShapeDtypeStruct((TEAMS, 8, rows), jnp.float32),
            jax.ShapeDtypeStruct((blocks, TEAMS, rows, rows), jnp.float32),
            jax.ShapeDtypeStruct((8, rows), jnp.float32),
        ],
        scratch_shapes=[
            pltpu.VMEM((TEAM_HEADS + 1, TEAMS, rows, HEAD_DIM), jnp.bfloat16),
            pltpu.VMEM((TEAMS, TEAM_WIDTH, rows), jnp.bfloat16),
            pltpu.VMEM((TEAMS, rows, rows), jnp.float32),
            pltpu.VMEM((TEAM_HEADS, TEAMS, rows, rows), jnp.float32),
            pltpu.VMEM((blocks, TEAM_WIDTH, rows), jnp.bfloat16),
            pltpu.VMEM((blocks, 8, rows), jnp.float32),
            pltpu.VMEM((TEAMS, lanes, TEAM_WIDTH, rows), jnp.bfloat16),
            pltpu.VMEM((TEAMS, lanes, 8, rows), jnp.float32),
            pltpu.VMEM((TEAMS, TEAM_WIDTH, rows), jnp.bfloat16),
            pltpu.VMEM((TEAMS, 8, rows), jnp.float32),
            pltpu.VMEM((TEAMS, TEAM_WIDTH, rows), jnp.bfloat16),
            pltpu.VMEM((TEAMS, 8, rows), jnp.float32),
            pltpu.SemaphoreType.DMA((2, blocks)),
            pltpu.SemaphoreType.DMA((2, TEAMS, lanes)),
            pltpu.SemaphoreType.DMA((2, TEAMS)),
            pltpu.SemaphoreType.DMA((2, TEAMS)),
        ],
        compiler_params=pltpu.CompilerParams(
            collective_id=collective, has_side_effects=True, vmem_limit_bytes=VMEM_BYTES
        ),
    )(length, threshold, queries, keys, values)


reduce_plan = [("lane", "second"), ("team", "spread"), ("team", "spread")]


def added(parts):
    total = parts[0].astype(jnp.float32)
    for part in parts[1:]:
        total = total + part.astype(jnp.float32)
    return total.astype(jnp.bfloat16)


def attend_back_body(
    q_ref,
    grad_ref,
    stat_ref,
    carried_ref,
    kk_ref,
    vv_ref,
    *refs,
    blocks,
    rows,
):
    plan = reduce_plan
    sources, refs = refs[:3], refs[3:]
    (query_grad_ref, key_grad_ref, value_grad_ref), reduced, refs = refs[:3], refs[3:6], refs[6:]
    key_heads, key_rows, value_heads, running, key_sum, value_sum = refs[:6]
    grad_all, stat_all, grad_send, grad_recv, send, receive, local = refs[6:13]
    targets = refs[13:]
    lanes = blocks // TEAMS
    me = lax.axis_index("seq")
    team, lane = me // lanes, lax.rem(me, lanes)
    step = pl.program_id(0)
    i = blocks - 1 - step
    scale = select_scale / (blocks * rows)
    span = [slice(h * HEAD_DIM, (h + 1) * HEAD_DIM) for h in range(TEAM_HEADS + 1)]
    key_iota = lax.broadcasted_iota(jnp.int32, (rows, rows), 0)
    query_iota = lax.broadcasted_iota(jnp.int32, (rows, rows), 1)

    place, owner = i // lanes, lax.rem(i, lanes)

    def grad_copies(z, start):
        return [
            push(
                buffer.at[lane, z],
                buffer.at[lane, z],
                grad_send.at[n, z, k],
                grad_recv.at[n, z, lane],
                {"seq": team * lanes + lax.rem(lane + k, lanes)},
                start,
            )
            for k in range(1, lanes)
            for n, buffer in enumerate((grad_all, stat_all))
        ]

    def own_copy(n):
        scope, kind = plan[n]
        mine = peers_of(scope)[0]
        return pltpu.make_async_copy(
            part_of(kind, sources[n], mine), targets[n].at[mine], local.at[n]
        )

    def plan_copies(scope, start):
        chosen = [n for n in range(len(plan)) if plan[n][0] == scope]
        copies = []
        for n in chosen:
            copies += remote_copies(
                plan[n : n + 1],
                sources[n : n + 1],
                targets[n : n + 1],
                send.at[n : n + 1],
                receive.at[n : n + 1],
                start,
            )
        return copies

    @pl.when(step == 0)
    def _():
        greet(["team", "lane"])
        grad_all[lane] = grad_ref[...]
        stat_all[lane] = stat_ref[...]
        for z in reversed(range(TEAMS)):
            grad_copies(z, True)
        plan_copies("lane", True)
        for n in range(len(plan)):
            own_copy(n).start()
        running[...] = jnp.zeros_like(running)
        key_sum[...] = jnp.zeros_like(key_sum)
        value_sum[...] = jnp.zeros_like(value_sum)
        for z in range(TEAMS):
            for h in range(TEAM_HEADS + 1):
                key_heads[h, z] = kk_ref[z, :, span[h]]
            for h in range(TEAM_HEADS):
                value_heads[h, z] = vv_ref[z, :, span[h]]
            key_rows[z] = kk_ref[z].T
        first = kk_ref[0, :, span[TEAM_HEADS]]
        slot = lax.broadcasted_iota(jnp.int32, first.shape, 0) + lane * rows
        key_heads[TEAM_HEADS, 0] = jnp.where(slot >= 1, first, jnp.zeros_like(first))

    @pl.when(step == 2)
    def _():
        plan_copies("team", True)

    @pl.when(owner != lane)
    def _():
        for n, buffer in enumerate((grad_all, stat_all)):
            at = buffer.at[owner, place]
            pltpu.make_async_copy(at, at, grad_recv.at[n, place, owner]).wait()

    active = jnp.where(i >= lane, (i - lane) // lanes + 1, 0)

    @pl.when(active == 0)
    def _():
        query_grad_ref[...] = jnp.zeros_like(query_grad_ref)

    def work(count):
        q_rows = q_ref[0, 0].T
        grad_rows = grad_all[owner, place].T
        q_row = [q_rows[span[h]] for h in range(TEAM_HEADS + 1)]
        q_col = [q_ref[0, 0, :, span[h]] for h in range(TEAM_HEADS + 1)]
        grad_row = [grad_rows[span[h]] for h in range(TEAM_HEADS)]
        grad_col = [grad_all[owner, place, :, span[h]] for h in range(TEAM_HEADS)]
        mass = [stat_all[owner, place, h : h + 1, :] for h in range(TEAM_HEADS)]
        inner = [stat_all[owner, place, TEAM_HEADS + h : TEAM_HEADS + h + 1, :] for h in range(TEAM_HEADS)]
        later = jnp.where(key_iota > query_iota, -scale, 0.0).astype(jnp.bfloat16)
        every = jnp.full((rows, rows), -scale, jnp.bfloat16)
        last = ((count - 1) * lanes + lane) * rows + key_iota
        query_pos = i * rows + query_iota
        lows = [[] for _ in range(TEAM_HEADS + 1)]
        totals = [None] * count
        for h in range(TEAM_HEADS):
            for z in range(count):
                probs = jnp.exp(dot(key_heads[h, z], q_row[h]) - carried_ref[0, z] - mass[h])
                value_sum[h, z] += dot(probs.astype(jnp.bfloat16), grad_col[h])
                grad_logit = probs * (dot(value_heads[h, z], grad_row[h]) - inner[h])
                totals[z] = grad_logit if h == 0 else totals[z] + grad_logit
                low = grad_logit.astype(jnp.bfloat16)
                key_sum[h, z] += dot(low, q_col[h])
                lows[h].append(low)
        for z in range(count):
            total = totals[z].astype(jnp.bfloat16)
            select_grad = running[z] + dot(total, later)
            running[z] = running[z] + dot(total, every)
            first = dot(key_heads[TEAM_HEADS, z], q_row[TEAM_HEADS])
            live = first > 0.0
            if z == count - 1:
                live = live & (last < query_pos)
            low = jnp.where(live, select_grad, 0.0).astype(jnp.bfloat16)
            key_sum[TEAM_HEADS, z] += dot(low, q_col[TEAM_HEADS])
            lows[TEAM_HEADS].append(low)
        for h in range(TEAM_HEADS + 1):
            left = jnp.concatenate([key_rows[z, span[h], :] for z in range(count)], axis=1)
            result = dot(left, jnp.concatenate(lows[h], axis=0))
            query_grad_ref[0, 0, span[h], :] = result.astype(jnp.bfloat16)

    for count in range(1, TEAMS + 1):
        pl.when(active == count)(functools.partial(work, count))

    @pl.when(step == blocks - 1)
    def _():
        for h in range(TEAM_HEADS + 1):
            key_grad_ref[:, :, span[h]] = key_sum[h].astype(jnp.bfloat16)
        for h in range(TEAM_HEADS):
            value_grad_ref[:, :, span[h]] = value_sum[h].astype(jnp.bfloat16)
        for z in range(TEAMS):
            for copy in grad_copies(z, False):
                copy.wait_send()
        for n in range(len(plan)):
            own_copy(n).wait()
        for scope in ("lane", "team"):
            for copy in plan_copies(scope, False):
                copy.wait()
        for n in range(len(plan)):
            for j in range(reduced[n].shape[0]):
                reduced[n][j] = added([targets[n][k, j] for k in range(targets[n].shape[0])])


def attend_back(queries, grads, stats, carried, keys, values, halves, blocks, rows, collective):
    lanes = blocks // TEAMS
    plan = reduce_plan
    shapes = exchange_shapes(plan, halves)

    def place(step):
        i = blocks - 1 - step
        return (lax.rem(i, lanes), i // lanes, 0, 0)

    return pl.pallas_call(
        functools.partial(attend_back_body, blocks=blocks, rows=rows),
        grid=(blocks,),
        in_specs=[
            pl.BlockSpec((1, 1, rows, QUERY_WIDTH), place),
            pl.BlockSpec((TEAMS, rows, TEAM_WIDTH), lambda step: (0, 0, 0)),
            pl.BlockSpec((TEAMS, 8, rows), lambda step: (0, 0, 0)),
            pl.BlockSpec((1, TEAMS, rows, rows), lambda step: (blocks - 1 - step, 0, 0, 0)),
            pl.BlockSpec((TEAMS, rows, QUERY_WIDTH), lambda step: (0, 0, 0)),
            pl.BlockSpec((TEAMS, rows, TEAM_WIDTH), lambda step: (0, 0, 0)),
        ]
        + [pl.BlockSpec(memory_space=pl.ANY)] * 3,
        out_specs=[
            pl.BlockSpec((1, 1, QUERY_WIDTH, rows), place),
            pl.BlockSpec((TEAMS, rows, QUERY_WIDTH), lambda step: (0, 0, 0)),
            pl.BlockSpec((TEAMS, rows, TEAM_WIDTH), lambda step: (0, 0, 0)),
        ]
        + [pl.BlockSpec(x.shape[1:], lambda step: (0, 0, 0)) for x in shapes],
        out_shape=[
            jax.ShapeDtypeStruct((lanes, TEAMS, QUERY_WIDTH, rows), jnp.bfloat16),
            jax.ShapeDtypeStruct((TEAMS, rows, QUERY_WIDTH), jnp.bfloat16),
            jax.ShapeDtypeStruct((TEAMS, rows, TEAM_WIDTH), jnp.bfloat16),
        ]
        + [jax.ShapeDtypeStruct(x.shape[1:], x.dtype) for x in shapes],
        scratch_shapes=[
            pltpu.VMEM((TEAM_HEADS + 1, TEAMS, rows, HEAD_DIM), jnp.bfloat16),
            pltpu.VMEM((TEAMS, QUERY_WIDTH, rows), jnp.bfloat16),
            pltpu.VMEM((TEAM_HEADS, TEAMS, rows, HEAD_DIM), jnp.bfloat16),
            pltpu.VMEM((TEAMS, rows, rows), jnp.float32),
            pltpu.VMEM((TEAM_HEADS + 1, TEAMS, rows, HEAD_DIM), jnp.float32),
            pltpu.VMEM((TEAM_HEADS, TEAMS, rows, HEAD_DIM), jnp.float32),
            pltpu.VMEM((lanes, TEAMS, rows, TEAM_WIDTH), jnp.bfloat16),
            pltpu.VMEM((lanes, TEAMS, 8, rows), jnp.float32),
            pltpu.SemaphoreType.DMA((2, TEAMS, lanes)),
            pltpu.SemaphoreType.DMA((2, TEAMS, lanes)),
        ]
        + exchange_sems(plan)
        + [pltpu.VMEM(x.shape, x.dtype) for x in shapes],
        compiler_params=pltpu.CompilerParams(
            collective_id=collective, has_side_effects=True, vmem_limit_bytes=VMEM_BYTES
        ),
    )(queries, grads, stats, carried, keys, values, *halves)


def finish_body(
    query_ref,
    key_ref,
    value_ref,
    lane_ref,
    weight_ref,
    gain_ref,
    bias_ref,
    norm_ref,
    excess_ref,
    length_ref,
    down_in,
    up_in,
    out_in,
    whole_ref,
    home_ref,
    total_ref,
    whole_down,
    whole_up,
    whole_out,
    query_parts,
    down_parts,
    up_parts,
    out_parts,
    down_ref,
    up_ref,
    out_ref,
    turned,
    weight_rows,
    weight_grad,
    rows_sum,
    rows_ref,
    main_ref,
    vector_ref,
    core_main,
    send_main,
    lane_main,
    team_send_main,
    team_main,
    assembled,
    vectors,
    ready,
    core_sems,
    lane_sems,
    team_sems,
    home_sems,
    vector_sems,
    out_lane_sems,
    out_core_sems,
    local_sems,
    early_team,
    early_lane,
    early_core,
    early_local,
    first_send,
    first_recv,
    first_local,
):
    lanes = lax.axis_size("seq") // TEAMS
    me = lax.axis_index("seq")
    core = lax.axis_index("batch")
    team, lane = me // lanes, lax.rem(me, lanes)

    def lane_peer(k):
        other = lax.rem(lane + k, lanes)
        return other, {"seq": team * lanes + other}

    def team_peer(k):
        other = lax.rem(team + k, TEAMS)
        return other, {"seq": other * lanes + lane}

    sibling = {"batch": 1 - core}
    spans = (slice(0, QUERY_WIDTH), slice(QUERY_WIDTH, 2 * QUERY_WIDTH), slice(2 * QUERY_WIDTH, None))

    def turn():
        for span in spans:
            weight_rows[span, :] = weight_ref[:, span].T
        weight_grad[...] = jnp.zeros_like(weight_grad)

    greet(["core", "team", "lane"], turn)
    first_sources = (query_ref, down_in, up_in, out_in)
    first_targets = (query_parts, down_parts, up_parts, out_parts)
    first_plan = [("team", "spread"), ("team", "spread"), ("lane", "spread"), ("lane", "spread")]
    first_copies = [[], [], []]
    for n in (1, 2, 3, 0):
        mine = peers_of(first_plan[n][0])[0]
        own = pltpu.make_async_copy(first_sources[n].at[mine], first_targets[n].at[mine], first_local.at[n])
        own.start()
        group = (2, 0, 1, 1)[n]
        first_copies[group].append(own)
        first_copies[group] += remote_copies(
            first_plan[n : n + 1],
            first_sources[n : n + 1],
            first_targets[n : n + 1],
            first_send.at[n : n + 1],
            first_recv.at[n : n + 1],
        )
    def place(n, p, t, part=None):
        if n == 0:
            ref, start, wide = whole_down.at[core, p, t], 0, whole_down.shape[4]
        else:
            ref = (None, whole_up, whole_out)[n]
            wide = ref.shape[3] // 2
            ref, start = ref.at[p, t], core * wide
        cut = (wide // 128 + 1) // 2 * 128
        if part is not None:
            start, wide = ((start, cut), (start + cut, wide - cut))[part]
        return ref.at[:, pl.ds(pl.multiple_of(start, 128), wide)]

    square = lanes == 4
    if square:
        across, along = lax.rem(lane, 2), lane // 2
        direct = [2 * along + 1 - across, 2 * (1 - along) + across]
        origins = direct
    else:
        direct = [lax.rem(lane + k, lanes) for k in range(1, lanes)]
        origins = [lax.rem(lane - k + lanes, lanes) for k in range(1, lanes)]
    corner = lanes - 1 - lane

    def lane_of(p):
        return {"seq": team * lanes + p}

    def landed(ref, sem):
        pltpu.make_async_copy(ref, ref, sem).wait()

    early = (down_ref, up_ref, out_ref)
    number = len(early)
    early_z = [[None] * TEAMS for _ in range(number)]
    early_kept = []

    def publish(n):
        for k in range(1, TEAMS):
            _, target = team_peer(k)
            sems = [early_team.at[side, n, k] for side in range(2)]
            early_z[n][k] = push(early[n], place(n, lane, team), *sems, target)
        copy = pltpu.make_async_copy(early[n], place(n, lane, team), early_local.at[n])
        copy.start()
        early_kept.append(copy)

    early_out = []
    early_sib = []

    def forward(j, chosen=(0, 1, 2)):
        t = lax.rem(team - j + TEAMS, TEAMS)
        for n in chosen:
            if j == 0:
                source = early[n]
            else:
                early_z[n][j].wait_recv()
                source = place(n, lane, t)
            target = place(n, lane, t)
            for m, p in enumerate(direct):
                sems = [early_lane.at[side, n, j, m] for side in range(2)]
                early_out.append(push(source, target, *sems, lane_of(p)))
            sems = [early_core.at[side, n, j, 0] for side in range(2)]
            early_sib.append(push(source, target, *sems, sibling))

    def relay(j):
        t = lax.rem(team - j + TEAMS, TEAMS)
        for n in range(number):
            for m, p in enumerate(origins):
                piece = place(n, p, t)
                landed(piece, early_lane.at[1, n, j, m])
                if square:
                    side = place(n, p, t, m)
                    sems = [early_lane.at[side_, n, j, 2 + m] for side_ in range(2)]
                    early_out.append(push(side, side, *sems, lane_of(direct[1 - m])))
                sems = [early_core.at[side_, n, j, 1 + m] for side_ in range(2)]
                early_sib.append(push(piece, piece, *sems, sibling))

    def settle(j):
        if not square:
            return
        t = lax.rem(team - j + TEAMS, TEAMS)
        for n in range(number):
            for m in range(2):
                landed(place(n, corner, t, m), early_lane.at[1, n, j, 2 + m])
            piece = place(n, corner, t)
            sems = [early_core.at[side, n, j, 3] for side in range(2)]
            early_sib.append(push(piece, piece, *sems, sibling))

    for copy in first_copies[0]:
        copy.wait()
    down_ref[...] = added([down_parts[k] for k in range(lanes)])
    publish(0)
    forward(0, (0,))

    def known(b, _):
        rows_low = lane_ref[b].T
        turned[b] = rows_low
        total = None
        for span, grads in ((spans[1], key_ref[b]), (spans[2], value_ref[b])):
            weight_grad[:, span] += dot(rows_low, grads)
            part = dot(grads, weight_rows[span, :])
            total = part if total is None else total + part
        rows_sum[b] = total
        return 0

    lax.fori_loop(0, TEAMS, known, 0)
    for copy in first_copies[1]:
        copy.wait()
    up_ref[...] = added([up_parts[k] for k in range(TEAMS)])
    out_ref[...] = added([out_parts[k] for k in range(TEAMS)])
    publish(1)
    publish(2)
    forward(0, (1, 2))
    for copy in first_copies[2]:
        copy.wait()
    gain = gain_ref[...][None, :]
    bias = bias_ref[...][None, :]

    def last(b, sums):
        query_rows = query_parts[0, b].astype(jnp.float32)
        for p in range(1, lanes):
            query_rows = query_rows + query_parts[p, b].astype(jnp.float32)
        grads = (query_rows * HEAD_DIM ** (-0.5)).astype(jnp.bfloat16).T
        weight_grad[:, spans[0]] += dot(turned[b], grads)
        total = rows_sum[b] + dot(grads, weight_rows[spans[0], :])
        rows_ref[b] = total.astype(jnp.bfloat16)
        shifted = lane_ref[b].astype(jnp.float32) - bias
        return (
            sums[0] + jnp.sum(total * shifted, axis=0, keepdims=True),
            sums[1] + jnp.sum(total, axis=0, keepdims=True),
        )

    nothing = jnp.zeros_like(gain)
    gain_sum, bias_sum = lax.fori_loop(0, TEAMS, last, (nothing, nothing))
    length = length_ref[0].astype(jnp.float32)
    pairs = (length - 1.0) * (length - 2.0) / (2.0 * TEAMS * lanes)
    excess = jnp.sum(jnp.sum(excess_ref[...], axis=0, keepdims=True), axis=1, keepdims=True)
    vector_ref[...] = jnp.zeros_like(vector_ref)
    vector_ref[0:1, :] = gain_sum / gain
    vector_ref[1:2, :] = bias_sum
    vector_ref[2:4, :] = norm_ref[...]
    vector_ref[4:5, :] = jnp.broadcast_to(excess, nothing.shape)
    vector_ref[5:6, :] = jnp.full(nothing.shape, pairs)
    depth = main_ref.shape[1]
    for chunk in range(2 * lanes):
        main_ref[chunk] = weight_grad[chunk * depth : (chunk + 1) * depth, :].astype(jnp.bfloat16)
    theirs = pl.ds((1 - core) * lanes, lanes)
    core_copies = [
        push(main_ref.at[theirs], core_main, core_sems.at[0, 0], core_sems.at[1, 0], sibling),
        push(vector_ref, vectors.at[0], vector_sems.at[0, 0], vector_sems.at[1, 0], sibling),
    ]
    for copy in core_copies:
        copy.wait()

    both = vector_ref[...] + vectors[0]
    vectors[1 + lane] = both
    ready[0] = both
    for j in range(lanes):
        send_main[j] = (
            main_ref[core * lanes + j].astype(jnp.float32) + core_main[j].astype(jnp.float32)
        ).astype(jnp.bfloat16)
    lane_copies = []
    for k in range(1, lanes):
        other, target = lane_peer(k)
        lane_copies += [
            push(send_main.at[other], lane_main.at[lane], lane_sems.at[0, 0, k], lane_sems.at[1, 0, k], target),
            push(ready.at[0], vectors.at[1 + lane], vector_sems.at[0, k], vector_sems.at[1, k], target),
        ]
    lane_main[lane] = send_main[lane]
    for copy in lane_copies:
        copy.wait()

    def total(ref, start, number):
        result = ref[start].astype(jnp.float32)
        for j in range(1, number):
            result = result + ref[start + j].astype(jnp.float32)
        return result

    whole_vector = total(vectors, 1, lanes)
    ready[1] = whole_vector
    vectors[1 + lanes + team] = whole_vector
    low_main = total(lane_main, 0, lanes).astype(jnp.bfloat16)
    team_send_main[...] = low_main
    team_main[team] = low_main
    team_copies = []
    for k in range(1, TEAMS):
        other, target = team_peer(k)
        at = lanes + k
        team_copies += [
            push(team_send_main, team_main.at[team], team_sems.at[0, 0, k], team_sems.at[1, 0, k], target),
            push(ready.at[1], vectors.at[1 + lanes + team], vector_sems.at[0, at], vector_sems.at[1, at], target),
        ]
    relay(0)
    home_copies = []
    for k in range(1, TEAMS):
        other, target = team_peer(k)
        home_copies.append(
            push(rows_ref.at[other], home_ref.at[team], home_sems.at[0, k], home_sems.at[1, k], target)
        )
    own = pltpu.make_async_copy(rows_ref.at[team], home_ref.at[team], local_sems.at[0])
    own.start()
    for j in range(1, TEAMS):
        forward(j)
        settle(j - 1)
        if j < TEAMS - 1:
            relay(j)
    for copy in team_copies:
        copy.wait()
    total_ref[...] = total(vectors, 1 + lanes, TEAMS)
    pieces = []
    for part in range(3):
        first = part * QUERY_WIDTH
        for g in range(TEAMS):
            piece = team_main[g, :, first : first + TEAM_WIDTH]
            if g == 0 and part < 2:
                more = piece[:, :HEAD_DIM].astype(jnp.float32)
                for other in range(TEAMS):
                    more = more + team_main[
                        other, :, first + TEAM_WIDTH : first + QUERY_WIDTH
                    ].astype(jnp.float32)
                pieces += [more.astype(jnp.bfloat16), piece[:, HEAD_DIM:]]
            else:
                pieces.append(piece)
    assembled[...] = jnp.concatenate(pieces, axis=1)

    def chunk_of(p, part=None):
        ref = whole_ref.at[core * lanes + p]
        half = whole_ref.shape[2] // 2
        return ref if part is None else ref.at[:, pl.ds(part * half, half)]

    out_copies, core_out = [], []
    for m, p in enumerate(direct):
        sems = [out_lane_sems.at[side, m] for side in range(2)]
        out_copies.append(push(assembled, chunk_of(lane), *sems, lane_of(p)))
    sems = [out_core_sems.at[side, 0] for side in range(2)]
    core_out.append(push(assembled, chunk_of(lane), *sems, sibling))
    kept = pltpu.make_async_copy(assembled, chunk_of(lane), local_sems.at[1])
    kept.start()
    relay(TEAMS - 1)
    for m, p in enumerate(origins):
        landed(chunk_of(p), out_lane_sems.at[1, m])
        if square:
            sems = [out_lane_sems.at[side, 2 + m] for side in range(2)]
            out_copies.append(push(chunk_of(p, m), chunk_of(p, m), *sems, lane_of(direct[1 - m])))
        sems = [out_core_sems.at[side, 1 + m] for side in range(2)]
        core_out.append(push(chunk_of(p), chunk_of(p), *sems, sibling))
    settle(TEAMS - 1)
    if square:
        for m in range(2):
            landed(chunk_of(corner, m), out_lane_sems.at[1, 2 + m])
        sems = [out_core_sems.at[side, 3] for side in range(2)]
        core_out.append(push(chunk_of(corner), chunk_of(corner), *sems, sibling))
    for copy in out_copies + early_out:
        copy.wait_send()
    for n in range(number):
        for k in range(1, TEAMS):
            early_z[n][k].wait_send()
    for copy in core_out + home_copies + early_sib + early_kept:
        copy.wait()
    own.wait()
    kept.wait()


def finish(
    queries, keys, values, lane_rows, weight, gain, bias, norm, excess, length, reduced, collective
):
    lanes = lax.axis_size("seq") // TEAMS
    width, columns = weight.shape
    rows = lane_rows.shape[1]
    vector = (8, width)
    chunks, depth = 2 * lanes, width // (2 * lanes)
    low = jnp.bfloat16
    dma = pltpu.SemaphoreType.DMA
    down, up, out = (x.shape[1:] for x in reduced)
    wholes = [
        (2, lanes, TEAMS) + down,
        (lanes, TEAMS, up[0], 2 * up[1]),
        (lanes, TEAMS, out[0], 2 * out[1]),
    ]
    anywhere = pl.BlockSpec(memory_space=pl.ANY)
    inside = pl.BlockSpec(memory_space=pltpu.VMEM)
    return pl.pallas_call(
        finish_body,
        out_shape=[
            jax.ShapeDtypeStruct((chunks, depth, 3 * width), low),
            jax.ShapeDtypeStruct(lane_rows.shape, low),
            jax.ShapeDtypeStruct(vector, jnp.float32),
        ]
        + [jax.ShapeDtypeStruct(shape, low) for shape in wholes],
        in_specs=[anywhere]
        + [inside] * 8
        + [pl.BlockSpec(memory_space=pltpu.SMEM)]
        + [anywhere] * 3,
        out_specs=[anywhere, anywhere, inside] + [anywhere] * 3,
        scratch_shapes=[
            pltpu.VMEM(queries.shape, low),
            pltpu.VMEM((lanes,) + down, low),
            pltpu.VMEM((TEAMS,) + up, low),
            pltpu.VMEM((TEAMS,) + out, low),
            pltpu.VMEM(down, low),
            pltpu.VMEM(up, low),
            pltpu.VMEM(out, low),
            pltpu.VMEM((TEAMS, width, rows), low),
            pltpu.VMEM((columns, width), low),
            pltpu.VMEM((width, columns), jnp.float32),
            pltpu.VMEM((TEAMS, rows, width), jnp.float32),
            pltpu.VMEM((TEAMS, rows, width), low),
            pltpu.VMEM((chunks, depth, columns), low),
            pltpu.VMEM(vector, jnp.float32),
            pltpu.VMEM((lanes, depth, columns), low),
            pltpu.VMEM((lanes, depth, columns), low),
            pltpu.VMEM((lanes, depth, columns), low),
            pltpu.VMEM((depth, columns), low),
            pltpu.VMEM((TEAMS, depth, columns), low),
            pltpu.VMEM((depth, 3 * width), low),
            pltpu.VMEM((1 + lanes + TEAMS,) + vector, jnp.float32),
            pltpu.VMEM((2,) + vector, jnp.float32),
            dma((2, 2)),
            dma((2, 2, lanes)),
            dma((2, 2, TEAMS)),
            dma((2, TEAMS)),
            dma((2, lanes + TEAMS)),
            dma((2, lanes)),
            dma((2, lanes)),
            dma((2,)),
            dma((2, 3, TEAMS)),
            dma((2, 3, TEAMS, lanes)),
            dma((2, 3, TEAMS, lanes)),
            dma((3,)),
            dma((4, max(lanes, TEAMS))),
            dma((4, max(lanes, TEAMS))),
            dma((4,)),
        ],
        compiler_params=pltpu.CompilerParams(
            collective_id=collective, has_side_effects=True, vmem_limit_bytes=VMEM_BYTES
        ),
    )(queries, keys, values, lane_rows, weight, gain, bias, norm, excess, length, *reduced)


def contract_cols(left, right):
    return lax.dot_general(left, right, (((1,), (1,)), ((), ())), preferred_element_type=jnp.float32)


def dense_body(
    length_ref,
    mixed_ref,
    mass_ref,
    tokens_ref,
    grad_ref,
    gain_ref,
    bias_ref,
    w_out_hbm,
    w_up_hbm,
    w_down_hbm,
    layer_ref,
    resid_ref,
    norm_ref,
    cols_ref,
    stats_ref,
    down_hbm,
    up_hbm,
    out_hbm,
    w_out,
    w_up,
    w_down,
    active,
    slope,
    top,
    normed,
    mixed,
    slant,
    active_other,
    slope_other,
    top_other,
    normed_other,
    mixed_other,
    slant_other,
    total,
    back,
    cols,
    stats,
    down_half,
    up_half,
    out_half,
    load_sems,
    core_sems,
    lane_sems,
    keep_sems,
    store_sems,
):
    rows, width = tokens_ref.shape
    hidden = w_up.shape[1]
    step = width
    count = lax.axis_size("seq")
    lanes = count // TEAMS
    me = lax.axis_index("seq")
    core = lax.axis_index("batch")
    team, lane = me // lanes, lax.rem(me, lanes)
    sibling = {"batch": 1 - core}
    loads = [
        pltpu.make_async_copy(source, target, load_sems.at[n])
        for n, (source, target) in enumerate(
            ((w_out_hbm, w_out), (w_up_hbm, w_up), (w_down_hbm, w_down))
        )
    ]
    for load in loads:
        load.start()

    def half_of(ref, which):
        half = ref.shape[1] // 2
        return ref.at[:, pl.ds(pl.multiple_of(which * half, 128), half)]

    pairs = (
        (active, active_other, True),
        (top, top_other, False),
        (normed, normed_other, False),
        (slope, slope_other, True),
        (mixed, mixed_other, False),
        (slant, slant_other, True),
    )

    def swap(n, start):
        source, target, halved = pairs[n]
        return push(
            half_of(source, 1 - core) if halved else source,
            target,
            core_sems.at[0, n],
            core_sems.at[1, n],
            sibling,
            start,
        )

    grad_top = grad_ref[...]
    valid = me * rows + lax.broadcasted_iota(jnp.int32, (rows, width), 0) < length_ref[0]
    mixed_rows = mixed_ref[...]

    def prepare():
        top[...] = grad_top.astype(jnp.bfloat16)
        mixed[...] = jnp.where(valid, mixed_rows.T, jnp.zeros((), jnp.bfloat16))
        loads[0].wait()
        total[...] = tokens_ref[...] + dot(mixed[...], w_out[...])

    greet(["core", "lane"], prepare)
    swap(1, True)
    swap(4, True)
    residual = total[...]
    row_mean = jnp.mean(residual, axis=1, keepdims=True)
    centred = residual - row_mean
    variance = jnp.mean(centred * centred, axis=1, keepdims=True)
    spread = lax.rsqrt(variance + epsilon)
    scaled = centred * spread
    gain = gain_ref[...][None, :]
    normed[...] = (scaled * gain + bias_ref[...][None, :]).astype(jnp.bfloat16)
    swap(2, True)
    back[...] = jnp.zeros_like(back)
    loads[1].wait()
    loads[2].wait()

    def chunk(c, _):
        at = pl.ds(pl.multiple_of(c * step, 128), step)
        up = w_up[:, at]
        down = w_down[at, :]
        u = dot(normed[...], up)
        squared = u * u
        bend = jnp.tanh(0.7978845608028654 * u * (1.0 + 0.044715 * squared))
        lift = 0.5 * (1.0 + bend)
        low = (u * lift).astype(jnp.bfloat16)
        active[:, at] = low
        turn = lift + (0.5 * 0.7978845608028654) * u * (1.0 - bend * bend) * (
            1.0 + (3.0 * 0.044715) * squared
        )
        grad_low = (contract_cols(top[...], down) * turn).astype(jnp.bfloat16)
        slope[:, at] = grad_low
        total[...] += dot(low, down)
        back[...] += contract_cols(grad_low, up)
        return 0

    lax.fori_loop(0, hidden // step, chunk, 0)
    swap(0, True)
    swap(3, True)
    layer_ref[...] = total[...]
    grad_normed = back[...]
    norm_ref[0:1, :] = jnp.sum(grad_normed * scaled, axis=0, keepdims=True)
    norm_ref[1:2, :] = jnp.sum(grad_normed, axis=0, keepdims=True)
    inner = grad_normed * gain
    resid = grad_top + spread * (
        inner
        - jnp.mean(inner, axis=1, keepdims=True)
        - scaled * jnp.mean(inner * scaled, axis=1, keepdims=True)
    )
    resid_ref[...] = resid
    slant[...] = resid.astype(jnp.bfloat16)
    swap(5, True)
    grad_mixed = contract_cols(slant[...], w_out[...]).astype(jnp.bfloat16)
    grad_mixed = jnp.where(valid, grad_mixed, jnp.zeros((), jnp.bfloat16))
    products = grad_mixed.T.astype(jnp.float32) * mixed_rows.astype(jnp.float32)
    for t in range(TEAMS):
        cols[t] = grad_mixed[:, t * TEAM_WIDTH : (t + 1) * TEAM_WIDTH]
        stats[t] = mass_ref[t]
        for h in range(TEAM_HEADS):
            first = t * TEAM_WIDTH + h * HEAD_DIM
            stats[t, TEAM_HEADS + h : TEAM_HEADS + h + 1, :] = jnp.sum(
                products[first : first + HEAD_DIM], axis=0, keepdims=True
            )
    copies = []
    for k in range(1, TEAMS):
        other = lax.rem(team + k, TEAMS)
        for n, (source, target) in enumerate(((cols, cols_ref), (stats, stats_ref))):
            copies.append(
                push(
                    source.at[other],
                    target.at[team],
                    lane_sems.at[0, n, k],
                    lane_sems.at[1, n, k],
                    {"seq": other * lanes + lane},
                )
            )
    for n, (source, target) in enumerate(((cols, cols_ref), (stats, stats_ref))):
        copy = pltpu.make_async_copy(source.at[team], target.at[team], keep_sems.at[n])
        copy.start()
        copies.append(copy)

    def pair_dot(left, left_other, right, right_other, at):
        return (
            dot(left[:, at].T, right[...]) + dot(left_other[:, at].T, right_other[...])
        ).astype(jnp.bfloat16)

    for n in range(len(pairs)):
        swap(n, False).wait()
    block = 384
    own_active = half_of(active, core)
    own_slope = half_of(slope, core)
    own_slant = half_of(slant, core)

    def down_rows(c, _):
        at = pl.ds(pl.multiple_of(c * block, 128), block)
        down_half[at, :] = pair_dot(own_active, active_other, top, top_other, at)
        return 0

    lax.fori_loop(0, down_half.shape[0] // block, down_rows, 0)
    stores = [pltpu.make_async_copy(down_half, down_hbm, store_sems.at[0])]
    stores[0].start()

    def up_rows(c, _):
        at = pl.ds(pl.multiple_of(c * block, 128), block)
        up_half[at, :] = pair_dot(normed, normed_other, own_slope, slope_other, at)
        out_half[at, :] = pair_dot(mixed, mixed_other, own_slant, slant_other, at)
        return 0

    lax.fori_loop(0, width // block, up_rows, 0)
    for n, (source, target) in enumerate(((up_half, up_hbm), (out_half, out_hbm))):
        copy = pltpu.make_async_copy(source, target, store_sems.at[1 + n])
        copy.start()
        stores.append(copy)
    for copy in copies + stores:
        copy.wait()


def dense(length, mixed, masses, tokens, grad, gain, bias, w_out, w_up, w_down, collective):
    rows, width = tokens.shape
    hidden = w_up.shape[1]
    low, full = jnp.bfloat16, jnp.float32
    inside = pl.BlockSpec(memory_space=pltpu.VMEM)
    anywhere = pl.BlockSpec(memory_space=pl.ANY)
    dma = pltpu.SemaphoreType.DMA
    half = hidden // 2
    return pl.pallas_call(
        dense_body,
        out_shape=[
            jax.ShapeDtypeStruct((rows, width), full),
            jax.ShapeDtypeStruct((rows, width), full),
            jax.ShapeDtypeStruct((2, width), full),
            jax.ShapeDtypeStruct((TEAMS, rows, TEAM_WIDTH), low),
            jax.ShapeDtypeStruct((TEAMS, 8, rows), full),
            jax.ShapeDtypeStruct((half, width), low),
            jax.ShapeDtypeStruct((width, half), low),
            jax.ShapeDtypeStruct((width, width // 2), low),
        ],
        in_specs=[pl.BlockSpec(memory_space=pltpu.SMEM)] + [inside] * 6 + [anywhere] * 3,
        out_specs=[inside] * 3 + [anywhere] * 5,
        scratch_shapes=[
            pltpu.VMEM((width, width), low),
            pltpu.VMEM((width, hidden), low),
            pltpu.VMEM((hidden, width), low),
            pltpu.VMEM((rows, hidden), low),
            pltpu.VMEM((rows, hidden), low),
            pltpu.VMEM((rows, width), low),
            pltpu.VMEM((rows, width), low),
            pltpu.VMEM((rows, width), low),
            pltpu.VMEM((rows, width), low),
            pltpu.VMEM((rows, half), low),
            pltpu.VMEM((rows, half), low),
            pltpu.VMEM((rows, width), low),
            pltpu.VMEM((rows, width), low),
            pltpu.VMEM((rows, width), low),
            pltpu.VMEM((rows, width // 2), low),
            pltpu.VMEM((rows, width), full),
            pltpu.VMEM((rows, width), full),
            pltpu.VMEM((TEAMS, rows, TEAM_WIDTH), low),
            pltpu.VMEM((TEAMS, 8, rows), full),
            pltpu.VMEM((half, width), low),
            pltpu.VMEM((width, half), low),
            pltpu.VMEM((width, width // 2), low),
            dma((3,)),
            dma((2, 6)),
            dma((2, 2, TEAMS)),
            dma((2,)),
            dma((3,)),
        ],
        compiler_params=pltpu.CompilerParams(
            collective_id=collective, has_side_effects=True, vmem_limit_bytes=VMEM_BYTES
        ),
    )(length, mixed, masses, tokens, grad, gain, bias, w_out, w_up, w_down)


def close_body(
    tokens_ref,
    gain_ref,
    resid_ref,
    home_ref,
    layer_ref,
    vector_ref,
    *refs,
):
    count = (len(refs) - 6) // 2
    weights, refs = refs[:count], refs[count:]
    grad_ref, layer_out, *refs = refs
    for source, target in zip(weights, refs[:count]):
        target[...] = source[...].astype(jnp.float32)
    layer_out[...] = layer_ref[...]
    tokens = tokens_ref[...]
    centred = tokens - jnp.mean(tokens, axis=1, keepdims=True)
    spread = lax.rsqrt(jnp.mean(centred * centred, axis=1, keepdims=True) + epsilon)
    scaled = centred * spread
    total = home_ref[0].astype(jnp.float32)
    for t in range(1, TEAMS):
        total = total + home_ref[t].astype(jnp.float32)
    inner = total * gain_ref[...][None, :]
    grad_ref[...] = resid_ref[...] + spread * (
        inner
        - jnp.mean(inner, axis=1, keepdims=True)
        - scaled * jnp.mean(inner * scaled, axis=1, keepdims=True)
    )

    @pl.when(pl.program_id(0) == 0)
    def _():
        for n in range(4):
            refs[count + n][...] = vector_ref[n]


def close(tokens, gain, resid, home, layer, vectors, weights):
    steps = 4
    rows, width = tokens.shape

    def band(x):
        return pl.BlockSpec((x.shape[0] // steps, x.shape[1]), lambda i: (i, 0))

    line = pl.BlockSpec((width,), lambda i: (0,))
    large = [tokens, layer] + weights
    return pl.pallas_call(
        close_body,
        grid=(steps,),
        in_specs=[
            band(tokens),
            line,
            band(resid),
            pl.BlockSpec((TEAMS, rows // steps, width), lambda i: (0, i, 0)),
            band(layer),
            pl.BlockSpec(vectors.shape, lambda i: (0, 0)),
        ]
        + [band(x) for x in weights],
        out_specs=[band(x) for x in large] + [line] * 4,
        out_shape=[jax.ShapeDtypeStruct(x.shape, jnp.float32) for x in large]
        + [jax.ShapeDtypeStruct((width,), jnp.float32)] * 4,
        compiler_params=pltpu.CompilerParams(vmem_limit_bytes=VMEM_BYTES),
    )(tokens, gain, resid, home, layer, vectors, *weights)


def per_device(
    block_input,
    ln1_gain,
    ln1_bias,
    w_qkv,
    w_out,
    ln2_gain,
    ln2_bias,
    w_up,
    w_down,
    length_draw,
    threshold_index,
    grad_out,
):
    rows = block_input.shape[1]
    width = block_input.shape[2]
    blocks = lax.axis_size("seq")
    lanes = blocks // TEAMS
    group_len = blocks * rows
    me = lax.axis_index("seq")
    team = me // lanes
    length = group_len - rows + 1 + length_draw % rows
    threshold = threshold_index.astype(jnp.float32) / 128.0
    tokens = block_input[0]
    grad_top = grad_out[0]

    lane_rows, team_weight, queries, keys, values = project(tokens, ln1_gain, ln1_bias, w_qkv, 0)

    head_out, masses, carried, excess = attend(
        length, threshold, queries, keys, values, blocks, rows, 1
    )
    layer_out, grad_resid, grad_ln2, grad_cols, stats, down_half, up_half, out_half = dense(
        length,
        head_out.reshape(width, rows),
        masses,
        tokens,
        grad_top,
        ln2_gain,
        ln2_bias,
        w_out,
        w_up,
        w_down,
        3,
    )
    halves = [x.reshape(lanes, TEAMS, -1, x.shape[1]) for x in (down_half, up_half, out_half)]
    query_grads, key_grads, value_grads, *halves = attend_back(
        queries, grad_cols, stats, carried, keys, values, halves, blocks, rows, 7
    )

    grad_w_qkv, home_rows, vectors, grad_w_down, grad_w_up, grad_w_out = finish(
        query_grads,
        key_grads,
        value_grads,
        lane_rows,
        team_weight,
        ln1_gain,
        ln1_bias,
        grad_ln2,
        excess,
        length,
        halves,
        6,
    )
    pruned_share = (vectors[4, 0] / vectors[5, 0]).reshape(1)
    grad_x, layer_out, grad_w_qkv, grad_w_out, grad_w_up, grad_w_down, *lines = close(
        tokens,
        ln1_gain,
        grad_resid,
        home_rows,
        layer_out,
        vectors,
        [
            grad_w_qkv.reshape(w_qkv.shape),
            grad_w_out.reshape(w_out.shape),
            grad_w_up.reshape(w_up.shape),
            grad_w_down.reshape(w_down.shape),
        ],
    )
    return (
        layer_out[None],
        grad_x[None],
        lines[0],
        lines[1],
        grad_w_qkv,
        grad_w_out,
        lines[2],
        lines[3],
        grad_w_up,
        grad_w_down,
        pruned_share,
    )


def solution(mesh):
    placed = (
        P("batch", "seq", None),
        P(),
        P(),
        P(),
        P(),
        P(),
        P(),
        P(),
        P(),
        P("batch"),
        P(),
        P("batch", "seq", None),
    )
    return jax.shard_map(
        per_device,
        mesh=mesh,
        in_specs=placed,
        out_specs=(
            P("batch", "seq", None),
            P("batch", "seq", None),
            P(),
            P(),
            P(),
            P(),
            P(),
            P(),
            P(),
            P(),
            P(),
        ),
        check_vma=False,
    )
```
